128 devices in a mesh: ctx: 32 (over z_lo, x, y), wsh: 4 (over z_hi, core).
Axes of the slice: x: 4, y: 4, z: 4 (z_hi: 2, z_lo: 2; z = z_hi * 2 + z_lo), core: 2. Of those that a mesh axis runs over, the one named last changes fastest.
Arguments:
- tokens: bfloat16 [4, 64, 64, 1024], P('wsh', 'ctx'), may hold values from -6 to 6
- w_query: bfloat16 [1024, 1024], P('wsh'), may hold values from -0.1875 to 0.1875
- w_key: bfloat16 [1024, 1024], P('wsh'), may hold values from -0.1875 to 0.1875
- w_value: bfloat16 [1024, 1024], P('wsh'), may hold values from -0.1875 to 0.1875
- w_output: bfloat16 [1024, 1024], P('wsh'), may hold values from -0.5 to 0.5
- w_inner: bfloat16 [1024, 4096], P('wsh'), may hold values from -0.1875 to 0.1875
- w_outer: bfloat16 [4096, 1024], P('wsh'), may hold values from -0.09375 to 0.09375
- ln_gain: float32 [2, 1024], P(None, 'wsh'), may hold values from 0.1 to 1.9
- ln_bias: float32 [2, 1024], P(None, 'wsh'), may hold values from -2 to 2
- block_mask: int32 [4, 64, 64], P('wsh'), may hold values from 0 to 1, as said below
- block_pairs: int32 [32, 2], replicated, may hold values from 0 to 63, as said below
- cotangent: bfloat16 [4, 64, 64, 1024], P('wsh', 'ctx'), may hold values from -6 to 6
Outputs:
- out_tokens: float32 [4, 64, 64, 1024], P('wsh', 'ctx')
- grad_tokens: float32 [4, 64, 64, 1024], P('wsh', 'ctx')
- grad_query: float32 [1024, 1024], P('wsh')
- grad_key: float32 [1024, 1024], P('wsh')
- grad_value: float32 [1024, 1024], P('wsh')
- grad_output: float32 [1024, 1024], P('wsh')
- grad_inner: float32 [1024, 4096], P('wsh')
- grad_outer: float32 [4096, 1024], P('wsh')
- grad_gain: float32 [2, 1024], P(None, 'wsh')
- grad_bias: float32 [2, 1024], P(None, 'wsh')
The draws below stay inside these ranges and needn't reach their ends.
Inputs may be any that keep to these rules, and one draw needn't show every extreme that they name: block_mask[b, i, j] is 0 for j > i and 1 for j == i. `block_pairs`: row c is the pair of blocks c' and 63 - c' in either order; every number of 0 to 63 appears once.
All inputs are finite; a program needn't handle non-finite values.
Results may differ from the reference program's by a relative error of at most 0.04.
Values may be sent and summed in bfloat16 or wider, within the bound.
A program may use at most 192 MiB of HBM per device.

```python
import math
import jax
import jax.numpy as jnp
from jax import lax

D = 1024
H = 16
HD = 64
FF = 4096
BLK = 64
SEQS = 4
NB = 64
LEN = 4096
N_CTX = 32


def draw_block_mask(key, part):
    key = jax.random.fold_in(key, 11)
    block_count = 2 * N_CTX
    coins = jax.random.randint(key, (SEQS, block_count, block_count), 0, 2)
    row_ids = jnp.arange(block_count, dtype=jnp.int32)[:, None]
    col_ids = jnp.arange(block_count, dtype=jnp.int32)[None, :]
    forced = jnp.where(col_ids == row_ids, 1, coins)
    return jnp.where(col_ids <= row_ids, forced, 0).astype(jnp.int32)


def draw_block_pairs(key, part):
    key = jax.random.fold_in(key, 23)
    shuffled = jax.random.permutation(jax.random.fold_in(key, 1), N_CTX).astype(jnp.int32)
    flipped = jax.random.randint(jax.random.fold_in(key, 2), (N_CTX,), 0, 2)
    upper_block = 2 * N_CTX - 1 - shuffled
    first_block = jnp.where(flipped == 1, upper_block, shuffled)
    second_block = jnp.where(flipped == 1, shuffled, upper_block)
    return jnp.stack([first_block, second_block], axis=1).astype(jnp.int32)


def levels(own_key, dims, shards, least, top_value):
    def one(position, blocks):
        draws = jax.random.uniform(jax.random.fold_in(jax.random.fold_in(own_key, 6), position), (blocks,), jnp.float32, least / len(shards), top_value / len(shards))
        return jnp.repeat(jnp.exp(draws), dims[position] // blocks).reshape((-1,) + (1,) * (len(dims) - position - 1))

    level = one(*shards[0])
    for cut in shards[1:]:
        level = level * one(*cut)
    return level


def normal_values(own_key, dims, scale, limit, split=(), kind=jnp.bfloat16):
    entries = scale * jax.random.normal(own_key, dims, jnp.float32)
    if split:
        entries = entries * levels(own_key, dims, split, -0.22, 0.18)
    return jnp.clip(entries, -limit, limit).astype(kind)


def setup_inputs(seed: int = 0) -> dict:
    key_of = jax.random.split(jax.random.key(seed), 13)
    tokens = normal_values(key_of[0], (SEQS, NB, BLK, D), 1.0, 6.0, ((0, 4), (1, 32)))
    w_query = normal_values(key_of[1], (D, D), D ** -0.5, 0.1875, ((0, 4),))
    w_key = normal_values(key_of[2], (D, D), D ** -0.5, 0.1875, ((0, 4),))
    w_value = normal_values(key_of[3], (D, D), D ** -0.5, 0.1875, ((0, 4),))
    w_output = normal_values(key_of[4], (D, D), (D // 8) ** -0.5, 0.5, ((0, 4),))
    w_inner = normal_values(key_of[5], (D, FF), D ** -0.5, 0.1875, ((0, 4),))
    w_outer = normal_values(key_of[6], (FF, D), FF ** -0.5, 0.09375, ((0, 4),))
    ln_gain = jnp.clip(1.0 + 0.18 * jax.random.normal(key_of[7], (2, D), jnp.float32), 0.1, 1.9)
    ln_bias = normal_values(key_of[8], (2, D), 0.3, 2.0, ((1, 4),), jnp.float32)
    block_mask = draw_block_mask(jax.random.fold_in(key_of[12], 71), 0)
    block_pairs = draw_block_pairs(jax.random.fold_in(key_of[12], 71), 0)
    cotangent = normal_values(key_of[11], (SEQS, NB, BLK, D), 1.0, 6.0, ((0, 4), (1, 32)))
    return dict(tokens=tokens, w_query=w_query, w_key=w_key, w_value=w_value, w_output=w_output, w_inner=w_inner, w_outer=w_outer, ln_gain=ln_gain, ln_bias=ln_bias, block_mask=block_mask, block_pairs=block_pairs, cotangent=cotangent)


@jax.custom_vjp
def low(v):
    return lax.optimization_barrier(v.astype(jnp.bfloat16)).astype(jnp.float32)

@jax.custom_vjp
def low_back(v):
    return v

def low_keep(v):
    return (low(v), None)

def low_pass(kept, grad):
    return (grad,)

def back_keep(v):
    return (v, None)

def back_low(kept, grad):
    return (low(grad),)
low.defvjp(low_keep, low_pass)
low_back.defvjp(back_keep, back_low)

def matmul(left_mat, right_mat):
    return jnp.dot(left_mat, right_mat, precision=lax.Precision.HIGHEST, preferred_element_type=jnp.float32)

def layer_norm(values, gain_row, bias_row):
    center = values - lax.optimization_barrier(jnp.mean(values, axis=-1, keepdims=True))
    spread = lax.optimization_barrier(jnp.mean(center * center, axis=-1, keepdims=True))
    return center * lax.rsqrt(spread + 1e-05) * gain_row + bias_row

def reference(tokens, w_query, w_key, w_value, w_output, w_inner, w_outer, ln_gain, ln_bias, block_mask, block_pairs, cotangent):
    slot_order = block_pairs.reshape(-1).astype(jnp.int32)
    ordered = jnp.zeros((SEQS, NB, BLK, D), jnp.float32).at[:, slot_order].set(tokens.astype(jnp.float32))
    seq_rows = ordered.reshape(SEQS * LEN, D)
    cot_ordered = jnp.zeros((SEQS, NB, BLK, D), jnp.float32).at[:, slot_order].set(cotangent.astype(jnp.float32))
    cot_rows = cot_ordered.reshape(SEQS * LEN, D)
    query_rows = min(512, LEN)
    per_seq = LEN // query_rows
    score_scale = 1.0 / math.sqrt(HD)

    def attend_block(queries, keys_all, values_all, block_index):
        seq_index = block_index // per_seq
        first_row = block_index % per_seq * query_rows
        query_part = lax.dynamic_slice(queries, (seq_index, first_row, jnp.int32(0)), (1, query_rows, D))[0].reshape(query_rows, H, HD)
        key_part = lax.dynamic_index_in_dim(keys_all, seq_index, 0, keepdims=False).reshape(LEN, H, HD)
        value_part = lax.dynamic_index_in_dim(values_all, seq_index, 0, keepdims=False).reshape(LEN, H, HD)
        query_pos = first_row + jnp.arange(query_rows, dtype=jnp.int32)
        key_pos = jnp.arange(LEN, dtype=jnp.int32)
        seq_mask = lax.dynamic_index_in_dim(block_mask, seq_index, 0, keepdims=False)
        block_ok = seq_mask[query_pos // BLK][:, key_pos // BLK] > 0
        allowed = block_ok & (key_pos[None, :] <= query_pos[:, None])
        raw_scores = jnp.einsum('qhd,khd->hqk', query_part, key_part, precision=lax.Precision.HIGHEST) * score_scale
        scores = jnp.where(allowed[None], low_back(raw_scores), -1e+30)
        row_top = lax.optimization_barrier(jnp.max(scores, axis=-1, keepdims=True))
        exponent = jnp.exp(scores - row_top)
        attn_probs = exponent / lax.optimization_barrier(jnp.sum(exponent, axis=-1, keepdims=True))
        head_mix = jnp.einsum('hqk,khd->qhd', low(attn_probs), value_part, precision=lax.Precision.HIGHEST)
        return head_mix.reshape(query_rows, D)
    checked = jax.checkpoint(attend_block)

    def forward(x_rows, wq_full, wk_full, wv_full, wo_full, wi_full, wu_full, gains, biases):
        queries = low(low_back(matmul(x_rows, wq_full))).reshape(SEQS, LEN, D)
        keys_all = low(low_back(matmul(x_rows, wk_full))).reshape(SEQS, LEN, D)
        values_all = low(low_back(matmul(x_rows, wv_full))).reshape(SEQS, LEN, D)
        indices = jnp.arange(SEQS * per_seq, dtype=jnp.int32)
        attended = lax.map(lambda block_index: checked(queries, keys_all, values_all, block_index), indices)
        attended = low(low_back(attended.reshape(SEQS * LEN, D)))
        branch = low_back(matmul(attended, wo_full))
        normed = layer_norm(x_rows + branch, gains[0], biases[0])
        inner = low_back(matmul(low(normed), wi_full))
        activated = low(jax.nn.gelu(inner, approximate=False))
        outer = low_back(matmul(activated, wu_full))
        return layer_norm(normed + outer, gains[1], biases[1])
    result, pull_back = jax.vjp(forward, seq_rows, w_query.astype(jnp.float32), w_key.astype(jnp.float32), w_value.astype(jnp.float32), w_output.astype(jnp.float32), w_inner.astype(jnp.float32), w_outer.astype(jnp.float32), ln_gain.astype(jnp.float32), ln_bias.astype(jnp.float32))
    gradients = pull_back(cot_rows)
    grad_scale = 1.0 / math.sqrt(SEQS * LEN)

    def to_slots(seq_array):
        return seq_array.reshape(SEQS, NB, BLK, D)[:, slot_order]
    return (to_slots(result).astype(jnp.float32), to_slots(gradients[0]), gradients[1] * grad_scale, gradients[2] * grad_scale, gradients[3] * grad_scale, gradients[4] * grad_scale, gradients[5] * grad_scale, gradients[6] * grad_scale, gradients[7] * grad_scale, gradients[8] * grad_scale)
```

```python
import math

import jax
import jax.numpy as jnp
from jax import lax
from jax.experimental import pallas as pl
from jax.experimental.pallas import tpu as pltpu
from jax.sharding import PartitionSpec as P

MESH = pl.DeviceIdType.MESH
BF = jnp.bfloat16
F32 = jnp.float32
ANY = pl.BlockSpec(memory_space=pl.ANY)
VM = pl.BlockSpec(memory_space=pltpu.VMEM)
SM = pl.BlockSpec(memory_space=pltpu.SMEM)
DMA = pltpu.SemaphoreType.DMA
LIMIT = 56 * 1024 * 1024
EPS = 1e-05
NEG = -1e30


def shp(shape, dtype):
    return jax.ShapeDtypeStruct(shape, dtype)


def dot(a, b, dims=((1,), (0,))):
    return lax.dot_general(a, b, (dims, ((), ())), preferred_element_type=F32)


NN = ((1,), (0,))
NT = ((1,), (1,))
TN = ((0,), (0,))


def place():
    c = lax.axis_index("ctx")
    w = lax.axis_index("wsh")
    return c // 16, (c // 4) % 4, c % 4, w // 2, w % 2


def device(zl, x, y, zh, co):
    return {"ctx": zl * 16 + x * 4 + y, "wsh": zh * 2 + co}


def greet(peers):
    bar = pltpu.get_barrier_semaphore()
    for p in peers:
        pl.semaphore_signal(bar, inc=1, device_id=p, device_id_type=MESH)
    pl.semaphore_wait(bar, len(peers))


class Wire:
    def __init__(self, send, recv):
        self.send, self.recv, self.n = send, recv, 0

    def __call__(self, src, dst, peer):
        k = self.n
        self.n += 1
        copy = pltpu.make_async_remote_copy(
            src_ref=src, dst_ref=dst, send_sem=self.send.at[k], recv_sem=self.recv.at[k],
            device_id=peer, device_id_type=MESH,
        )
        copy.start()
        return copy


def gather_kernel(wq, wk, wv, x_ref, ln_ref, wall, xs, lnf, ss, rs, ls):
    zl, x, y, zh, co = place()
    me = zh * 2 + co
    other = (1 - zh) * 2 + co
    core = device(zl, x, y, zh, 1 - co)
    far = device(zl, x, y, 1 - zh, co)
    diag = device(zl, x, y, 1 - zh, 1 - co)
    xp = [device(zl, (x + s) % 4, y, zh, co) for s in (1, 2, 3)]
    yp = [device(zl, x, (y + s) % 4, zh, co) for s in (1, 2, 3)]
    greet([core, far, diag] + xp + yp)
    wire = Wire(ss, rs)
    ws = (wq, wk, wv)
    rows_a = pl.ds(pl.multiple_of(x * 32, 32), 32)
    rows_b = pl.ds(pl.multiple_of(128 + y * 32, 32), 32)
    first_a, first_b = [], []
    for m in range(3):
        first_a.append(wire(ws[m].at[rows_a], wall.at[me, m, rows_a], far))
        first_b.append(wire(ws[m].at[rows_b], wall.at[me, m, rows_b], far))
    rest = []
    for p, idx in ((core, zh * 2 + 1 - co), (far, other), (diag, (1 - zh) * 2 + 1 - co)):
        cols = pl.ds(pl.multiple_of(idx * 256, 256), 256)
        rest.append(wire(x_ref.at[:, cols], xs.at[me], p))
        rest.append(wire(ln_ref, lnf.at[me], p))
    for m in range(3):
        rest.append(wire(ws[m], wall.at[me, m], core))
    local = []
    for m in range(3):
        local.append(pltpu.make_async_copy(ws[m], wall.at[me, m], ls.at[m]))
    own = pl.ds(pl.multiple_of(me * 256, 256), 256)
    local.append(pltpu.make_async_copy(x_ref.at[:, own], xs.at[me], ls.at[3]))
    local.append(pltpu.make_async_copy(ln_ref, lnf.at[me], ls.at[4]))
    for c in local:
        c.start()
    for c in first_a:
        c.wait_recv()
    second = []
    for m in range(3):
        part = wall.at[other, m, rows_a]
        for p in xp:
            second.append(wire(part, part, p))
    for c in first_b:
        c.wait_recv()
    for m in range(3):
        part = wall.at[other, m, rows_b]
        for p in yp:
            second.append(wire(part, part, p))
    for c in second:
        c.wait_recv()
    last = [wire(wall.at[other, m], wall.at[other, m], core) for m in range(3)]
    for c in last:
        c.wait()
    for c in first_a + first_b + second:
        c.wait_send()
    for c in rest:
        c.wait()
    for c in local:
        c.wait()


def gather_weights(wq, wk, wv, tok, lnp):
    n = 6 + 6 + 3 + 18 + 3
    return pl.pallas_call(
        gather_kernel,
        out_shape=[shp((4, 3, 256, 1024), BF), shp((4, 128, 256), BF), shp((4, 8, 256), F32)],
        in_specs=[ANY] * 5,
        out_specs=[ANY] * 3,
        scratch_shapes=[DMA((n,)), DMA((n,)), DMA((5,))],
        compiler_params=pltpu.CompilerParams(collective_id=1, has_side_effects=True),
        name="gather_qkv",
    )(wq, wk, wv, tok, lnp)


def qkv_kernel(x_ref, w_ref, kv_ref, q_ref):
    x = x_ref[...]

    def proj(m):
        return dot(x, w_ref[:, m].reshape(1024, 128)).astype(BF)

    q = (proj(0).astype(F32) * 0.125).astype(BF)
    k = proj(1)
    v = proj(2)
    for u in range(2):
        lanes = slice(64 * u, 64 * u + 64)
        kv_ref[u] = jnp.concatenate([k[:, lanes], v[:, lanes]], axis=1)
        q_ref[u] = jnp.concatenate([q[:64, lanes], q[64:, lanes]], axis=1)


def project(tok, wall):
    return pl.pallas_call(
        qkv_kernel,
        grid=(8,),
        out_shape=[shp((16, 128, 128), BF), shp((16, 64, 128), BF)],
        in_specs=[
            pl.BlockSpec((128, 1024), lambda j: (0, 0)),
            pl.BlockSpec((4, 3, 256, 128), lambda j: (0, 0, 0, j)),
        ],
        out_specs=[
            pl.BlockSpec((2, 128, 128), lambda j: (j, 0, 0)),
            pl.BlockSpec((2, 64, 128), lambda j: (j, 0, 0)),
        ],
        compiler_params=pltpu.CompilerParams(vmem_limit_bytes=LIMIT),
        cost_estimate=pl.CostEstimate(flops=805306368, bytes_accessed=8 << 20, transcendentals=0),
        name="qkv",
    )(tok, wall)


def exchange(wide, narrow, collective):
    has = wide is not None
    n = 32 if has else 16

    def kernel(*refs):
        if has:
            wi, na, wo, no, sw, rw, sn, rn, ls = refs
        else:
            na, no, sn, rn, ls = refs
        me = lax.axis_index("ctx")
        zl = me // 16
        flat = me % 16
        bar = pltpu.get_barrier_semaphore()

        def peer(i):
            if has:
                return (me + i) % 32
            return zl * 16 + (flat + i) % 16

        def greet_one(i, carry):
            pl.semaphore_signal(bar, inc=1, device_id={"ctx": peer(i)}, device_id_type=MESH)
            return carry

        lax.fori_loop(1, n, greet_one, 0)
        pl.semaphore_wait(bar, n - 1)

        def narrow_copy(i):
            p = (flat + i) % 16
            return pltpu.make_async_remote_copy(
                src_ref=na.at[p], dst_ref=no.at[flat], send_sem=sn.at[i], recv_sem=rn.at[i],
                device_id={"ctx": zl * 16 + p}, device_id_type=MESH,
            )

        def wide_copy(i):
            p = (me + i) % 32
            src = p if wide.shape[0] == 32 else p % 16
            return pltpu.make_async_remote_copy(
                src_ref=wi.at[src], dst_ref=wo.at[me], send_sem=sw.at[i], recv_sem=rw.at[i],
                device_id={"ctx": p}, device_id_type=MESH,
            )

        def start(make):
            def one(i, carry):
                make(i).start()
                return carry
            return one

        def wait(make):
            def one(i, carry):
                make(i).wait()
                return carry
            return one

        if has:
            lax.fori_loop(1, 32, start(wide_copy), 0)
        lax.fori_loop(1, 16, start(narrow_copy), 0)
        local = [pltpu.make_async_copy(na.at[flat], no.at[flat], ls.at[0])]
        if has:
            own = me if wide.shape[0] == 32 else flat
            local.append(pltpu.make_async_copy(wi.at[own], wo.at[me], ls.at[1]))
        for c in local:
            c.start()
        for c in local:
            c.wait()
        if has:
            lax.fori_loop(1, 32, wait(wide_copy), 0)
        lax.fori_loop(1, 16, wait(narrow_copy), 0)

    sems = ([DMA((32,)), DMA((32,))] if has else []) + [DMA((16,)), DMA((16,)), DMA((2,))]
    outs = ([shp((32,) + wide.shape[1:], wide.dtype)] if has else []) + [shp(narrow.shape, narrow.dtype)]
    args = ([wide] if has else []) + [narrow]
    return pl.pallas_call(
        kernel,
        out_shape=outs,
        in_specs=[ANY] * len(args),
        out_specs=[ANY] * len(outs),
        scratch_shapes=sems,
        compiler_params=pltpu.CompilerParams(collective_id=collective, has_side_effects=True),
        name=f"exchange_{collective}",
    )(*args)


def attention_setup(blk, mask, kvr, qr, kvs, kaug, kvt, bias, qs, inv, order, oblk):
    first = (lax.axis_index("ctx") // 16) * 32

    def note(s, carry):
        inv[blk[s]] = s
        return carry

    lax.fori_loop(0, 64, note, 0)

    def pick(b, count):
        local = inv[b] - first
        order[count] = local
        oblk[count] = b
        mine = jnp.logical_and(local >= 0, local < 32)
        return count + mine.astype(jnp.int32)

    lax.fori_loop(0, 64, pick, 0)
    for s in range(64):
        at = pl.ds(pl.multiple_of(blk[s] * 64, 64), 64)
        kvs[at, :] = kvr[s // 2, (s % 2) * 64:(s % 2) * 64 + 64, :]
    for j in range(16):
        pair = qr[j]
        qs[2 * j] = pair[:, :64]
        qs[2 * j + 1] = pair[:, 64:]
    rows = lax.broadcasted_iota(jnp.int32, (512, 64), 0) // 64
    lanes = lax.broadcasted_iota(jnp.int32, (512, 64), 1)
    for c in range(8):
        part = kvs[512 * c:512 * c + 512, :]
        hot = jnp.where(rows + 8 * c == lanes, 1.0, 0.0).astype(BF)
        kaug[512 * c:512 * c + 512, :] = jnp.concatenate([part[:, :64], hot], axis=1)
        kvt[c] = part.astype(F32).T.astype(BF)
    qi = lax.broadcasted_iota(jnp.int32, (64, 64), 0)
    ki = lax.broadcasted_iota(jnp.int32, (64, 64), 1)
    bias[...] = jnp.where(jnp.logical_and(mask[0] != 0, ki < qi), 0.0, NEG)


def triangle():
    key = lax.broadcasted_iota(jnp.int32, (64, 256), 0)
    query = lax.broadcasted_iota(jnp.int32, (64, 256), 1) % 64
    return key <= query


def attend_kernel(blk, mask, kvr, qr, o_ref, ot_ref, lse_ref, kvs, kaug, kvt, bias, qs, qa, os, inv, order, oblk):
    attention_setup(blk, mask, kvr, qr, kvs, kaug, kvt, bias, qs, inv, order, oblk)

    def tile(g, carry):
        score, vals = [], []
        for u in range(4):
            i = oblk[4 * g + u]
            q = qs[order[4 * g + u]]
            row = jnp.broadcast_to(bias[pl.ds(i, 1), :], (64, 64)).astype(BF)
            qa[64 * u:64 * u + 64, :] = jnp.concatenate([q, row], axis=1)
            kv = kvs[pl.ds(pl.multiple_of(i * 64, 64), 64), :]
            score.append(dot(kv[:, :64], q, NT))
            vals.append(kv[:, 64:])
        s = jnp.where(triangle(), jnp.concatenate(score, axis=1), NEG)
        top = jnp.max(s, axis=0, keepdims=True)
        p = jnp.exp(s - top)
        total = jnp.sum(p, axis=0, keepdims=True)
        pb = p.astype(BF)
        mix = jnp.concatenate([dot(vals[u], pb[:, 64 * u:64 * u + 64], TN) for u in range(4)], axis=1)
        queries = qa[...]

        def chunk(c, state):
            top, total, mix = state
            keys = kaug[pl.ds(pl.multiple_of(c * 512, 512), 512), :]
            s = dot(keys, queries, NT)
            new = jnp.maximum(top, jnp.max(s, axis=0, keepdims=True))
            shrink = jnp.exp(top - new)
            p = jnp.exp(s - new)
            total = total * shrink + jnp.sum(p, axis=0, keepdims=True)
            mix = mix * shrink + dot(kvt[c, 64:, :], p.astype(BF))
            return new, total, mix

        chunks = (oblk[4 * g + 3] + 7) // 8
        top, total, mix = lax.fori_loop(0, chunks, chunk, (top, total, mix))
        out = mix / total
        ot_ref[g] = out
        lse_ref[g] = top + jnp.log(total)
        back = out.T.astype(BF)
        for u in range(4):
            os[order[4 * g + u]] = back[64 * u:64 * u + 64, :]
        return carry

    lax.fori_loop(0, 8, tile, 0)
    for j in range(16):
        o_ref[j] = jnp.concatenate([os[2 * j], os[2 * j + 1]], axis=1)


def attention_scratch():
    return [
        pltpu.VMEM((4096, 128), BF),
        pltpu.VMEM((4096, 128), BF),
        pltpu.VMEM((8, 128, 512), BF),
        pltpu.VMEM((64, 64), F32),
        pltpu.VMEM((32, 64, 64), BF),
        pltpu.VMEM((256, 128), BF),
        pltpu.VMEM((32, 64, 64), BF),
        pltpu.SMEM((64,), jnp.int32),
        pltpu.SMEM((72,), jnp.int32),
        pltpu.SMEM((72,), jnp.int32),
    ]


def attend(blk, mask, kvr, qr):
    return pl.pallas_call(
        attend_kernel,
        out_shape=[shp((16, 64, 128), BF), shp((8, 64, 256), F32), shp((8, 1, 256), F32)],
        in_specs=[SM, VM, VM, VM],
        out_specs=[VM] * 3,
        scratch_shapes=attention_scratch(),
        compiler_params=pltpu.CompilerParams(vmem_limit_bytes=LIMIT),
        cost_estimate=pl.CostEstimate(flops=10 << 30, bytes_accessed=32 << 20, transcendentals=4 << 20),
        name="attend",
    )(blk, mask, kvr, qr)


def attend_back_kernel(
    blk, mask, kvr, qr, dor, ot_ref, lse_ref, dkv_ref, dq_ref,
    kvs, kaug, kvt, bias, qs, qa, dqs, inv, order, oblk, dos, qz, dz, dkv,
):
    attention_setup(blk, mask, kvr, qr, kvs, kaug, kvt, bias, qs, inv, order, oblk)
    for j in range(16):
        pair = dor[j]
        dos[2 * j] = pair[:, :64]
        dos[2 * j + 1] = pair[:, 64:]
    dkv[...] = jnp.zeros_like(dkv)
    zero = jnp.zeros((64, 64), BF)

    def tile(g, carry):
        score, dprob, places, keys_own, q_own, d_own = [], [], [], [], [], []
        for u in range(4):
            i = oblk[4 * g + u]
            q = qs[order[4 * g + u]]
            do = dos[order[4 * g + u]]
            rows = slice(64 * u, 64 * u + 64)
            row = jnp.broadcast_to(bias[pl.ds(i, 1), :], (64, 64)).astype(BF)
            qa[rows, :] = jnp.concatenate([q, row], axis=1)
            qz[rows, :] = jnp.concatenate([q, zero], axis=1)
            dz[rows, :] = jnp.concatenate([zero, do], axis=1)
            at = pl.ds(pl.multiple_of(i * 64, 64), 64)
            kv = kvs[at, :]
            score.append(dot(kv[:, :64], q, NT))
            dprob.append(dot(kv[:, 64:], do, NT))
            places.append(at)
            keys_own.append(kv[:, :64])
            q_own.append(q)
            d_own.append(do)
        lse = lse_ref[g]
        queries = qa[...]
        qpad = qz[...]
        dpad = dz[...]
        dot_t = dpad[:, 64:].astype(F32).T
        delta = jnp.sum(ot_ref[g] * dot_t, axis=0, keepdims=True)
        s = jnp.where(triangle(), jnp.concatenate(score, axis=1), NEG)
        p = jnp.exp(s - lse)
        ds = (p * (jnp.concatenate(dprob, axis=1) - delta)).astype(BF)
        pb = p.astype(BF)
        dq = []
        for u in range(4):
            lanes = slice(64 * u, 64 * u + 64)
            grad = jnp.concatenate([dot(ds[:, lanes], q_own[u]), dot(pb[:, lanes], d_own[u])], axis=1)
            dkv[places[u], :] += grad
            dq.append(dot(keys_own[u], ds[:, lanes], TN))

        def chunk(c, dq):
            at = pl.ds(pl.multiple_of(c * 512, 512), 512)
            p = jnp.exp(dot(kaug[at, :], queries, NT) - lse)
            dp = dot(kvs[at, :], dpad, NT)
            ds = (p * (dp - delta)).astype(BF)
            dkv[at, :] += dot(ds, qpad) + dot(p.astype(BF), dpad)
            return dq + dot(kvt[c, :64, :], ds)

        chunks = (oblk[4 * g + 3] + 7) // 8
        dq = lax.fori_loop(0, chunks, chunk, jnp.concatenate(dq, axis=1))
        back = (dq * 0.125).T.astype(BF)
        for u in range(4):
            dqs[order[4 * g + u]] = back[64 * u:64 * u + 64, :]
        return carry

    lax.fori_loop(0, 8, tile, 0)
    for j in range(16):
        dq_ref[j] = jnp.concatenate([dqs[2 * j], dqs[2 * j + 1]], axis=1)
    for s in range(64):
        at = pl.ds(pl.multiple_of(blk[s] * 64, 64), 64)
        dkv_ref[s // 2, (s % 2) * 64:(s % 2) * 64 + 64, :] = dkv[at, :].astype(BF)


def attend_back(blk, mask, kvr, qr, dor, ot, lse):
    return pl.pallas_call(
        attend_back_kernel,
        out_shape=[shp((32, 128, 128), BF), shp((16, 64, 128), BF)],
        in_specs=[SM] + [VM] * 6,
        out_specs=[VM] * 2,
        scratch_shapes=attention_scratch()
        + [
            pltpu.VMEM((32, 64, 64), BF),
            pltpu.VMEM((256, 128), BF),
            pltpu.VMEM((256, 128), BF),
            pltpu.VMEM((4096, 128), F32),
        ],
        compiler_params=pltpu.CompilerParams(vmem_limit_bytes=LIMIT),
        cost_estimate=pl.CostEstimate(flops=25 << 30, bytes_accessed=64 << 20, transcendentals=4 << 20),
        name="attend_back",
    )(blk, mask, kvr, qr, dor, ot, lse)


def norm_parts(v):
    center = v - jnp.mean(v, axis=1, keepdims=True)
    r = lax.rsqrt(jnp.mean(center * center, axis=1, keepdims=True) + EPS)
    return center * r, r


def norm_back(e, gain, z, r):
    g = e * gain
    return r * (g - jnp.mean(g, axis=1, keepdims=True) - z * jnp.mean(g * z, axis=1, keepdims=True))


def middle_kernel(
    o_ref, x_ref, e_ref, ln_ref, a0, a1, a2, a3, u0, u1, u2, u3,
    y_ref, dr_ref, do_ref, zpay, cpay, l_ref, gb_ref,
    woi, wu, us, gs, dus, nl, ob, so, si, su,
):
    w = lax.axis_index("wsh")
    zh, co = w // 2, w % 2
    where = [w, zh * 2 + 1 - co, (1 - zh) * 2 + co, (1 - zh) * 2 + 1 - co]
    copies = [[], [], []]
    for r, (a, u) in enumerate(((a0, u0), (a1, u1), (a2, u2), (a3, u3))):
        rows = pl.ds(pl.multiple_of(where[r] * 256, 256), 256)
        copies[0].append(pltpu.make_async_copy(a.at[:, :1024], woi.at[rows, :1024], so.at[r]))
        copies[1].append(pltpu.make_async_copy(a.at[:, 1024:], woi.at[rows, 1024:], si.at[r]))
        rows = pl.ds(pl.multiple_of(where[r] * 1024, 1024), 1024)
        copies[2].append(pltpu.make_async_copy(u, wu.at[rows, :], su.at[r]))
    for group in copies:
        for c in group:
            c.start()

    ln = jnp.concatenate([ln_ref[k] for k in range(4)], axis=1)
    gain0, gain1, bias0, bias1 = (ln[k:k + 1, :] for k in range(4))
    for h in range(16):
        pair = o_ref[h]
        ob[:64, 64 * h:64 * h + 64] = pair[:, :64]
        ob[64:, 64 * h:64 * h + 64] = pair[:, 64:]
    for c in copies[0]:
        c.wait()
    z0, r0 = norm_parts(x_ref[...].astype(F32) + dot(ob[...], woi[:, :1024]))
    n1 = z0 * gain0 + bias0
    nl[...] = n1.astype(BF)
    for c in copies[1]:
        c.wait()

    half = math.sqrt(0.5)

    def up(c, carry):
        cols = pl.ds(pl.multiple_of(1024 + c * 512, 512), 512)
        u = dot(nl[...], woi[:, cols])
        us[c] = u
        gs[:, pl.ds(pl.multiple_of(c * 512, 512), 512)] = (0.5 * u * (1.0 + lax.erf(u * half))).astype(BF)
        return carry

    lax.fori_loop(0, 8, up, 0)
    for c in copies[2]:
        c.wait()

    def down(c, total):
        cols = pl.ds(pl.multiple_of(c * 512, 512), 512)
        return total + dot(gs[:, cols], wu[cols, :])

    r2 = lax.fori_loop(0, 8, down, n1)
    z1, r1 = norm_parts(r2)
    y_ref[...] = z1 * gain1 + bias1
    e = e_ref[...].astype(F32)
    dr2 = norm_back(e, gain1, z1, r1)
    dm = dr2.astype(BF)
    gb_ref[1:2, :] = jnp.sum(e * z1, axis=0, keepdims=True)
    gb_ref[3:4, :] = jnp.sum(e, axis=0, keepdims=True)

    def back(c, total):
        rows = pl.ds(pl.multiple_of(c * 512, 512), 512)
        cols = pl.ds(pl.multiple_of(1024 + c * 512, 512), 512)
        u = us[c]
        dg = dot(dm, wu[rows, :], NT)
        slope = 0.5 * (1.0 + lax.erf(u * half)) + u * (jnp.exp(-0.5 * u * u) * (1.0 / math.sqrt(2 * math.pi)))
        du = (dg * slope).astype(BF)
        dus[:, rows] = du
        return total + dot(du, woi[:, cols], NT)

    dn1 = lax.fori_loop(0, 8, back, dr2)
    gb_ref[0:1, :] = jnp.sum(dn1 * z0, axis=0, keepdims=True)
    gb_ref[2:3, :] = jnp.sum(dn1, axis=0, keepdims=True)
    gb_ref[4:8, :] = jnp.zeros((4, 1024), F32)
    dr1 = norm_back(dn1, gain0, z0, r0)
    dr_ref[...] = dr1
    da = dr1.astype(BF)
    do = dot(da, woi[:, :1024], NT).astype(BF)
    for h in range(16):
        lanes = slice(64 * h, 64 * h + 64)
        do_ref[h] = jnp.concatenate([do[:64, lanes], do[64:, lanes]], axis=1)
    du = dus[...]
    for ref, at in ((zpay, 1536), (cpay, 0)):
        ref[:, at:at + 4096] = du
        ref[:, at + 4096:at + 5120] = dm
        ref[:, at + 5120:at + 6144] = da
    for r, (ref, at) in enumerate(((l_ref, 0), (cpay, 6144), (zpay, 0), (zpay, 7680))):
        few = pl.ds(pl.multiple_of(where[r] * 256, 256), 256)
        many = pl.ds(pl.multiple_of(where[r] * 1024, 1024), 1024)
        ref[:, at:at + 256] = nl[:, few]
        ref[:, at + 256:at + 512] = ob[:, few]
        ref[:, at + 512:at + 1536] = gs[:, many]


def middle(o, tok, cot, lnf, a, u):
    return pl.pallas_call(
        middle_kernel,
        out_shape=[
            shp((128, 1024), F32), shp((128, 1024), F32), shp((16, 64, 128), BF),
            shp((128, 9216), BF), shp((128, 7680), BF), shp((128, 1536), BF), shp((8, 1024), F32),
        ],
        in_specs=[VM] * 4 + [ANY] * 8,
        out_specs=[VM] * 7,
        scratch_shapes=[
            pltpu.VMEM((1024, 5120), BF),
            pltpu.VMEM((4096, 1024), BF),
            pltpu.VMEM((8, 128, 512), F32),
            pltpu.VMEM((128, 4096), BF),
            pltpu.VMEM((128, 4096), BF),
            pltpu.VMEM((128, 1024), BF),
            pltpu.VMEM((128, 1024), BF),
            DMA((4,)), DMA((4,)), DMA((4,)),
        ],
        compiler_params=pltpu.CompilerParams(vmem_limit_bytes=LIMIT),
        cost_estimate=pl.CostEstimate(flops=10 << 30, bytes_accessed=32 << 20, transcendentals=2 << 20),
        name="middle",
    )(o, tok, cot, lnf, *a, *u)


def wgrad_mid_kernel(own_l, own, zr, c1, c2, out, ll, rr, lt, sem):
    copies = []
    for k, (lsrc, rsrc) in enumerate((
        (own_l, own.at[:, :6144]),
        (zr.at[:, :1536], zr.at[:, 1536:7680]),
        (c1.at[:, 6144:], c1.at[:, :6144]),
        (c2.at[:, 6144:], c2.at[:, :6144]),
    )):
        rows = slice(128 * k, 128 * k + 128)
        copies.append(pltpu.make_async_copy(lsrc, ll.at[rows, :], sem.at[2 * k]))
        copies.append(pltpu.make_async_copy(rsrc, rr.at[rows, :], sem.at[2 * k + 1]))
    for c in copies:
        c.start()
    for c in copies:
        c.wait()
    for k in range(6):
        lt[256 * k:256 * k + 256, :] = ll[:, 256 * k:256 * k + 256].astype(F32).T.astype(BF)
    out[0:256, :] = dot(lt[256:512, :], rr[:, 5120:6144]).astype(BF)
    for k in range(4):
        out[256 + 256 * k:512 + 256 * k, :] = dot(lt[0:256, :], rr[:, 1024 * k:1024 * k + 1024]).astype(BF)
    for k in range(4):
        rows = slice(512 + 256 * k, 768 + 256 * k)
        out[1280 + 256 * k:1536 + 256 * k, :] = dot(lt[rows, :], rr[:, 4096:5120]).astype(BF)


def wgrad_mid(own_l, own, zr, c1, c2):
    return pl.pallas_call(
        wgrad_mid_kernel,
        out_shape=shp((2304, 1024), BF),
        in_specs=[ANY] * 5,
        out_specs=VM,
        scratch_shapes=[
            pltpu.VMEM((512, 1536), BF), pltpu.VMEM((512, 6144), BF), pltpu.VMEM((1536, 512), BF), DMA((8,)),
        ],
        compiler_params=pltpu.CompilerParams(vmem_limit_bytes=LIMIT),
        cost_estimate=pl.CostEstimate(flops=2 << 30, bytes_accessed=16 << 20, transcendentals=0),
        name="wgrad_mid",
    )(own_l, own, zr, c1, c2)


def wgrad_tail_kernel(xs, p0, p1, p2, p3, out, vec, ll, rr, sem):
    w = lax.axis_index("wsh")
    zh, co = w // 2, w % 2
    where = [w, zh * 2 + 1 - co, (1 - zh) * 2 + co, (1 - zh) * 2 + 1 - co]
    copies = []
    for k, p in enumerate((p0, p1, p2, p3)):
        rows = slice(128 * k, 128 * k + 128)
        copies.append(pltpu.make_async_copy(xs.at[where[k]], ll.at[rows, :], sem.at[2 * k]))
        copies.append(pltpu.make_async_copy(p, rr.at[k], sem.at[2 * k + 1]))
    for c in copies:
        c.start()
    for c in copies:
        c.wait()
    lt = ll[...].astype(F32).T.astype(BF)
    for m in range(3):
        cols = slice(1024 * m, 1024 * m + 1024)
        total = dot(lt[:, 0:128], rr[0, :128, cols])
        for k in range(1, 4):
            total += dot(lt[:, 128 * k:128 * k + 128], rr[k, :128, cols])
        out[256 * m:256 * m + 256, :] = total.astype(BF)
    mine = pl.ds(pl.multiple_of(w * 256, 256), 256)
    vec[...] = sum(rr[k, 128:144, mine].astype(F32) for k in range(4))[:8]


def wgrad_tail(xs, p0, p1, p2, p3):
    return pl.pallas_call(
        wgrad_tail_kernel,
        out_shape=[shp((768, 1024), BF), shp((8, 256), F32)],
        in_specs=[ANY] * 5,
        out_specs=[VM] * 2,
        scratch_shapes=[pltpu.VMEM((512, 256), BF), pltpu.VMEM((4, 144, 3072), BF), DMA((8,))],
        compiler_params=pltpu.CompilerParams(vmem_limit_bytes=LIMIT),
        cost_estimate=pl.CostEstimate(flops=1 << 30, bytes_accessed=8 << 20, transcendentals=0),
        name="wgrad_tail",
    )(xs, p0, p1, p2, p3)


def tokens_back_kernel(dkv, dqp, w_ref, dr_ref, gb, gt, pay):
    for h in range(16):
        lanes = slice(64 * h, 64 * h + 64)
        pair = dqp[h]
        pay[:64, lanes] = pair[:, :64]
        pay[64:128, lanes] = pair[:, 64:]
        both = (dkv[h].astype(F32) + dkv[16 + h].astype(F32)).astype(BF)
        pay[:128, 1024 + 64 * h:1088 + 64 * h] = both[:, :64]
        pay[:128, 2048 + 64 * h:2112 + 64 * h] = both[:, 64:]
    pay[128:144, :1024] = jnp.concatenate([gb[...], jnp.zeros((8, 1024), F32)], axis=0).astype(BF)
    pay[128:144, 1024:] = jnp.zeros((16, 2048), BF)
    for k in range(4):
        cols = slice(256 * k, 256 * k + 256)
        total = dr_ref[:, cols]
        for m in range(3):
            total += dot(pay[:128, 1024 * m:1024 * m + 1024], w_ref[k, m], NT)
        gt[:, cols] = total


def tokens_back(dkv, dqp, wall, dr, gb):
    return pl.pallas_call(
        tokens_back_kernel,
        out_shape=[shp((128, 1024), F32), shp((144, 3072), BF)],
        in_specs=[VM] * 5,
        out_specs=[VM] * 2,
        compiler_params=pltpu.CompilerParams(vmem_limit_bytes=LIMIT),
        cost_estimate=pl.CostEstimate(flops=1 << 30, bytes_accessed=8 << 20, transcendentals=0),
        name="tokens_back",
    )(dkv, dqp, wall, dr, gb)


def total_kernel(hc, outs_of, with_vec, scale, refs):
    refs = list(refs)
    g = refs.pop(0)
    vec = refs.pop(0) if with_vec else None
    n_out = len(outs_of)
    outs = [refs.pop(0) for _ in range(n_out)]
    vout = refs.pop(0) if with_vec else None
    r1, s1, r2, s2, r3, full, ss, rs = refs[:8]
    if with_vec:
        vx, vy, vz, tx, ty = refs[8:]
    zl, x, y, zh, co = place()
    xp = [device(zl, (x + s) % 4, y, zh, co) for s in (1, 2, 3)]
    yp = [device(zl, x, (y + s) % 4, zh, co) for s in (1, 2, 3)]
    zp = device(1 - zl, x, y, zh, co)
    greet(xp + yp + [zp])
    wire = Wire(ss, rs)
    first = [xp, yp]
    second = [yp, xp]
    at1 = [x, y]
    at2 = [y, x]

    def rows(h, k):
        return pl.ds(pl.multiple_of(h * 4 * hc + k * hc, 16), hc)

    def cols(k, width):
        return pl.ds(pl.multiple_of(k * width, 128), width)

    sends = []
    one = [[], []]
    for s in range(3):
        for h in range(2):
            one[h].append(wire(g.at[rows(h, (at1[h] + s + 1) % 4)], r1.at[h, s], first[h][s]))
    if with_vec:
        vone = [wire(vec, vx.at[s], xp[s]) for s in range(3)]
        sends += vone
    two = [[], []]
    for h in range(2):
        for c in one[h]:
            c.wait_recv()
        total = g[rows(h, at1[h]), :].astype(F32)
        for s in range(3):
            total += r1[h, s].astype(F32)
        s1[h] = total.astype(BF)
        for s in range(3):
            two[h].append(wire(s1.at[h, :, cols((at2[h] + s + 1) % 4, 256)], r2.at[h, s], second[h][s]))
    if with_vec:
        for c in vone:
            c.wait_recv()
        tx[...] = vec[...] + vx[0] + vx[1] + vx[2]
        vtwo = [wire(tx, vy.at[s], yp[s]) for s in range(3)]
        sends += vtwo
    three = []
    for h in range(2):
        for c in two[h]:
            c.wait_recv()
        total = s1[h, :, cols(at2[h], 256)].astype(F32)
        for s in range(3):
            total += r2[h, s].astype(F32)
        s2[h] = total.astype(BF)
        three.append(wire(s2.at[h, :, cols(1 - zl, 128)], r3.at[h], zp))
    if with_vec:
        for c in vtwo:
            c.wait_recv()
        ty[...] = tx[...] + vy[0] + vy[1] + vy[2]
        vthree = wire(ty, vz, zp)
        sends.append(vthree)
    four = []
    for h in range(2):
        three[h].wait_recv()
        total = s2[h, :, cols(zl, 128)].astype(F32) + r3[h].astype(F32)
        spot = full.at[rows(h, at1[h]), cols(at2[h] * 2 + zl, 128)]
        spot[...] = total.astype(BF)
        four.append(wire(spot, spot, zp))
    five = [[], []]
    for h in range(2):
        four[h].wait()
        spot = full.at[rows(h, at1[h]), cols(at2[h], 256)]
        for s in range(3):
            five[h].append(wire(spot, spot, second[h][s]))
    six = [[], []]
    for h in range(2):
        for c in five[h]:
            c.wait()
        spot = full.at[rows(h, at1[h])]
        for s in range(3):
            six[h].append(wire(spot, spot, first[h][s]))
    for c in sends + one[0] + one[1] + two[0] + two[1] + three:
        c.wait_send()
    if with_vec:
        vthree.wait_recv()
        vout[...] = (ty[...] + vz[...]) * scale
    for c in six[0] + six[1]:
        c.wait()
    for ref, spots in zip(outs, outs_of):
        for row, col, start, size in spots:
            ref[row:row + size, col:col + 1024] = full[start:start + size, :].astype(F32) * scale


def total(g, vec, outs_of, shapes, collective, scale):
    rows = g.shape[0]
    hc = rows // 8
    with_vec = vec is not None
    n = 28 + (7 if with_vec else 0)

    def kernel(*refs):
        total_kernel(hc, outs_of, with_vec, scale, refs)

    scratch = [
        pltpu.VMEM((2, 3, hc, 1024), BF),
        pltpu.VMEM((2, hc, 1024), BF),
        pltpu.VMEM((2, 3, hc, 256), BF),
        pltpu.VMEM((2, hc, 256), BF),
        pltpu.VMEM((2, hc, 128), BF),
        pltpu.VMEM((rows, 1024), BF),
        DMA((n,)), DMA((n,)),
    ]
    outs = [shp(s, F32) for s in shapes]
    if with_vec:
        scratch += [
            pltpu.VMEM((3, 8, 256), F32), pltpu.VMEM((3, 8, 256), F32), pltpu.VMEM((8, 256), F32),
            pltpu.VMEM((8, 256), F32), pltpu.VMEM((8, 256), F32),
        ]
        outs.append(shp((8, 256), F32))
    args = [g] + ([vec] if with_vec else [])
    return pl.pallas_call(
        kernel,
        out_shape=outs,
        in_specs=[VM] * len(args),
        out_specs=[VM] * len(outs),
        scratch_shapes=scratch,
        compiler_params=pltpu.CompilerParams(
            collective_id=collective, has_side_effects=True, vmem_limit_bytes=LIMIT
        ),
        name=f"total_{collective}",
    )(*args)


FLIP_CORE = [(0, 1), (1, 0), (2, 3), (3, 2)]
FLIP_FAR = [(0, 2), (2, 0), (1, 3), (3, 1)]


def body(
    tokens, w_query, w_key, w_value, w_output, w_inner, w_outer, ln_gain, ln_bias, block_mask, block_pairs, cotangent,
):
    tok = tokens.reshape(128, 1024)
    cot = cotangent.reshape(128, 1024)
    scale = 1.0 / math.sqrt(16384)
    lnp = jnp.concatenate([ln_gain, ln_bias, jnp.zeros((4, 256), F32)], axis=0)
    blk = block_pairs.reshape(-1)

    wall, xs, lnf = gather_weights(w_query, w_key, w_value, tok, lnp)
    a_own = jnp.concatenate([w_output, w_inner], axis=1)
    a_own, u_own, wall = lax.optimization_barrier((a_own, w_outer, wall))
    a_far = lax.ppermute(a_own, "wsh", FLIP_FAR)
    u_far = lax.ppermute(u_own, "wsh", FLIP_FAR)
    a_core = lax.ppermute(a_own, "wsh", FLIP_CORE)
    u_core = lax.ppermute(u_own, "wsh", FLIP_CORE)
    a_diag = lax.ppermute(a_far, "wsh", FLIP_CORE)
    u_diag = lax.ppermute(u_far, "wsh", FLIP_CORE)

    kvp, qp = project(tok, wall)
    kvr, qr = exchange(kvp, qp, 2)
    o, ot, lse = attend(blk, block_mask, kvr, qr)
    (o_back,) = exchange(None, o, 3)
    y, dr1, do, zpay, cpay, own_l, gb = middle(
        o_back, tok, cot, lnf, (a_own, a_core, a_far, a_diag), (u_own, u_core, u_far, u_diag)
    )
    zr = lax.ppermute(zpay, "wsh", FLIP_FAR)
    c1 = lax.ppermute(cpay, "wsh", FLIP_CORE)
    c2 = lax.ppermute(zr[:, 1536:], "wsh", FLIP_CORE)

    (dor,) = exchange(None, do, 3)
    dkvp, dqp = attend_back(blk, block_mask, kvr, qr, dor, ot, lse)
    dkvr, dqr = exchange(dkvp, dqp, 4)
    grad_tok, pay = tokens_back(dkvr, dqr, wall, dr1, gb)
    t1 = lax.ppermute(pay, "wsh", FLIP_CORE)
    t2 = lax.ppermute(pay, "wsh", FLIP_FAR)
    t3 = lax.ppermute(t2, "wsh", FLIP_CORE)

    gmid = wgrad_mid(own_l, cpay, zr, c1, c2)
    s_o, s_i, s_u = total(
        gmid, None,
        [
            [(0, 0, 0, 256)],
            [(0, 1024 * k, 256 + 256 * k, 256) for k in range(4)],
            [(0, 0, 1280, 1024)],
        ],
        [(256, 1024), (256, 4096), (1024, 1024)], 5, scale,
    )
    gtail, vec = wgrad_tail(xs, pay, t1, t2, t3)
    s_q, s_k, s_v, s_vec = total(
        gtail, vec, [[(0, 0, 256 * k, 256)] for k in range(3)], [(256, 1024)] * 3, 6, scale
    )
    out_shape = tokens.shape
    return (
        y.reshape(out_shape), grad_tok.reshape(out_shape), s_q, s_k, s_v, s_o, s_i, s_u, s_vec[0:2], s_vec[2:4],
    )


def solution(mesh):
    return jax.shard_map(
        body,
        mesh=mesh,
        in_specs=(
            P("wsh", "ctx", None, None),
            P("wsh", None), P("wsh", None), P("wsh", None), P("wsh", None), P("wsh", None), P("wsh", None),
            P(None, "wsh"), P(None, "wsh"),
            P("wsh", None, None),
            P(),
            P("wsh", "ctx", None, None),
        ),
        out_specs=(
            P("wsh", "ctx", None, None), P("wsh", "ctx", None, None),
            P("wsh", None), P("wsh", None), P("wsh", None), P("wsh", None), P("wsh", None), P("wsh", None),
            P(None, "wsh"), P(None, "wsh"),
        ),
        check_vma=False,
    )
```

```python
import math

import jax
import jax.numpy as jnp
from jax import lax
from jax.experimental import pallas as pl
from jax.experimental.pallas import tpu as pltpu
from jax.sharding import PartitionSpec as P

MESH = pl.DeviceIdType.MESH
BF = jnp.bfloat16
F32 = jnp.float32
ANY = pl.BlockSpec(memory_space=pl.ANY)
VM = pl.BlockSpec(memory_space=pltpu.VMEM)
SM = pl.BlockSpec(memory_space=pltpu.SMEM)
DMA = pltpu.SemaphoreType.DMA
LIMIT = 56 * 1024 * 1024
EPS = 1e-05
NEG = -1e30


def shp(shape, dtype):
    return jax.ShapeDtypeStruct(shape, dtype)


def dot(a, b, dims=((1,), (0,))):
    return lax.dot_general(a, b, (dims, ((), ())), preferred_element_type=F32)


NN = ((1,), (0,))
NT = ((1,), (1,))
TN = ((0,), (0,))


def place():
    c = lax.axis_index("ctx")
    w = lax.axis_index("wsh")
    return c // 16, (c // 4) % 4, c % 4, w // 2, w % 2


def device(zl, x, y, zh, co):
    return {"ctx": zl * 16 + x * 4 + y, "wsh": zh * 2 + co}


def greet(peers):
    bar = pltpu.get_barrier_semaphore()
    for p in peers:
        pl.semaphore_signal(bar, inc=1, device_id=p, device_id_type=MESH)
    pl.semaphore_wait(bar, len(peers))


class Wire:
    def __init__(self, send, recv):
        self.send, self.recv, self.n = send, recv, 0

    def __call__(self, src, dst, peer):
        k = self.n
        self.n += 1
        copy = pltpu.make_async_remote_copy(
            src_ref=src, dst_ref=dst, send_sem=self.send.at[k], recv_sem=self.recv.at[k],
            device_id=peer, device_id_type=MESH,
        )
        copy.start()
        return copy


def gather_kernel(wq, wk, wv, x_ref, ln_ref, wo, wi, wu, wall, xs, lnf, co_ref, ci_ref, cu_ref, ss, rs):
    zl, x, y, zh, co = place()
    me = zh * 2 + co
    other = (1 - zh) * 2 + co
    core = device(zl, x, y, zh, 1 - co)
    far = device(zl, x, y, 1 - zh, co)
    diag = device(zl, x, y, 1 - zh, 1 - co)
    xp = [device(zl, (x + s) % 4, y, zh, co) for s in (1, 2, 3)]
    yp = [device(zl, x, (y + s) % 4, zh, co) for s in (1, 2, 3)]
    greet([core, far, diag] + xp + yp)
    wire = Wire(ss, rs)
    ws = (wq, wk, wv)
    rows_a = pl.ds(pl.multiple_of(x * 32, 32), 32)
    rows_b = pl.ds(pl.multiple_of(128 + y * 32, 32), 32)
    first_a, first_b = [], []
    for m in range(3):
        first_a.append(wire(ws[m].at[rows_a], wall.at[me, m, rows_a], far))
        first_b.append(wire(ws[m].at[rows_b], wall.at[me, m, rows_b], far))
    rest = []
    for m in range(3):
        rest.append(wire(ws[m], wall.at[me, m], core))
    for p, idx in ((core, zh * 2 + 1 - co), (far, other), (diag, (1 - zh) * 2 + 1 - co)):
        cols = pl.ds(pl.multiple_of(idx * 256, 256), 256)
        rest.append(wire(x_ref.at[:, cols], xs.at[me], p))
        rest.append(wire(ln_ref, lnf.at[me], p))
    for c in first_a:
        c.wait_recv()
    second = []
    for m in range(3):
        part = wall.at[other, m, rows_a]
        for p in xp:
            second.append(wire(part, part, p))
    for c in first_b:
        c.wait_recv()
    for m in range(3):
        part = wall.at[other, m, rows_b]
        for p in yp:
            second.append(wire(part, part, p))
    for src, dst in ((wo, co_ref), (wi, ci_ref), (wu, cu_ref)):
        rest.append(wire(src, dst, core))
    for c in second:
        c.wait_recv()
    last = [wire(wall.at[other, m], wall.at[other, m], core) for m in range(3)]
    for c in last:
        c.wait()
    for c in first_a + first_b + second:
        c.wait_send()
    for c in rest:
        c.wait()


def gather_weights(wq, wk, wv, tok, lnp, wo, wi, wu):
    n = 6 + 3 + 6 + 18 + 3 + 3
    return pl.pallas_call(
        gather_kernel,
        out_shape=[
            shp((4, 3, 256, 1024), BF), shp((4, 128, 256), BF), shp((4, 8, 256), F32),
            shp(wo.shape, BF), shp(wi.shape, BF), shp(wu.shape, BF),
        ],
        in_specs=[ANY] * 8,
        out_specs=[ANY] * 6,
        scratch_shapes=[DMA((n,)), DMA((n,))],
        compiler_params=pltpu.CompilerParams(collective_id=1, has_side_effects=True),
        name="gather_qkv",
    )(wq, wk, wv, tok, lnp, wo, wi, wu)


def load_qkv(wall, own, weights, sem):
    w = lax.axis_index("wsh")
    copies = [
        pltpu.make_async_copy(own[m], weights.at[w, m], sem.at[m]) for m in range(3)
    ]
    for r in range(1, 4):
        k = (w + r) % 4
        copies.append(pltpu.make_async_copy(wall.at[k], weights.at[k], sem.at[2 + r]))
    for c in copies:
        c.start()
    return copies


def qkv_kernel(x_ref, wall, wq, wk, wv, kv_ref, q_ref, weights, sem):
    for c in load_qkv(wall, (wq, wk, wv), weights, sem):
        c.wait()

    def block(j, carry):
        lanes = pl.ds(pl.multiple_of(j * 256, 256), 256)

        def proj(m):
            total = dot(x_ref[:, :256], weights[0, m, :, lanes])
            for k in range(1, 4):
                total += dot(x_ref[:, 256 * k:256 * k + 256], weights[k, m, :, lanes])
            return total.astype(BF)

        q = (proj(0).astype(F32) * 0.125).astype(BF)
        k = proj(1)
        v = proj(2)
        for u in range(4):
            part = slice(64 * u, 64 * u + 64)
            kv_ref[4 * j + u] = jnp.concatenate([k[:, part], v[:, part]], axis=1)
            q_ref[4 * j + u] = jnp.concatenate([q[:64, part], q[64:, part]], axis=1)
        return carry

    lax.fori_loop(0, 4, block, 0)


def project(tok, wall, own):
    return pl.pallas_call(
        qkv_kernel,
        out_shape=[shp((16, 128, 128), BF), shp((16, 64, 128), BF)],
        in_specs=[VM] + [ANY] * 4,
        out_specs=[VM] * 2,
        scratch_shapes=[pltpu.VMEM((4, 3, 256, 1024), BF), DMA((6,))],
        compiler_params=pltpu.CompilerParams(vmem_limit_bytes=LIMIT),
        cost_estimate=pl.CostEstimate(flops=805306368, bytes_accessed=8 << 20, transcendentals=0),
        name="qkv",
    )(tok, wall, *own)


def exchange(wide, narrow, collective):
    has = wide is not None
    n = 32 if has else 16

    def kernel(*refs):
        if has:
            wi, na, wo, no, sw, rw, sn, rn, ls = refs
        else:
            na, no, sn, rn, ls = refs
        me = lax.axis_index("ctx")
        zl = me // 16
        flat = me % 16
        bar = pltpu.get_barrier_semaphore()

        def peer(i):
            if has:
                return (me + i) % 32
            return zl * 16 + (flat + i) % 16

        def greet_one(i, carry):
            pl.semaphore_signal(bar, inc=1, device_id={"ctx": peer(i)}, device_id_type=MESH)
            return carry

        lax.fori_loop(1, n, greet_one, 0)
        pl.semaphore_wait(bar, n - 1)

        def narrow_copy(i):
            p = (flat + i) % 16
            return pltpu.make_async_remote_copy(
                src_ref=na.at[p], dst_ref=no.at[flat], send_sem=sn.at[i], recv_sem=rn.at[i],
                device_id={"ctx": zl * 16 + p}, device_id_type=MESH,
            )

        def wide_copy(i):
            p = (me + i) % 32
            src = p if wide.shape[0] == 32 else p % 16
            return pltpu.make_async_remote_copy(
                src_ref=wi.at[src], dst_ref=wo.at[me], send_sem=sw.at[i], recv_sem=rw.at[i],
                device_id={"ctx": p}, device_id_type=MESH,
            )

        def start(make):
            def one(i, carry):
                make(i).start()
                return carry
            return one

        def wait(make):
            def one(i, carry):
                make(i).wait()
                return carry
            return one

        if has:
            lax.fori_loop(1, 32, start(wide_copy), 0)
        lax.fori_loop(1, 16, start(narrow_copy), 0)
        local = [pltpu.make_async_copy(na.at[flat], no.at[flat], ls.at[0])]
        if has:
            own = me if wide.shape[0] == 32 else flat
            local.append(pltpu.make_async_copy(wi.at[own], wo.at[me], ls.at[1]))
        for c in local:
            c.start()
        for c in local:
            c.wait()
        if has:
            lax.fori_loop(1, 32, wait(wide_copy), 0)
        lax.fori_loop(1, 16, wait(narrow_copy), 0)

    sems = ([DMA((32,)), DMA((32,))] if has else []) + [DMA((16,)), DMA((16,)), DMA((2,))]
    outs = ([shp((32,) + wide.shape[1:], wide.dtype)] if has else []) + [shp(narrow.shape, narrow.dtype)]
    args = ([wide] if has else []) + [narrow]
    return pl.pallas_call(
        kernel,
        out_shape=outs,
        in_specs=[ANY] * len(args),
        out_specs=[ANY] * len(outs),
        scratch_shapes=sems,
        compiler_params=pltpu.CompilerParams(collective_id=collective, has_side_effects=True),
        name=f"exchange_{collective}",
    )(*args)


def attention_setup(blk, mask, kvr, qr, kvs, kaug, kvt, bias, qs, inv, order, oblk):
    first = (lax.axis_index("ctx") // 16) * 32

    def note(s, carry):
        inv[blk[s]] = s
        return carry

    lax.fori_loop(0, 64, note, 0)

    def pick(b, count):
        local = inv[b] - first
        order[count] = local
        oblk[count] = b
        mine = jnp.logical_and(local >= 0, local < 32)
        return count + mine.astype(jnp.int32)

    lax.fori_loop(0, 64, pick, 0)
    for s in range(64):
        at = pl.ds(pl.multiple_of(blk[s] * 64, 64), 64)
        kvs[at, :] = kvr[s // 2, (s % 2) * 64:(s % 2) * 64 + 64, :]
    for j in range(16):
        pair = qr[j]
        qs[2 * j] = pair[:, :64]
        qs[2 * j + 1] = pair[:, 64:]
    rows = lax.broadcasted_iota(jnp.int32, (512, 64), 0) // 64
    lanes = lax.broadcasted_iota(jnp.int32, (512, 64), 1)
    for c in range(8):
        part = kvs[512 * c:512 * c + 512, :]
        hot = jnp.where(rows + 8 * c == lanes, 1.0, 0.0).astype(BF)
        kaug[512 * c:512 * c + 512, :] = jnp.concatenate([part[:, :64], hot], axis=1)
        kvt[c] = part.astype(F32).T.astype(BF)
    qi = lax.broadcasted_iota(jnp.int32, (64, 64), 0)
    ki = lax.broadcasted_iota(jnp.int32, (64, 64), 1)
    bias[...] = jnp.where(jnp.logical_and(mask[0] != 0, ki < qi), 0.0, NEG)


def triangle():
    key = lax.broadcasted_iota(jnp.int32, (64, 256), 0)
    query = lax.broadcasted_iota(jnp.int32, (64, 256), 1) % 64
    return key <= query


def attend_kernel(blk, mask, kvr, qr, o_ref, ot_ref, lse_ref, kvs, kaug, kvt, bias, qs, qa, os, inv, order, oblk):
    attention_setup(blk, mask, kvr, qr, kvs, kaug, kvt, bias, qs, inv, order, oblk)

    def tile(g, carry):
        score, vals = [], []
        for u in range(4):
            i = oblk[4 * g + u]
            q = qs[order[4 * g + u]]
            row = jnp.broadcast_to(bias[pl.ds(i, 1), :], (64, 64)).astype(BF)
            qa[64 * u:64 * u + 64, :] = jnp.concatenate([q, row], axis=1)
            kv = kvs[pl.ds(pl.multiple_of(i * 64, 64), 64), :]
            score.append(dot(kv[:, :64], q, NT))
            vals.append(kv[:, 64:])
        s = jnp.where(triangle(), jnp.concatenate(score, axis=1), NEG)
        top = jnp.max(s, axis=0, keepdims=True)
        p = jnp.exp(s - top)
        total = jnp.sum(p, axis=0, keepdims=True)
        pb = p.astype(BF)
        mix = jnp.concatenate([dot(vals[u], pb[:, 64 * u:64 * u + 64], TN) for u in range(4)], axis=1)
        queries = qa[...]

        def chunk(c, state):
            top, total, mix = state
            keys = kaug[pl.ds(pl.multiple_of(c * 512, 512), 512), :]
            s = dot(keys, queries, NT)
            new = jnp.maximum(top, jnp.max(s, axis=0, keepdims=True))
            shrink = jnp.exp(top - new)
            p = jnp.exp(s - new)
            total = total * shrink + jnp.sum(p, axis=0, keepdims=True)
            mix = mix * shrink + dot(kvt[c, 64:, :], p.astype(BF))
            return new, total, mix

        chunks = (oblk[4 * g + 3] + 7) // 8
        top, total, mix = lax.fori_loop(0, chunks, chunk, (top, total, mix))
        out = mix / total
        ot_ref[g] = out
        lse_ref[g] = top + jnp.log(total)
        back = out.T.astype(BF)
        for u in range(4):
            os[order[4 * g + u]] = back[64 * u:64 * u + 64, :]
        return carry

    lax.fori_loop(0, 8, tile, 0)
    for j in range(16):
        o_ref[j] = jnp.concatenate([os[2 * j], os[2 * j + 1]], axis=1)


def attention_scratch():
    return [
        pltpu.VMEM((4096, 128), BF),
        pltpu.VMEM((4096, 128), BF),
        pltpu.VMEM((8, 128, 512), BF),
        pltpu.VMEM((64, 64), F32),
        pltpu.VMEM((32, 64, 64), BF),
        pltpu.VMEM((256, 128), BF),
        pltpu.VMEM((32, 64, 64), BF),
        pltpu.SMEM((64,), jnp.int32),
        pltpu.SMEM((72,), jnp.int32),
        pltpu.SMEM((72,), jnp.int32),
    ]


def attend(blk, mask, kvr, qr):
    return pl.pallas_call(
        attend_kernel,
        out_shape=[shp((16, 64, 128), BF), shp((8, 64, 256), F32), shp((8, 1, 256), F32)],
        in_specs=[SM, VM, VM, VM],
        out_specs=[VM] * 3,
        scratch_shapes=attention_scratch(),
        compiler_params=pltpu.CompilerParams(vmem_limit_bytes=LIMIT),
        cost_estimate=pl.CostEstimate(flops=10 << 30, bytes_accessed=32 << 20, transcendentals=4 << 20),
        name="attend",
    )(blk, mask, kvr, qr)


def attend_back_kernel(
    blk, mask, kvr, qr, dor, ot_ref, lse_ref, dkv_ref, dq_ref,
    kvs, kaug, kvt, bias, qs, qa, dqs, inv, order, oblk, dos, qz, dz, dkv,
):
    attention_setup(blk, mask, kvr, qr, kvs, kaug, kvt, bias, qs, inv, order, oblk)
    for j in range(16):
        pair = dor[j]
        dos[2 * j] = pair[:, :64]
        dos[2 * j + 1] = pair[:, 64:]
    dkv[...] = jnp.zeros_like(dkv)
    zero = jnp.zeros((64, 64), BF)

    def tile(g, carry):
        score, dprob, places, keys_own, q_own, d_own = [], [], [], [], [], []
        for u in range(4):
            i = oblk[4 * g + u]
            q = qs[order[4 * g + u]]
            do = dos[order[4 * g + u]]
            rows = slice(64 * u, 64 * u + 64)
            row = jnp.broadcast_to(bias[pl.ds(i, 1), :], (64, 64)).astype(BF)
            qa[rows, :] = jnp.concatenate([q, row], axis=1)
            qz[rows, :] = jnp.concatenate([q, zero], axis=1)
            dz[rows, :] = jnp.concatenate([zero, do], axis=1)
            at = pl.ds(pl.multiple_of(i * 64, 64), 64)
            kv = kvs[at, :]
            score.append(dot(kv[:, :64], q, NT))
            dprob.append(dot(kv[:, 64:], do, NT))
            places.append(at)
            keys_own.append(kv[:, :64])
            q_own.append(q)
            d_own.append(do)
        lse = lse_ref[g]
        queries = qa[...]
        qpad = qz[...]
        dpad = dz[...]
        dot_t = dpad[:, 64:].astype(F32).T
        delta = jnp.sum(ot_ref[g] * dot_t, axis=0, keepdims=True)
        s = jnp.where(triangle(), jnp.concatenate(score, axis=1), NEG)
        p = jnp.exp(s - lse)
        ds = (p * (jnp.concatenate(dprob, axis=1) - delta)).astype(BF)
        pb = p.astype(BF)
        dq = []
        for u in range(4):
            lanes = slice(64 * u, 64 * u + 64)
            grad = jnp.concatenate([dot(ds[:, lanes], q_own[u]), dot(pb[:, lanes], d_own[u])], axis=1)
            dkv[places[u], :] += grad
            dq.append(dot(keys_own[u], ds[:, lanes], TN))

        def chunk(c, dq):
            at = pl.ds(pl.multiple_of(c * 512, 512), 512)
            p = jnp.exp(dot(kaug[at, :], queries, NT) - lse)
            dp = dot(kvs[at, :], dpad, NT)
            ds = (p * (dp - delta)).astype(BF)
            dkv[at, :] += dot(ds, qpad) + dot(p.astype(BF), dpad)
            return dq + dot(kvt[c, :64, :], ds)

        chunks = (oblk[4 * g + 3] + 7) // 8
        dq = lax.fori_loop(0, chunks, chunk, jnp.concatenate(dq, axis=1))
        back = (dq * 0.125).T.astype(BF)
        for u in range(4):
            dqs[order[4 * g + u]] = back[64 * u:64 * u + 64, :]
        return carry

    lax.fori_loop(0, 8, tile, 0)
    for j in range(16):
        dq_ref[j] = jnp.concatenate([dqs[2 * j], dqs[2 * j + 1]], axis=1)
    for s in range(64):
        at = pl.ds(pl.multiple_of(blk[s] * 64, 64), 64)
        dkv_ref[s // 2, (s % 2) * 64:(s % 2) * 64 + 64, :] = dkv[at, :].astype(BF)


def attend_back(blk, mask, kvr, qr, dor, ot, lse):
    return pl.pallas_call(
        attend_back_kernel,
        out_shape=[shp((32, 128, 128), BF), shp((16, 64, 128), BF)],
        in_specs=[SM] + [VM] * 6,
        out_specs=[VM] * 2,
        scratch_shapes=attention_scratch()
        + [
            pltpu.VMEM((32, 64, 64), BF),
            pltpu.VMEM((256, 128), BF),
            pltpu.VMEM((256, 128), BF),
            pltpu.VMEM((4096, 128), F32),
        ],
        compiler_params=pltpu.CompilerParams(vmem_limit_bytes=LIMIT),
        cost_estimate=pl.CostEstimate(flops=25 << 30, bytes_accessed=64 << 20, transcendentals=4 << 20),
        name="attend_back",
    )(blk, mask, kvr, qr, dor, ot, lse)


def norm_parts(v):
    center = v - jnp.mean(v, axis=1, keepdims=True)
    r = lax.rsqrt(jnp.mean(center * center, axis=1, keepdims=True) + EPS)
    return center * r, r


def norm_back(e, gain, z, r):
    g = e * gain
    return r * (g - jnp.mean(g, axis=1, keepdims=True) - z * jnp.mean(g * z, axis=1, keepdims=True))


def middle_kernel(*refs):
    o_ref, x_ref, e_ref, ln_ref, ln_own = refs[:5]
    shards = (refs[5:8], refs[8:11])
    pieces = (refs[11:18], refs[18:25])
    y_ref, dr_ref, do_ref, zpay, cpay, l_ref, gb_ref = refs[25:32]
    wo, wi, wu, us, gs, dus, nl, ob, sw, sp = refs[32:]
    zl, x, y, zh, co = place()
    w = zh * 2 + co
    where = [w, zh * 2 + 1 - co, (1 - zh) * 2 + co, (1 - zh) * 2 + 1 - co]
    copies = [[], [], []]
    for r, (a, b, c) in enumerate(shards):
        rows = pl.ds(pl.multiple_of(where[r] * 256, 256), 256)
        copies[0].append(pltpu.make_async_copy(a, wo.at[rows], sw.at[r, 0]))
        for k in range(4):
            cols = slice(1024 * k, 1024 * k + 1024)
            copies[1].append(pltpu.make_async_copy(b.at[:, cols], wi.at[k, rows], sw.at[r, 1 + k]))
        groups = pl.ds(where[r] * 8, 8)
        copies[2].append(pltpu.make_async_copy(c, wu.at[groups], sw.at[r, 5]))
    for r, parts in enumerate(pieces):
        t = where[2 + r]
        own = parts[0]
        quarters = [(own.at[0], 0, x), (own.at[1], 1, y)]
        for s in range(3):
            quarters.append((parts[1 + s].at[0], 0, (x + 3 - s) % 4))
            quarters.append((parts[4 + s].at[0], 1, (y + 3 - s) % 4))
        for n, (ref, h, q) in enumerate(quarters):
            rows = pl.ds(pl.multiple_of(t * 256 + h * 128 + q * 32, 32), 32)
            copies[0].append(pltpu.make_async_copy(ref.at[0], wo.at[rows], sp.at[r, n, 0]))
            copies[1].append(pltpu.make_async_copy(ref.at[1:5], wi.at[:, rows], sp.at[r, n, 1]))
            copies[2].append(pltpu.make_async_copy(ref.at[5:9], wu.at[t * 8 + h * 4 + q], sp.at[r, n, 2]))
    for group in copies:
        for c in group:
            c.start()

    ln = jnp.concatenate([jnp.where(w == k, ln_own[...], ln_ref[k]) for k in range(4)], axis=1)
    gain0, gain1, bias0, bias1 = (ln[k:k + 1, :] for k in range(4))
    for h in range(16):
        pair = o_ref[h]
        ob[:64, 64 * h:64 * h + 64] = pair[:, :64]
        ob[64:, 64 * h:64 * h + 64] = pair[:, 64:]
    for c in copies[0]:
        c.wait()
    z0, r0 = norm_parts(x_ref[...].astype(F32) + dot(ob[...], wo[...]))
    n1 = z0 * gain0 + bias0
    nl[...] = n1.astype(BF)
    for c in copies[1]:
        c.wait()

    half = math.sqrt(0.5)

    def up(c, carry):
        u = dot(nl[...], wi[c])
        us[c] = u
        gs[:, pl.ds(pl.multiple_of(c * 1024, 1024), 1024)] = (0.5 * u * (1.0 + lax.erf(u * half))).astype(BF)
        return carry

    lax.fori_loop(0, 4, up, 0)
    for c in copies[2]:
        c.wait()

    def down(c, total):
        cols = pl.ds(pl.multiple_of(c * 1024, 1024), 1024)
        return total + dot(gs[:, cols], wu[pl.ds(c * 8, 8)].reshape(1024, 1024))

    r2 = lax.fori_loop(0, 4, down, n1)
    z1, r1 = norm_parts(r2)
    y_ref[...] = z1 * gain1 + bias1
    e = e_ref[...].astype(F32)
    dr2 = norm_back(e, gain1, z1, r1)
    dm = dr2.astype(BF)
    gb_ref[1:2, :] = jnp.sum(e * z1, axis=0, keepdims=True)
    gb_ref[3:4, :] = jnp.sum(e, axis=0, keepdims=True)

    def back(c, total):
        rows = pl.ds(pl.multiple_of(c * 1024, 1024), 1024)
        u = us[c]
        dg = dot(dm, wu[pl.ds(c * 8, 8)].reshape(1024, 1024), NT)
        slope = 0.5 * (1.0 + lax.erf(u * half)) + u * (jnp.exp(-0.5 * u * u) * (1.0 / math.sqrt(2 * math.pi)))
        du = (dg * slope).astype(BF)
        dus[:, rows] = du
        return total + dot(du, wi[c], NT)

    dn1 = lax.fori_loop(0, 4, back, dr2)
    gb_ref[0:1, :] = jnp.sum(dn1 * z0, axis=0, keepdims=True)
    gb_ref[2:3, :] = jnp.sum(dn1, axis=0, keepdims=True)
    gb_ref[4:8, :] = jnp.zeros((4, 1024), F32)
    dr1 = norm_back(dn1, gain0, z0, r0)
    dr_ref[...] = dr1
    da = dr1.astype(BF)
    do = dot(da, wo[...], NT).astype(BF)
    for h in range(16):
        lanes = slice(64 * h, 64 * h + 64)
        do_ref[h] = jnp.concatenate([do[:64, lanes], do[64:, lanes]], axis=1)
    du = dus[...]
    for ref, at in ((zpay, 1536), (cpay, 0)):
        ref[:, at:at + 4096] = du
        ref[:, at + 4096:at + 5120] = dm
        ref[:, at + 5120:at + 6144] = da
    for r, (ref, at) in enumerate(((l_ref, 0), (cpay, 6144), (zpay, 0), (zpay, 7680))):
        few = pl.ds(pl.multiple_of(where[r] * 256, 256), 256)
        many = pl.ds(pl.multiple_of(where[r] * 1024, 1024), 1024)
        ref[:, at:at + 256] = nl[:, few]
        ref[:, at + 256:at + 512] = ob[:, few]
        ref[:, at + 512:at + 1536] = gs[:, many]


def middle(o, tok, cot, lnf, lnp, shards, pieces):
    return pl.pallas_call(
        middle_kernel,
        out_shape=[
            shp((128, 1024), F32), shp((128, 1024), F32), shp((16, 64, 128), BF),
            shp((128, 9216), BF), shp((128, 7680), BF), shp((128, 1536), BF), shp((8, 1024), F32),
        ],
        in_specs=[VM] * 5 + [ANY] * 20,
        out_specs=[VM] * 7,
        scratch_shapes=[
            pltpu.VMEM((1024, 1024), BF),
            pltpu.VMEM((4, 1024, 1024), BF),
            pltpu.VMEM((32, 4, 32, 1024), BF),
            pltpu.VMEM((4, 128, 1024), F32),
            pltpu.VMEM((128, 4096), BF),
            pltpu.VMEM((128, 4096), BF),
            pltpu.VMEM((128, 1024), BF),
            pltpu.VMEM((128, 1024), BF),
            DMA((2, 6)), DMA((2, 8, 3)),
        ],
        compiler_params=pltpu.CompilerParams(vmem_limit_bytes=LIMIT),
        cost_estimate=pl.CostEstimate(flops=10 << 30, bytes_accessed=32 << 20, transcendentals=2 << 20),
        name="middle",
    )(o, tok, cot, lnf, lnp, *shards[0], *shards[1], *pieces[0], *pieces[1])


def wgrad_mid_kernel(own_l, own, zr, c1, c2, out, ll, rr, lt, sem):
    copies = []
    for k, (lsrc, rsrc) in enumerate((
        (own_l, own.at[:, :6144]),
        (zr.at[:, :1536], zr.at[:, 1536:7680]),
        (c1.at[:, 6144:], c1.at[:, :6144]),
        (c2.at[:, 6144:], c2.at[:, :6144]),
    )):
        rows = slice(128 * k, 128 * k + 128)
        copies.append(pltpu.make_async_copy(lsrc, ll.at[rows, :], sem.at[2 * k]))
        copies.append(pltpu.make_async_copy(rsrc, rr.at[rows, :], sem.at[2 * k + 1]))
    for c in copies:
        c.start()
    for c in copies:
        c.wait()
    for k in range(6):
        lt[256 * k:256 * k + 256, :] = ll[:, 256 * k:256 * k + 256].astype(F32).T.astype(BF)
    out[0:256, :] = dot(lt[256:512, :], rr[:, 5120:6144]).astype(BF)
    for k in range(4):
        out[256 + 256 * k:512 + 256 * k, :] = dot(lt[0:256, :], rr[:, 1024 * k:1024 * k + 1024]).astype(BF)
    for k in range(4):
        rows = slice(512 + 256 * k, 768 + 256 * k)
        out[1280 + 256 * k:1536 + 256 * k, :] = dot(lt[rows, :], rr[:, 4096:5120]).astype(BF)


def wgrad_mid(own_l, own, zr, c1, c2):
    return pl.pallas_call(
        wgrad_mid_kernel,
        out_shape=shp((2304, 1024), BF),
        in_specs=[ANY] * 5,
        out_specs=VM,
        scratch_shapes=[
            pltpu.VMEM((512, 1536), BF), pltpu.VMEM((512, 6144), BF), pltpu.VMEM((1536, 512), BF), DMA((8,)),
        ],
        compiler_params=pltpu.CompilerParams(vmem_limit_bytes=LIMIT),
        cost_estimate=pl.CostEstimate(flops=2 << 30, bytes_accessed=16 << 20, transcendentals=0),
        name="wgrad_mid",
    )(own_l, own, zr, c1, c2)


def tokens_back_kernel(dkv, dqp, dr_ref, gb, wall, wq, wk, wv, gt, pay, weights, sem):
    copies = load_qkv(wall, (wq, wk, wv), weights, sem)
    for h in range(16):
        lanes = slice(64 * h, 64 * h + 64)
        pair = dqp[h]
        pay[:64, lanes] = pair[:, :64]
        pay[64:128, lanes] = pair[:, 64:]
        both = (dkv[h].astype(F32) + dkv[16 + h].astype(F32)).astype(BF)
        pay[:128, 1024 + 64 * h:1088 + 64 * h] = both[:, :64]
        pay[:128, 2048 + 64 * h:2112 + 64 * h] = both[:, 64:]
    pay[128:144, :1024] = jnp.concatenate([gb[...], jnp.zeros((8, 1024), F32)], axis=0).astype(BF)
    pay[128:144, 1024:] = jnp.zeros((16, 2048), BF)
    for c in copies:
        c.wait()
    for k in range(4):
        cols = slice(256 * k, 256 * k + 256)
        total = dr_ref[:, cols]
        for m in range(3):
            total += dot(pay[:128, 1024 * m:1024 * m + 1024], weights[k, m], NT)
        gt[:, cols] = total


def tokens_back(dkv, dqp, dr, gb, wall, own):
    return pl.pallas_call(
        tokens_back_kernel,
        out_shape=[shp((128, 1024), F32), shp((144, 3072), BF)],
        in_specs=[VM] * 4 + [ANY] * 4,
        out_specs=[VM] * 2,
        scratch_shapes=[pltpu.VMEM((4, 3, 256, 1024), BF), DMA((6,))],
        compiler_params=pltpu.CompilerParams(vmem_limit_bytes=LIMIT),
        cost_estimate=pl.CostEstimate(flops=1 << 30, bytes_accessed=8 << 20, transcendentals=0),
        name="tokens_back",
    )(dkv, dqp, dr, gb, wall, *own)


class Sum:
    def __init__(self, hc, refs, wire, where, xp, yp, zp):
        self.hc, self.wire, self.zp = hc, wire, zp
        self.r1, self.s1, self.r2, self.s2, self.r3, self.full = refs
        zl, x, y, zh, co = where
        self.zl = zl
        self.first, self.second = (xp, yp), (yp, xp)
        self.at1, self.at2 = (x, y), (y, x)
        self.sent = []

    def rows(self, h, k):
        return pl.ds(pl.multiple_of(h * 4 * self.hc + k * self.hc, 16), self.hc)

    def cols(self, k, width):
        return pl.ds(pl.multiple_of(k * width, 128), width)

    def spread(self, g):
        self.g = g
        self.one = [[], []]
        for s in range(3):
            for h in range(2):
                src = g.at[self.rows(h, (self.at1[h] + s + 1) % 4)]
                self.one[h].append(self.wire(src, self.r1.at[h, s], self.first[h][s]))

    def spread_second(self):
        self.two = [[], []]
        for h in range(2):
            for c in self.one[h]:
                c.wait_recv()
            total = self.g[self.rows(h, self.at1[h]), :].astype(F32)
            for s in range(3):
                total += self.r1[h, s].astype(F32)
            self.s1[h] = total.astype(BF)
            for s in range(3):
                src = self.s1.at[h, :, self.cols((self.at2[h] + s + 1) % 4, 256)]
                self.two[h].append(self.wire(src, self.r2.at[h, s], self.second[h][s]))

    def spread_third(self):
        self.three = []
        for h in range(2):
            for c in self.two[h]:
                c.wait_recv()
            total = self.s1[h, :, self.cols(self.at2[h], 256)].astype(F32)
            for s in range(3):
                total += self.r2[h, s].astype(F32)
            self.s2[h] = total.astype(BF)
            self.three.append(self.wire(self.s2.at[h, :, self.cols(1 - self.zl, 128)], self.r3.at[h], self.zp))

    def collect(self):
        self.four = []
        for h in range(2):
            self.three[h].wait_recv()
            total = self.s2[h, :, self.cols(self.zl, 128)].astype(F32) + self.r3[h].astype(F32)
            spot = self.full.at[self.rows(h, self.at1[h]), self.cols(self.at2[h] * 2 + self.zl, 128)]
            spot[...] = total.astype(BF)
            self.four.append(self.wire(spot, spot, self.zp))

    def collect_second(self):
        self.five = [[], []]
        for h in range(2):
            self.four[h].wait()
            spot = self.full.at[self.rows(h, self.at1[h]), self.cols(self.at2[h], 256)]
            for s in range(3):
                self.five[h].append(self.wire(spot, spot, self.second[h][s]))

    def collect_third(self):
        self.six = [[], []]
        for h in range(2):
            for c in self.five[h]:
                c.wait()
            spot = self.full.at[self.rows(h, self.at1[h])]
            for s in range(3):
                self.six[h].append(self.wire(spot, spot, self.first[h][s]))

    def finish(self):
        for c in self.one[0] + self.one[1] + self.two[0] + self.two[1] + self.three:
            c.wait_send()
        for c in self.six[0] + self.six[1]:
            c.wait()


def sum_scratch(rows):
    hc = rows // 8
    return [
        pltpu.VMEM((2, 3, hc, 1024), BF),
        pltpu.VMEM((2, hc, 1024), BF),
        pltpu.VMEM((2, 3, hc, 256), BF),
        pltpu.VMEM((2, hc, 256), BF),
        pltpu.VMEM((2, hc, 128), BF),
        pltpu.VMEM((rows, 1024), BF),
    ]


def finish_kernel(*refs):
    mid, pay, xs, x_ref = refs[:4]
    s_q, s_k, s_v, s_o, s_i, s_u, s_vec = refs[4:11]
    mid_refs, tail_refs = refs[11:17], refs[17:23]
    ll, rr, tail, v0, vx, vy, vz, tx, ty, ss, rs, ls = refs[23:]
    scale = 1.0 / math.sqrt(16384)
    where = place()
    zl, x, y, zh, co = where
    w = zh * 2 + co
    core = device(zl, x, y, zh, 1 - co)
    far = device(zl, x, y, 1 - zh, co)
    xp = [device(zl, (x + s) % 4, y, zh, co) for s in (1, 2, 3)]
    yp = [device(zl, x, (y + s) % 4, zh, co) for s in (1, 2, 3)]
    zp = device(1 - zl, x, y, zh, co)
    greet([core, far, zp] + xp + yp)
    wire = Wire(ss, rs)
    big = Sum(288, mid_refs, wire, where, xp, yp, zp)
    small = Sum(96, tail_refs, wire, where, xp, yp, zp)

    to_far = wire(pay, rr.at[1], far)
    to_core = wire(pay, rr.at[0], core)
    big.spread(mid)
    order = [w, zh * 2 + 1 - co, (1 - zh) * 2 + co, (1 - zh) * 2 + 1 - co]
    mine = pl.ds(pl.multiple_of(w * 256, 256), 256)
    local = [pltpu.make_async_copy(x_ref.at[:, mine], ll.at[0:128, :], ls.at[0])]
    for k in range(1, 4):
        local.append(pltpu.make_async_copy(xs.at[order[k]], ll.at[128 * k:128 * k + 128, :], ls.at[k]))
    for c in local:
        c.start()
    for c in local:
        c.wait()
    lt = ll[...].astype(F32).T.astype(BF)
    to_far.wait_recv()
    on_core = wire(rr.at[1], rr.at[2], core)
    to_core.wait_recv()
    on_core.wait_recv()
    for m in range(3):
        cols = slice(1024 * m, 1024 * m + 1024)
        total = dot(lt[:, 0:128], pay[:128, cols])
        for k in range(3):
            total += dot(lt[:, 128 * k + 128:128 * k + 256], rr[k, :128, cols])
        tail[256 * m:256 * m + 256, :] = total.astype(BF)
    small.spread(tail)
    vec = pay[128:144, mine].astype(F32)
    for k in range(3):
        vec += rr[k, 128:144, mine].astype(F32)
    v0[...] = vec[:8]
    vone = [wire(v0, vx.at[s], xp[s]) for s in range(3)]
    big.spread_second()
    small.spread_second()
    for c in vone:
        c.wait_recv()
    tx[...] = v0[...] + vx[0] + vx[1] + vx[2]
    vtwo = [wire(tx, vy.at[s], yp[s]) for s in range(3)]
    big.spread_third()
    small.spread_third()
    for c in vtwo:
        c.wait_recv()
    ty[...] = tx[...] + vy[0] + vy[1] + vy[2]
    vthree = wire(ty, vz, zp)
    big.collect()
    small.collect()
    big.collect_second()
    small.collect_second()
    big.collect_third()
    small.collect_third()
    vthree.wait()
    s_vec[...] = (ty[...] + vz[...]) * scale
    for c in vone + vtwo + [to_far, to_core, on_core]:
        c.wait_send()
    big.finish()
    full = big.full
    s_o[...] = full[:256, :].astype(F32) * scale
    for k in range(4):
        s_i[:, 1024 * k:1024 * k + 1024] = full[256 + 256 * k:512 + 256 * k, :].astype(F32) * scale
    s_u[...] = full[1280:2304, :].astype(F32) * scale
    small.finish()
    for k, ref in enumerate((s_q, s_k, s_v)):
        ref[...] = small.full[256 * k:256 * k + 256, :].astype(F32) * scale


def finish(mid, pay, xs, tok):
    n = 28 * 2 + 3 + 7
    return pl.pallas_call(
        finish_kernel,
        out_shape=[
            shp((256, 1024), F32), shp((256, 1024), F32), shp((256, 1024), F32), shp((256, 1024), F32),
            shp((256, 4096), F32), shp((1024, 1024), F32), shp((8, 256), F32),
        ],
        in_specs=[VM, VM, ANY, ANY],
        out_specs=[VM] * 7,
        scratch_shapes=sum_scratch(2304) + sum_scratch(768) + [
            pltpu.VMEM((512, 256), BF), pltpu.VMEM((3, 144, 3072), BF), pltpu.VMEM((768, 1024), BF),
            pltpu.VMEM((8, 256), F32), pltpu.VMEM((3, 8, 256), F32), pltpu.VMEM((3, 8, 256), F32),
            pltpu.VMEM((8, 256), F32), pltpu.VMEM((8, 256), F32), pltpu.VMEM((8, 256), F32),
            DMA((n,)), DMA((n,)), DMA((4,)),
        ],
        compiler_params=pltpu.CompilerParams(collective_id=6, has_side_effects=True, vmem_limit_bytes=LIMIT),
        name="finish",
    )(mid, pay, xs, tok)


FLIP_CORE = [(0, 1), (1, 0), (2, 3), (3, 2)]
FLIP_FAR = [(0, 2), (2, 0), (1, 3), (3, 1)]


def along_x(s):
    return [(c, c // 16 * 16 + (c // 4 + s) % 4 * 4 + c % 4) for c in range(32)]


def along_y(s):
    return [(c, c // 4 * 4 + (c + s) % 4) for c in range(32)]


def body(
    tokens, w_query, w_key, w_value, w_output, w_inner, w_outer, ln_gain, ln_bias, block_mask, block_pairs, cotangent,
):
    tok = tokens.reshape(128, 1024)
    cot = cotangent.reshape(128, 1024)
    lnp = jnp.concatenate([ln_gain, ln_bias, jnp.zeros((4, 256), F32)], axis=0)
    blk = block_pairs.reshape(-1)
    own = (w_query, w_key, w_value)
    outer = w_outer.reshape(8, 4, 32, 1024)
    zl, x, y, zh, co = place()

    def quarter(k):
        first = lax.dynamic_slice_in_dim(w_output, 32 * k, 32, 0)[None]
        second = lax.dynamic_slice_in_dim(w_inner, 32 * k, 32, 0).reshape(32, 4, 1024).transpose(1, 0, 2)
        third = lax.dynamic_index_in_dim(outer, k, 0, keepdims=False)
        return jnp.concatenate([first, second, third], axis=0)

    quarters = jnp.stack([quarter(x), quarter(4 + y)])
    wall, xs, lnf, *core_shard = gather_weights(*own, tok, lnp, w_output, w_inner, outer)
    quarters, wall = lax.optimization_barrier((quarters, wall))
    far_own = lax.ppermute(quarters, "wsh", FLIP_FAR)

    kvp, qp = project(tok, wall, own)
    kvr, qr = exchange(kvp, qp, 2)
    far_own, kvr = lax.optimization_barrier((far_own, kvr))
    far = [far_own]
    far += [lax.ppermute(far_own[:1], "ctx", along_x(s)) for s in (1, 2, 3)]
    far += [lax.ppermute(far_own[1:], "ctx", along_y(s)) for s in (1, 2, 3)]
    o, ot, lse = attend(blk, block_mask, kvr, qr)
    *far, o = lax.optimization_barrier((*far, o))
    diag = [lax.ppermute(p, "wsh", FLIP_CORE) for p in far]
    (o_back,) = exchange(None, o, 3)
    y_out, dr1, do, zpay, cpay, own_l, gb = middle(
        o_back, tok, cot, lnf, lnp, ((w_output, w_inner, outer), core_shard), (far, diag)
    )
    zr = lax.ppermute(zpay, "wsh", FLIP_FAR)
    c1 = lax.ppermute(cpay, "wsh", FLIP_CORE)

    (dor,) = exchange(None, do, 3)
    dkvp, dqp = attend_back(blk, block_mask, kvr, qr, dor, ot, lse)
    dkvr, dqr = exchange(dkvp, dqp, 4)
    zr, dkvr = lax.optimization_barrier((zr, dkvr))
    c2 = lax.ppermute(zr[:, 1536:], "wsh", FLIP_CORE)
    grad_tok, pay = tokens_back(dkvr, dqr, dr1, gb, wall, own)
    gmid = wgrad_mid(own_l, cpay, zr, c1, c2)
    s_q, s_k, s_v, s_o, s_i, s_u, s_vec = finish(gmid, pay, xs, tok)
    out_shape = tokens.shape
    return (
        y_out.reshape(out_shape), grad_tok.reshape(out_shape), s_q, s_k, s_v, s_o, s_i, s_u, s_vec[0:2], s_vec[2:4],
    )


def solution(mesh):
    return jax.shard_map(
        body,
        mesh=mesh,
        in_specs=(
            P("wsh", "ctx", None, None),
            P("wsh", None), P("wsh", None), P("wsh", None), P("wsh", None), P("wsh", None), P("wsh", None),
            P(None, "wsh"), P(None, "wsh"),
            P("wsh", None, None),
            P(),
            P("wsh", "ctx", None, None),
        ),
        out_specs=(
            P("wsh", "ctx", None, None), P("wsh", "ctx", None, None),
            P("wsh", None), P("wsh", None), P("wsh", None), P("wsh", None), P("wsh", None), P("wsh", None),
            P(None, "wsh"), P(None, "wsh"),
        ),
        check_vma=False,
    )
```

```python
import math

import jax
import jax.numpy as jnp
from jax import lax
from jax.experimental import pallas as pl
from jax.experimental.pallas import tpu as pltpu
from jax.sharding import PartitionSpec as P

MESH = pl.DeviceIdType.MESH
BF = jnp.bfloat16
F32 = jnp.float32
ANY = pl.BlockSpec(memory_space=pl.ANY)
VM = pl.BlockSpec(memory_space=pltpu.VMEM)
SM = pl.BlockSpec(memory_space=pltpu.SMEM)
DMA = pltpu.SemaphoreType.DMA
LIMIT = 56 * 1024 * 1024
EPS = 1e-05
NEG = -1e30


def shp(shape, dtype):
    return jax.ShapeDtypeStruct(shape, dtype)


def dot(a, b, dims=((1,), (0,))):
    return lax.dot_general(a, b, (dims, ((), ())), preferred_element_type=F32)


NN = ((1,), (0,))
NT = ((1,), (1,))
TN = ((0,), (0,))


def place():
    c = lax.axis_index("ctx")
    w = lax.axis_index("wsh")
    return c // 16, (c // 4) % 4, c % 4, w // 2, w % 2


def device(zl, x, y, zh, co):
    return {"ctx": zl * 16 + x * 4 + y, "wsh": zh * 2 + co}


def greet(peers):
    bar = pltpu.get_barrier_semaphore()
    for p in peers:
        pl.semaphore_signal(bar, inc=1, device_id=p, device_id_type=MESH)
    pl.semaphore_wait(bar, len(peers))


class Wire:
    def __init__(self, send, recv):
        self.send, self.recv, self.n = send, recv, 0

    def __call__(self, src, dst, peer):
        k = self.n
        self.n += 1
        copy = pltpu.make_async_remote_copy(
            src_ref=src, dst_ref=dst, send_sem=self.send.at[k], recv_sem=self.recv.at[k],
            device_id=peer, device_id_type=MESH,
        )
        copy.start()
        return copy


def gather_kernel(wq, wk, wv, x_ref, ln_ref, wo, wi, wu, wall, xs, lnf, co_ref, ci_ref, cu_ref, qa_ref, qb_ref, ss, rs):
    zl, x, y, zh, co = place()
    me = zh * 2 + co
    other = (1 - zh) * 2 + co
    core = device(zl, x, y, zh, 1 - co)
    far = device(zl, x, y, 1 - zh, co)
    diag = device(zl, x, y, 1 - zh, 1 - co)
    xp = [device(zl, (x + s) % 4, y, zh, co) for s in (1, 2, 3)]
    yp = [device(zl, x, (y + s) % 4, zh, co) for s in (1, 2, 3)]
    greet([core, far, diag] + xp + yp)
    wire = Wire(ss, rs)
    ws = (wq, wk, wv)
    rows_a = pl.ds(pl.multiple_of(x * 32, 32), 32)
    rows_b = pl.ds(pl.multiple_of(128 + y * 32, 32), 32)
    first_a, first_b = [], []
    for m in range(3):
        first_a.append(wire(ws[m].at[rows_a], wall.at[me, m, rows_a], far))
        first_b.append(wire(ws[m].at[rows_b], wall.at[me, m, rows_b], far))
    rest = []
    for m in range(3):
        rest.append(wire(ws[m], wall.at[me, m], core))
    for p, idx in ((core, zh * 2 + 1 - co), (far, other), (diag, (1 - zh) * 2 + 1 - co)):
        cols = pl.ds(pl.multiple_of(idx * 256, 256), 256)
        rest.append(wire(x_ref.at[:, cols], xs.at[me], p))
        rest.append(wire(ln_ref, lnf.at[me], p))
    quarters = []
    for ref, k, n in ((qa_ref, x, y), (qb_ref, 4 + y, x)):
        rows = pl.ds(pl.multiple_of(k * 32, 32), 32)
        cols = pl.ds(pl.multiple_of(n * 256, 256), 256)
        quarters.append(wire(wo.at[rows, cols], ref.at[0, :, cols], far))
        for b in range(4):
            at = pl.ds(pl.multiple_of(1024 * b + n * 256, 256), 256)
            quarters.append(wire(wi.at[rows, at], ref.at[1 + b, :, cols], far))
        quarters.append(wire(wu.at[k, :, :, cols], ref.at[5:9, :, cols], far))
    for c in first_a:
        c.wait_recv()
    second = []
    for m in range(3):
        part = wall.at[other, m, rows_a]
        for p in xp:
            second.append(wire(part, part, p))
    for c in first_b:
        c.wait_recv()
    for m in range(3):
        part = wall.at[other, m, rows_b]
        for p in yp:
            second.append(wire(part, part, p))
    for src, dst in ((wo, co_ref), (wi, ci_ref), (wu, cu_ref)):
        rest.append(wire(src, dst, core))
    for c in quarters:
        c.wait_recv()
    for ref, n, peers in ((qa_ref, y, yp), (qb_ref, x, xp)):
        spot = ref.at[:, :, pl.ds(pl.multiple_of(n * 256, 256), 256)]
        for p in peers:
            rest.append(wire(spot, spot, p))
    for c in second:
        c.wait_recv()
    last = [wire(wall.at[other, m], wall.at[other, m], core) for m in range(3)]
    for c in last:
        c.wait()
    for c in first_a + first_b + second + quarters:
        c.wait_send()
    for c in rest:
        c.wait()


def gather_weights(wq, wk, wv, tok, lnp, wo, wi, wu):
    n = 6 + 3 + 6 + 12 + 18 + 3 + 6 + 3
    return pl.pallas_call(
        gather_kernel,
        out_shape=[
            shp((4, 3, 256, 1024), BF), shp((4, 128, 256), BF), shp((4, 8, 256), F32),
            shp(wo.shape, BF), shp(wi.shape, BF), shp(wu.shape, BF), shp((9, 32, 1024), BF), shp((9, 32, 1024), BF),
        ],
        in_specs=[ANY] * 8,
        out_specs=[ANY] * 8,
        scratch_shapes=[DMA((n,)), DMA((n,))],
        compiler_params=pltpu.CompilerParams(collective_id=1, has_side_effects=True),
        name="gather_qkv",
    )(wq, wk, wv, tok, lnp, wo, wi, wu)


def load_qkv(wall, own, weights, sem):
    w = lax.axis_index("wsh")
    copies = [
        pltpu.make_async_copy(own[m], weights.at[w, m], sem.at[m]) for m in range(3)
    ]
    for r in range(1, 4):
        k = (w + r) % 4
        copies.append(pltpu.make_async_copy(wall.at[k], weights.at[k], sem.at[2 + r]))
    for c in copies:
        c.start()
    return copies


def qkv_kernel(x_ref, wall, wq, wk, wv, kv_ref, q_ref, weights, sem):
    for c in load_qkv(wall, (wq, wk, wv), weights, sem):
        c.wait()

    def block(j, carry):
        lanes = pl.ds(pl.multiple_of(j * 256, 256), 256)

        def proj(m):
            total = dot(x_ref[:, :256], weights[0, m, :, lanes])
            for k in range(1, 4):
                total += dot(x_ref[:, 256 * k:256 * k + 256], weights[k, m, :, lanes])
            return total.astype(BF)

        q = (proj(0).astype(F32) * 0.125).astype(BF)
        k = proj(1)
        v = proj(2)
        for u in range(4):
            part = slice(64 * u, 64 * u + 64)
            kv_ref[4 * j + u] = jnp.concatenate([k[:, part], v[:, part]], axis=1)
            q_ref[4 * j + u] = jnp.concatenate([q[:64, part], q[64:, part]], axis=1)
        return carry

    lax.fori_loop(0, 4, block, 0)


def project(tok, wall, own):
    return pl.pallas_call(
        qkv_kernel,
        out_shape=[shp((16, 128, 128), BF), shp((16, 64, 128), BF)],
        in_specs=[VM] + [ANY] * 4,
        out_specs=[VM] * 2,
        scratch_shapes=[pltpu.VMEM((4, 3, 256, 1024), BF), DMA((6,))],
        compiler_params=pltpu.CompilerParams(vmem_limit_bytes=LIMIT),
        cost_estimate=pl.CostEstimate(flops=805306368, bytes_accessed=8 << 20, transcendentals=0),
        name="qkv",
    )(tok, wall, *own)


def exchange(wide, narrow, collective):
    has = wide is not None
    n = 32 if has else 16

    def kernel(*refs):
        if has:
            wi, na, wo, no, sw, rw, sn, rn, ls = refs
        else:
            na, no, sn, rn, ls = refs
        me = lax.axis_index("ctx")
        zl = me // 16
        flat = me % 16
        bar = pltpu.get_barrier_semaphore()

        def peer(i):
            if has:
                return (me + i) % 32
            return zl * 16 + (flat + i) % 16

        def greet_one(i, carry):
            pl.semaphore_signal(bar, inc=1, device_id={"ctx": peer(i)}, device_id_type=MESH)
            return carry

        lax.fori_loop(1, n, greet_one, 0)
        pl.semaphore_wait(bar, n - 1)

        def narrow_copy(i):
            p = (flat + i) % 16
            return pltpu.make_async_remote_copy(
                src_ref=na.at[p], dst_ref=no.at[flat], send_sem=sn.at[i], recv_sem=rn.at[i],
                device_id={"ctx": zl * 16 + p}, device_id_type=MESH,
            )

        def wide_copy(i):
            p = (me + i) % 32
            src = p if wide.shape[0] == 32 else p % 16
            return pltpu.make_async_remote_copy(
                src_ref=wi.at[src], dst_ref=wo.at[me], send_sem=sw.at[i], recv_sem=rw.at[i],
                device_id={"ctx": p}, device_id_type=MESH,
            )

        def start(make):
            def one(i, carry):
                make(i).start()
                return carry
            return one

        def wait(make):
            def one(i, carry):
                make(i).wait()
                return carry
            return one

        if has:
            lax.fori_loop(1, 32, start(wide_copy), 0)
        lax.fori_loop(1, 16, start(narrow_copy), 0)
        local = [pltpu.make_async_copy(na.at[flat], no.at[flat], ls.at[0])]
        if has:
            own = me if wide.shape[0] == 32 else flat
            local.append(pltpu.make_async_copy(wi.at[own], wo.at[me], ls.at[1]))
        for c in local:
            c.start()
        for c in local:
            c.wait()
        if has:
            lax.fori_loop(1, 32, wait(wide_copy), 0)
        lax.fori_loop(1, 16, wait(narrow_copy), 0)

    sems = ([DMA((32,)), DMA((32,))] if has else []) + [DMA((16,)), DMA((16,)), DMA((2,))]
    outs = ([shp((32,) + wide.shape[1:], wide.dtype)] if has else []) + [shp(narrow.shape, narrow.dtype)]
    args = ([wide] if has else []) + [narrow]
    return pl.pallas_call(
        kernel,
        out_shape=outs,
        in_specs=[ANY] * len(args),
        out_specs=[ANY] * len(outs),
        scratch_shapes=sems,
        compiler_params=pltpu.CompilerParams(collective_id=collective, has_side_effects=True),
        cost_estimate=pl.CostEstimate(flops=16 << 30, bytes_accessed=32 << 20, transcendentals=0),
        name=f"exchange_{collective}",
    )(*args)


def attention_setup(blk, mask, kvr, qr, kvs, kaug, kvt, bias, qs, inv, order, oblk):
    first = (lax.axis_index("ctx") // 16) * 32

    def note(s, carry):
        inv[blk[s]] = s
        return carry

    lax.fori_loop(0, 64, note, 0)

    def pick(b, count):
        local = inv[b] - first
        order[count] = local
        oblk[count] = b
        mine = jnp.logical_and(local >= 0, local < 32)
        return count + mine.astype(jnp.int32)

    lax.fori_loop(0, 64, pick, 0)
    for s in range(64):
        at = pl.ds(pl.multiple_of(blk[s] * 64, 64), 64)
        kvs[at, :] = kvr[s // 2, (s % 2) * 64:(s % 2) * 64 + 64, :]
    for j in range(16):
        pair = qr[j]
        qs[2 * j] = pair[:, :64]
        qs[2 * j + 1] = pair[:, 64:]
    rows = lax.broadcasted_iota(jnp.int32, (512, 64), 0) // 64
    lanes = lax.broadcasted_iota(jnp.int32, (512, 64), 1)
    for c in range(8):
        part = kvs[512 * c:512 * c + 512, :]
        hot = jnp.where(rows + 8 * c == lanes, 1.0, 0.0).astype(BF)
        kaug[512 * c:512 * c + 512, :] = jnp.concatenate([part[:, :64], hot], axis=1)
        kvt[c] = part.astype(F32).T.astype(BF)
    qi = lax.broadcasted_iota(jnp.int32, (64, 64), 0)
    ki = lax.broadcasted_iota(jnp.int32, (64, 64), 1)
    bias[...] = jnp.where(jnp.logical_and(mask[0] != 0, ki < qi), 0.0, NEG)


def triangle():
    key = lax.broadcasted_iota(jnp.int32, (64, 256), 0)
    query = lax.broadcasted_iota(jnp.int32, (64, 256), 1) % 64
    return key <= query


def attend_kernel(blk, mask, kvr, qr, o_ref, ot_ref, lse_ref, kvs, kaug, kvt, bias, qs, qa, os, inv, order, oblk):
    attention_setup(blk, mask, kvr, qr, kvs, kaug, kvt, bias, qs, inv, order, oblk)

    def tile(g, carry):
        score, vals = [], []
        for u in range(4):
            i = oblk[4 * g + u]
            q = qs[order[4 * g + u]]
            row = jnp.broadcast_to(bias[pl.ds(i, 1), :], (64, 64)).astype(BF)
            qa[64 * u:64 * u + 64, :] = jnp.concatenate([q, row], axis=1)
            kv = kvs[pl.ds(pl.multiple_of(i * 64, 64), 64), :]
            score.append(dot(kv[:, :64], q, NT))
            vals.append(kv[:, 64:])
        s = jnp.where(triangle(), jnp.concatenate(score, axis=1), NEG)
        top = jnp.max(s, axis=0, keepdims=True)
        p = jnp.exp(s - top)
        total = jnp.sum(p, axis=0, keepdims=True)
        pb = p.astype(BF)
        mix = jnp.concatenate([dot(vals[u], pb[:, 64 * u:64 * u + 64], TN) for u in range(4)], axis=1)
        queries = qa[...]

        def chunk(c, state):
            top, total, mix = state
            keys = kaug[pl.ds(pl.multiple_of(c * 512, 512), 512), :]
            s = dot(keys, queries, NT)
            new = jnp.maximum(top, jnp.max(s, axis=0, keepdims=True))
            shrink = jnp.exp(top - new)
            p = jnp.exp(s - new)
            total = total * shrink + jnp.sum(p, axis=0, keepdims=True)
            mix = mix * shrink + dot(kvt[c, 64:, :], p.astype(BF))
            return new, total, mix

        chunks = (oblk[4 * g + 3] + 7) // 8
        top, total, mix = lax.fori_loop(0, chunks, chunk, (top, total, mix))
        out = mix / total
        ot_ref[g] = out
        lse_ref[g] = top + jnp.log(total)
        back = out.T.astype(BF)
        for u in range(4):
            os[order[4 * g + u]] = back[64 * u:64 * u + 64, :]
        return carry

    lax.fori_loop(0, 8, tile, 0)
    for j in range(16):
        o_ref[j] = jnp.concatenate([os[2 * j], os[2 * j + 1]], axis=1)


def attention_scratch():
    return [
        pltpu.VMEM((4096, 128), BF),
        pltpu.VMEM((4096, 128), BF),
        pltpu.VMEM((8, 128, 512), BF),
        pltpu.VMEM((64, 64), F32),
        pltpu.VMEM((32, 64, 64), BF),
        pltpu.VMEM((256, 128), BF),
        pltpu.VMEM((32, 64, 64), BF),
        pltpu.SMEM((64,), jnp.int32),
        pltpu.SMEM((72,), jnp.int32),
        pltpu.SMEM((72,), jnp.int32),
    ]


def attend(blk, mask, kvr, qr):
    return pl.pallas_call(
        attend_kernel,
        out_shape=[shp((16, 64, 128), BF), shp((8, 64, 256), F32), shp((8, 1, 256), F32)],
        in_specs=[SM, VM, VM, VM],
        out_specs=[VM] * 3,
        scratch_shapes=attention_scratch(),
        compiler_params=pltpu.CompilerParams(vmem_limit_bytes=LIMIT),
        cost_estimate=pl.CostEstimate(flops=10 << 30, bytes_accessed=32 << 20, transcendentals=4 << 20),
        name="attend",
    )(blk, mask, kvr, qr)


def attend_back_kernel(
    blk, mask, kvr, qr, dor, ot_ref, lse_ref, dkv_ref, dq_ref,
    kvs, kaug, kvt, bias, qs, qa, dqs, inv, order, oblk, dos, qz, dz, dkv,
):
    attention_setup(blk, mask, kvr, qr, kvs, kaug, kvt, bias, qs, inv, order, oblk)
    for j in range(16):
        pair = dor[j]
        dos[2 * j] = pair[:, :64]
        dos[2 * j + 1] = pair[:, 64:]
    dkv[...] = jnp.zeros_like(dkv)
    zero = jnp.zeros((64, 64), BF)

    def tile(g, carry):
        score, dprob, places, keys_own, q_own, d_own = [], [], [], [], [], []
        for u in range(4):
            i = oblk[4 * g + u]
            q = qs[order[4 * g + u]]
            do = dos[order[4 * g + u]]
            rows = slice(64 * u, 64 * u + 64)
            row = jnp.broadcast_to(bias[pl.ds(i, 1), :], (64, 64)).astype(BF)
            qa[rows, :] = jnp.concatenate([q, row], axis=1)
            qz[rows, :] = jnp.concatenate([q, zero], axis=1)
            dz[rows, :] = jnp.concatenate([zero, do], axis=1)
            at = pl.ds(pl.multiple_of(i * 64, 64), 64)
            kv = kvs[at, :]
            score.append(dot(kv[:, :64], q, NT))
            dprob.append(dot(kv[:, 64:], do, NT))
            places.append(at)
            keys_own.append(kv[:, :64])
            q_own.append(q)
            d_own.append(do)
        lse = lse_ref[g]
        queries = qa[...]
        qpad = qz[...]
        dpad = dz[...]
        dot_t = dpad[:, 64:].astype(F32).T
        delta = jnp.sum(ot_ref[g] * dot_t, axis=0, keepdims=True)
        s = jnp.where(triangle(), jnp.concatenate(score, axis=1), NEG)
        p = jnp.exp(s - lse)
        ds = (p * (jnp.concatenate(dprob, axis=1) - delta)).astype(BF)
        pb = p.astype(BF)
        dq = []
        for u in range(4):
            lanes = slice(64 * u, 64 * u + 64)
            grad = jnp.concatenate([dot(ds[:, lanes], q_own[u]), dot(pb[:, lanes], d_own[u])], axis=1)
            dkv[places[u], :] += grad
            dq.append(dot(keys_own[u], ds[:, lanes], TN))

        def chunk(c, dq):
            at = pl.ds(pl.multiple_of(c * 512, 512), 512)
            p = jnp.exp(dot(kaug[at, :], queries, NT) - lse)
            dp = dot(kvs[at, :], dpad, NT)
            ds = (p * (dp - delta)).astype(BF)
            dkv[at, :] += dot(ds, qpad) + dot(p.astype(BF), dpad)
            return dq + dot(kvt[c, :64, :], ds)

        chunks = (oblk[4 * g + 3] + 7) // 8
        dq = lax.fori_loop(0, chunks, chunk, jnp.concatenate(dq, axis=1))
        back = (dq * 0.125).T.astype(BF)
        for u in range(4):
            dqs[order[4 * g + u]] = back[64 * u:64 * u + 64, :]
        return carry

    lax.fori_loop(0, 8, tile, 0)
    for j in range(16):
        dq_ref[j] = jnp.concatenate([dqs[2 * j], dqs[2 * j + 1]], axis=1)
    for s in range(64):
        at = pl.ds(pl.multiple_of(blk[s] * 64, 64), 64)
        dkv_ref[s // 2, (s % 2) * 64:(s % 2) * 64 + 64, :] = dkv[at, :].astype(BF)


def attend_back(blk, mask, kvr, qr, dor, ot, lse):
    return pl.pallas_call(
        attend_back_kernel,
        out_shape=[shp((32, 128, 128), BF), shp((16, 64, 128), BF)],
        in_specs=[SM] + [VM] * 6,
        out_specs=[VM] * 2,
        scratch_shapes=attention_scratch()
        + [
            pltpu.VMEM((32, 64, 64), BF),
            pltpu.VMEM((256, 128), BF),
            pltpu.VMEM((256, 128), BF),
            pltpu.VMEM((4096, 128), F32),
        ],
        compiler_params=pltpu.CompilerParams(vmem_limit_bytes=LIMIT),
        cost_estimate=pl.CostEstimate(flops=1 << 30, bytes_accessed=4 << 20, transcendentals=0),
        name="attend_back",
    )(blk, mask, kvr, qr, dor, ot, lse)


def norm_parts(v):
    center = v - jnp.mean(v, axis=1, keepdims=True)
    r = lax.rsqrt(jnp.mean(center * center, axis=1, keepdims=True) + EPS)
    return center * r, r


def norm_back(e, gain, z, r):
    g = e * gain
    return r * (g - jnp.mean(g, axis=1, keepdims=True) - z * jnp.mean(g * z, axis=1, keepdims=True))


def middle_kernel(*refs):
    o_ref, x_ref, e_ref, ln_ref, ln_own = refs[:5]
    shards = (refs[5:8], refs[8:11])
    pieces = (refs[11:19], refs[19:27])
    y_ref, dr_ref, do_ref, zpay, l_ref, gb_ref = refs[27:33]
    wo, wi, wu, us, gs, dus, nl, ob, sw, sp = refs[33:]
    zl, x, y, zh, co = place()
    w = zh * 2 + co
    where = [w, zh * 2 + 1 - co, (1 - zh) * 2 + co, (1 - zh) * 2 + 1 - co]
    copies = [[], [], []]
    for r, (a, b, c) in enumerate(shards):
        rows = pl.ds(pl.multiple_of(where[r] * 256, 256), 256)
        copies[0].append(pltpu.make_async_copy(a, wo.at[rows], sw.at[r, 0]))
        for k in range(4):
            cols = slice(1024 * k, 1024 * k + 1024)
            copies[1].append(pltpu.make_async_copy(b.at[:, cols], wi.at[k, rows], sw.at[r, 1 + k]))
        groups = pl.ds(where[r] * 8, 8)
        copies[2].append(pltpu.make_async_copy(c, wu.at[groups], sw.at[r, 5]))
    for r, parts in enumerate(pieces):
        t = where[2 + r]
        quarters = [(parts[s], 0, (x + 4 - s) % 4) for s in range(4)]
        quarters += [(parts[4 + s], 1, (y + 4 - s) % 4) for s in range(4)]
        for n, (ref, h, q) in enumerate(quarters):
            rows = pl.ds(pl.multiple_of(t * 256 + h * 128 + q * 32, 32), 32)
            copies[0].append(pltpu.make_async_copy(ref.at[0], wo.at[rows], sp.at[r, n, 0]))
            copies[1].append(pltpu.make_async_copy(ref.at[1:5], wi.at[:, rows], sp.at[r, n, 1]))
            copies[2].append(pltpu.make_async_copy(ref.at[5:9], wu.at[t * 8 + h * 4 + q], sp.at[r, n, 2]))
    for group in copies:
        for c in group:
            c.start()

    ln = jnp.concatenate([jnp.where(w == k, ln_own[...], ln_ref[k]) for k in range(4)], axis=1)
    gain0, gain1, bias0, bias1 = (ln[k:k + 1, :] for k in range(4))
    for h in range(16):
        pair = o_ref[h]
        ob[:64, 64 * h:64 * h + 64] = pair[:, :64]
        ob[64:, 64 * h:64 * h + 64] = pair[:, 64:]
    for c in copies[0]:
        c.wait()
    z0, r0 = norm_parts(x_ref[...].astype(F32) + dot(ob[...], wo[...]))
    n1 = z0 * gain0 + bias0
    nl[...] = n1.astype(BF)
    for c in copies[1]:
        c.wait()

    half = math.sqrt(0.5)

    def up(c, carry):
        u = dot(nl[...], wi[c])
        us[c] = u
        gs[:, pl.ds(pl.multiple_of(c * 1024, 1024), 1024)] = (0.5 * u * (1.0 + lax.erf(u * half))).astype(BF)
        return carry

    lax.fori_loop(0, 4, up, 0)
    for c in copies[2]:
        c.wait()

    def down(c, total):
        cols = pl.ds(pl.multiple_of(c * 1024, 1024), 1024)
        return total + dot(gs[:, cols], wu[pl.ds(c * 8, 8)].reshape(1024, 1024))

    r2 = lax.fori_loop(0, 4, down, n1)
    z1, r1 = norm_parts(r2)
    y_ref[...] = z1 * gain1 + bias1
    e = e_ref[...].astype(F32)
    dr2 = norm_back(e, gain1, z1, r1)
    dm = dr2.astype(BF)
    gb_ref[1:2, :] = jnp.sum(e * z1, axis=0, keepdims=True)
    gb_ref[3:4, :] = jnp.sum(e, axis=0, keepdims=True)

    def back(c, total):
        rows = pl.ds(pl.multiple_of(c * 1024, 1024), 1024)
        u = us[c]
        dg = dot(dm, wu[pl.ds(c * 8, 8)].reshape(1024, 1024), NT)
        slope = 0.5 * (1.0 + lax.erf(u * half)) + u * (jnp.exp(-0.5 * u * u) * (1.0 / math.sqrt(2 * math.pi)))
        du = (dg * slope).astype(BF)
        dus[:, rows] = du
        return total + dot(du, wi[c], NT)

    dn1 = lax.fori_loop(0, 4, back, dr2)
    gb_ref[0:1, :] = jnp.sum(dn1 * z0, axis=0, keepdims=True)
    gb_ref[2:3, :] = jnp.sum(dn1, axis=0, keepdims=True)
    gb_ref[4:8, :] = jnp.zeros((4, 1024), F32)
    dr1 = norm_back(dn1, gain0, z0, r0)
    dr_ref[...] = dr1
    da = dr1.astype(BF)
    do = dot(da, wo[...], NT).astype(BF)
    for h in range(16):
        lanes = slice(64 * h, 64 * h + 64)
        do_ref[h] = jnp.concatenate([do[:64, lanes], do[64:, lanes]], axis=1)
    du = dus[...]
    zpay[:, 1536:5632] = du
    zpay[:, 5632:6656] = dm
    zpay[:, 6656:7680] = da
    for r, (ref, at) in enumerate(((l_ref, 0), (l_ref, 1536), (zpay, 0), (zpay, 7680))):
        few = pl.ds(pl.multiple_of(where[r] * 256, 256), 256)
        many = pl.ds(pl.multiple_of(where[r] * 1024, 1024), 1024)
        ref[:, at:at + 256] = nl[:, few]
        ref[:, at + 256:at + 512] = ob[:, few]
        ref[:, at + 512:at + 1536] = gs[:, many]


def middle(o, tok, cot, lnf, lnp, shards, pieces):
    return pl.pallas_call(
        middle_kernel,
        out_shape=[
            shp((128, 1024), F32), shp((128, 1024), F32), shp((16, 64, 128), BF),
            shp((128, 9216), BF), shp((128, 3072), BF), shp((8, 1024), F32),
        ],
        in_specs=[VM] * 5 + [ANY] * 22,
        out_specs=[VM] * 6,
        scratch_shapes=[
            pltpu.VMEM((1024, 1024), BF),
            pltpu.VMEM((4, 1024, 1024), BF),
            pltpu.VMEM((32, 4, 32, 1024), BF),
            pltpu.VMEM((4, 128, 1024), F32),
            pltpu.VMEM((128, 4096), BF),
            pltpu.VMEM((128, 4096), BF),
            pltpu.VMEM((128, 1024), BF),
            pltpu.VMEM((128, 1024), BF),
            DMA((2, 6)), DMA((2, 8, 3)),
        ],
        compiler_params=pltpu.CompilerParams(vmem_limit_bytes=LIMIT),
        cost_estimate=pl.CostEstimate(flops=10 << 30, bytes_accessed=32 << 20, transcendentals=2 << 20),
        name="middle",
    )(o, tok, cot, lnf, lnp, *shards[0], *shards[1], *pieces[0], *pieces[1])


class Spread:
    def __init__(self, wire, plus, minus, at, piece, bufs):
        self.wire, self.plus, self.minus, self.at, self.piece = wire, plus, minus, at, piece
        self.rp, self.rm, self.m, self.f = bufs

    def part(self, s, u):
        return self.piece((self.at + s) % 4, u)

    def start(self):
        self.a = self.wire(self.part(2, 0), self.m.at[0], self.plus)
        self.b = self.wire(self.part(2, 1), self.m.at[1], self.minus)
        self.c = self.wire(self.part(1, 1), self.rp.at[1], self.plus)
        self.d = self.wire(self.part(3, 0), self.rm.at[0], self.minus)

    def relay(self):
        self.a.wait_recv()
        self.f[0] = (self.part(1, 0)[...].astype(F32) + self.m[0].astype(F32)).astype(BF)
        self.e = self.wire(self.f.at[0], self.rp.at[0], self.plus)
        self.b.wait_recv()
        self.f[1] = (self.part(3, 1)[...].astype(F32) + self.m[1].astype(F32)).astype(BF)
        self.g = self.wire(self.f.at[1], self.rm.at[1], self.minus)

    def total(self):
        for c in (self.c, self.d, self.e, self.g):
            c.wait_recv()
        return [
            self.part(0, u)[...].astype(F32) + self.rp[u].astype(F32) + self.rm[u].astype(F32) for u in range(2)
        ]

    def sent(self):
        for c in (self.a, self.b, self.c, self.d, self.e, self.g):
            c.wait_send()


class Gather:
    def __init__(self, wire, plus, minus, at, block):
        self.wire, self.plus, self.minus, self.at, self.block = wire, plus, minus, at, block

    def send(self, s, u, peer):
        spot = self.block((self.at + s) % 4, u)
        return self.wire(spot, spot, peer)

    def start(self):
        self.p0 = self.send(0, 0, self.plus)
        self.m1 = self.send(0, 1, self.minus)
        self.p1 = self.send(0, 1, self.plus)
        self.m0 = self.send(0, 0, self.minus)

    def relay(self):
        self.p0.wait_recv()
        self.rp = self.send(3, 0, self.plus)
        self.m1.wait_recv()
        self.rm = self.send(1, 1, self.minus)

    def done(self):
        for c in (self.p1, self.m0, self.rp, self.rm):
            c.wait()
        for c in (self.p0, self.m1):
            c.wait_send()


class Sum:
    def __init__(self, g, hc, refs, wire, where, xp, yp, zp):
        bufs1, s1, bufs2, s2, self.r3, full = refs[:4], refs[4], refs[5:9], refs[9], refs[10], refs[11]
        zl, x, y, zh, co = where
        self.wire, self.zp, self.zl, self.hc = wire, zp, zl, hc
        self.s1, self.s2, self.full = s1, s2, full
        hh = hc // 2
        first, second = (xp, yp), (yp, xp)
        self.at1, self.at2 = (x, y), (y, x)

        def rows(h, k, u):
            return pl.ds(pl.multiple_of(h * 4 * hc + k * hc + u * hh, 16), hh)

        def cols(k, width):
            return pl.ds(pl.multiple_of(k * width, 128), width)

        self.cols = cols

        def one(h):
            return lambda k, u: g.at[rows(h, k, u)]

        def two(h):
            return lambda k, u: s1.at[h, u, :, cols(k, 256)]

        def five(h):
            return lambda k, u: full.at[rows(h, self.at1[h], u), cols(k, 256)]

        def six(h):
            return lambda k, u: full.at[rows(h, k, u)]

        def ends(peers):
            return wire, peers[0], peers[2]

        self.one = [Spread(*ends(first[h]), self.at1[h], one(h), [r.at[h] for r in bufs1]) for h in range(2)]
        self.two = [Spread(*ends(second[h]), self.at2[h], two(h), [r.at[h] for r in bufs2]) for h in range(2)]
        self.five = [Gather(*ends(second[h]), self.at2[h], five(h)) for h in range(2)]
        self.six = [Gather(*ends(first[h]), self.at1[h], six(h)) for h in range(2)]

    def steps(self):
        for t in self.one:
            t.start()
        yield
        for t in self.one:
            t.relay()
        yield
        for h in range(2):
            for u, total in enumerate(self.one[h].total()):
                self.s1[h, u] = total.astype(BF)
            self.two[h].start()
        yield
        for t in self.two:
            t.relay()
        yield
        three = []
        for h in range(2):
            for u, total in enumerate(self.two[h].total()):
                self.s2[h, u] = total.astype(BF)
            three.append(self.wire(self.s2.at[h, :, :, self.cols(1 - self.zl, 128)], self.r3.at[h], self.zp))
        yield
        four = []
        for h in range(2):
            three[h].wait_recv()
            for u in range(2):
                total = self.s2[h, u, :, self.cols(self.zl, 128)].astype(F32) + self.r3[h, u].astype(F32)
                rows = pl.ds(pl.multiple_of(h * 4 * self.hc + self.at1[h] * self.hc + u * (self.hc // 2), 16), self.hc // 2)
                spot = self.full.at[rows, self.cols(self.at2[h] * 2 + self.zl, 128)]
                spot[...] = total.astype(BF)
                four.append(self.wire(spot, spot, self.zp))
        yield
        for h in range(2):
            four[2 * h].wait()
            four[2 * h + 1].wait()
            self.five[h].start()
        yield
        for t in self.five:
            t.relay()
        yield
        for h in range(2):
            self.five[h].done()
            self.six[h].start()
        yield
        for t in self.six:
            t.relay()
        yield
        for t in self.one + self.two:
            t.sent()
        for c in three:
            c.wait_send()
        for t in self.six:
            t.done()
        yield


SUM_COPIES = 12 + 12 + 2 + 4 + 12 + 12


def sum_scratch(rows):
    hc = rows // 8
    hh = hc // 2
    return (
        [pltpu.VMEM((2, 2, hh, 1024), BF)] * 4
        + [pltpu.VMEM((2, 2, hh, 1024), BF)]
        + [pltpu.VMEM((2, 2, hh, 256), BF)] * 4
        + [pltpu.VMEM((2, 2, hh, 256), BF), pltpu.VMEM((2, 2, hh, 128), BF)]
    )


def finish_kernel(*refs):
    dkvp, dqp, dr_ref, gb, wall, wq, wk, wv, l_ref, own, zr, xs, x_ref = refs[:13]
    gt, mid_full, tail_full, s_vec = refs[13:17]
    mid_refs, tail_refs = list(refs[17:28]) + [mid_full], list(refs[28:39]) + [tail_full]
    (dkv, dq, weights, ll2, rr2, lt2, mid, pay, ll, rr, tail, v0, vx, vy, vz, tx, ty,
     sw, rw, sn, rn, ss, rs, ls, lw) = refs[39:]
    scale = 1.0 / math.sqrt(16384)
    where = place()
    zl, x, y, zh, co = where
    w = zh * 2 + co
    me = lax.axis_index("ctx")
    flat = me % 16
    core = device(zl, x, y, zh, 1 - co)
    far = device(zl, x, y, 1 - zh, co)
    xp = [device(zl, (x + s) % 4, y, zh, co) for s in (1, 2, 3)]
    yp = [device(zl, x, (y + s) % 4, zh, co) for s in (1, 2, 3)]
    zp = device(1 - zl, x, y, zh, co)
    bar = pltpu.get_barrier_semaphore()

    def greet_one(i, carry):
        pl.semaphore_signal(bar, inc=1, device_id={"ctx": (me + i) % 32}, device_id_type=MESH)
        return carry

    for p in (core, far):
        pl.semaphore_signal(bar, inc=1, device_id=p, device_id_type=MESH)
    lax.fori_loop(1, 32, greet_one, 0)

    mine = pl.ds(pl.multiple_of(w * 256, 256), 256)
    order = [w, zh * 2 + 1 - co, (1 - zh) * 2 + co, (1 - zh) * 2 + 1 - co]
    local = [
        pltpu.make_async_copy(l_ref.at[:, :1536], ll2.at[0:128, :], ls.at[0]),
        pltpu.make_async_copy(own.at[:, 1536:7680], rr2.at[0:128, :], ls.at[1]),
        pltpu.make_async_copy(zr.at[:, :1536], ll2.at[256:384, :], ls.at[2]),
        pltpu.make_async_copy(zr.at[:, 1536:7680], rr2.at[256:384, :], ls.at[3]),
        pltpu.make_async_copy(x_ref.at[:, mine], ll.at[0:128, :], ls.at[4]),
    ]
    for k in range(1, 4):
        local.append(pltpu.make_async_copy(xs.at[order[k]], ll.at[128 * k:128 * k + 128, :], ls.at[4 + k]))
    for c in local:
        c.start()
    loads = load_qkv(wall, (wq, wk, wv), weights, lw)
    pl.semaphore_wait(bar, 33)

    def narrow_copy(i):
        p = (flat + i) % 16
        return pltpu.make_async_remote_copy(
            src_ref=dqp.at[p], dst_ref=dq.at[flat], send_sem=sn.at[i], recv_sem=rn.at[i],
            device_id={"ctx": zl * 16 + p}, device_id_type=MESH,
        )

    def wide_copy(i):
        p = (me + i) % 32
        return pltpu.make_async_remote_copy(
            src_ref=dkvp.at[p], dst_ref=dkv.at[me], send_sem=sw.at[i], recv_sem=rw.at[i],
            device_id={"ctx": p}, device_id_type=MESH,
        )

    def start(make):
        def one(i, carry):
            make(i).start()
            return carry
        return one

    def wait(make):
        def one(i, carry):
            make(i).wait()
            return carry
        return one

    lax.fori_loop(1, 32, start(wide_copy), 0)
    lax.fori_loop(1, 16, start(narrow_copy), 0)
    home = [
        pltpu.make_async_copy(dkvp.at[me], dkv.at[me], ls.at[8]),
        pltpu.make_async_copy(dqp.at[flat], dq.at[flat], ls.at[9]),
    ]
    for c in home:
        c.start()
    wire = Wire(ss, rs)
    near = [
        wire(l_ref.at[:, 1536:], ll2.at[128:256, :], core),
        wire(own.at[:, 1536:7680], rr2.at[128:256, :], core),
        wire(zr.at[:, 7680:], ll2.at[384:512, :], core),
        wire(zr.at[:, 1536:7680], rr2.at[384:512, :], core),
    ]
    big = Sum(mid, 288, mid_refs, wire, where, xp, yp, zp).steps()
    small = Sum(tail, 96, tail_refs, wire, where, xp, yp, zp).steps()
    for c in local:
        c.wait()
    lt = ll[...].astype(F32).T.astype(BF)
    for c in near:
        c.wait()
    for k in range(6):
        lt2[256 * k:256 * k + 256, :] = ll2[:, 256 * k:256 * k + 256].astype(F32).T.astype(BF)
    mid[0:256, :] = dot(lt2[256:512, :], rr2[:, 5120:6144]).astype(BF)
    for k in range(4):
        mid[256 + 256 * k:512 + 256 * k, :] = dot(lt2[0:256, :], rr2[:, 1024 * k:1024 * k + 1024]).astype(BF)
    for k in range(4):
        rows = slice(512 + 256 * k, 768 + 256 * k)
        mid[1280 + 256 * k:1536 + 256 * k, :] = dot(lt2[rows, :], rr2[:, 4096:5120]).astype(BF)
    next(big)

    for c in home:
        c.wait()
    lax.fori_loop(1, 32, wait(wide_copy), 0)
    lax.fori_loop(1, 16, wait(narrow_copy), 0)
    for h in range(16):
        lanes = slice(64 * h, 64 * h + 64)
        pair = dq[h]
        pay[:64, lanes] = pair[:, :64]
        pay[64:128, lanes] = pair[:, 64:]
        both = (dkv[h].astype(F32) + dkv[16 + h].astype(F32)).astype(BF)
        pay[:128, 1024 + 64 * h:1088 + 64 * h] = both[:, :64]
        pay[:128, 2048 + 64 * h:2112 + 64 * h] = both[:, 64:]
    pay[128:144, :1024] = jnp.concatenate([gb[...], jnp.zeros((8, 1024), F32)], axis=0).astype(BF)
    pay[128:144, 1024:] = jnp.zeros((16, 2048), BF)
    to_far = wire(pay, rr.at[1], far)
    to_core = wire(pay, rr.at[0], core)
    next(big)
    for c in loads:
        c.wait()
    for k in range(4):
        cols = slice(256 * k, 256 * k + 256)
        total = dr_ref[:, cols]
        for m in range(3):
            total += dot(pay[:128, 1024 * m:1024 * m + 1024], weights[k, m], NT)
        gt[:, cols] = total
    to_far.wait_recv()
    on_core = wire(rr.at[1], rr.at[2], core)
    next(big)
    to_core.wait_recv()
    on_core.wait_recv()
    for m in range(3):
        cols = slice(1024 * m, 1024 * m + 1024)
        total = dot(lt[:, 0:128], pay[:128, cols])
        for k in range(3):
            total += dot(lt[:, 128 * k + 128:128 * k + 256], rr[k, :128, cols])
        tail[256 * m:256 * m + 256, :] = total.astype(BF)
    next(small)
    vec = pay[128:144, mine].astype(F32)
    for k in range(3):
        vec += rr[k, 128:144, mine].astype(F32)
    v0[...] = vec[:8]
    vone = [wire(v0, vx.at[s], xp[s]) for s in range(3)]
    next(big)
    next(small)
    next(big)
    next(small)
    for c in vone:
        c.wait_recv()
    tx[...] = v0[...] + vx[0] + vx[1] + vx[2]
    vtwo = [wire(tx, vy.at[s], yp[s]) for s in range(3)]
    next(big)
    next(small)
    next(big)
    next(small)
    for c in vtwo:
        c.wait_recv()
    ty[...] = tx[...] + vy[0] + vy[1] + vy[2]
    vthree = wire(ty, vz, zp)
    next(big)
    next(small)
    next(big)
    next(small)
    next(big)
    next(small)
    vthree.wait()
    s_vec[...] = (ty[...] + vz[...]) * scale
    for c in vone + vtwo + [to_far, to_core, on_core]:
        c.wait_send()
    next(small)
    next(small)
    next(big)
    next(small)


def finish(dkvp, dqp, dr, gb, wall, own, l01, zpay, zr, xs, tok):
    n = SUM_COPIES * 2 + 4 + 3 + 7
    return pl.pallas_call(
        finish_kernel,
        out_shape=[shp((128, 1024), F32), shp((2304, 1024), BF), shp((768, 1024), BF), shp((8, 256), F32)],
        in_specs=[ANY, ANY, VM, VM] + [ANY] * 9,
        out_specs=[VM] * 4,
        scratch_shapes=sum_scratch(2304) + sum_scratch(768) + [
            pltpu.VMEM((32, 128, 128), BF), pltpu.VMEM((16, 64, 128), BF), pltpu.VMEM((4, 3, 256, 1024), BF),
            pltpu.VMEM((512, 1536), BF), pltpu.VMEM((512, 6144), BF), pltpu.VMEM((1536, 512), BF),
            pltpu.VMEM((2304, 1024), BF), pltpu.VMEM((144, 3072), BF),
            pltpu.VMEM((512, 256), BF), pltpu.VMEM((3, 144, 3072), BF), pltpu.VMEM((768, 1024), BF),
            pltpu.VMEM((8, 256), F32), pltpu.VMEM((3, 8, 256), F32), pltpu.VMEM((3, 8, 256), F32),
            pltpu.VMEM((8, 256), F32), pltpu.VMEM((8, 256), F32), pltpu.VMEM((8, 256), F32),
            DMA((32,)), DMA((32,)), DMA((16,)), DMA((16,)), DMA((n,)), DMA((n,)), DMA((10,)), DMA((6,)),
        ],
        compiler_params=pltpu.CompilerParams(collective_id=6, has_side_effects=True, vmem_limit_bytes=LIMIT),
        name="finish",
    )(dkvp, dqp, dr, gb, wall, *own, l01, zpay, zr, xs, tok)


def scale_kernel(o, i0, i1, i2, i3, u, q, k, v, out_q, out_k, out_v, out_o, out_i, out_u):
    scale = 1.0 / math.sqrt(16384)
    for src, dst in ((q, out_q), (k, out_k), (v, out_v), (o, out_o), (u, out_u)):
        dst[...] = src[...].astype(F32) * scale
    for n, src in enumerate((i0, i1, i2, i3)):
        out_i[:, 1024 * n:1024 * n + 1024] = src[...].astype(F32) * scale


def scaled(mid, tail):
    def rows(first, n=32):
        return pl.BlockSpec((n, 1024), lambda j: (first // n + j, 0))

    return pl.pallas_call(
        scale_kernel,
        grid=(8,),
        out_shape=[shp((256, 1024), F32)] * 4 + [shp((256, 4096), F32), shp((1024, 1024), F32)],
        in_specs=[rows(0)] + [rows(256 + 256 * k) for k in range(4)] + [rows(1280, 128)] + [rows(256 * k) for k in range(3)],
        out_specs=[rows(0)] * 4 + [pl.BlockSpec((32, 4096), lambda j: (j, 0)), rows(0, 128)],
        compiler_params=pltpu.CompilerParams(vmem_limit_bytes=LIMIT),
        name="scaled",
    )(*[mid] * 6, *[tail] * 3)


FLIP_CORE = [(0, 1), (1, 0), (2, 3), (3, 2)]
FLIP_FAR = [(0, 2), (2, 0), (1, 3), (3, 1)]


def along_x(s):
    return [(c, c // 16 * 16 + (c // 4 + s) % 4 * 4 + c % 4) for c in range(32)]


def along_y(s):
    return [(c, c // 4 * 4 + (c + s) % 4) for c in range(32)]


def body(
    tokens, w_query, w_key, w_value, w_output, w_inner, w_outer, ln_gain, ln_bias, block_mask, block_pairs, cotangent,
):
    tok = tokens.reshape(128, 1024)
    cot = cotangent.reshape(128, 1024)
    lnp = jnp.concatenate([ln_gain, ln_bias, jnp.zeros((4, 256), F32)], axis=0)
    blk = block_pairs.reshape(-1)
    own = (w_query, w_key, w_value)
    outer = w_outer.reshape(8, 4, 32, 1024)
    wall, xs, lnf, *core_shard, qa, qb = gather_weights(*own, tok, lnp, w_output, w_inner, outer)
    qa, qb, wall = lax.optimization_barrier((qa, qb, wall))
    x2 = lax.ppermute(qa, "ctx", along_x(2))
    y2 = lax.ppermute(qb, "ctx", along_y(2))
    diag_a = lax.ppermute(qa, "wsh", FLIP_CORE)
    diag_b = lax.ppermute(qb, "wsh", FLIP_CORE)

    kvp, qp = project(tok, wall, own)
    kvr, qr = exchange(kvp, qp, 2)
    qa, qb, x2, y2, diag_a, diag_b, kvr = lax.optimization_barrier((qa, qb, x2, y2, diag_a, diag_b, kvr))
    x1, x3 = (lax.ppermute(qa, "ctx", along_x(s)) for s in (1, 3))
    y1, y3 = (lax.ppermute(qb, "ctx", along_y(s)) for s in (1, 3))
    o, ot, lse = attend(blk, block_mask, kvr, qr)
    x1, x2, x3, y1, y2, y3, o = lax.optimization_barrier((x1, x2, x3, y1, y2, y3, o))
    far = [qa, x1, x2, x3, qb, y1, y2, y3]
    d1, d2, d3, e1, e2, e3 = (lax.ppermute(p, "wsh", FLIP_CORE) for p in (x1, x2, x3, y1, y2, y3))
    diag = [diag_a, d1, d2, d3, diag_b, e1, e2, e3]
    (o_back,) = exchange(None, o, 3)
    y_out, dr1, do, zpay, l01, gb = middle(
        o_back, tok, cot, lnf, lnp, ((w_output, w_inner, outer), core_shard), (far, diag)
    )
    zr = lax.ppermute(zpay, "wsh", FLIP_FAR)

    (dor,) = exchange(None, do, 3)
    dkvp, dqp = attend_back(blk, block_mask, kvr, qr, dor, ot, lse)
    zr, dkvp = lax.optimization_barrier((zr, dkvp))
    grad_tok, mid, tail, s_vec = finish(dkvp, dqp, dr1, gb, wall, own, l01, zpay, zr, xs, tok)
    s_q, s_k, s_v, s_o, s_i, s_u = scaled(mid, tail)
    out_shape = tokens.shape
    return (
        y_out.reshape(out_shape), grad_tok.reshape(out_shape), s_q, s_k, s_v, s_o, s_i, s_u, s_vec[0:2], s_vec[2:4],
    )


def solution(mesh):
    return jax.shard_map(
        body,
        mesh=mesh,
        in_specs=(
            P("wsh", "ctx", None, None),
            P("wsh", None), P("wsh", None), P("wsh", None), P("wsh", None), P("wsh", None), P("wsh", None),
            P(None, "wsh"), P(None, "wsh"),
            P("wsh", None, None),
            P(),
            P("wsh", "ctx", None, None),
        ),
        out_specs=(
            P("wsh", "ctx", None, None), P("wsh", "ctx", None, None),
            P("wsh", None), P("wsh", None), P("wsh", None), P("wsh", None), P("wsh", None), P("wsh", None),
            P(None, "wsh"), P(None, "wsh"),
        ),
        check_vma=False,
    )
```

```python
import math

import jax
import jax.numpy as jnp
from jax import lax
from jax.experimental import pallas as pl
from jax.experimental.pallas import tpu as pltpu
from jax.sharding import PartitionSpec as P

MESH = pl.DeviceIdType.MESH
BF = jnp.bfloat16
F32 = jnp.float32
ANY = pl.BlockSpec(memory_space=pl.ANY)
VM = pl.BlockSpec(memory_space=pltpu.VMEM)
SM = pl.BlockSpec(memory_space=pltpu.SMEM)
DMA = pltpu.SemaphoreType.DMA
LIMIT = 56 * 1024 * 1024
EPS = 1e-05
NEG = -1e30


def shp(shape, dtype):
    return jax.ShapeDtypeStruct(shape, dtype)


def dot(a, b, dims=((1,), (0,))):
    return lax.dot_general(a, b, (dims, ((), ())), preferred_element_type=F32)


NN = ((1,), (0,))
NT = ((1,), (1,))
TN = ((0,), (0,))


def place():
    c = lax.axis_index("ctx")
    w = lax.axis_index("wsh")
    return c // 16, (c // 4) % 4, c % 4, w // 2, w % 2


def device(zl, x, y, zh, co):
    return {"ctx": zl * 16 + x * 4 + y, "wsh": zh * 2 + co}


def greet(peers):
    bar = pltpu.get_barrier_semaphore()
    for p in peers:
        pl.semaphore_signal(bar, inc=1, device_id=p, device_id_type=MESH)
    pl.semaphore_wait(bar, len(peers))


class Wire:
    def __init__(self, send, recv):
        self.send, self.recv, self.n = send, recv, 0

    def __call__(self, src, dst, peer):
        k = self.n
        self.n += 1
        copy = pltpu.make_async_remote_copy(
            src_ref=src, dst_ref=dst, send_sem=self.send.at[k], recv_sem=self.recv.at[k],
            device_id=peer, device_id_type=MESH,
        )
        copy.start()
        return copy


def gather_kernel(wq, wk, wv, x_ref, ln_ref, wo, wi, wu, wall, xs, lnf, co_ref, ci_ref, cu_ref, qa_ref, qb_ref, ss, rs):
    zl, x, y, zh, co = place()
    me = zh * 2 + co
    other = (1 - zh) * 2 + co
    core = device(zl, x, y, zh, 1 - co)
    far = device(zl, x, y, 1 - zh, co)
    diag = device(zl, x, y, 1 - zh, 1 - co)
    xp = [device(zl, (x + s) % 4, y, zh, co) for s in (1, 2, 3)]
    yp = [device(zl, x, (y + s) % 4, zh, co) for s in (1, 2, 3)]
    greet([core, far, diag] + xp + yp)
    wire = Wire(ss, rs)
    ws = (wq, wk, wv)
    rows_a = pl.ds(pl.multiple_of(x * 32, 32), 32)
    rows_b = pl.ds(pl.multiple_of(128 + y * 32, 32), 32)
    first_a, first_b = [], []
    for m in range(3):
        first_a.append(wire(ws[m].at[rows_a], wall.at[me, m, rows_a], far))
        first_b.append(wire(ws[m].at[rows_b], wall.at[me, m, rows_b], far))
    rest = []
    for m in range(3):
        rest.append(wire(ws[m], wall.at[me, m], core))
    for p in (core, far, diag):
        rest.append(wire(ln_ref, lnf.at[me], p))
    for n, idx in enumerate((zh * 2 + 1 - co, (1 - zh) * 2 + 1 - co)):
        rest.append(wire(x_ref.at[:, pl.ds(pl.multiple_of(idx * 256, 256), 256)], xs.at[n], core))
    quarters = []
    for ref, k, n in ((qa_ref, x, y), (qb_ref, 4 + y, x)):
        rows = pl.ds(pl.multiple_of(k * 32, 32), 32)
        cols = pl.ds(pl.multiple_of(n * 256, 256), 256)
        quarters.append(wire(wo.at[rows, cols], ref.at[0, :, cols], far))
        for b in range(4):
            at = pl.ds(pl.multiple_of(1024 * b + n * 256, 256), 256)
            quarters.append(wire(wi.at[rows, at], ref.at[1 + b, :, cols], far))
        quarters.append(wire(wu.at[k, :, :, cols], ref.at[5:9, :, cols], far))
    for c in first_a:
        c.wait_recv()
    second = []
    for m in range(3):
        part = wall.at[other, m, rows_a]
        for p in xp:
            second.append(wire(part, part, p))
    for c in first_b:
        c.wait_recv()
    for m in range(3):
        part = wall.at[other, m, rows_b]
        for p in yp:
            second.append(wire(part, part, p))
    for src, dst in ((wo, co_ref), (wi, ci_ref), (wu, cu_ref)):
        rest.append(wire(src, dst, core))
    for c in quarters:
        c.wait_recv()
    for ref, n, peers in ((qa_ref, y, yp), (qb_ref, x, xp)):
        spot = ref.at[:, :, pl.ds(pl.multiple_of(n * 256, 256), 256)]
        for p in peers:
            rest.append(wire(spot, spot, p))
    for c in second:
        c.wait_recv()
    last = [wire(wall.at[other, m], wall.at[other, m], core) for m in range(3)]
    for c in last:
        c.wait()
    for c in first_a + first_b + second + quarters:
        c.wait_send()
    for c in rest:
        c.wait()


def gather_weights(wq, wk, wv, tok, lnp, wo, wi, wu):
    n = 6 + 3 + 5 + 12 + 18 + 3 + 6 + 3
    return pl.pallas_call(
        gather_kernel,
        out_shape=[
            shp((4, 3, 256, 1024), BF), shp((2, 128, 256), BF), shp((4, 8, 256), F32),
            shp(wo.shape, BF), shp(wi.shape, BF), shp(wu.shape, BF), shp((9, 32, 1024), BF), shp((9, 32, 1024), BF),
        ],
        in_specs=[ANY] * 8,
        out_specs=[ANY] * 8,
        scratch_shapes=[DMA((n,)), DMA((n,))],
        compiler_params=pltpu.CompilerParams(collective_id=1, has_side_effects=True),
        name="gather_qkv",
    )(wq, wk, wv, tok, lnp, wo, wi, wu)


def load_qkv(wall, own, weights, sem):
    w = lax.axis_index("wsh")
    copies = [
        pltpu.make_async_copy(own[m], weights.at[w, m], sem.at[m]) for m in range(3)
    ]
    for r in range(1, 4):
        k = (w + r) % 4
        copies.append(pltpu.make_async_copy(wall.at[k], weights.at[k], sem.at[2 + r]))
    for c in copies:
        c.start()
    return copies


def qkv_kernel(x_ref, wall, wq, wk, wv, kv_ref, q_ref, weights, sem):
    for c in load_qkv(wall, (wq, wk, wv), weights, sem):
        c.wait()

    def block(j, carry):
        lanes = pl.ds(pl.multiple_of(j * 256, 256), 256)

        def proj(m):
            total = dot(x_ref[:, :256], weights[0, m, :, lanes])
            for k in range(1, 4):
                total += dot(x_ref[:, 256 * k:256 * k + 256], weights[k, m, :, lanes])
            return total.astype(BF)

        q = (proj(0).astype(F32) * 0.125).astype(BF)
        k = proj(1)
        v = proj(2)
        for u in range(4):
            part = slice(64 * u, 64 * u + 64)
            kv_ref[4 * j + u] = jnp.concatenate([k[:, part], v[:, part]], axis=1)
            q_ref[4 * j + u] = jnp.concatenate([q[:64, part], q[64:, part]], axis=1)
        return carry

    lax.fori_loop(0, 4, block, 0)


def project(tok, wall, own):
    return pl.pallas_call(
        qkv_kernel,
        out_shape=[shp((16, 128, 128), BF), shp((16, 64, 128), BF)],
        in_specs=[VM] + [ANY] * 4,
        out_specs=[VM] * 2,
        scratch_shapes=[pltpu.VMEM((4, 3, 256, 1024), BF), DMA((6,))],
        compiler_params=pltpu.CompilerParams(vmem_limit_bytes=LIMIT),
        cost_estimate=pl.CostEstimate(flops=805306368, bytes_accessed=8 << 20, transcendentals=0),
        name="qkv",
    )(tok, wall, *own)


def exchange(wide, narrow, collective):
    has = wide is not None
    n = 32 if has else 16

    def kernel(*refs):
        if has:
            wi, na, wo, no, sw, rw, sn, rn, ls = refs
        else:
            na, no, sn, rn, ls = refs
        me = lax.axis_index("ctx")
        zl = me // 16
        flat = me % 16
        bar = pltpu.get_barrier_semaphore()

        def peer(i):
            if has:
                return (me + i) % 32
            return zl * 16 + (flat + i) % 16

        def greet_one(i, carry):
            pl.semaphore_signal(bar, inc=1, device_id={"ctx": peer(i)}, device_id_type=MESH)
            return carry

        lax.fori_loop(1, n, greet_one, 0)
        pl.semaphore_wait(bar, n - 1)

        def narrow_copy(i):
            p = (flat + i) % 16
            return pltpu.make_async_remote_copy(
                src_ref=na.at[p], dst_ref=no.at[flat], send_sem=sn.at[i], recv_sem=rn.at[i],
                device_id={"ctx": zl * 16 + p}, device_id_type=MESH,
            )

        def wide_copy(i):
            p = (me + i) % 32
            src = p if wide.shape[0] == 32 else p % 16
            return pltpu.make_async_remote_copy(
                src_ref=wi.at[src], dst_ref=wo.at[me], send_sem=sw.at[i], recv_sem=rw.at[i],
                device_id={"ctx": p}, device_id_type=MESH,
            )

        def start(make):
            def one(i, carry):
                make(i).start()
                return carry
            return one

        def wait(make):
            def one(i, carry):
                make(i).wait()
                return carry
            return one

        if has:
            lax.fori_loop(1, 32, start(wide_copy), 0)
        lax.fori_loop(1, 16, start(narrow_copy), 0)
        local = [pltpu.make_async_copy(na.at[flat], no.at[flat], ls.at[0])]
        if has:
            own = me if wide.shape[0] == 32 else flat
            local.append(pltpu.make_async_copy(wi.at[own], wo.at[me], ls.at[1]))
        for c in local:
            c.start()
        for c in local:
            c.wait()
        if has:
            lax.fori_loop(1, 32, wait(wide_copy), 0)
        lax.fori_loop(1, 16, wait(narrow_copy), 0)

    sems = ([DMA((32,)), DMA((32,))] if has else []) + [DMA((16,)), DMA((16,)), DMA((2,))]
    outs = ([shp((32,) + wide.shape[1:], wide.dtype)] if has else []) + [shp(narrow.shape, narrow.dtype)]
    args = ([wide] if has else []) + [narrow]
    return pl.pallas_call(
        kernel,
        out_shape=outs,
        in_specs=[ANY] * len(args),
        out_specs=[ANY] * len(outs),
        scratch_shapes=sems,
        compiler_params=pltpu.CompilerParams(collective_id=collective, has_side_effects=True),
        cost_estimate=pl.CostEstimate(flops=16 << 30, bytes_accessed=32 << 20, transcendentals=0),
        name=f"exchange_{collective}",
    )(*args)


def attention_setup(blk, mask, kvr, qr, kvs, kaug, kvt, bias, qs, inv, order, oblk):
    first = (lax.axis_index("ctx") // 16) * 32

    def note(s, carry):
        inv[blk[s]] = s
        return carry

    lax.fori_loop(0, 64, note, 0)

    def pick(b, count):
        local = inv[b] - first
        order[count] = local
        oblk[count] = b
        mine = jnp.logical_and(local >= 0, local < 32)
        return count + mine.astype(jnp.int32)

    lax.fori_loop(0, 64, pick, 0)
    for s in range(64):
        at = pl.ds(pl.multiple_of(blk[s] * 64, 64), 64)
        kvs[at, :] = kvr[s // 2, (s % 2) * 64:(s % 2) * 64 + 64, :]
    for j in range(16):
        pair = qr[j]
        qs[2 * j] = pair[:, :64]
        qs[2 * j + 1] = pair[:, 64:]
    rows = lax.broadcasted_iota(jnp.int32, (512, 64), 0) // 64
    lanes = lax.broadcasted_iota(jnp.int32, (512, 64), 1)
    for c in range(8):
        part = kvs[512 * c:512 * c + 512, :]
        hot = jnp.where(rows + 8 * c == lanes, 1.0, 0.0).astype(BF)
        kaug[512 * c:512 * c + 512, :] = jnp.concatenate([part[:, :64], hot], axis=1)
        kvt[c] = part.astype(F32).T.astype(BF)
    qi = lax.broadcasted_iota(jnp.int32, (64, 64), 0)
    ki = lax.broadcasted_iota(jnp.int32, (64, 64), 1)
    bias[...] = jnp.where(jnp.logical_and(mask[0] != 0, ki < qi), 0.0, NEG)


def triangle():
    key = lax.broadcasted_iota(jnp.int32, (64, 256), 0)
    query = lax.broadcasted_iota(jnp.int32, (64, 256), 1) % 64
    return key <= query


def attend_kernel(blk, mask, kvr, qr, o_ref, ot_ref, lse_ref, kvs, kaug, kvt, bias, qs, qa, os, inv, order, oblk):
    attention_setup(blk, mask, kvr, qr, kvs, kaug, kvt, bias, qs, inv, order, oblk)

    def tile(g, carry):
        score, vals = [], []
        for u in range(4):
            i = oblk[4 * g + u]
            q = qs[order[4 * g + u]]
            row = jnp.broadcast_to(bias[pl.ds(i, 1), :], (64, 64)).astype(BF)
            qa[64 * u:64 * u + 64, :] = jnp.concatenate([q, row], axis=1)
            kv = kvs[pl.ds(pl.multiple_of(i * 64, 64), 64), :]
            score.append(dot(kv[:, :64], q, NT))
            vals.append(kv[:, 64:])
        s = jnp.where(triangle(), jnp.concatenate(score, axis=1), NEG)
        top = jnp.max(s, axis=0, keepdims=True)
        p = jnp.exp(s - top)
        total = jnp.sum(p, axis=0, keepdims=True)
        pb = p.astype(BF)
        mix = jnp.concatenate([dot(vals[u], pb[:, 64 * u:64 * u + 64], TN) for u in range(4)], axis=1)
        queries = qa[...]

        def chunk(c, state):
            top, total, mix = state
            keys = kaug[pl.ds(pl.multiple_of(c * 512, 512), 512), :]
            s = dot(keys, queries, NT)
            new = jnp.maximum(top, jnp.max(s, axis=0, keepdims=True))
            shrink = jnp.exp(top - new)
            p = jnp.exp(s - new)
            total = total * shrink + jnp.sum(p, axis=0, keepdims=True)
            mix = mix * shrink + dot(kvt[c, 64:, :], p.astype(BF))
            return new, total, mix

        chunks = (oblk[4 * g + 3] + 7) // 8
        def pair(c, state):
            top, total, mix = state
            parts = [dot(kaug[pl.ds(pl.multiple_of(c * 1024 + 512 * k, 512), 512), :], queries, NT) for k in range(2)]
            new = top
            for s in parts:
                new = jnp.maximum(new, jnp.max(s, axis=0, keepdims=True))
            shrink = jnp.exp(top - new)
            total, mix = total * shrink, mix * shrink
            for k, s in enumerate(parts):
                p = jnp.exp(s - new)
                total += jnp.sum(p, axis=0, keepdims=True)
                mix += dot(kvt[2 * c + k, 64:, :], p.astype(BF))
            return new, total, mix

        top, total, mix = lax.fori_loop(0, chunks // 2, pair, (top, total, mix))
        top, total, mix = lax.fori_loop(chunks // 2 * 2, chunks, chunk, (top, total, mix))
        out = mix / total
        ot_ref[g] = out
        lse_ref[g] = top + jnp.log(total)
        back = out.T.astype(BF)
        for u in range(4):
            os[order[4 * g + u]] = back[64 * u:64 * u + 64, :]
        return carry

    lax.fori_loop(0, 8, tile, 0)
    for j in range(16):
        o_ref[j] = jnp.concatenate([os[2 * j], os[2 * j + 1]], axis=1)


def attention_scratch():
    return [
        pltpu.VMEM((4096, 128), BF),
        pltpu.VMEM((4096, 128), BF),
        pltpu.VMEM((8, 128, 512), BF),
        pltpu.VMEM((64, 64), F32),
        pltpu.VMEM((32, 64, 64), BF),
        pltpu.VMEM((256, 128), BF),
        pltpu.VMEM((32, 64, 64), BF),
        pltpu.SMEM((64,), jnp.int32),
        pltpu.SMEM((72,), jnp.int32),
        pltpu.SMEM((72,), jnp.int32),
    ]


def attend(blk, mask, kvr, qr):
    return pl.pallas_call(
        attend_kernel,
        out_shape=[shp((16, 64, 128), BF), shp((8, 64, 256), F32), shp((8, 1, 256), F32)],
        in_specs=[SM, VM, VM, VM],
        out_specs=[VM] * 3,
        scratch_shapes=attention_scratch(),
        compiler_params=pltpu.CompilerParams(vmem_limit_bytes=LIMIT),
        cost_estimate=pl.CostEstimate(flops=10 << 30, bytes_accessed=32 << 20, transcendentals=4 << 20),
        name="attend",
    )(blk, mask, kvr, qr)


def attend_back_kernel(
    blk, mask, kvr, qr, dor, ot_ref, lse_ref, dkv_ref, dq_ref,
    kvs, kaug, kvt, bias, qs, qa, dqs, inv, order, oblk, dos, qz, dz, dkv,
):
    attention_setup(blk, mask, kvr, qr, kvs, kaug, kvt, bias, qs, inv, order, oblk)
    for j in range(16):
        pair = dor[j]
        dos[2 * j] = pair[:, :64]
        dos[2 * j + 1] = pair[:, 64:]
    dkv[...] = jnp.zeros_like(dkv)
    zero = jnp.zeros((64, 64), BF)

    def tile(g, carry):
        score, dprob, places, keys_own, q_own, d_own = [], [], [], [], [], []
        for u in range(4):
            i = oblk[4 * g + u]
            q = qs[order[4 * g + u]]
            do = dos[order[4 * g + u]]
            rows = slice(64 * u, 64 * u + 64)
            row = jnp.broadcast_to(bias[pl.ds(i, 1), :], (64, 64)).astype(BF)
            qa[rows, :] = jnp.concatenate([q, row], axis=1)
            qz[rows, :] = jnp.concatenate([q, zero], axis=1)
            dz[rows, :] = jnp.concatenate([zero, do], axis=1)
            at = pl.ds(pl.multiple_of(i * 64, 64), 64)
            kv = kvs[at, :]
            score.append(dot(kv[:, :64], q, NT))
            dprob.append(dot(kv[:, 64:], do, NT))
            places.append(at)
            keys_own.append(kv[:, :64])
            q_own.append(q)
            d_own.append(do)
        lse = lse_ref[g]
        queries = qa[...]
        qpad = qz[...]
        dpad = dz[...]
        dot_t = dpad[:, 64:].astype(F32).T
        delta = jnp.sum(ot_ref[g] * dot_t, axis=0, keepdims=True)
        s = jnp.where(triangle(), jnp.concatenate(score, axis=1), NEG)
        p = jnp.exp(s - lse)
        ds = (p * (jnp.concatenate(dprob, axis=1) - delta)).astype(BF)
        pb = p.astype(BF)
        dq = []
        for u in range(4):
            lanes = slice(64 * u, 64 * u + 64)
            grad = jnp.concatenate([dot(ds[:, lanes], q_own[u]), dot(pb[:, lanes], d_own[u])], axis=1)
            dkv[places[u], :] += grad
            dq.append(dot(keys_own[u], ds[:, lanes], TN))

        def chunk(c, dq):
            at = pl.ds(pl.multiple_of(c * 512, 512), 512)
            p = jnp.exp(dot(kaug[at, :], queries, NT) - lse)
            dp = dot(kvs[at, :], dpad, NT)
            ds = (p * (dp - delta)).astype(BF)
            dkv[at, :] += dot(ds, qpad) + dot(p.astype(BF), dpad)
            return dq + dot(kvt[c, :64, :], ds)

        chunks = (oblk[4 * g + 3] + 7) // 8
        dq = lax.fori_loop(0, chunks // 2, lambda c, dq: chunk(2 * c + 1, chunk(2 * c, dq)), jnp.concatenate(dq, axis=1))
        dq = lax.fori_loop(chunks // 2 * 2, chunks, chunk, dq)
        back = (dq * 0.125).T.astype(BF)
        for u in range(4):
            dqs[order[4 * g + u]] = back[64 * u:64 * u + 64, :]
        return carry

    lax.fori_loop(0, 8, tile, 0)
    for j in range(16):
        dq_ref[j] = jnp.concatenate([dqs[2 * j], dqs[2 * j + 1]], axis=1)
    for s in range(64):
        at = pl.ds(pl.multiple_of(blk[s] * 64, 64), 64)
        dkv_ref[s // 2, (s % 2) * 64:(s % 2) * 64 + 64, :] = dkv[at, :].astype(BF)


def attend_back(blk, mask, kvr, qr, dor, ot, lse):
    return pl.pallas_call(
        attend_back_kernel,
        out_shape=[shp((32, 128, 128), BF), shp((16, 64, 128), BF)],
        in_specs=[SM] + [VM] * 6,
        out_specs=[VM] * 2,
        scratch_shapes=attention_scratch()
        + [
            pltpu.VMEM((32, 64, 64), BF),
            pltpu.VMEM((256, 128), BF),
            pltpu.VMEM((256, 128), BF),
            pltpu.VMEM((4096, 128), F32),
        ],
        compiler_params=pltpu.CompilerParams(vmem_limit_bytes=LIMIT),
        cost_estimate=pl.CostEstimate(flops=1 << 30, bytes_accessed=4 << 20, transcendentals=0),
        name="attend_back",
    )(blk, mask, kvr, qr, dor, ot, lse)


def norm_parts(v):
    center = v - jnp.mean(v, axis=1, keepdims=True)
    r = lax.rsqrt(jnp.mean(center * center, axis=1, keepdims=True) + EPS)
    return center * r, r


def norm_back(e, gain, z, r):
    g = e * gain
    return r * (g - jnp.mean(g, axis=1, keepdims=True) - z * jnp.mean(g * z, axis=1, keepdims=True))


def middle_kernel(*refs):
    o_ref, x_ref, e_ref, ln_ref, ln_own = refs[:5]
    shards = (refs[5:8], refs[8:11])
    pieces = (refs[11:19], refs[19:27])
    y_ref, dr_ref, do_ref, zpay, gpay, cpay, lown, gb_ref = refs[27:35]
    wo, wi, wu, us, gs, nl, ob, sw, sp = refs[35:]
    zl, x, y, zh, co = place()
    w = zh * 2 + co
    where = [w, zh * 2 + 1 - co, (1 - zh) * 2 + co, (1 - zh) * 2 + 1 - co]
    copies = [[], [], []]
    for r, (a, b, c) in enumerate(shards):
        rows = pl.ds(pl.multiple_of(where[r] * 256, 256), 256)
        copies[0].append(pltpu.make_async_copy(a, wo.at[rows], sw.at[r, 0]))
        for k in range(4):
            cols = slice(1024 * k, 1024 * k + 1024)
            copies[1].append(pltpu.make_async_copy(b.at[:, cols], wi.at[k, rows], sw.at[r, 1 + k]))
        groups = pl.ds(where[r] * 8, 8)
        copies[2].append(pltpu.make_async_copy(c, wu.at[groups], sw.at[r, 5]))
    for r, parts in enumerate(pieces):
        t = where[2 + r]
        quarters = [(parts[s], 0, (x + 4 - s) % 4) for s in range(4)]
        quarters += [(parts[4 + s], 1, (y + 4 - s) % 4) for s in range(4)]
        for n, (ref, h, q) in enumerate(quarters):
            rows = pl.ds(pl.multiple_of(t * 256 + h * 128 + q * 32, 32), 32)
            copies[0].append(pltpu.make_async_copy(ref.at[0], wo.at[rows], sp.at[r, n, 0]))
            copies[1].append(pltpu.make_async_copy(ref.at[1:5], wi.at[:, rows], sp.at[r, n, 1]))
            copies[2].append(pltpu.make_async_copy(ref.at[5:9], wu.at[t * 8 + h * 4 + q], sp.at[r, n, 2]))
    for group in copies:
        for c in group:
            c.start()

    ln = jnp.concatenate([jnp.where(w == k, ln_own[...], ln_ref[k]) for k in range(4)], axis=1)
    gain0, gain1, bias0, bias1 = (ln[k:k + 1, :] for k in range(4))
    for h in range(16):
        pair = o_ref[h]
        ob[:64, 64 * h:64 * h + 64] = pair[:, :64]
        ob[64:, 64 * h:64 * h + 64] = pair[:, 64:]
    for c in copies[0]:
        c.wait()
    z0, r0 = norm_parts(x_ref[...].astype(F32) + dot(ob[...], wo[...]))
    n1 = z0 * gain0 + bias0
    nl[...] = n1.astype(BF)
    for c in copies[1]:
        c.wait()

    half = math.sqrt(0.5)

    def up(c, carry):
        u = dot(nl[...], wi[c])
        us[c] = u
        gs[:, pl.ds(pl.multiple_of(c * 1024, 1024), 1024)] = (0.5 * u * (1.0 + lax.erf(u * half))).astype(BF)
        return carry

    lax.fori_loop(0, 4, up, 0)
    for c in copies[2]:
        c.wait()

    def down(c, total):
        cols = pl.ds(pl.multiple_of(c * 1024, 1024), 1024)
        return total + dot(gs[:, cols], wu[pl.ds(c * 8, 8)].reshape(1024, 1024))

    r2 = lax.fori_loop(0, 4, down, n1)
    z1, r1 = norm_parts(r2)
    y_ref[...] = z1 * gain1 + bias1
    e = e_ref[...].astype(F32)
    dr2 = norm_back(e, gain1, z1, r1)
    dm = dr2.astype(BF)
    gb_ref[1:2, :] = jnp.sum(e * z1, axis=0, keepdims=True)
    gb_ref[3:4, :] = jnp.sum(e, axis=0, keepdims=True)

    def back(c, total):
        rows = pl.ds(pl.multiple_of(c * 1024, 1024), 1024)
        u = us[c]
        dg = dot(dm, wu[pl.ds(c * 8, 8)].reshape(1024, 1024), NT)
        slope = 0.5 * (1.0 + lax.erf(u * half)) + u * (jnp.exp(-0.5 * u * u) * (1.0 / math.sqrt(2 * math.pi)))
        du = (dg * slope).astype(BF)
        cpay[:, rows] = du
        return total + dot(du, wi[c], NT)

    dn1 = lax.fori_loop(0, 4, back, dr2)
    gb_ref[0:1, :] = jnp.sum(dn1 * z0, axis=0, keepdims=True)
    gb_ref[2:3, :] = jnp.sum(dn1, axis=0, keepdims=True)
    gb_ref[4:8, :] = jnp.zeros((4, 1024), F32)
    dr1 = norm_back(dn1, gain0, z0, r0)
    dr_ref[...] = dr1
    da = dr1.astype(BF)
    do = dot(da, wo[...], NT).astype(BF)
    for h in range(16):
        lanes = slice(64 * h, 64 * h + 64)
        do_ref[h] = jnp.concatenate([do[:64, lanes], do[64:, lanes]], axis=1)
    cpay[:, 4096:5120] = da
    zpay[:, 1024:2048] = dm
    for r, (ref, at, gref, gat) in enumerate((
        (lown, 0, gpay, 0), (cpay, 5120, gpay, 1024), (lown, 512, zpay, 0), (cpay, 5632, zpay, 2048)
    )):
        few = pl.ds(pl.multiple_of(where[r] * 256, 256), 256)
        many = pl.ds(pl.multiple_of(where[r] * 1024, 1024), 1024)
        ref[:, at:at + 256] = nl[:, few]
        ref[:, at + 256:at + 512] = ob[:, few]
        gref[:, gat:gat + 1024] = gs[:, many]


def middle(o, tok, cot, lnf, lnp, shards, pieces):
    return pl.pallas_call(
        middle_kernel,
        out_shape=[
            shp((128, 1024), F32), shp((128, 1024), F32), shp((16, 64, 128), BF),
            shp((128, 3072), BF), shp((128, 2048), BF), shp((128, 6144), BF), shp((128, 1024), BF), shp((8, 1024), F32),
        ],
        in_specs=[VM] * 5 + [ANY] * 22,
        out_specs=[VM] * 8,
        scratch_shapes=[
            pltpu.VMEM((1024, 1024), BF),
            pltpu.VMEM((4, 1024, 1024), BF),
            pltpu.VMEM((32, 4, 32, 1024), BF),
            pltpu.VMEM((4, 128, 1024), F32),
            pltpu.VMEM((128, 4096), BF),
            pltpu.VMEM((128, 1024), BF),
            pltpu.VMEM((128, 1024), BF),
            DMA((2, 6)), DMA((2, 8, 3)),
        ],
        compiler_params=pltpu.CompilerParams(vmem_limit_bytes=LIMIT),
        cost_estimate=pl.CostEstimate(flops=10 << 30, bytes_accessed=32 << 20, transcendentals=2 << 20),
        name="middle",
    )(o, tok, cot, lnf, lnp, *shards[0], *shards[1], *pieces[0], *pieces[1])


def turn_kernel(do, cpay, lown, dor, own_a, plus_a, minus_a, own_b, plus_b, minus_b, rr, ll, lt, mid, sn, rn, ss, rs, ls, lo):
    zl, x, y, zh, co = place()
    flat = lax.axis_index("ctx") % 16
    core = device(zl, x, y, zh, 1 - co)
    bar = pltpu.get_barrier_semaphore()

    def greet_one(i, carry):
        pl.semaphore_signal(bar, inc=1, device_id={"ctx": zl * 16 + (flat + i) % 16}, device_id_type=MESH)
        return carry

    pl.semaphore_signal(bar, inc=1, device_id=core, device_id_type=MESH)
    lax.fori_loop(1, 16, greet_one, 0)
    local = [
        pltpu.make_async_copy(cpay.at[:, :5120], rr.at[0:128, :], ls.at[0]),
        pltpu.make_async_copy(lown, ll.at[0:128, :], ls.at[1]),
    ]
    for c in local:
        c.start()
    pl.semaphore_wait(bar, 16)

    def narrow_copy(i):
        p = (flat + i) % 16
        return pltpu.make_async_remote_copy(
            src_ref=do.at[p], dst_ref=dor.at[flat], send_sem=sn.at[i], recv_sem=rn.at[i],
            device_id={"ctx": zl * 16 + p}, device_id_type=MESH,
        )

    def start_one(i, carry):
        narrow_copy(i).start()
        return carry

    def wait_one(i, carry):
        narrow_copy(i).wait()
        return carry

    wire = Wire(ss, rs)
    near = [wire(cpay.at[:, 5120:], ll.at[128:256, :], core), wire(cpay.at[:, :5120], rr.at[128:256, :], core)]
    lax.fori_loop(1, 16, start_one, 0)
    home = pltpu.make_async_copy(do.at[flat], dor.at[flat], ls.at[2])
    home.start()
    for c in local:
        c.wait()
    for c in near:
        c.wait()
    for k in range(4):
        lt[256 * k:256 * k + 256, :] = ll[:, 256 * k:256 * k + 256].astype(F32).T.astype(BF)
    for z in range(2):
        mid[z, 0:256, :] = dot(lt[512 * z + 256:512 * z + 512, :], rr[:, 4096:5120]).astype(BF)
        for k in range(4):
            rows = slice(256 + 256 * k, 512 + 256 * k)
            mid[z, rows, :] = dot(lt[512 * z:512 * z + 256, :], rr[:, 1024 * k:1024 * k + 1024]).astype(BF)
    out = []
    for h, (at, own, plus, minus) in enumerate(((x, own_a, plus_a, minus_a), (y, own_b, plus_b, minus_b))):

        def rows(s, first, size):
            return pl.ds(pl.multiple_of(h * 640 + (at + s) % 4 * 160 + first, 16), size)

        for src, dst in (
            (rows(0, 0, 160), own),
            (rows(1, 0, 160), plus.at[:, :160]), (rows(2, 0, 80), plus.at[:, 160:]),
            (rows(3, 0, 160), minus.at[:, :160]), (rows(2, 80, 80), minus.at[:, 160:]),
        ):
            out.append(pltpu.make_async_copy(mid.at[:, src], dst, lo.at[len(out)]))
    for c in out:
        c.start()
    home.wait()
    lax.fori_loop(1, 16, wait_one, 0)
    for c in out:
        c.wait()


def turn(do, cpay, lown):
    return pl.pallas_call(
        turn_kernel,
        out_shape=[shp(do.shape, BF)] + [shp((2, 160, 1024), BF), shp((2, 240, 1024), BF), shp((2, 240, 1024), BF)] * 2,
        in_specs=[ANY] * 3,
        out_specs=[ANY] * 7,
        scratch_shapes=[
            pltpu.VMEM((256, 5120), BF), pltpu.VMEM((256, 1024), BF), pltpu.VMEM((1024, 256), BF),
            pltpu.VMEM((2, 1280, 1024), BF),
            DMA((16,)), DMA((16,)), DMA((2,)), DMA((2,)), DMA((3,)), DMA((10,)),
        ],
        compiler_params=pltpu.CompilerParams(collective_id=5, has_side_effects=True, vmem_limit_bytes=LIMIT),
        cost_estimate=pl.CostEstimate(flops=16 << 30, bytes_accessed=32 << 20, transcendentals=0),
        name="turn",
    )(do, cpay, lown)


class Spread:
    def __init__(self, wire, plus, minus, at, piece, bufs):
        self.wire, self.plus, self.minus, self.at, self.piece = wire, plus, minus, at, piece
        self.rp, self.rm, self.m, self.f = bufs

    def part(self, s, u):
        return self.piece((self.at + s) % 4, u)

    def start(self):
        self.a = self.wire(self.part(2, 0), self.m.at[0], self.plus)
        self.b = self.wire(self.part(2, 1), self.m.at[1], self.minus)
        self.c = self.wire(self.part(1, 1), self.rp.at[1], self.plus)
        self.d = self.wire(self.part(3, 0), self.rm.at[0], self.minus)

    def relay(self):
        self.a.wait_recv()
        self.f[0] = (self.part(1, 0)[...].astype(F32) + self.m[0].astype(F32)).astype(BF)
        self.e = self.wire(self.f.at[0], self.rp.at[0], self.plus)
        self.b.wait_recv()
        self.f[1] = (self.part(3, 1)[...].astype(F32) + self.m[1].astype(F32)).astype(BF)
        self.g = self.wire(self.f.at[1], self.rm.at[1], self.minus)

    def total(self):
        for c in (self.c, self.d, self.e, self.g):
            c.wait_recv()
        return [
            self.part(0, u)[...].astype(F32) + self.rp[u].astype(F32) + self.rm[u].astype(F32) for u in range(2)
        ]

    def sent(self):
        for c in (self.a, self.b, self.c, self.d, self.e, self.g):
            c.wait_send()


class Gather:
    def __init__(self, wire, plus, minus, at, block):
        self.wire, self.plus, self.minus, self.at, self.block = wire, plus, minus, at, block

    def send(self, s, u, peer):
        spot = self.block((self.at + s) % 4, u)
        return self.wire(spot, spot, peer)

    def start(self):
        self.p0 = self.send(0, 0, self.plus)
        self.m1 = self.send(0, 1, self.minus)
        self.p1 = self.send(0, 1, self.plus)
        self.m0 = self.send(0, 0, self.minus)

    def relay(self):
        self.p0.wait_recv()
        self.rp = self.send(3, 0, self.plus)
        self.m1.wait_recv()
        self.rm = self.send(1, 1, self.minus)

    def done(self):
        for c in (self.p1, self.m0, self.rp, self.rm):
            c.wait()
        for c in (self.p0, self.m1):
            c.wait_send()


class DirectSpread:
    def __init__(self, wire, peers, at, piece, bufs):
        self.wire, self.peers, self.at, self.piece, self.bufs = wire, peers, at, piece, bufs

    def start(self):
        self.copies = []
        for s in range(3):
            for u in range(2):
                src = self.piece((self.at + s + 1) % 4, u)
                self.copies.append(self.wire(src, self.bufs[s].at[u], self.peers[s]))

    def relay(self):
        pass

    def total(self):
        for c in self.copies:
            c.wait_recv()
        out = []
        for u in range(2):
            total = self.piece(self.at, u)[...].astype(F32)
            for s in range(3):
                total += self.bufs[s][u].astype(F32)
            out.append(total)
        return out

    def sent(self):
        for c in self.copies:
            c.wait_send()


class DirectGather:
    def __init__(self, wire, peers, at, block):
        self.wire, self.peers, self.at, self.block = wire, peers, at, block

    def start(self):
        self.copies = []
        for u in range(2):
            spot = self.block(self.at, u)
            for p in self.peers:
                self.copies.append(self.wire(spot, spot, p))

    def relay(self):
        pass

    def done(self):
        for c in self.copies:
            c.wait()


class Sum:
    direct = False

    def cut(self, g, rows):
        return g.at[rows]

    def __init__(self, g, hc, refs, wire, where, xp, yp, zp):
        bufs1, s1, bufs2, s2, self.r3, full = refs[:4], refs[4], refs[5:9], refs[9], refs[10], refs[11]
        zl, x, y, zh, co = where
        self.wire, self.zp, self.zl = wire, zp, zl
        self.s1, self.s2, self.last, self.full = s1, s2, s2, full
        hh = hc // 2
        first, second = (xp, yp), (yp, xp)
        self.at1, self.at2 = (x, y), (y, x)
        self.peers = [(first[h][0], first[h][2]) for h in range(2)]

        def rows(h, k, u):
            return pl.ds(pl.multiple_of(h * 4 * hc + k * hc + u * hh, 16), hh)

        def cols(k, width):
            return pl.ds(pl.multiple_of(k * width, 128), width)

        self.rows, self.cols = rows, cols

        def one(h):
            return lambda k, u: self.cut(g, rows(h, k, u))

        def two(h):
            return lambda k, u: s1.at[h, u, :, cols(k, 256)]

        def five(h):
            return lambda k, u: full.at[rows(h, self.at1[h], u), cols(k, 256)]

        def six(h):
            return lambda k, u: full.at[rows(h, k, u)]

        def ends(peers):
            return wire, peers[0], peers[2]

        if g is not None:
            self.one = [Spread(*ends(first[h]), self.at1[h], one(h), [r.at[h] for r in bufs1]) for h in range(2)]
        if self.direct:
            self.two = [DirectSpread(wire, second[h], self.at2[h], two(h), [r.at[h] for r in bufs2]) for h in range(2)]
            self.five = [DirectGather(wire, second[h], self.at2[h], five(h)) for h in range(2)]
        else:
            self.two = [Spread(*ends(second[h]), self.at2[h], two(h), [r.at[h] for r in bufs2]) for h in range(2)]
            self.five = [Gather(*ends(second[h]), self.at2[h], five(h)) for h in range(2)]
        self.six = [Gather(*ends(first[h]), self.at1[h], six(h)) for h in range(2)]

    def begin(self):
        for t in self.one:
            t.start()

    def relay(self):
        for t in self.one:
            t.relay()

    def totals(self, h):
        return self.one[h].total()

    def across(self):
        pass

    def settle(self):
        for t in self.one:
            t.sent()

    def steps(self):
        self.begin()
        yield
        self.relay()
        yield
        for h in range(2):
            for u, total in enumerate(self.totals(h)):
                self.s1[h, u] = total.astype(BF)
            self.two[h].start()
        yield
        for t in self.two:
            t.relay()
        yield
        for h in range(2):
            for u, total in enumerate(self.two[h].total()):
                self.s2[h, u] = total.astype(BF)
        self.across()
        yield
        three = []
        for h in range(2):
            self.ready(h)
            three.append(self.wire(self.last.at[h, :, :, self.cols(1 - self.zl, 128)], self.r3.at[h], self.zp))
        yield
        four = []
        for h in range(2):
            three[h].wait_recv()
            for u in range(2):
                total = self.last[h, u, :, self.cols(self.zl, 128)].astype(F32) + self.r3[h, u].astype(F32)
                spot = self.full.at[self.rows(h, self.at1[h], u), self.cols(self.at2[h] * 2 + self.zl, 128)]
                spot[...] = total.astype(BF)
                four.append(self.wire(spot, spot, self.zp))
        yield
        for h in range(2):
            four[2 * h].wait()
            four[2 * h + 1].wait()
            self.five[h].start()
        yield
        for t in self.five:
            t.relay()
        yield
        for h in range(2):
            self.five[h].done()
            self.six[h].start()
        yield
        for t in self.six:
            t.relay()
        yield
        for t in self.two:
            t.sent()
        for c in three:
            c.wait_send()
        self.settle()
        for t in self.six:
            t.done()
        yield

    def ready(self, h):
        pass


class PairSum(Sum):
    direct = True

    def cut(self, g, rows):
        return g.at[:, rows]

    def __init__(self, g, hc, refs, wire, where, xp, yp, zp, far):
        self.rf, self.s3 = refs[:2]
        super().__init__(g, hc, refs[2:], wire, where, xp, yp, zp)
        self.far, self.hh, self.last = far, hc // 2, self.s3

    def totals(self, h):
        return [t.reshape(2 * self.hh, 1024) for t in self.one[h].total()]

    def across(self):
        self.crossed = [self.wire(self.s2.at[h, :, self.hh:], self.rf.at[h], self.far) for h in range(2)]

    def ready(self, h):
        self.crossed[h].wait_recv()
        for u in range(2):
            self.s3[h, u] = (self.s2[h, u, :self.hh].astype(F32) + self.rf[h, u].astype(F32)).astype(BF)

    def settle(self):
        for t in self.one:
            t.sent()
        for c in self.crossed:
            c.wait_send()


class BegunSum(PairSum):
    direct = False

    def __init__(self, hc, refs, wire, where, xp, yp, zp, far, own, plus, minus):
        self.own, self.fwd = refs[:2]
        super().__init__(None, hc, list(refs[2:4]) + [None] * 4 + list(refs[4:]), wire, where, xp, yp, zp, far)
        self.plus, self.minus = plus, minus

    def begin(self):
        hc = 2 * self.hh
        self.passed = []
        for h in range(2):
            plus, minus = self.peers[h]
            self.passed.append((
                self.wire(self.plus[h].at[:, hc:], self.fwd.at[h, 0], plus),
                self.wire(self.minus[h].at[:, hc:], self.fwd.at[h, 1], minus),
            ))

    def relay(self):
        pass

    def totals(self, h):
        hh = self.hh
        for c in self.passed[h]:
            c.wait_recv()
        out = []
        for u in range(2):
            rows = slice(u * hh, u * hh + hh)
            total = self.own[h, 0, :, rows].astype(F32) + self.own[h, 1, :, rows].astype(F32)
            total += self.own[h, 2, :, rows].astype(F32) + self.fwd[h, u].astype(F32)
            out.append(total.reshape(2 * hh, 1024))
        return out

    def settle(self):
        for c in self.crossed:
            c.wait_send()
        for pair in self.passed:
            for c in pair:
                c.wait_send()


SUM_COPIES = 12 + 12 + 2 + 4 + 12 + 12


BEGUN_COPIES = 4 + 12 + 2 + 2 + 4 + 12 + 12
PAIR_COPIES = 12 + 12 + 2 + 2 + 4 + 12 + 12


def sum_scratch(rows):
    hh = rows // 16
    return (
        [pltpu.VMEM((2, 2, hh, 1024), BF)] * 4
        + [pltpu.VMEM((2, 2, hh, 1024), BF)]
        + [pltpu.VMEM((2, 2, hh, 256), BF)] * 4
        + [pltpu.VMEM((2, 2, hh, 256), BF), pltpu.VMEM((2, 2, hh, 128), BF)]
    )


def pair_scratch(rows, begun):
    hh = rows // 16
    begin = [pltpu.VMEM((2, 3, 2, 2 * hh, 1024), BF), pltpu.VMEM((2, 2, 2, hh, 1024), BF)]
    first = [pltpu.VMEM((2, 2, 2, hh, 1024), BF)] * 4
    return (
        (begin if begun else [])
        + [pltpu.VMEM((2, 2, hh, 256), BF)] * 2
        + ([] if begun else first)
        + [pltpu.VMEM((2, 2, 2 * hh, 1024), BF)]
        + [pltpu.VMEM((2, 2, 2 * hh, 256), BF)] * 4
        + [pltpu.VMEM((2, 2, 2 * hh, 256), BF), pltpu.VMEM((2, 2, hh, 128), BF)]
    )


def finish_kernel(*refs):
    dkvp, dqp, dr_ref, gb, wall, wq, wk, wv, gpay, zpay, zr, xs, x_ref = refs[:13]
    got = ((refs[13], refs[16]), (refs[14], refs[17]), (refs[15], refs[18]))
    gt, io_full, u_full, tail_full, s_vec = refs[19:24]
    io_refs = list(refs[24:35]) + [io_full]
    u_refs, tail_refs = list(refs[35:46]) + [u_full], list(refs[46:59]) + [tail_full]
    (dkv, dq, weights, ll2, rr2, lt2, mid, pay, ll, rr, tail, v0, vf, v1, vx, vy, vz, tx, ty,
     sw, rw, sn, rn, ss, rs, ls, lw) = refs[59:]
    scale = 1.0 / math.sqrt(16384)
    where = place()
    zl, x, y, zh, co = where
    w = zh * 2 + co
    me = lax.axis_index("ctx")
    flat = me % 16
    core = device(zl, x, y, zh, 1 - co)
    far = device(zl, x, y, 1 - zh, co)
    xp = [device(zl, (x + s) % 4, y, zh, co) for s in (1, 2, 3)]
    yp = [device(zl, x, (y + s) % 4, zh, co) for s in (1, 2, 3)]
    zp = device(1 - zl, x, y, zh, co)
    bar = pltpu.get_barrier_semaphore()

    def greet_one(i, carry):
        pl.semaphore_signal(bar, inc=1, device_id={"ctx": (me + i) % 32}, device_id_type=MESH)
        return carry

    for p in (core, far):
        pl.semaphore_signal(bar, inc=1, device_id=p, device_id_type=MESH)
    lax.fori_loop(1, 32, greet_one, 0)

    mine = [pl.ds(pl.multiple_of(k * 256, 256), 256) for k in (w, (1 - zh) * 2 + co)]
    parts = []
    for h in range(2):
        for n in range(3):
            parts.append(pltpu.make_async_copy(got[n][h].at[:, :160], io_refs[0].at[h, n], ls.at[10 + 3 * h + n]))
    local = [
        pltpu.make_async_copy(gpay.at[:, :1024], ll2.at[0:128, :], ls.at[0]),
        pltpu.make_async_copy(zpay.at[:, 1024:2048], rr2.at[0:128, :], ls.at[1]),
        pltpu.make_async_copy(zr.at[:, :1024], ll2.at[256:384, :], ls.at[2]),
        pltpu.make_async_copy(zr.at[:, 1024:2048], rr2.at[256:384, :], ls.at[3]),
    ]
    for k in range(2):
        cols = slice(256 * k, 256 * k + 256)
        local.append(pltpu.make_async_copy(x_ref.at[:, mine[k]], ll.at[0:128, cols], ls.at[4 + k]))
        local.append(pltpu.make_async_copy(xs.at[k], ll.at[128:256, cols], ls.at[6 + k]))
    for c in local + parts:
        c.start()
    loads = load_qkv(wall, (wq, wk, wv), weights, lw)
    pl.semaphore_wait(bar, 33)

    def narrow_copy(i):
        p = (flat + i) % 16
        return pltpu.make_async_remote_copy(
            src_ref=dqp.at[p], dst_ref=dq.at[flat], send_sem=sn.at[i], recv_sem=rn.at[i],
            device_id={"ctx": zl * 16 + p}, device_id_type=MESH,
        )

    def wide_copy(i):
        p = (me + i) % 32
        return pltpu.make_async_remote_copy(
            src_ref=dkvp.at[p], dst_ref=dkv.at[me], send_sem=sw.at[i], recv_sem=rw.at[i],
            device_id={"ctx": p}, device_id_type=MESH,
        )

    def start(make):
        def one(i, carry):
            make(i).start()
            return carry
        return one

    def wait(make):
        def one(i, carry):
            make(i).wait()
            return carry
        return one

    lax.fori_loop(1, 32, start(wide_copy), 0)
    lax.fori_loop(1, 16, start(narrow_copy), 0)
    home = [
        pltpu.make_async_copy(dkvp.at[me], dkv.at[me], ls.at[8]),
        pltpu.make_async_copy(dqp.at[flat], dq.at[flat], ls.at[9]),
    ]
    for c in home:
        c.start()
    wire = Wire(ss, rs)
    near = [
        wire(gpay.at[:, 1024:], ll2.at[128:256, :], core),
        wire(zpay.at[:, 1024:2048], rr2.at[128:256, :], core),
        wire(zr.at[:, 2048:], ll2.at[384:512, :], core),
        wire(zr.at[:, 1024:2048], rr2.at[384:512, :], core),
    ]
    io = BegunSum(160, io_refs, wire, where, xp, yp, zp, far, *got).steps()
    big = Sum(mid, 128, u_refs, wire, where, xp, yp, zp).steps()
    small = PairSum(tail, 96, tail_refs, wire, where, xp, yp, zp, far).steps()
    next(io)
    next(io)
    for c in local:
        c.wait()
    lt = ll[...].astype(F32).T.astype(BF)
    for c in near:
        c.wait()
    for k in range(4):
        lt2[256 * k:256 * k + 256, :] = ll2[:, 256 * k:256 * k + 256].astype(F32).T.astype(BF)
    for k in range(4):
        rows = slice(256 * k, 256 * k + 256)
        mid[rows, :] = dot(lt2[rows, :], rr2[...]).astype(BF)
    next(big)
    for c in parts:
        c.wait()
    next(io)

    for c in home:
        c.wait()
    lax.fori_loop(1, 32, wait(wide_copy), 0)
    lax.fori_loop(1, 16, wait(narrow_copy), 0)
    for h in range(16):
        lanes = slice(64 * h, 64 * h + 64)
        pair = dq[h]
        pay[:64, lanes] = pair[:, :64]
        pay[64:128, lanes] = pair[:, 64:]
        both = (dkv[h].astype(F32) + dkv[16 + h].astype(F32)).astype(BF)
        pay[:128, 1024 + 64 * h:1088 + 64 * h] = both[:, :64]
        pay[:128, 2048 + 64 * h:2112 + 64 * h] = both[:, 64:]
    pay[128:144, :1024] = jnp.concatenate([gb[...], jnp.zeros((8, 1024), F32)], axis=0).astype(BF)
    pay[128:144, 1024:] = jnp.zeros((16, 2048), BF)
    to_core = wire(pay, rr, core)
    next(big)
    next(io)
    for c in loads:
        c.wait()
    for k in range(4):
        cols = slice(256 * k, 256 * k + 256)
        total = dr_ref[:, cols]
        for m in range(3):
            total += dot(pay[:128, 1024 * m:1024 * m + 1024], weights[k, m], NT)
        gt[:, cols] = total
    to_core.wait_recv()
    for z in range(2):
        for m in range(3):
            cols = slice(1024 * m, 1024 * m + 1024)
            total = dot(lt[256 * z:256 * z + 256, :128], pay[:128, cols])
            total += dot(lt[256 * z:256 * z + 256, 128:], rr[:128, cols])
            tail[z, 256 * m:256 * m + 256, :] = total.astype(BF)
    next(small)
    for z in range(2):
        v0[z] = (pay[128:144, mine[z]].astype(F32) + rr[128:144, mine[z]].astype(F32))[:8]
    vfar = wire(v0.at[1], vf, far)
    next(io)
    next(big)
    next(small)
    next(io)
    next(big)
    next(small)
    vfar.wait_recv()
    v1[...] = v0[0] + vf[...]
    vone = [wire(v1, vx.at[s], xp[s]) for s in range(3)]
    next(io)
    next(big)
    next(small)
    next(io)
    next(big)
    next(small)
    for c in vone:
        c.wait_recv()
    tx[...] = v1[...] + vx[0] + vx[1] + vx[2]
    vtwo = [wire(tx, vy.at[s], yp[s]) for s in range(3)]
    next(io)
    next(big)
    next(small)
    next(io)
    next(big)
    next(small)
    for c in vtwo:
        c.wait_recv()
    ty[...] = tx[...] + vy[0] + vy[1] + vy[2]
    vthree = wire(ty, vz, zp)
    next(io)
    next(big)
    next(small)
    next(big)
    next(small)
    next(big)
    next(small)
    vthree.wait()
    s_vec[...] = (ty[...] + vz[...]) * scale
    for c in vone + vtwo + [to_core, vfar]:
        c.wait_send()
    next(small)
    next(io)
    next(big)
    next(small)


def finish(dkvp, dqp, dr, gb, wall, own, gpay, zpay, zr, xs, tok, parts):
    n = SUM_COPIES + BEGUN_COPIES + PAIR_COPIES + 4 + 2 + 7
    return pl.pallas_call(
        finish_kernel,
        out_shape=[
            shp((128, 1024), F32), shp((1280, 1024), BF), shp((1024, 1024), BF), shp((768, 1024), BF), shp((8, 256), F32),
        ],
        in_specs=[ANY, ANY, VM, VM] + [ANY] * 15,
        out_specs=[VM] * 5,
        scratch_shapes=pair_scratch(1280, True) + sum_scratch(1024) + pair_scratch(768, False) + [
            pltpu.VMEM((32, 128, 128), BF), pltpu.VMEM((16, 64, 128), BF), pltpu.VMEM((4, 3, 256, 1024), BF),
            pltpu.VMEM((512, 1024), BF), pltpu.VMEM((512, 1024), BF), pltpu.VMEM((1024, 512), BF),
            pltpu.VMEM((1024, 1024), BF), pltpu.VMEM((144, 3072), BF),
            pltpu.VMEM((256, 512), BF), pltpu.VMEM((144, 3072), BF), pltpu.VMEM((2, 768, 1024), BF),
            pltpu.VMEM((2, 8, 256), F32), pltpu.VMEM((8, 256), F32), pltpu.VMEM((8, 256), F32),
            pltpu.VMEM((3, 8, 256), F32), pltpu.VMEM((3, 8, 256), F32),
            pltpu.VMEM((8, 256), F32), pltpu.VMEM((8, 256), F32), pltpu.VMEM((8, 256), F32),
            DMA((32,)), DMA((32,)), DMA((16,)), DMA((16,)), DMA((n,)), DMA((n,)), DMA((16,)), DMA((6,)),
        ],
        compiler_params=pltpu.CompilerParams(collective_id=6, has_side_effects=True, vmem_limit_bytes=LIMIT),
        name="finish",
    )(dkvp, dqp, dr, gb, wall, *own, gpay, zpay, zr, xs, tok, *parts)


def scale_kernel(o, i0, i1, i2, i3, u, q, k, v, out_q, out_k, out_v, out_o, out_i, out_u):
    scale = 1.0 / math.sqrt(16384)
    for src, dst in ((q, out_q), (k, out_k), (v, out_v), (o, out_o), (u, out_u)):
        dst[...] = src[...].astype(F32) * scale
    for n, src in enumerate((i0, i1, i2, i3)):
        out_i[:, 1024 * n:1024 * n + 1024] = src[...].astype(F32) * scale


def scaled(io, u, tail):
    def rows(first, n=32):
        return pl.BlockSpec((n, 1024), lambda j: (first // n + j, 0))

    return pl.pallas_call(
        scale_kernel,
        grid=(8,),
        out_shape=[shp((256, 1024), F32)] * 4 + [shp((256, 4096), F32), shp((1024, 1024), F32)],
        in_specs=[rows(0)] + [rows(256 + 256 * k) for k in range(4)] + [rows(0, 128)] + [rows(256 * k) for k in range(3)],
        out_specs=[rows(0)] * 4 + [pl.BlockSpec((32, 4096), lambda j: (j, 0)), rows(0, 128)],
        compiler_params=pltpu.CompilerParams(vmem_limit_bytes=LIMIT),
        name="scaled",
    )(*[io] * 5, u, *[tail] * 3)


FLIP_CORE = [(0, 1), (1, 0), (2, 3), (3, 2)]
FLIP_FAR = [(0, 2), (2, 0), (1, 3), (3, 1)]


def along_x(s):
    return [(c, c // 16 * 16 + (c // 4 + s) % 4 * 4 + c % 4) for c in range(32)]


def along_y(s):
    return [(c, c // 4 * 4 + (c + s) % 4) for c in range(32)]


def body(
    tokens, w_query, w_key, w_value, w_output, w_inner, w_outer, ln_gain, ln_bias, block_mask, block_pairs, cotangent,
):
    tok = tokens.reshape(128, 1024)
    cot = cotangent.reshape(128, 1024)
    lnp = jnp.concatenate([ln_gain, ln_bias, jnp.zeros((4, 256), F32)], axis=0)
    blk = block_pairs.reshape(-1)
    own = (w_query, w_key, w_value)
    outer = w_outer.reshape(8, 4, 32, 1024)
    wall, xs, lnf, *core_shard, qa, qb = gather_weights(*own, tok, lnp, w_output, w_inner, outer)
    qa, qb, wall = lax.optimization_barrier((qa, qb, wall))
    x2 = lax.ppermute(qa, "ctx", along_x(2))
    y2 = lax.ppermute(qb, "ctx", along_y(2))
    diag_a = lax.ppermute(qa, "wsh", FLIP_CORE)
    diag_b = lax.ppermute(qb, "wsh", FLIP_CORE)

    kvp, qp = project(tok, wall, own)
    kvr, qr = exchange(kvp, qp, 2)
    qa, qb, x2, y2, diag_a, diag_b, kvr = lax.optimization_barrier((qa, qb, x2, y2, diag_a, diag_b, kvr))
    x1, x3 = (lax.ppermute(qa, "ctx", along_x(s)) for s in (1, 3))
    y1, y3 = (lax.ppermute(qb, "ctx", along_y(s)) for s in (1, 3))
    o, ot, lse = attend(blk, block_mask, kvr, qr)
    x1, x2, x3, y1, y2, y3, o = lax.optimization_barrier((x1, x2, x3, y1, y2, y3, o))
    far = [qa, x1, x2, x3, qb, y1, y2, y3]
    d1, d2, d3, e1, e2, e3 = (lax.ppermute(p, "wsh", FLIP_CORE) for p in (x1, x2, x3, y1, y2, y3))
    diag = [diag_a, d1, d2, d3, diag_b, e1, e2, e3]
    (o_back,) = exchange(None, o, 3)
    y_out, dr1, do, zpay, gpay, cpay, lown, gb = middle(
        o_back, tok, cot, lnf, lnp, ((w_output, w_inner, outer), core_shard), (far, diag)
    )
    zr = lax.ppermute(zpay, "wsh", FLIP_FAR)
    dor, own_a, plus_a, minus_a, own_b, plus_b, minus_b = turn(do, cpay, lown)
    plus_a = lax.ppermute(plus_a, "ctx", along_x(1))
    minus_a = lax.ppermute(minus_a, "ctx", along_x(3))
    plus_b = lax.ppermute(plus_b, "ctx", along_y(1))
    minus_b = lax.ppermute(minus_b, "ctx", along_y(3))
    dkvp, dqp = attend_back(blk, block_mask, kvr, qr, dor, ot, lse)
    zr, plus_a, minus_a, plus_b, minus_b, dkvp = lax.optimization_barrier((zr, plus_a, minus_a, plus_b, minus_b, dkvp))
    grad_tok, io, u, tail, s_vec = finish(
        dkvp, dqp, dr1, gb, wall, own, gpay, zpay, zr, xs, tok, (own_a, plus_a, minus_a, own_b, plus_b, minus_b)
    )
    s_q, s_k, s_v, s_o, s_i, s_u = scaled(io, u, tail)
    out_shape = tokens.shape
    return (
        y_out.reshape(out_shape), grad_tok.reshape(out_shape), s_q, s_k, s_v, s_o, s_i, s_u, s_vec[0:2], s_vec[2:4],
    )


def solution(mesh):
    return jax.shard_map(
        body,
        mesh=mesh,
        in_specs=(
            P("wsh", "ctx", None, None),
            P("wsh", None), P("wsh", None), P("wsh", None), P("wsh", None), P("wsh", None), P("wsh", None),
            P(None, "wsh"), P(None, "wsh"),
            P("wsh", None, None),
            P(),
            P("wsh", "ctx", None, None),
        ),
        out_specs=(
            P("wsh", "ctx", None, None), P("wsh", "ctx", None, None),
            P("wsh", None), P("wsh", None), P("wsh", None), P("wsh", None), P("wsh", None), P("wsh", None),
            P(None, "wsh"), P(None, "wsh"),
        ),
        check_vma=False,
    )
```

```python
import math

import jax
import jax.numpy as jnp
from jax import lax
from jax.experimental import pallas as pl
from jax.experimental.pallas import tpu as pltpu
from jax.sharding import PartitionSpec as P

MESH = pl.DeviceIdType.MESH
BF = jnp.bfloat16
F32 = jnp.float32
ANY = pl.BlockSpec(memory_space=pl.ANY)
VM = pl.BlockSpec(memory_space=pltpu.VMEM)
SM = pl.BlockSpec(memory_space=pltpu.SMEM)
DMA = pltpu.SemaphoreType.DMA
LIMIT = 56 * 1024 * 1024
EPS = 1e-05
NEG = -1e30


def shp(shape, dtype):
    return jax.ShapeDtypeStruct(shape, dtype)


def dot(a, b, dims=((1,), (0,))):
    return lax.dot_general(a, b, (dims, ((), ())), preferred_element_type=F32)


NN = ((1,), (0,))
NT = ((1,), (1,))
TN = ((0,), (0,))


def place():
    c = lax.axis_index("ctx")
    w = lax.axis_index("wsh")
    return c // 16, (c // 4) % 4, c % 4, w // 2, w % 2


def device(zl, x, y, zh, co):
    return {"ctx": zl * 16 + x * 4 + y, "wsh": zh * 2 + co}


def greet(peers):
    bar = pltpu.get_barrier_semaphore()
    for p in peers:
        pl.semaphore_signal(bar, inc=1, device_id=p, device_id_type=MESH)
    pl.semaphore_wait(bar, len(peers))


class Wire:
    def __init__(self, send, recv):
        self.send, self.recv, self.n = send, recv, 0

    def __call__(self, src, dst, peer):
        k = self.n
        self.n += 1
        copy = pltpu.make_async_remote_copy(
            src_ref=src, dst_ref=dst, send_sem=self.send.at[k], recv_sem=self.recv.at[k],
            device_id=peer, device_id_type=MESH,
        )
        copy.start()
        return copy


def front_kernel(*refs):
    x_ref, wq, wk, wv, x_any, ln_ref, wo, wi, wu = refs[:9]
    wall, xs, lnf, co_ref, ci_ref, cu_ref, qa_ref, qb_ref, x2_ref, y2_ref, da_ref, db_ref, kvr, qr = refs[9:23]
    weights, acc, kvp, qp, ss, rs, sw, rw, sf, rf, sn, rn, ls = refs[23:]
    zl, x, y, zh, co = place()
    me = zh * 2 + co
    slots = [me, zh * 2 + 1 - co, (1 - zh) * 2 + co, (1 - zh) * 2 + 1 - co]
    here = lax.axis_index("ctx")
    flat = here % 16
    core = device(zl, x, y, zh, 1 - co)
    far = device(zl, x, y, 1 - zh, co)
    diag = device(zl, x, y, 1 - zh, 1 - co)
    zp = device(1 - zl, x, y, zh, co)
    xp = [device(zl, (x + s) % 4, y, zh, co) for s in (1, 2, 3)]
    yp = [device(zl, x, (y + s) % 4, zh, co) for s in (1, 2, 3)]
    bar = pltpu.get_barrier_semaphore()

    def greet_one(i, carry):
        pl.semaphore_signal(bar, inc=1, device_id={"ctx": zl * 16 + (flat + i) % 16}, device_id_type=MESH)
        return carry

    for p in (far, core, diag, zp):
        pl.semaphore_signal(bar, inc=1, device_id=p, device_id_type=MESH)
    lax.fori_loop(1, 16, greet_one, 0)
    ws = (wq, wk, wv)
    local = [pltpu.make_async_copy(ws[m], weights.at[me, m], ls.at[m]) for m in range(3)]
    for c in local:
        c.start()
    pl.semaphore_wait(bar, 19)
    wire = Wire(ss, rs)
    rows_a = pl.ds(pl.multiple_of(x * 32, 32), 32)
    rows_b = pl.ds(pl.multiple_of(128 + y * 32, 32), 32)
    first_a, first_b = [], []
    for m in range(3):
        first_a.append(wire(ws[m].at[rows_a], weights.at[me, m, rows_a], far))
        first_b.append(wire(ws[m].at[rows_b], weights.at[me, m, rows_b], far))
    near = [wire(ws[m], weights.at[me, m], core) for m in range(3)]
    quarters = []
    for ref, k, n in ((qa_ref, x, y), (qb_ref, 4 + y, x)):
        rows = pl.ds(pl.multiple_of(k * 32, 32), 32)
        cols = pl.ds(pl.multiple_of(n * 256, 256), 256)
        quarters.append(wire(wo.at[rows, cols], ref.at[0, :, cols], far))
        for b in range(4):
            at = pl.ds(pl.multiple_of(1024 * b + n * 256, 256), 256)
            quarters.append(wire(wi.at[rows, at], ref.at[1 + b, :, cols], far))
        quarters.append(wire(wu.at[k, :, :, cols], ref.at[5:9, :, cols], far))
    rest = []
    for p in (core, far, diag):
        rest.append(wire(ln_ref, lnf.at[me], p))
    for n, idx in enumerate((slots[1], slots[3])):
        rest.append(wire(x_any.at[:, pl.ds(pl.multiple_of(idx * 256, 256), 256)], xs.at[n], core))

    def add(k, fresh):
        cols = x_ref[:, pl.ds(pl.multiple_of(slots[k] * 256, 256), 256)]
        for m in range(3):
            part = dot(cols, weights[slots[k], m])
            acc[m] = part if fresh else acc[m] + part

    for c in first_a:
        c.wait_recv()
    second = []
    for m in range(3):
        part = weights.at[slots[2], m, rows_a]
        for p in xp:
            second.append(wire(part, part, p))
    for c in first_b:
        c.wait_recv()
    for m in range(3):
        part = weights.at[slots[2], m, rows_b]
        for p in yp:
            second.append(wire(part, part, p))
    for c in local:
        c.wait()
    add(0, True)
    for c in near:
        c.wait_recv()
    add(1, False)
    for c in second:
        c.wait_recv()
    last = [wire(weights.at[slots[2], m], weights.at[slots[2], m], core) for m in range(3)]
    add(2, False)
    for c in last:
        c.wait_recv()
    add(3, False)
    keep = pltpu.make_async_copy(weights, wall, ls.at[0])
    keep.start()
    for j in range(8):
        lanes = slice(128 * j, 128 * j + 128)
        q = (acc[0, :, lanes].astype(BF).astype(F32) * 0.125).astype(BF)
        k = acc[1, :, lanes].astype(BF)
        v = acc[2, :, lanes].astype(BF)
        for u in range(2):
            part = slice(64 * u, 64 * u + 64)
            kvp[2 * j + u] = jnp.concatenate([k[:, part], v[:, part]], axis=1)
            qp[2 * j + u] = jnp.concatenate([q[:64, part], q[64:, part]], axis=1)

    def plane(i):
        return {"ctx": zl * 16 + (flat + i) % 16}

    def wide_copy(i):
        return pltpu.make_async_remote_copy(
            src_ref=kvp.at[(flat + i) % 16], dst_ref=kvr.at[here], send_sem=sw.at[i], recv_sem=rw.at[i],
            device_id=plane(i), device_id_type=MESH,
        )

    def narrow_copy(i):
        return pltpu.make_async_remote_copy(
            src_ref=qp.at[(flat + i) % 16], dst_ref=qr.at[flat], send_sem=sn.at[i], recv_sem=rn.at[i],
            device_id=plane(i), device_id_type=MESH,
        )

    def pass_copy(i):
        spot = kvr.at[zl * 16 + (flat + 16 - i) % 16]
        return pltpu.make_async_remote_copy(
            src_ref=spot, dst_ref=spot, send_sem=sf.at[i], recv_sem=rf.at[i], device_id=zp, device_id_type=MESH,
        )

    def start_wide(i, carry):
        wide_copy(i).start()
        return carry

    def start_narrow(i, carry):
        narrow_copy(i).start()
        return carry

    def pass_on(i, carry):
        wide_copy(i).wait_recv()
        pass_copy(i).start()
        return carry

    def wait_all(i, carry):
        wide_copy(i).wait_send()
        narrow_copy(i).wait()
        pass_copy(i).wait()
        return carry

    to_z = wire(kvp.at[flat], kvr.at[here], zp)
    lax.fori_loop(1, 16, start_wide, 0)
    lax.fori_loop(1, 16, start_narrow, 0)
    home = [
        pltpu.make_async_copy(kvp.at[flat], kvr.at[here], ls.at[1]),
        pltpu.make_async_copy(qp.at[flat], qr.at[flat], ls.at[2]),
    ]
    for c in home:
        c.start()
    for c in quarters:
        c.wait_recv()
    subs = []
    for ref, n, peers in ((qa_ref, y, yp), (qb_ref, x, xp)):
        spot = ref.at[:, :, pl.ds(pl.multiple_of(n * 256, 256), 256)]
        for p in peers:
            subs.append(wire(spot, spot, p))
    for src, dst in ((wo, co_ref), (wi, ci_ref), (wu, cu_ref)):
        rest.append(wire(src, dst, core))
    lax.fori_loop(1, 16, pass_on, 0)
    for c in subs:
        c.wait_recv()
    for src, dst, p in ((qa_ref, x2_ref, xp[1]), (qb_ref, y2_ref, yp[1]), (qa_ref, da_ref, core), (qb_ref, db_ref, core)):
        rest.append(wire(src, dst, p))
    for c in home:
        c.wait()
    keep.wait()
    lax.fori_loop(1, 16, wait_all, 0)
    to_z.wait()
    for c in first_a + first_b + near + second + last + quarters + subs:
        c.wait_send()
    for c in rest:
        c.wait()


def front(tok, own, lnp, wo, wi, wu):
    n = 6 + 3 + 12 + 3 + 2 + 18 + 3 + 1 + 6 + 3 + 4
    piece = shp((9, 32, 1024), BF)
    return pl.pallas_call(
        front_kernel,
        out_shape=[shp((4, 3, 256, 1024), BF), shp((2, 128, 256), BF), shp((4, 8, 256), F32)]
        + [shp(wo.shape, BF), shp(wi.shape, BF), shp(wu.shape, BF)] + [piece] * 6
        + [shp((32, 128, 128), BF), shp((16, 64, 128), BF)],
        in_specs=[VM] + [ANY] * 8,
        out_specs=[ANY] * 14,
        scratch_shapes=[
            pltpu.VMEM((4, 3, 256, 1024), BF), pltpu.VMEM((3, 128, 1024), F32),
            pltpu.VMEM((16, 128, 128), BF), pltpu.VMEM((16, 64, 128), BF),
            DMA((n,)), DMA((n,)), DMA((16,)), DMA((16,)), DMA((16,)), DMA((16,)), DMA((16,)), DMA((16,)), DMA((3,)),
        ],
        compiler_params=pltpu.CompilerParams(collective_id=1, has_side_effects=True, vmem_limit_bytes=LIMIT),
        cost_estimate=pl.CostEstimate(flops=16 << 30, bytes_accessed=32 << 20, transcendentals=0),
        name="front",
    )(tok, *own, tok, lnp, wo, wi, wu)


def exchange(wide, narrow, collective):
    has = wide is not None
    n = 32 if has else 16

    def kernel(*refs):
        if has:
            wi, na, wo, no, sw, rw, sn, rn, ls = refs
        else:
            na, no, sn, rn, ls = refs
        me = lax.axis_index("ctx")
        zl = me // 16
        flat = me % 16
        bar = pltpu.get_barrier_semaphore()

        def peer(i):
            if has:
                return (me + i) % 32
            return zl * 16 + (flat + i) % 16

        def greet_one(i, carry):
            pl.semaphore_signal(bar, inc=1, device_id={"ctx": peer(i)}, device_id_type=MESH)
            return carry

        lax.fori_loop(1, n, greet_one, 0)
        pl.semaphore_wait(bar, n - 1)

        def narrow_copy(i):
            p = (flat + i) % 16
            return pltpu.make_async_remote_copy(
                src_ref=na.at[p], dst_ref=no.at[flat], send_sem=sn.at[i], recv_sem=rn.at[i],
                device_id={"ctx": zl * 16 + p}, device_id_type=MESH,
            )

        def wide_copy(i):
            p = (me + i) % 32
            src = p if wide.shape[0] == 32 else p % 16
            return pltpu.make_async_remote_copy(
                src_ref=wi.at[src], dst_ref=wo.at[me], send_sem=sw.at[i], recv_sem=rw.at[i],
                device_id={"ctx": p}, device_id_type=MESH,
            )

        def start(make):
            def one(i, carry):
                make(i).start()
                return carry
            return one

        def wait(make):
            def one(i, carry):
                make(i).wait()
                return carry
            return one

        if has:
            lax.fori_loop(1, 32, start(wide_copy), 0)
        lax.fori_loop(1, 16, start(narrow_copy), 0)
        local = [pltpu.make_async_copy(na.at[flat], no.at[flat], ls.at[0])]
        if has:
            own = me if wide.shape[0] == 32 else flat
            local.append(pltpu.make_async_copy(wi.at[own], wo.at[me], ls.at[1]))
        for c in local:
            c.start()
        for c in local:
            c.wait()
        if has:
            lax.fori_loop(1, 32, wait(wide_copy), 0)
        lax.fori_loop(1, 16, wait(narrow_copy), 0)

    sems = ([DMA((32,)), DMA((32,))] if has else []) + [DMA((16,)), DMA((16,)), DMA((2,))]
    outs = ([shp((32,) + wide.shape[1:], wide.dtype)] if has else []) + [shp(narrow.shape, narrow.dtype)]
    args = ([wide] if has else []) + [narrow]
    return pl.pallas_call(
        kernel,
        out_shape=outs,
        in_specs=[ANY] * len(args),
        out_specs=[ANY] * len(outs),
        scratch_shapes=sems,
        compiler_params=pltpu.CompilerParams(collective_id=collective, has_side_effects=True),
        cost_estimate=pl.CostEstimate(flops=16 << 30, bytes_accessed=32 << 20, transcendentals=0),
        name=f"exchange_{collective}",
    )(*args)


def attention_setup(blk, mask, kvr, qr, kvs, kaug, kvt, bias, qs, inv, order, oblk):
    first = (lax.axis_index("ctx") // 16) * 32

    def note(s, carry):
        inv[blk[s]] = s
        return carry

    lax.fori_loop(0, 64, note, 0)

    def pick(b, count):
        local = inv[b] - first
        order[count] = local
        oblk[count] = b
        mine = jnp.logical_and(local >= 0, local < 32)
        return count + mine.astype(jnp.int32)

    lax.fori_loop(0, 64, pick, 0)
    for s in range(64):
        at = pl.ds(pl.multiple_of(blk[s] * 64, 64), 64)
        kvs[at, :] = kvr[s // 2, (s % 2) * 64:(s % 2) * 64 + 64, :]
    for j in range(16):
        pair = qr[j]
        qs[2 * j] = pair[:, :64]
        qs[2 * j + 1] = pair[:, 64:]
    rows = lax.broadcasted_iota(jnp.int32, (512, 64), 0) // 64
    lanes = lax.broadcasted_iota(jnp.int32, (512, 64), 1)
    for c in range(8):
        part = kvs[512 * c:512 * c + 512, :]
        hot = jnp.where(rows + 8 * c == lanes, 1.0, 0.0).astype(BF)
        kaug[512 * c:512 * c + 512, :] = jnp.concatenate([part[:, :64], hot], axis=1)
        kvt[c] = part.astype(F32).T.astype(BF)
    qi = lax.broadcasted_iota(jnp.int32, (64, 64), 0)
    ki = lax.broadcasted_iota(jnp.int32, (64, 64), 1)
    bias[...] = jnp.where(jnp.logical_and(mask[0] != 0, ki < qi), 0.0, NEG)


def triangle():
    key = lax.broadcasted_iota(jnp.int32, (64, 256), 0)
    query = lax.broadcasted_iota(jnp.int32, (64, 256), 1) % 64
    return key <= query


def attend_kernel(blk, mask, kvr, qr, o_ref, ot_ref, lse_ref, kvs, kaug, kvt, bias, qs, qa, os, inv, order, oblk):
    attention_setup(blk, mask, kvr, qr, kvs, kaug, kvt, bias, qs, inv, order, oblk)

    def tile(g, carry):
        score, vals = [], []
        for u in range(4):
            i = oblk[4 * g + u]
            q = qs[order[4 * g + u]]
            row = jnp.broadcast_to(bias[pl.ds(i, 1), :], (64, 64)).astype(BF)
            qa[64 * u:64 * u + 64, :] = jnp.concatenate([q, row], axis=1)
            kv = kvs[pl.ds(pl.multiple_of(i * 64, 64), 64), :]
            score.append(dot(kv[:, :64], q, NT))
            vals.append(kv[:, 64:])
        s = jnp.where(triangle(), jnp.concatenate(score, axis=1), NEG)
        top = jnp.max(s, axis=0, keepdims=True)
        p = jnp.exp(s - top)
        total = jnp.sum(p, axis=0, keepdims=True)
        pb = p.astype(BF)
        mix = jnp.concatenate([dot(vals[u], pb[:, 64 * u:64 * u + 64], TN) for u in range(4)], axis=1)
        queries = qa[...]

        def chunk(c, state):
            top, total, mix = state
            keys = kaug[pl.ds(pl.multiple_of(c * 512, 512), 512), :]
            s = dot(keys, queries, NT)
            new = jnp.maximum(top, jnp.max(s, axis=0, keepdims=True))
            shrink = jnp.exp(top - new)
            p = jnp.exp(s - new)
            total = total * shrink + jnp.sum(p, axis=0, keepdims=True)
            mix = mix * shrink + dot(kvt[c, 64:, :], p.astype(BF))
            return new, total, mix

        chunks = (oblk[4 * g + 3] + 7) // 8
        def pair(c, state):
            top, total, mix = state
            parts = [dot(kaug[pl.ds(pl.multiple_of(c * 1024 + 512 * k, 512), 512), :], queries, NT) for k in range(2)]
            new = top
            for s in parts:
                new = jnp.maximum(new, jnp.max(s, axis=0, keepdims=True))
            shrink = jnp.exp(top - new)
            total, mix = total * shrink, mix * shrink
            for k, s in enumerate(parts):
                p = jnp.exp(s - new)
                total += jnp.sum(p, axis=0, keepdims=True)
                mix += dot(kvt[2 * c + k, 64:, :], p.astype(BF))
            return new, total, mix

        top, total, mix = lax.fori_loop(0, chunks // 2, pair, (top, total, mix))
        top, total, mix = lax.fori_loop(chunks // 2 * 2, chunks, chunk, (top, total, mix))
        out = mix / total
        ot_ref[g] = out
        lse_ref[g] = top + jnp.log(total)
        back = out.T.astype(BF)
        for u in range(4):
            os[order[4 * g + u]] = back[64 * u:64 * u + 64, :]
        return carry

    lax.fori_loop(0, 8, tile, 0)
    for j in range(16):
        o_ref[j] = jnp.concatenate([os[2 * j], os[2 * j + 1]], axis=1)


def attention_scratch():
    return [
        pltpu.VMEM((4096, 128), BF),
        pltpu.VMEM((4096, 128), BF),
        pltpu.VMEM((8, 128, 512), BF),
        pltpu.VMEM((64, 64), F32),
        pltpu.VMEM((32, 64, 64), BF),
        pltpu.VMEM((256, 128), BF),
        pltpu.VMEM((32, 64, 64), BF),
        pltpu.SMEM((64,), jnp.int32),
        pltpu.SMEM((72,), jnp.int32),
        pltpu.SMEM((72,), jnp.int32),
    ]


def attend(blk, mask, kvr, qr):
    return pl.pallas_call(
        attend_kernel,
        out_shape=[shp((16, 64, 128), BF), shp((8, 64, 256), F32), shp((8, 1, 256), F32)],
        in_specs=[SM, VM, VM, VM],
        out_specs=[VM] * 3,
        scratch_shapes=attention_scratch(),
        compiler_params=pltpu.CompilerParams(vmem_limit_bytes=LIMIT),
        cost_estimate=pl.CostEstimate(flops=10 << 30, bytes_accessed=32 << 20, transcendentals=4 << 20),
        name="attend",
    )(blk, mask, kvr, qr)


def attend_back_kernel(
    blk, mask, kvr, qr, dor, ot_ref, lse_ref, dkv_ref, dq_ref,
    kvs, kaug, kvt, bias, qs, qa, dqs, inv, order, oblk, dos, qz, dz, dkv,
):
    attention_setup(blk, mask, kvr, qr, kvs, kaug, kvt, bias, qs, inv, order, oblk)
    for j in range(16):
        pair = dor[j]
        dos[2 * j] = pair[:, :64]
        dos[2 * j + 1] = pair[:, 64:]
    dkv[...] = jnp.zeros_like(dkv)
    zero = jnp.zeros((64, 64), BF)

    def tile(g, carry):
        score, dprob, places, keys_own, q_own, d_own = [], [], [], [], [], []
        for u in range(4):
            i = oblk[4 * g + u]
            q = qs[order[4 * g + u]]
            do = dos[order[4 * g + u]]
            rows = slice(64 * u, 64 * u + 64)
            row = jnp.broadcast_to(bias[pl.ds(i, 1), :], (64, 64)).astype(BF)
            qa[rows, :] = jnp.concatenate([q, row], axis=1)
            qz[rows, :] = jnp.concatenate([q, zero], axis=1)
            dz[rows, :] = jnp.concatenate([zero, do], axis=1)
            at = pl.ds(pl.multiple_of(i * 64, 64), 64)
            kv = kvs[at, :]
            score.append(dot(kv[:, :64], q, NT))
            dprob.append(dot(kv[:, 64:], do, NT))
            places.append(at)
            keys_own.append(kv[:, :64])
            q_own.append(q)
            d_own.append(do)
        lse = lse_ref[g]
        queries = qa[...]
        qpad = qz[...]
        dpad = dz[...]
        dot_t = dpad[:, 64:].astype(F32).T
        delta = jnp.sum(ot_ref[g] * dot_t, axis=0, keepdims=True)
        s = jnp.where(triangle(), jnp.concatenate(score, axis=1), NEG)
        p = jnp.exp(s - lse)
        ds = (p * (jnp.concatenate(dprob, axis=1) - delta)).astype(BF)
        pb = p.astype(BF)
        dq = []
        for u in range(4):
            lanes = slice(64 * u, 64 * u + 64)
            grad = jnp.concatenate([dot(ds[:, lanes], q_own[u]), dot(pb[:, lanes], d_own[u])], axis=1)
            dkv[places[u], :] += grad
            dq.append(dot(keys_own[u], ds[:, lanes], TN))

        def chunk(c, dq):
            at = pl.ds(pl.multiple_of(c * 512, 512), 512)
            p = jnp.exp(dot(kaug[at, :], queries, NT) - lse)
            dp = dot(kvs[at, :], dpad, NT)
            ds = (p * (dp - delta)).astype(BF)
            dkv[at, :] += dot(ds, qpad) + dot(p.astype(BF), dpad)
            return dq + dot(kvt[c, :64, :], ds)

        chunks = (oblk[4 * g + 3] + 7) // 8
        dq = lax.fori_loop(0, chunks // 2, lambda c, dq: chunk(2 * c + 1, chunk(2 * c, dq)), jnp.concatenate(dq, axis=1))
        dq = lax.fori_loop(chunks // 2 * 2, chunks, chunk, dq)
        back = (dq * 0.125).T.astype(BF)
        for u in range(4):
            dqs[order[4 * g + u]] = back[64 * u:64 * u + 64, :]
        return carry

    lax.fori_loop(0, 8, tile, 0)
    for j in range(16):
        dq_ref[j] = jnp.concatenate([dqs[2 * j], dqs[2 * j + 1]], axis=1)
    for s in range(64):
        at = pl.ds(pl.multiple_of(blk[s] * 64, 64), 64)
        dkv_ref[s // 2, (s % 2) * 64:(s % 2) * 64 + 64, :] = dkv[at, :].astype(BF)


def attend_back(blk, mask, kvr, qr, dor, ot, lse):
    return pl.pallas_call(
        attend_back_kernel,
        out_shape=[shp((32, 128, 128), BF), shp((16, 64, 128), BF)],
        in_specs=[SM] + [VM] * 6,
        out_specs=[VM] * 2,
        scratch_shapes=attention_scratch()
        + [
            pltpu.VMEM((32, 64, 64), BF),
            pltpu.VMEM((256, 128), BF),
            pltpu.VMEM((256, 128), BF),
            pltpu.VMEM((4096, 128), F32),
        ],
        compiler_params=pltpu.CompilerParams(vmem_limit_bytes=LIMIT),
        cost_estimate=pl.CostEstimate(flops=1 << 30, bytes_accessed=4 << 20, transcendentals=0),
        name="attend_back",
    )(blk, mask, kvr, qr, dor, ot, lse)


def norm_parts(v):
    center = v - jnp.mean(v, axis=1, keepdims=True)
    r = lax.rsqrt(jnp.mean(center * center, axis=1, keepdims=True) + EPS)
    return center * r, r


def norm_back(e, gain, z, r):
    g = e * gain
    return r * (g - jnp.mean(g, axis=1, keepdims=True) - z * jnp.mean(g * z, axis=1, keepdims=True))


def middle_kernel(*refs):
    o_ref, x_ref, e_ref, ln_ref, ln_own = refs[:5]
    shards = (refs[5:8], refs[8:11])
    pieces = (refs[11:19], refs[19:27])
    y_ref, dr_ref, do_ref, zpay, gpay, cpay, lown, gb_ref = refs[27:35]
    wo, wi, wu, us, gs, nl, ob, sw, sp = refs[35:]
    zl, x, y, zh, co = place()
    w = zh * 2 + co
    where = [w, zh * 2 + 1 - co, (1 - zh) * 2 + co, (1 - zh) * 2 + 1 - co]
    copies = [[], [], []]
    for r, (a, b, c) in enumerate(shards):
        rows = pl.ds(pl.multiple_of(where[r] * 256, 256), 256)
        copies[0].append(pltpu.make_async_copy(a, wo.at[rows], sw.at[r, 0]))
        for k in range(4):
            cols = slice(1024 * k, 1024 * k + 1024)
            copies[1].append(pltpu.make_async_copy(b.at[:, cols], wi.at[k, rows], sw.at[r, 1 + k]))
        groups = pl.ds(where[r] * 8, 8)
        copies[2].append(pltpu.make_async_copy(c, wu.at[groups], sw.at[r, 5]))
    for r, parts in enumerate(pieces):
        t = where[2 + r]
        quarters = [(parts[s], 0, (x + 4 - s) % 4) for s in range(4)]
        quarters += [(parts[4 + s], 1, (y + 4 - s) % 4) for s in range(4)]
        for n, (ref, h, q) in enumerate(quarters):
            rows = pl.ds(pl.multiple_of(t * 256 + h * 128 + q * 32, 32), 32)
            copies[0].append(pltpu.make_async_copy(ref.at[0], wo.at[rows], sp.at[r, n, 0]))
            copies[1].append(pltpu.make_async_copy(ref.at[1:5], wi.at[:, rows], sp.at[r, n, 1]))
            copies[2].append(pltpu.make_async_copy(ref.at[5:9], wu.at[t * 8 + h * 4 + q], sp.at[r, n, 2]))
    for group in copies:
        for c in group:
            c.start()

    ln = jnp.concatenate([jnp.where(w == k, ln_own[...], ln_ref[k]) for k in range(4)], axis=1)
    gain0, gain1, bias0, bias1 = (ln[k:k + 1, :] for k in range(4))
    for h in range(16):
        pair = o_ref[h]
        ob[:64, 64 * h:64 * h + 64] = pair[:, :64]
        ob[64:, 64 * h:64 * h + 64] = pair[:, 64:]
    for c in copies[0]:
        c.wait()
    z0, r0 = norm_parts(x_ref[...].astype(F32) + dot(ob[...], wo[...]))
    n1 = z0 * gain0 + bias0
    nl[...] = n1.astype(BF)
    for c in copies[1]:
        c.wait()

    half = math.sqrt(0.5)

    def up(c, carry):
        u = dot(nl[...], wi[c])
        us[c] = u
        gs[:, pl.ds(pl.multiple_of(c * 1024, 1024), 1024)] = (0.5 * u * (1.0 + lax.erf(u * half))).astype(BF)
        return carry

    lax.fori_loop(0, 4, up, 0)
    for c in copies[2]:
        c.wait()

    def down(c, total):
        cols = pl.ds(pl.multiple_of(c * 1024, 1024), 1024)
        return total + dot(gs[:, cols], wu[pl.ds(c * 8, 8)].reshape(1024, 1024))

    r2 = lax.fori_loop(0, 4, down, n1)
    z1, r1 = norm_parts(r2)
    y_ref[...] = z1 * gain1 + bias1
    e = e_ref[...].astype(F32)
    dr2 = norm_back(e, gain1, z1, r1)
    dm = dr2.astype(BF)
    gb_ref[1:2, :] = jnp.sum(e * z1, axis=0, keepdims=True)
    gb_ref[3:4, :] = jnp.sum(e, axis=0, keepdims=True)

    def back(c, total):
        rows = pl.ds(pl.multiple_of(c * 1024, 1024), 1024)
        u = us[c]
        dg = dot(dm, wu[pl.ds(c * 8, 8)].reshape(1024, 1024), NT)
        slope = 0.5 * (1.0 + lax.erf(u * half)) + u * (jnp.exp(-0.5 * u * u) * (1.0 / math.sqrt(2 * math.pi)))
        du = (dg * slope).astype(BF)
        cpay[:, rows] = du
        return total + dot(du, wi[c], NT)

    dn1 = lax.fori_loop(0, 4, back, dr2)
    gb_ref[0:1, :] = jnp.sum(dn1 * z0, axis=0, keepdims=True)
    gb_ref[2:3, :] = jnp.sum(dn1, axis=0, keepdims=True)
    gb_ref[4:8, :] = jnp.zeros((4, 1024), F32)
    dr1 = norm_back(dn1, gain0, z0, r0)
    dr_ref[...] = dr1
    da = dr1.astype(BF)
    do = dot(da, wo[...], NT).astype(BF)
    for h in range(16):
        lanes = slice(64 * h, 64 * h + 64)
        do_ref[h] = jnp.concatenate([do[:64, lanes], do[64:, lanes]], axis=1)
    cpay[:, 4096:5120] = da
    zpay[:, 1024:2048] = dm
    for r, (ref, at, gref, gat) in enumerate((
        (lown, 0, gpay, 0), (cpay, 5120, gpay, 1024), (lown, 512, zpay, 0), (cpay, 5632, zpay, 2048)
    )):
        few = pl.ds(pl.multiple_of(where[r] * 256, 256), 256)
        many = pl.ds(pl.multiple_of(where[r] * 1024, 1024), 1024)
        ref[:, at:at + 256] = nl[:, few]
        ref[:, at + 256:at + 512] = ob[:, few]
        gref[:, gat:gat + 1024] = gs[:, many]


def middle(o, tok, cot, lnf, lnp, shards, pieces):
    return pl.pallas_call(
        middle_kernel,
        out_shape=[
            shp((128, 1024), F32), shp((128, 1024), F32), shp((16, 64, 128), BF),
            shp((128, 3072), BF), shp((128, 2048), BF), shp((128, 6144), BF), shp((128, 1024), BF), shp((8, 1024), F32),
        ],
        in_specs=[VM] * 5 + [ANY] * 22,
        out_specs=[VM] * 8,
        scratch_shapes=[
            pltpu.VMEM((1024, 1024), BF),
            pltpu.VMEM((4, 1024, 1024), BF),
            pltpu.VMEM((32, 4, 32, 1024), BF),
            pltpu.VMEM((4, 128, 1024), F32),
            pltpu.VMEM((128, 4096), BF),
            pltpu.VMEM((128, 1024), BF),
            pltpu.VMEM((128, 1024), BF),
            DMA((2, 6)), DMA((2, 8, 3)),
        ],
        compiler_params=pltpu.CompilerParams(vmem_limit_bytes=LIMIT),
        cost_estimate=pl.CostEstimate(flops=10 << 30, bytes_accessed=32 << 20, transcendentals=2 << 20),
        name="middle",
    )(o, tok, cot, lnf, lnp, *shards[0], *shards[1], *pieces[0], *pieces[1])


def turn_kernel(do, cpay, lown, dor, own_a, plus_a, minus_a, own_b, plus_b, minus_b, rr, ll, lt, mid, sn, rn, ss, rs, ls, lo):
    zl, x, y, zh, co = place()
    flat = lax.axis_index("ctx") % 16
    core = device(zl, x, y, zh, 1 - co)
    bar = pltpu.get_barrier_semaphore()

    def greet_one(i, carry):
        pl.semaphore_signal(bar, inc=1, device_id={"ctx": zl * 16 + (flat + i) % 16}, device_id_type=MESH)
        return carry

    pl.semaphore_signal(bar, inc=1, device_id=core, device_id_type=MESH)
    lax.fori_loop(1, 16, greet_one, 0)
    local = [
        pltpu.make_async_copy(cpay.at[:, :5120], rr.at[0:128, :], ls.at[0]),
        pltpu.make_async_copy(lown, ll.at[0:128, :], ls.at[1]),
    ]
    for c in local:
        c.start()
    pl.semaphore_wait(bar, 16)

    def narrow_copy(i):
        p = (flat + i) % 16
        return pltpu.make_async_remote_copy(
            src_ref=do.at[p], dst_ref=dor.at[flat], send_sem=sn.at[i], recv_sem=rn.at[i],
            device_id={"ctx": zl * 16 + p}, device_id_type=MESH,
        )

    def start_one(i, carry):
        narrow_copy(i).start()
        return carry

    def wait_one(i, carry):
        narrow_copy(i).wait()
        return carry

    wire = Wire(ss, rs)
    near = [wire(cpay.at[:, 5120:], ll.at[128:256, :], core), wire(cpay.at[:, :5120], rr.at[128:256, :], core)]
    lax.fori_loop(1, 16, start_one, 0)
    home = pltpu.make_async_copy(do.at[flat], dor.at[flat], ls.at[2])
    home.start()
    for c in local:
        c.wait()
    for c in near:
        c.wait()
    for k in range(4):
        lt[256 * k:256 * k + 256, :] = ll[:, 256 * k:256 * k + 256].astype(F32).T.astype(BF)
    for z in range(2):
        mid[z, 0:256, :] = dot(lt[512 * z + 256:512 * z + 512, :], rr[:, 4096:5120]).astype(BF)
        for k in range(4):
            rows = slice(256 + 256 * k, 512 + 256 * k)
            mid[z, rows, :] = dot(lt[512 * z:512 * z + 256, :], rr[:, 1024 * k:1024 * k + 1024]).astype(BF)
    out = []
    for h, (at, own, plus, minus) in enumerate(((x, own_a, plus_a, minus_a), (y, own_b, plus_b, minus_b))):

        def rows(s, first, size):
            return pl.ds(pl.multiple_of(h * 640 + (at + s) % 4 * 160 + first, 16), size)

        for src, dst in (
            (rows(0, 0, 160), own),
            (rows(1, 0, 160), plus.at[:, :160]), (rows(2, 0, 80), plus.at[:, 160:]),
            (rows(3, 0, 160), minus.at[:, :160]), (rows(2, 80, 80), minus.at[:, 160:]),
        ):
            out.append(pltpu.make_async_copy(mid.at[:, src], dst, lo.at[len(out)]))
    for c in out:
        c.start()
    home.wait()
    lax.fori_loop(1, 16, wait_one, 0)
    for c in out:
        c.wait()


def turn(do, cpay, lown):
    return pl.pallas_call(
        turn_kernel,
        out_shape=[shp(do.shape, BF)] + [shp((2, 160, 1024), BF), shp((2, 240, 1024), BF), shp((2, 240, 1024), BF)] * 2,
        in_specs=[ANY] * 3,
        out_specs=[ANY] * 7,
        scratch_shapes=[
            pltpu.VMEM((256, 5120), BF), pltpu.VMEM((256, 1024), BF), pltpu.VMEM((1024, 256), BF),
            pltpu.VMEM((2, 1280, 1024), BF),
            DMA((16,)), DMA((16,)), DMA((2,)), DMA((2,)), DMA((3,)), DMA((10,)),
        ],
        compiler_params=pltpu.CompilerParams(collective_id=5, has_side_effects=True, vmem_limit_bytes=LIMIT),
        cost_estimate=pl.CostEstimate(flops=16 << 30, bytes_accessed=32 << 20, transcendentals=0),
        name="turn",
    )(do, cpay, lown)


class Spread:
    def __init__(self, wire, plus, minus, at, piece, bufs):
        self.wire, self.plus, self.minus, self.at, self.piece = wire, plus, minus, at, piece
        self.rp, self.rm, self.m, self.f = bufs

    def part(self, s, u):
        return self.piece((self.at + s) % 4, u)

    def start(self):
        self.a = self.wire(self.part(2, 0), self.m.at[0], self.plus)
        self.b = self.wire(self.part(2, 1), self.m.at[1], self.minus)
        self.c = self.wire(self.part(1, 1), self.rp.at[1], self.plus)
        self.d = self.wire(self.part(3, 0), self.rm.at[0], self.minus)

    def relay(self):
        self.a.wait_recv()
        self.f[0] = (self.part(1, 0)[...].astype(F32) + self.m[0].astype(F32)).astype(BF)
        self.e = self.wire(self.f.at[0], self.rp.at[0], self.plus)
        self.b.wait_recv()
        self.f[1] = (self.part(3, 1)[...].astype(F32) + self.m[1].astype(F32)).astype(BF)
        self.g = self.wire(self.f.at[1], self.rm.at[1], self.minus)

    def total(self):
        for c in (self.c, self.d, self.e, self.g):
            c.wait_recv()
        return [
            self.part(0, u)[...].astype(F32) + self.rp[u].astype(F32) + self.rm[u].astype(F32) for u in range(2)
        ]

    def sent(self):
        for c in (self.a, self.b, self.c, self.d, self.e, self.g):
            c.wait_send()


class Gather:
    def __init__(self, wire, plus, minus, at, block):
        self.wire, self.plus, self.minus, self.at, self.block = wire, plus, minus, at, block

    def send(self, s, u, peer):
        spot = self.block((self.at + s) % 4, u)
        return self.wire(spot, spot, peer)

    def start(self):
        self.p0 = self.send(0, 0, self.plus)
        self.m1 = self.send(0, 1, self.minus)
        self.p1 = self.send(0, 1, self.plus)
        self.m0 = self.send(0, 0, self.minus)

    def relay(self):
        self.p0.wait_recv()
        self.rp = self.send(3, 0, self.plus)
        self.m1.wait_recv()
        self.rm = self.send(1, 1, self.minus)

    def done(self):
        for c in (self.p1, self.m0, self.rp, self.rm):
            c.wait()
        for c in (self.p0, self.m1):
            c.wait_send()


class DirectSpread:
    def __init__(self, wire, peers, at, piece, bufs):
        self.wire, self.peers, self.at, self.piece, self.bufs = wire, peers, at, piece, bufs

    def start(self):
        self.copies = []
        for s in range(3):
            for u in range(2):
                src = self.piece((self.at + s + 1) % 4, u)
                self.copies.append(self.wire(src, self.bufs[s].at[u], self.peers[s]))

    def relay(self):
        pass

    def total(self):
        for c in self.copies:
            c.wait_recv()
        out = []
        for u in range(2):
            total = self.piece(self.at, u)[...].astype(F32)
            for s in range(3):
                total += self.bufs[s][u].astype(F32)
            out.append(total)
        return out

    def sent(self):
        for c in self.copies:
            c.wait_send()


class DirectGather:
    def __init__(self, wire, peers, at, block):
        self.wire, self.peers, self.at, self.block = wire, peers, at, block

    def start(self):
        self.copies = []
        for u in range(2):
            spot = self.block(self.at, u)
            for p in self.peers:
                self.copies.append(self.wire(spot, spot, p))

    def relay(self):
        pass

    def done(self):
        for c in self.copies:
            c.wait()


class Sum:
    direct = False

    def cut(self, g, rows):
        return g.at[rows]

    def __init__(self, g, hc, refs, wire, where, xp, yp, zp):
        bufs1, s1, bufs2, s2, self.r3, full = refs[:4], refs[4], refs[5:9], refs[9], refs[10], refs[11]
        zl, x, y, zh, co = where
        self.wire, self.zp, self.zl = wire, zp, zl
        self.s1, self.s2, self.last, self.full = s1, s2, s2, full
        hh = hc // 2
        first, second = (xp, yp), (yp, xp)
        self.at1, self.at2 = (x, y), (y, x)
        self.peers = [(first[h][0], first[h][2]) for h in range(2)]

        def rows(h, k, u):
            return pl.ds(pl.multiple_of(h * 4 * hc + k * hc + u * hh, 16), hh)

        def cols(k, width):
            return pl.ds(pl.multiple_of(k * width, 128), width)

        self.rows, self.cols = rows, cols

        def one(h):
            return lambda k, u: self.cut(g, rows(h, k, u))

        def two(h):
            return lambda k, u: s1.at[h, u, :, cols(k, 256)]

        def five(h):
            return lambda k, u: full.at[rows(h, self.at1[h], u), cols(k, 256)]

        def six(h):
            return lambda k, u: full.at[rows(h, k, u)]

        def ends(peers):
            return wire, peers[0], peers[2]

        if g is not None:
            self.one = [Spread(*ends(first[h]), self.at1[h], one(h), [r.at[h] for r in bufs1]) for h in range(2)]
        if self.direct:
            self.two = [DirectSpread(wire, second[h], self.at2[h], two(h), [r.at[h] for r in bufs2]) for h in range(2)]
            self.five = [DirectGather(wire, second[h], self.at2[h], five(h)) for h in range(2)]
        else:
            self.two = [Spread(*ends(second[h]), self.at2[h], two(h), [r.at[h] for r in bufs2]) for h in range(2)]
            self.five = [Gather(*ends(second[h]), self.at2[h], five(h)) for h in range(2)]
        self.six = [Gather(*ends(first[h]), self.at1[h], six(h)) for h in range(2)]

    def begin(self):
        for t in self.one:
            t.start()

    def relay(self):
        for t in self.one:
            t.relay()

    def totals(self, h):
        return self.one[h].total()

    def across(self):
        pass

    def settle(self):
        for t in self.one:
            t.sent()

    def steps(self):
        self.begin()
        yield
        self.relay()
        yield
        for h in range(2):
            for u, total in enumerate(self.totals(h)):
                self.s1[h, u] = total.astype(BF)
            self.two[h].start()
        yield
        for t in self.two:
            t.relay()
        yield
        for h in range(2):
            for u, total in enumerate(self.two[h].total()):
                self.s2[h, u] = total.astype(BF)
        self.across()
        yield
        three = []
        for h in range(2):
            self.ready(h)
            three.append(self.wire(self.last.at[h, :, :, self.cols(1 - self.zl, 128)], self.r3.at[h], self.zp))
        yield
        four = []
        for h in range(2):
            three[h].wait_recv()
            for u in range(2):
                total = self.last[h, u, :, self.cols(self.zl, 128)].astype(F32) + self.r3[h, u].astype(F32)
                spot = self.full.at[self.rows(h, self.at1[h], u), self.cols(self.at2[h] * 2 + self.zl, 128)]
                spot[...] = total.astype(BF)
                four.append(self.wire(spot, spot, self.zp))
        yield
        for h in range(2):
            four[2 * h].wait()
            four[2 * h + 1].wait()
            self.five[h].start()
        yield
        for t in self.five:
            t.relay()
        yield
        for h in range(2):
            self.five[h].done()
            self.six[h].start()
        yield
        for t in self.six:
            t.relay()
        yield
        for t in self.two:
            t.sent()
        for c in three:
            c.wait_send()
        self.settle()
        for t in self.six:
            t.done()
        yield

    def ready(self, h):
        pass


class PairSum(Sum):
    direct = True

    def cut(self, g, rows):
        return g.at[:, rows]

    def __init__(self, g, hc, refs, wire, where, xp, yp, zp, far):
        self.rf, self.s3 = refs[:2]
        super().__init__(g, hc, refs[2:], wire, where, xp, yp, zp)
        self.far, self.hh, self.last = far, hc // 2, self.s3

    def totals(self, h):
        return [t.reshape(2 * self.hh, 1024) for t in self.one[h].total()]

    def across(self):
        self.crossed = [self.wire(self.s2.at[h, :, self.hh:], self.rf.at[h], self.far) for h in range(2)]

    def ready(self, h):
        self.crossed[h].wait_recv()
        for u in range(2):
            self.s3[h, u] = (self.s2[h, u, :self.hh].astype(F32) + self.rf[h, u].astype(F32)).astype(BF)

    def settle(self):
        for t in self.one:
            t.sent()
        for c in self.crossed:
            c.wait_send()


class BegunSum(PairSum):
    direct = False

    def __init__(self, hc, refs, wire, where, xp, yp, zp, far, own, plus, minus):
        self.own, self.fwd = refs[:2]
        super().__init__(None, hc, list(refs[2:4]) + [None] * 4 + list(refs[4:]), wire, where, xp, yp, zp, far)
        self.plus, self.minus = plus, minus

    def begin(self):
        hc = 2 * self.hh
        self.passed = []
        for h in range(2):
            plus, minus = self.peers[h]
            self.passed.append((
                self.wire(self.plus[h].at[:, hc:], self.fwd.at[h, 0], plus),
                self.wire(self.minus[h].at[:, hc:], self.fwd.at[h, 1], minus),
            ))

    def relay(self):
        pass

    def totals(self, h):
        hh = self.hh
        for c in self.passed[h]:
            c.wait_recv()
        out = []
        for u in range(2):
            rows = slice(u * hh, u * hh + hh)
            total = self.own[h, 0, :, rows].astype(F32) + self.own[h, 1, :, rows].astype(F32)
            total += self.own[h, 2, :, rows].astype(F32) + self.fwd[h, u].astype(F32)
            out.append(total.reshape(2 * hh, 1024))
        return out

    def settle(self):
        for c in self.crossed:
            c.wait_send()
        for pair in self.passed:
            for c in pair:
                c.wait_send()


SUM_COPIES = 12 + 12 + 2 + 4 + 12 + 12


BEGUN_COPIES = 4 + 12 + 2 + 2 + 4 + 12 + 12
PAIR_COPIES = 12 + 12 + 2 + 2 + 4 + 12 + 12


def sum_scratch(rows):
    hh = rows // 16
    return (
        [pltpu.VMEM((2, 2, hh, 1024), BF)] * 4
        + [pltpu.VMEM((2, 2, hh, 1024), BF)]
        + [pltpu.VMEM((2, 2, hh, 256), BF)] * 4
        + [pltpu.VMEM((2, 2, hh, 256), BF), pltpu.VMEM((2, 2, hh, 128), BF)]
    )


def pair_scratch(rows, begun):
    hh = rows // 16
    begin = [pltpu.VMEM((2, 3, 2, 2 * hh, 1024), BF), pltpu.VMEM((2, 2, 2, hh, 1024), BF)]
    first = [pltpu.VMEM((2, 2, 2, hh, 1024), BF)] * 4
    return (
        (begin if begun else [])
        + [pltpu.VMEM((2, 2, hh, 256), BF)] * 2
        + ([] if begun else first)
        + [pltpu.VMEM((2, 2, 2 * hh, 1024), BF)]
        + [pltpu.VMEM((2, 2, 2 * hh, 256), BF)] * 4
        + [pltpu.VMEM((2, 2, 2 * hh, 256), BF), pltpu.VMEM((2, 2, hh, 128), BF)]
    )


def finish_kernel(*refs):
    dkvp, dqp, dr_ref, gb, wall, gpay, zpay, zr, xs, x_ref = refs[:10]
    got = ((refs[10], refs[13]), (refs[11], refs[14]), (refs[12], refs[15]))

    gt, io_full, u_full, tail_full, s_vec = refs[16:21]
    io_refs = list(refs[21:32]) + [io_full]
    u_refs, tail_refs = list(refs[32:43]) + [u_full], list(refs[43:56]) + [tail_full]
    (dkv, dq, weights, ll2, rr2, lt2, mid, pay, ll, rr, tail, v0, vf, v1, vx, vy, vz, tx, ty,
     sw, rw, sn, rn, ss, rs, ls, lw) = refs[56:]
    scale = 1.0 / math.sqrt(16384)
    where = place()
    zl, x, y, zh, co = where
    w = zh * 2 + co
    me = lax.axis_index("ctx")
    flat = me % 16
    core = device(zl, x, y, zh, 1 - co)
    far = device(zl, x, y, 1 - zh, co)
    xp = [device(zl, (x + s) % 4, y, zh, co) for s in (1, 2, 3)]
    yp = [device(zl, x, (y + s) % 4, zh, co) for s in (1, 2, 3)]
    zp = device(1 - zl, x, y, zh, co)
    bar = pltpu.get_barrier_semaphore()

    def greet_one(i, carry):
        pl.semaphore_signal(bar, inc=1, device_id={"ctx": (me + i) % 32}, device_id_type=MESH)
        return carry

    for p in (core, far):
        pl.semaphore_signal(bar, inc=1, device_id=p, device_id_type=MESH)
    lax.fori_loop(1, 32, greet_one, 0)

    mine = [pl.ds(pl.multiple_of(k * 256, 256), 256) for k in (w, (1 - zh) * 2 + co)]
    parts = []
    for h in range(2):
        for n in range(3):
            parts.append(pltpu.make_async_copy(got[n][h].at[:, :160], io_refs[0].at[h, n], ls.at[10 + 3 * h + n]))
    local = [
        pltpu.make_async_copy(gpay.at[:, :1024], ll2.at[0:128, :], ls.at[0]),
        pltpu.make_async_copy(zpay.at[:, 1024:2048], rr2.at[0:128, :], ls.at[1]),
        pltpu.make_async_copy(zr.at[:, :1024], ll2.at[256:384, :], ls.at[2]),
        pltpu.make_async_copy(zr.at[:, 1024:2048], rr2.at[256:384, :], ls.at[3]),
    ]
    for k in range(2):
        cols = slice(256 * k, 256 * k + 256)
        local.append(pltpu.make_async_copy(x_ref.at[:, mine[k]], ll.at[0:128, cols], ls.at[4 + k]))
        local.append(pltpu.make_async_copy(xs.at[k], ll.at[128:256, cols], ls.at[6 + k]))
    for c in local + parts:
        c.start()
    loads = [pltpu.make_async_copy(wall, weights, lw.at[0])]
    loads[0].start()
    pl.semaphore_wait(bar, 33)

    def narrow_copy(i):
        p = (flat + i) % 16
        return pltpu.make_async_remote_copy(
            src_ref=dqp.at[p], dst_ref=dq.at[flat], send_sem=sn.at[i], recv_sem=rn.at[i],
            device_id={"ctx": zl * 16 + p}, device_id_type=MESH,
        )

    def wide_copy(i):
        p = (me + i) % 32
        return pltpu.make_async_remote_copy(
            src_ref=dkvp.at[p], dst_ref=dkv.at[me], send_sem=sw.at[i], recv_sem=rw.at[i],
            device_id={"ctx": p}, device_id_type=MESH,
        )

    def start(make):
        def one(i, carry):
            make(i).start()
            return carry
        return one

    def wait(make):
        def one(i, carry):
            make(i).wait()
            return carry
        return one

    lax.fori_loop(1, 32, start(wide_copy), 0)
    lax.fori_loop(1, 16, start(narrow_copy), 0)
    home = [
        pltpu.make_async_copy(dkvp.at[me], dkv.at[me], ls.at[8]),
        pltpu.make_async_copy(dqp.at[flat], dq.at[flat], ls.at[9]),
    ]
    for c in home:
        c.start()
    wire = Wire(ss, rs)
    near = [
        wire(gpay.at[:, 1024:], ll2.at[128:256, :], core),
        wire(zpay.at[:, 1024:2048], rr2.at[128:256, :], core),
        wire(zr.at[:, 2048:], ll2.at[384:512, :], core),
        wire(zr.at[:, 1024:2048], rr2.at[384:512, :], core),
    ]
    io = BegunSum(160, io_refs, wire, where, xp, yp, zp, far, *got).steps()
    big = Sum(mid, 128, u_refs, wire, where, xp, yp, zp).steps()
    small = PairSum(tail, 96, tail_refs, wire, where, xp, yp, zp, far).steps()
    next(io)
    next(io)
    for c in local:
        c.wait()
    lt = ll[...].astype(F32).T.astype(BF)
    for c in near:
        c.wait()
    for k in range(4):
        lt2[256 * k:256 * k + 256, :] = ll2[:, 256 * k:256 * k + 256].astype(F32).T.astype(BF)
    for k in range(4):
        rows = slice(256 * k, 256 * k + 256)
        mid[rows, :] = dot(lt2[rows, :], rr2[...]).astype(BF)
    next(big)
    for c in parts:
        c.wait()
    next(io)

    for c in home:
        c.wait()
    lax.fori_loop(1, 32, wait(wide_copy), 0)
    lax.fori_loop(1, 16, wait(narrow_copy), 0)
    for h in range(16):
        lanes = slice(64 * h, 64 * h + 64)
        pair = dq[h]
        pay[:64, lanes] = pair[:, :64]
        pay[64:128, lanes] = pair[:, 64:]
        both = (dkv[h].astype(F32) + dkv[16 + h].astype(F32)).astype(BF)
        pay[:128, 1024 + 64 * h:1088 + 64 * h] = both[:, :64]
        pay[:128, 2048 + 64 * h:2112 + 64 * h] = both[:, 64:]
    pay[128:144, :1024] = jnp.concatenate([gb[...], jnp.zeros((8, 1024), F32)], axis=0).astype(BF)
    pay[128:144, 1024:] = jnp.zeros((16, 2048), BF)
    to_core = wire(pay, rr, core)
    next(big)
    next(io)
    for c in loads:
        c.wait()
    for k in range(4):
        cols = slice(256 * k, 256 * k + 256)
        total = dr_ref[:, cols]
        for m in range(3):
            total += dot(pay[:128, 1024 * m:1024 * m + 1024], weights[k, m], NT)
        gt[:, cols] = total
    to_core.wait_recv()
    for z in range(2):
        for m in range(3):
            cols = slice(1024 * m, 1024 * m + 1024)
            total = dot(lt[256 * z:256 * z + 256, :128], pay[:128, cols])
            total += dot(lt[256 * z:256 * z + 256, 128:], rr[:128, cols])
            tail[z, 256 * m:256 * m + 256, :] = total.astype(BF)
    next(small)
    for z in range(2):
        v0[z] = (pay[128:144, mine[z]].astype(F32) + rr[128:144, mine[z]].astype(F32))[:8]
    vfar = wire(v0.at[1], vf, far)
    next(io)
    next(big)
    next(small)
    next(io)
    next(big)
    next(small)
    vfar.wait_recv()
    v1[...] = v0[0] + vf[...]
    vone = [wire(v1, vx.at[s], xp[s]) for s in range(3)]
    next(io)
    next(big)
    next(small)
    next(io)
    next(big)
    next(small)
    for c in vone:
        c.wait_recv()
    tx[...] = v1[...] + vx[0] + vx[1] + vx[2]
    vtwo = [wire(tx, vy.at[s], yp[s]) for s in range(3)]
    next(io)
    next(big)
    next(small)
    next(io)
    next(big)
    next(small)
    for c in vtwo:
        c.wait_recv()
    ty[...] = tx[...] + vy[0] + vy[1] + vy[2]
    vthree = wire(ty, vz, zp)
    next(io)
    next(big)
    next(small)
    next(big)
    next(small)
    next(big)
    next(small)
    vthree.wait()
    s_vec[...] = (ty[...] + vz[...]) * scale
    for c in vone + vtwo + [to_core, vfar]:
        c.wait_send()
    next(small)
    next(io)
    next(big)
    next(small)


def finish(dkvp, dqp, dr, gb, wall, gpay, zpay, zr, xs, tok, parts):
    n = SUM_COPIES + BEGUN_COPIES + PAIR_COPIES + 4 + 2 + 7
    return pl.pallas_call(
        finish_kernel,
        out_shape=[
            shp((128, 1024), F32), shp((1280, 1024), BF), shp((1024, 1024), BF), shp((768, 1024), BF), shp((8, 256), F32),
        ],
        in_specs=[ANY, ANY, VM, VM] + [ANY] * 12,
        out_specs=[VM] * 5,
        scratch_shapes=pair_scratch(1280, True) + sum_scratch(1024) + pair_scratch(768, False) + [
            pltpu.VMEM((32, 128, 128), BF), pltpu.VMEM((16, 64, 128), BF), pltpu.VMEM((4, 3, 256, 1024), BF),
            pltpu.VMEM((512, 1024), BF), pltpu.VMEM((512, 1024), BF), pltpu.VMEM((1024, 512), BF),
            pltpu.VMEM((1024, 1024), BF), pltpu.VMEM((144, 3072), BF),
            pltpu.VMEM((256, 512), BF), pltpu.VMEM((144, 3072), BF), pltpu.VMEM((2, 768, 1024), BF),
            pltpu.VMEM((2, 8, 256), F32), pltpu.VMEM((8, 256), F32), pltpu.VMEM((8, 256), F32),
            pltpu.VMEM((3, 8, 256), F32), pltpu.VMEM((3, 8, 256), F32),
            pltpu.VMEM((8, 256), F32), pltpu.VMEM((8, 256), F32), pltpu.VMEM((8, 256), F32),
            DMA((32,)), DMA((32,)), DMA((16,)), DMA((16,)), DMA((n,)), DMA((n,)), DMA((16,)), DMA((1,)),
        ],
        compiler_params=pltpu.CompilerParams(collective_id=6, has_side_effects=True, vmem_limit_bytes=LIMIT),
        name="finish",
    )(dkvp, dqp, dr, gb, wall, gpay, zpay, zr, xs, tok, *parts)


def scale_kernel(o, i0, i1, i2, i3, u, q, k, v, out_q, out_k, out_v, out_o, out_i, out_u):
    scale = 1.0 / math.sqrt(16384)
    for src, dst in ((q, out_q), (k, out_k), (v, out_v), (o, out_o), (u, out_u)):
        dst[...] = src[...].astype(F32) * scale
    for n, src in enumerate((i0, i1, i2, i3)):
        out_i[:, 1024 * n:1024 * n + 1024] = src[...].astype(F32) * scale


def scaled(io, u, tail):
    def rows(first, n=32):
        return pl.BlockSpec((n, 1024), lambda j: (first // n + j, 0))

    return pl.pallas_call(
        scale_kernel,
        grid=(8,),
        out_shape=[shp((256, 1024), F32)] * 4 + [shp((256, 4096), F32), shp((1024, 1024), F32)],
        in_specs=[rows(0)] + [rows(256 + 256 * k) for k in range(4)] + [rows(0, 128)] + [rows(256 * k) for k in range(3)],
        out_specs=[rows(0)] * 4 + [pl.BlockSpec((32, 4096), lambda j: (j, 0)), rows(0, 128)],
        compiler_params=pltpu.CompilerParams(vmem_limit_bytes=LIMIT),
        name="scaled",
    )(*[io] * 5, u, *[tail] * 3)


FLIP_CORE = [(0, 1), (1, 0), (2, 3), (3, 2)]
FLIP_FAR = [(0, 2), (2, 0), (1, 3), (3, 1)]


def along_x(s):
    return [(c, c // 16 * 16 + (c // 4 + s) % 4 * 4 + c % 4) for c in range(32)]


def along_y(s):
    return [(c, c // 4 * 4 + (c + s) % 4) for c in range(32)]


def body(
    tokens, w_query, w_key, w_value, w_output, w_inner, w_outer, ln_gain, ln_bias, block_mask, block_pairs, cotangent,
):
    tok = tokens.reshape(128, 1024)
    cot = cotangent.reshape(128, 1024)
    lnp = jnp.concatenate([ln_gain, ln_bias, jnp.zeros((4, 256), F32)], axis=0)
    blk = block_pairs.reshape(-1)
    own = (w_query, w_key, w_value)
    outer = w_outer.reshape(8, 4, 32, 1024)
    wall, xs, lnf, *rest = front(tok, own, lnp, w_output, w_inner, outer)
    core_shard, (qa, qb, x2, y2, diag_a, diag_b, kvr, qr) = rest[:3], rest[3:]
    x1, x3 = (lax.ppermute(qa, "ctx", along_x(s)) for s in (1, 3))
    y1, y3 = (lax.ppermute(qb, "ctx", along_y(s)) for s in (1, 3))
    o, ot, lse = attend(blk, block_mask, kvr, qr)
    x1, x2, x3, y1, y2, y3, o = lax.optimization_barrier((x1, x2, x3, y1, y2, y3, o))
    far = [qa, x1, x2, x3, qb, y1, y2, y3]
    d1, d2, d3, e1, e2, e3 = (lax.ppermute(p, "wsh", FLIP_CORE) for p in (x1, x2, x3, y1, y2, y3))
    diag = [diag_a, d1, d2, d3, diag_b, e1, e2, e3]
    (o_back,) = exchange(None, o, 3)
    y_out, dr1, do, zpay, gpay, cpay, lown, gb = middle(
        o_back, tok, cot, lnf, lnp, ((w_output, w_inner, outer), core_shard), (far, diag)
    )
    zr = lax.ppermute(zpay, "wsh", FLIP_FAR)
    dor, own_a, plus_a, minus_a, own_b, plus_b, minus_b = turn(do, cpay, lown)
    plus_a = lax.ppermute(plus_a, "ctx", along_x(1))
    minus_a = lax.ppermute(minus_a, "ctx", along_x(3))
    plus_b = lax.ppermute(plus_b, "ctx", along_y(1))
    minus_b = lax.ppermute(minus_b, "ctx", along_y(3))
    dkvp, dqp = attend_back(blk, block_mask, kvr, qr, dor, ot, lse)
    zr, plus_a, minus_a, plus_b, minus_b, dkvp = lax.optimization_barrier((zr, plus_a, minus_a, plus_b, minus_b, dkvp))
    grad_tok, io, u, tail, s_vec = finish(
        dkvp, dqp, dr1, gb, wall, gpay, zpay, zr, xs, tok, (own_a, plus_a, minus_a, own_b, plus_b, minus_b)
    )
    s_q, s_k, s_v, s_o, s_i, s_u = scaled(io, u, tail)
    out_shape = tokens.shape
    return (
        y_out.reshape(out_shape), grad_tok.reshape(out_shape), s_q, s_k, s_v, s_o, s_i, s_u, s_vec[0:2], s_vec[2:4],
    )


def solution(mesh):
    return jax.shard_map(
        body,
        mesh=mesh,
        in_specs=(
            P("wsh", "ctx", None, None),
            P("wsh", None), P("wsh", None), P("wsh", None), P("wsh", None), P("wsh", None), P("wsh", None),
            P(None, "wsh"), P(None, "wsh"),
            P("wsh", None, None),
            P(),
            P("wsh", "ctx", None, None),
        ),
        out_specs=(
            P("wsh", "ctx", None, None), P("wsh", "ctx", None, None),
            P("wsh", None), P("wsh", None), P("wsh", None), P("wsh", None), P("wsh", None), P("wsh", None),
            P(None, "wsh"), P(None, "wsh"),
        ),
        check_vma=False,
    )
```

```python
import math

import jax
import jax.numpy as jnp
from jax import lax
from jax.experimental import pallas as pl
from jax.experimental.pallas import tpu as pltpu
from jax.sharding import PartitionSpec as P

MESH = pl.DeviceIdType.MESH
BF = jnp.bfloat16
F32 = jnp.float32
ANY = pl.BlockSpec(memory_space=pl.ANY)
VM = pl.BlockSpec(memory_space=pltpu.VMEM)
SM = pl.BlockSpec(memory_space=pltpu.SMEM)
DMA = pltpu.SemaphoreType.DMA
LIMIT = 56 * 1024 * 1024
EPS = 1e-05
NEG = -1e30


def shp(shape, dtype):
    return jax.ShapeDtypeStruct(shape, dtype)


def dot(a, b, dims=((1,), (0,))):
    return lax.dot_general(a, b, (dims, ((), ())), preferred_element_type=F32)


NN = ((1,), (0,))
NT = ((1,), (1,))
TN = ((0,), (0,))


def place():
    c = lax.axis_index("ctx")
    w = lax.axis_index("wsh")
    return c // 16, (c // 4) % 4, c % 4, w // 2, w % 2


def device(zl, x, y, zh, co):
    return {"ctx": zl * 16 + x * 4 + y, "wsh": zh * 2 + co}


def greet(peers):
    bar = pltpu.get_barrier_semaphore()
    for p in peers:
        pl.semaphore_signal(bar, inc=1, device_id=p, device_id_type=MESH)
    pl.semaphore_wait(bar, len(peers))


class Wire:
    def __init__(self, send, recv):
        self.send, self.recv, self.n = send, recv, 0

    def __call__(self, src, dst, peer):
        k = self.n
        self.n += 1
        copy = pltpu.make_async_remote_copy(
            src_ref=src, dst_ref=dst, send_sem=self.send.at[k], recv_sem=self.recv.at[k],
            device_id=peer, device_id_type=MESH,
        )
        copy.start()
        return copy


def front_kernel(*refs):
    x_ref, wq, wk, wv, x_any, ln_ref, wo, wi, wu = refs[:9]
    wall, xs, lnf, co_ref, ci_ref, cu_ref, qa_ref, qb_ref, x2_ref, y2_ref, da_ref, db_ref, kvr, qr = refs[9:23]
    weights, acc, kvp, qp, ss, rs, sw, rw, sf, rf, sn, rn, ls = refs[23:]
    zl, x, y, zh, co = place()
    me = zh * 2 + co
    slots = [me, zh * 2 + 1 - co, (1 - zh) * 2 + co, (1 - zh) * 2 + 1 - co]
    here = lax.axis_index("ctx")
    flat = here % 16
    core = device(zl, x, y, zh, 1 - co)
    far = device(zl, x, y, 1 - zh, co)
    diag = device(zl, x, y, 1 - zh, 1 - co)
    zp = device(1 - zl, x, y, zh, co)
    xp = [device(zl, (x + s) % 4, y, zh, co) for s in (1, 2, 3)]
    yp = [device(zl, x, (y + s) % 4, zh, co) for s in (1, 2, 3)]
    bar = pltpu.get_barrier_semaphore()

    def greet_one(i, carry):
        pl.semaphore_signal(bar, inc=1, device_id={"ctx": zl * 16 + (flat + i) % 16}, device_id_type=MESH)
        return carry

    for p in (far, core, diag, zp):
        pl.semaphore_signal(bar, inc=1, device_id=p, device_id_type=MESH)
    lax.fori_loop(1, 16, greet_one, 0)
    ws = (wq, wk, wv)
    local = [pltpu.make_async_copy(ws[m], weights.at[me, m], ls.at[m]) for m in range(3)]
    for c in local:
        c.start()
    pl.semaphore_wait(bar, 19)
    wire = Wire(ss, rs)
    rows_a = pl.ds(pl.multiple_of(x * 32, 32), 32)
    rows_b = pl.ds(pl.multiple_of(128 + y * 32, 32), 32)
    first_a, first_b = [], []
    for m in range(3):
        first_a.append(wire(ws[m].at[rows_a], weights.at[me, m, rows_a], far))
        first_b.append(wire(ws[m].at[rows_b], weights.at[me, m, rows_b], far))
    near = [wire(ws[m], weights.at[me, m], core) for m in range(3)]
    quarters = []
    for ref, k, n in ((qa_ref, x, y), (qb_ref, 4 + y, x)):
        rows = pl.ds(pl.multiple_of(k * 32, 32), 32)
        cols = pl.ds(pl.multiple_of(n * 256, 256), 256)
        quarters.append(wire(wo.at[rows, cols], ref.at[0, :, cols], far))
        for b in range(4):
            at = pl.ds(pl.multiple_of(1024 * b + n * 256, 256), 256)
            quarters.append(wire(wi.at[rows, at], ref.at[1 + b, :, cols], far))
        quarters.append(wire(wu.at[k, :, :, cols], ref.at[5:9, :, cols], far))
    rest = []
    for p in (core, far, diag):
        rest.append(wire(ln_ref, lnf.at[me], p))
    for n, idx in enumerate((slots[1], slots[3])):
        rest.append(wire(x_any.at[:, pl.ds(pl.multiple_of(idx * 256, 256), 256)], xs.at[n], core))

    def add(k, fresh):
        cols = x_ref[:, pl.ds(pl.multiple_of(slots[k] * 256, 256), 256)]
        for m in range(3):
            part = dot(cols, weights[slots[k], m])
            acc[m] = part if fresh else acc[m] + part

    for c in first_a:
        c.wait_recv()
    second = []
    for m in range(3):
        part = weights.at[slots[2], m, rows_a]
        for p in xp:
            second.append(wire(part, part, p))
    for c in first_b:
        c.wait_recv()
    for m in range(3):
        part = weights.at[slots[2], m, rows_b]
        for p in yp:
            second.append(wire(part, part, p))
    for c in local:
        c.wait()
    add(0, True)
    for c in near:
        c.wait_recv()
    add(1, False)
    for c in second:
        c.wait_recv()
    last = [wire(weights.at[slots[2], m], weights.at[slots[2], m], core) for m in range(3)]
    add(2, False)
    for c in last:
        c.wait_recv()
    add(3, False)
    keep = pltpu.make_async_copy(weights, wall, ls.at[0])
    keep.start()
    for j in range(8):
        lanes = slice(128 * j, 128 * j + 128)
        q = (acc[0, :, lanes].astype(BF).astype(F32) * 0.125).astype(BF)
        k = acc[1, :, lanes].astype(BF)
        v = acc[2, :, lanes].astype(BF)
        for u in range(2):
            part = slice(64 * u, 64 * u + 64)
            kvp[2 * j + u] = jnp.concatenate([k[:, part], v[:, part]], axis=1)
            qp[2 * j + u] = jnp.concatenate([q[:64, part], q[64:, part]], axis=1)

    def plane(i):
        return {"ctx": zl * 16 + (flat + i) % 16}

    def wide_copy(i):
        return pltpu.make_async_remote_copy(
            src_ref=kvp.at[(flat + i) % 16], dst_ref=kvr.at[here], send_sem=sw.at[i], recv_sem=rw.at[i],
            device_id=plane(i), device_id_type=MESH,
        )

    def narrow_copy(i):
        return pltpu.make_async_remote_copy(
            src_ref=qp.at[(flat + i) % 16], dst_ref=qr.at[flat], send_sem=sn.at[i], recv_sem=rn.at[i],
            device_id=plane(i), device_id_type=MESH,
        )

    def pass_copy(i):
        spot = kvr.at[zl * 16 + (flat + 16 - i) % 16]
        return pltpu.make_async_remote_copy(
            src_ref=spot, dst_ref=spot, send_sem=sf.at[i], recv_sem=rf.at[i], device_id=zp, device_id_type=MESH,
        )

    def start_wide(i, carry):
        wide_copy(i).start()
        return carry

    def start_narrow(i, carry):
        narrow_copy(i).start()
        return carry

    def pass_on(i, carry):
        wide_copy(i).wait_recv()
        pass_copy(i).start()
        return carry

    def wait_all(i, carry):
        wide_copy(i).wait_send()
        narrow_copy(i).wait()
        pass_copy(i).wait()
        return carry

    to_z = wire(kvp.at[flat], kvr.at[here], zp)
    lax.fori_loop(1, 16, start_wide, 0)
    lax.fori_loop(1, 16, start_narrow, 0)
    home = [
        pltpu.make_async_copy(kvp.at[flat], kvr.at[here], ls.at[1]),
        pltpu.make_async_copy(qp.at[flat], qr.at[flat], ls.at[2]),
    ]
    for c in home:
        c.start()
    for c in quarters:
        c.wait_recv()
    subs = []
    for ref, n, peers in ((qa_ref, y, yp), (qb_ref, x, xp)):
        spot = ref.at[:, :, pl.ds(pl.multiple_of(n * 256, 256), 256)]
        for p in peers:
            subs.append(wire(spot, spot, p))
    for src, dst in ((wo, co_ref), (wi, ci_ref), (wu, cu_ref)):
        rest.append(wire(src, dst, core))
    lax.fori_loop(1, 16, pass_on, 0)
    for c in subs:
        c.wait_recv()
    for src, dst, p in ((qa_ref, x2_ref, xp[1]), (qb_ref, y2_ref, yp[1]), (qa_ref, da_ref, core), (qb_ref, db_ref, core)):
        rest.append(wire(src, dst, p))
    for c in home:
        c.wait()
    keep.wait()
    lax.fori_loop(1, 16, wait_all, 0)
    to_z.wait()
    for c in first_a + first_b + near + second + last + quarters + subs:
        c.wait_send()
    for c in rest:
        c.wait()


def front(tok, own, lnp, wo, wi, wu):
    n = 6 + 3 + 12 + 3 + 2 + 18 + 3 + 1 + 6 + 3 + 4
    piece = shp((9, 32, 1024), BF)
    return pl.pallas_call(
        front_kernel,
        out_shape=[shp((4, 3, 256, 1024), BF), shp((2, 128, 256), BF), shp((4, 8, 256), F32)]
        + [shp(wo.shape, BF), shp(wi.shape, BF), shp(wu.shape, BF)] + [piece] * 6
        + [shp((32, 128, 128), BF), shp((16, 64, 128), BF)],
        in_specs=[VM] + [ANY] * 8,
        out_specs=[ANY] * 14,
        scratch_shapes=[
            pltpu.VMEM((4, 3, 256, 1024), BF), pltpu.VMEM((3, 128, 1024), F32),
            pltpu.VMEM((16, 128, 128), BF), pltpu.VMEM((16, 64, 128), BF),
            DMA((n,)), DMA((n,)), DMA((16,)), DMA((16,)), DMA((16,)), DMA((16,)), DMA((16,)), DMA((16,)), DMA((3,)),
        ],
        compiler_params=pltpu.CompilerParams(collective_id=1, has_side_effects=True, vmem_limit_bytes=LIMIT),
        cost_estimate=pl.CostEstimate(flops=16 << 30, bytes_accessed=32 << 20, transcendentals=0),
        name="front",
    )(tok, *own, tok, lnp, wo, wi, wu)


def exchange(wide, narrow, collective):
    has = wide is not None
    n = 32 if has else 16

    def kernel(*refs):
        if has:
            wi, na, wo, no, sw, rw, sn, rn, ls = refs
        else:
            na, no, sn, rn, ls = refs
        me = lax.axis_index("ctx")
        zl = me // 16
        flat = me % 16
        bar = pltpu.get_barrier_semaphore()

        def peer(i):
            if has:
                return (me + i) % 32
            return zl * 16 + (flat + i) % 16

        def greet_one(i, carry):
            pl.semaphore_signal(bar, inc=1, device_id={"ctx": peer(i)}, device_id_type=MESH)
            return carry

        lax.fori_loop(1, n, greet_one, 0)
        pl.semaphore_wait(bar, n - 1)

        def narrow_copy(i):
            p = (flat + i) % 16
            return pltpu.make_async_remote_copy(
                src_ref=na.at[p], dst_ref=no.at[flat], send_sem=sn.at[i], recv_sem=rn.at[i],
                device_id={"ctx": zl * 16 + p}, device_id_type=MESH,
            )

        def wide_copy(i):
            p = (me + i) % 32
            src = p if wide.shape[0] == 32 else p % 16
            return pltpu.make_async_remote_copy(
                src_ref=wi.at[src], dst_ref=wo.at[me], send_sem=sw.at[i], recv_sem=rw.at[i],
                device_id={"ctx": p}, device_id_type=MESH,
            )

        def start(make):
            def one(i, carry):
                make(i).start()
                return carry
            return one

        def wait(make):
            def one(i, carry):
                make(i).wait()
                return carry
            return one

        if has:
            lax.fori_loop(1, 32, start(wide_copy), 0)
        lax.fori_loop(1, 16, start(narrow_copy), 0)
        local = [pltpu.make_async_copy(na.at[flat], no.at[flat], ls.at[0])]
        if has:
            own = me if wide.shape[0] == 32 else flat
            local.append(pltpu.make_async_copy(wi.at[own], wo.at[me], ls.at[1]))
        for c in local:
            c.start()
        for c in local:
            c.wait()
        if has:
            lax.fori_loop(1, 32, wait(wide_copy), 0)
        lax.fori_loop(1, 16, wait(narrow_copy), 0)

    sems = ([DMA((32,)), DMA((32,))] if has else []) + [DMA((16,)), DMA((16,)), DMA((2,))]
    outs = ([shp((32,) + wide.shape[1:], wide.dtype)] if has else []) + [shp(narrow.shape, narrow.dtype)]
    args = ([wide] if has else []) + [narrow]
    return pl.pallas_call(
        kernel,
        out_shape=outs,
        in_specs=[ANY] * len(args),
        out_specs=[ANY] * len(outs),
        scratch_shapes=sems,
        compiler_params=pltpu.CompilerParams(collective_id=collective, has_side_effects=True),
        cost_estimate=pl.CostEstimate(flops=16 << 30, bytes_accessed=32 << 20, transcendentals=0),
        name=f"exchange_{collective}",
    )(*args)


def attention_setup(blk, mask, kvr, qr, kvs, kaug, kvt, bias, qs, inv, order, oblk):
    first = (lax.axis_index("ctx") // 16) * 32

    def note(s, carry):
        inv[blk[s]] = s
        return carry

    lax.fori_loop(0, 64, note, 0)

    def pick(b, count):
        local = inv[b] - first
        order[count] = local
        oblk[count] = b
        mine = jnp.logical_and(local >= 0, local < 32)
        return count + mine.astype(jnp.int32)

    lax.fori_loop(0, 64, pick, 0)
    for s in range(64):
        at = pl.ds(pl.multiple_of(blk[s] * 64, 64), 64)
        kvs[at, :] = kvr[s // 2, (s % 2) * 64:(s % 2) * 64 + 64, :]
    for j in range(16):
        pair = qr[j]
        qs[2 * j] = pair[:, :64]
        qs[2 * j + 1] = pair[:, 64:]
    rows = lax.broadcasted_iota(jnp.int32, (512, 64), 0) // 64
    lanes = lax.broadcasted_iota(jnp.int32, (512, 64), 1)
    for c in range(8):
        part = kvs[512 * c:512 * c + 512, :]
        hot = jnp.where(rows + 8 * c == lanes, 1.0, 0.0).astype(BF)
        kaug[512 * c:512 * c + 512, :] = jnp.concatenate([part[:, :64], hot], axis=1)
        kvt[c] = part.astype(F32).T.astype(BF)
    qi = lax.broadcasted_iota(jnp.int32, (64, 64), 0)
    ki = lax.broadcasted_iota(jnp.int32, (64, 64), 1)
    bias[...] = jnp.where(jnp.logical_and(mask[0] != 0, ki < qi), 0.0, NEG)


def triangle():
    key = lax.broadcasted_iota(jnp.int32, (64, 256), 0)
    query = lax.broadcasted_iota(jnp.int32, (64, 256), 1) % 64
    return key <= query


def attend_kernel(blk, mask, kvr, qr, o_ref, ot_ref, lse_ref, kvs, kaug, kvt, bias, qs, qa, os, inv, order, oblk):
    attention_setup(blk, mask, kvr, qr, kvs, kaug, kvt, bias, qs, inv, order, oblk)

    def tile(g, carry):
        score, vals = [], []
        for u in range(4):
            i = oblk[4 * g + u]
            q = qs[order[4 * g + u]]
            row = jnp.broadcast_to(bias[pl.ds(i, 1), :], (64, 64)).astype(BF)
            qa[64 * u:64 * u + 64, :] = jnp.concatenate([q, row], axis=1)
            kv = kvs[pl.ds(pl.multiple_of(i * 64, 64), 64), :]
            score.append(dot(kv[:, :64], q, NT))
            vals.append(kv[:, 64:])
        s = jnp.where(triangle(), jnp.concatenate(score, axis=1), NEG)
        top = jnp.max(s, axis=0, keepdims=True)
        p = jnp.exp(s - top)
        total = jnp.sum(p, axis=0, keepdims=True)
        pb = p.astype(BF)
        mix = jnp.concatenate([dot(vals[u], pb[:, 64 * u:64 * u + 64], TN) for u in range(4)], axis=1)
        queries = qa[...]

        def chunk(c, state):
            top, total, mix = state
            keys = kaug[pl.ds(pl.multiple_of(c * 512, 512), 512), :]
            s = dot(keys, queries, NT)
            new = jnp.maximum(top, jnp.max(s, axis=0, keepdims=True))
            shrink = jnp.exp(top - new)
            p = jnp.exp(s - new)
            total = total * shrink + jnp.sum(p, axis=0, keepdims=True)
            mix = mix * shrink + dot(kvt[c, 64:, :], p.astype(BF))
            return new, total, mix

        chunks = (oblk[4 * g + 3] + 7) // 8
        def pair(c, state):
            top, total, mix = state
            parts = [dot(kaug[pl.ds(pl.multiple_of(c * 1024 + 512 * k, 512), 512), :], queries, NT) for k in range(2)]
            new = top
            for s in parts:
                new = jnp.maximum(new, jnp.max(s, axis=0, keepdims=True))
            shrink = jnp.exp(top - new)
            total, mix = total * shrink, mix * shrink
            for k, s in enumerate(parts):
                p = jnp.exp(s - new)
                total += jnp.sum(p, axis=0, keepdims=True)
                mix += dot(kvt[2 * c + k, 64:, :], p.astype(BF))
            return new, total, mix

        top, total, mix = lax.fori_loop(0, chunks // 2, pair, (top, total, mix))
        top, total, mix = lax.fori_loop(chunks // 2 * 2, chunks, chunk, (top, total, mix))
        out = mix / total
        ot_ref[g] = out
        lse_ref[g] = top + jnp.log(total)
        back = out.T.astype(BF)
        for u in range(4):
            os[order[4 * g + u]] = back[64 * u:64 * u + 64, :]
        return carry

    lax.fori_loop(0, 8, tile, 0)
    for j in range(16):
        o_ref[j] = jnp.concatenate([os[2 * j], os[2 * j + 1]], axis=1)


def attention_scratch():
    return [
        pltpu.VMEM((4096, 128), BF),
        pltpu.VMEM((4096, 128), BF),
        pltpu.VMEM((8, 128, 512), BF),
        pltpu.VMEM((64, 64), F32),
        pltpu.VMEM((32, 64, 64), BF),
        pltpu.VMEM((256, 128), BF),
        pltpu.VMEM((32, 64, 64), BF),
        pltpu.SMEM((64,), jnp.int32),
        pltpu.SMEM((72,), jnp.int32),
        pltpu.SMEM((72,), jnp.int32),
    ]


def attend(blk, mask, kvr, qr):
    return pl.pallas_call(
        attend_kernel,
        out_shape=[shp((16, 64, 128), BF), shp((8, 64, 256), F32), shp((8, 1, 256), F32)],
        in_specs=[SM, VM, VM, VM],
        out_specs=[VM] * 3,
        scratch_shapes=attention_scratch(),
        compiler_params=pltpu.CompilerParams(vmem_limit_bytes=LIMIT),
        cost_estimate=pl.CostEstimate(flops=10 << 30, bytes_accessed=32 << 20, transcendentals=4 << 20),
        name="attend",
    )(blk, mask, kvr, qr)


def attend_back_kernel(
    blk, mask, kvr, qr, dor, ot_ref, lse_ref, dkv_ref, dq_ref,
    kvs, kaug, kvt, bias, qs, qa, dqs, inv, order, oblk, dos, qz, dz, dkv,
):
    attention_setup(blk, mask, kvr, qr, kvs, kaug, kvt, bias, qs, inv, order, oblk)
    for j in range(16):
        pair = dor[j]
        dos[2 * j] = pair[:, :64]
        dos[2 * j + 1] = pair[:, 64:]
    dkv[...] = jnp.zeros_like(dkv)
    zero = jnp.zeros((64, 64), BF)

    def tile(g, carry):
        score, dprob, places, keys_own, q_own, d_own = [], [], [], [], [], []
        for u in range(4):
            i = oblk[4 * g + u]
            q = qs[order[4 * g + u]]
            do = dos[order[4 * g + u]]
            rows = slice(64 * u, 64 * u + 64)
            row = jnp.broadcast_to(bias[pl.ds(i, 1), :], (64, 64)).astype(BF)
            qa[rows, :] = jnp.concatenate([q, row], axis=1)
            qz[rows, :] = jnp.concatenate([q, zero], axis=1)
            dz[rows, :] = jnp.concatenate([zero, do], axis=1)
            at = pl.ds(pl.multiple_of(i * 64, 64), 64)
            kv = kvs[at, :]
            score.append(dot(kv[:, :64], q, NT))
            dprob.append(dot(kv[:, 64:], do, NT))
            places.append(at)
            keys_own.append(kv[:, :64])
            q_own.append(q)
            d_own.append(do)
        lse = lse_ref[g]
        queries = qa[...]
        qpad = qz[...]
        dpad = dz[...]
        dot_t = dpad[:, 64:].astype(F32).T
        delta = jnp.sum(ot_ref[g] * dot_t, axis=0, keepdims=True)
        s = jnp.where(triangle(), jnp.concatenate(score, axis=1), NEG)
        p = jnp.exp(s - lse)
        ds = (p * (jnp.concatenate(dprob, axis=1) - delta)).astype(BF)
        pb = p.astype(BF)
        dq = []
        for u in range(4):
            lanes = slice(64 * u, 64 * u + 64)
            grad = jnp.concatenate([dot(ds[:, lanes], q_own[u]), dot(pb[:, lanes], d_own[u])], axis=1)
            dkv[places[u], :] += grad
            dq.append(dot(keys_own[u], ds[:, lanes], TN))

        def chunk(c, dq):
            at = pl.ds(pl.multiple_of(c * 512, 512), 512)
            p = jnp.exp(dot(kaug[at, :], queries, NT) - lse)
            dp = dot(kvs[at, :], dpad, NT)
            ds = (p * (dp - delta)).astype(BF)
            dkv[at, :] += dot(ds, qpad) + dot(p.astype(BF), dpad)
            return dq + dot(kvt[c, :64, :], ds)

        chunks = (oblk[4 * g + 3] + 7) // 8
        dq = lax.fori_loop(0, chunks // 2, lambda c, dq: chunk(2 * c + 1, chunk(2 * c, dq)), jnp.concatenate(dq, axis=1))
        dq = lax.fori_loop(chunks // 2 * 2, chunks, chunk, dq)
        back = (dq * 0.125).T.astype(BF)
        for u in range(4):
            dqs[order[4 * g + u]] = back[64 * u:64 * u + 64, :]
        return carry

    lax.fori_loop(0, 8, tile, 0)
    for j in range(16):
        dq_ref[j] = jnp.concatenate([dqs[2 * j], dqs[2 * j + 1]], axis=1)
    for s in range(64):
        at = pl.ds(pl.multiple_of(blk[s] * 64, 64), 64)
        dkv_ref[s // 2, (s % 2) * 64:(s % 2) * 64 + 64, :] = dkv[at, :].astype(BF)


def attend_back(blk, mask, kvr, qr, dor, ot, lse):
    return pl.pallas_call(
        attend_back_kernel,
        out_shape=[shp((32, 128, 128), BF), shp((16, 64, 128), BF)],
        in_specs=[SM] + [VM] * 6,
        out_specs=[VM] * 2,
        scratch_shapes=attention_scratch()
        + [
            pltpu.VMEM((32, 64, 64), BF),
            pltpu.VMEM((256, 128), BF),
            pltpu.VMEM((256, 128), BF),
            pltpu.VMEM((4096, 128), F32),
        ],
        compiler_params=pltpu.CompilerParams(vmem_limit_bytes=LIMIT),
        cost_estimate=pl.CostEstimate(flops=1 << 30, bytes_accessed=4 << 20, transcendentals=0),
        name="attend_back",
    )(blk, mask, kvr, qr, dor, ot, lse)


def norm_parts(v):
    center = v - jnp.mean(v, axis=1, keepdims=True)
    r = lax.rsqrt(jnp.mean(center * center, axis=1, keepdims=True) + EPS)
    return center * r, r


def norm_back(e, gain, z, r):
    g = e * gain
    return r * (g - jnp.mean(g, axis=1, keepdims=True) - z * jnp.mean(g * z, axis=1, keepdims=True))


def middle_kernel(*refs):
    o_ref, x_ref, e_ref, ln_ref, ln_own = refs[:5]
    shards = (refs[5:8], refs[8:11])
    pieces = (refs[11:19], refs[19:27])
    y_ref, dr_ref, do_ref, zpay, gpay, cpay, lown, gb_ref = refs[27:35]
    wo, wi, wu, us, gs, nl, ob, sw, sp = refs[35:]
    zl, x, y, zh, co = place()
    w = zh * 2 + co
    where = [w, zh * 2 + 1 - co, (1 - zh) * 2 + co, (1 - zh) * 2 + 1 - co]
    copies = [[], [], []]
    for r, (a, b, c) in enumerate(shards):
        rows = pl.ds(pl.multiple_of(where[r] * 256, 256), 256)
        copies[0].append(pltpu.make_async_copy(a, wo.at[rows], sw.at[r, 0]))
        for k in range(4):
            cols = slice(1024 * k, 1024 * k + 1024)
            copies[1].append(pltpu.make_async_copy(b.at[:, cols], wi.at[k, rows], sw.at[r, 1 + k]))
        groups = pl.ds(where[r] * 8, 8)
        copies[2].append(pltpu.make_async_copy(c, wu.at[groups], sw.at[r, 5]))
    for r, parts in enumerate(pieces):
        t = where[2 + r]
        quarters = [(parts[s], 0, (x + 4 - s) % 4) for s in range(4)]
        quarters += [(parts[4 + s], 1, (y + 4 - s) % 4) for s in range(4)]
        for n, (ref, h, q) in enumerate(quarters):
            rows = pl.ds(pl.multiple_of(t * 256 + h * 128 + q * 32, 32), 32)
            copies[0].append(pltpu.make_async_copy(ref.at[0], wo.at[rows], sp.at[r, n, 0]))
            copies[1].append(pltpu.make_async_copy(ref.at[1:5], wi.at[:, rows], sp.at[r, n, 1]))
            copies[2].append(pltpu.make_async_copy(ref.at[5:9], wu.at[t * 8 + h * 4 + q], sp.at[r, n, 2]))
    for group in copies:
        for c in group:
            c.start()

    ln = jnp.concatenate([jnp.where(w == k, ln_own[...], ln_ref[k]) for k in range(4)], axis=1)
    gain0, gain1, bias0, bias1 = (ln[k:k + 1, :] for k in range(4))
    for h in range(16):
        pair = o_ref[h]
        ob[:64, 64 * h:64 * h + 64] = pair[:, :64]
        ob[64:, 64 * h:64 * h + 64] = pair[:, 64:]
    for c in copies[0]:
        c.wait()
    z0, r0 = norm_parts(x_ref[...].astype(F32) + dot(ob[...], wo[...]))
    n1 = z0 * gain0 + bias0
    nl[...] = n1.astype(BF)
    for c in copies[1]:
        c.wait()

    half = math.sqrt(0.5)

    def up(c, carry):
        u = dot(nl[...], wi[c])
        us[c] = u
        gs[:, pl.ds(pl.multiple_of(c * 1024, 1024), 1024)] = (0.5 * u * (1.0 + lax.erf(u * half))).astype(BF)
        return carry

    lax.fori_loop(0, 4, up, 0)
    for c in copies[2]:
        c.wait()

    def down(c, total):
        cols = pl.ds(pl.multiple_of(c * 1024, 1024), 1024)
        return total + dot(gs[:, cols], wu[pl.ds(c * 8, 8)].reshape(1024, 1024))

    r2 = lax.fori_loop(0, 4, down, n1)
    z1, r1 = norm_parts(r2)
    y_ref[...] = z1 * gain1 + bias1
    e = e_ref[...].astype(F32)
    dr2 = norm_back(e, gain1, z1, r1)
    dm = dr2.astype(BF)
    gb_ref[1:2, :] = jnp.sum(e * z1, axis=0, keepdims=True)
    gb_ref[3:4, :] = jnp.sum(e, axis=0, keepdims=True)

    def back(c, total):
        rows = pl.ds(pl.multiple_of(c * 1024, 1024), 1024)
        u = us[c]
        dg = dot(dm, wu[pl.ds(c * 8, 8)].reshape(1024, 1024), NT)
        slope = 0.5 * (1.0 + lax.erf(u * half)) + u * (jnp.exp(-0.5 * u * u) * (1.0 / math.sqrt(2 * math.pi)))
        du = (dg * slope).astype(BF)
        cpay[:, rows] = du
        return total + dot(du, wi[c], NT)

    dn1 = lax.fori_loop(0, 4, back, dr2)
    gb_ref[0:1, :] = jnp.sum(dn1 * z0, axis=0, keepdims=True)
    gb_ref[2:3, :] = jnp.sum(dn1, axis=0, keepdims=True)
    gb_ref[4:8, :] = jnp.zeros((4, 1024), F32)
    dr1 = norm_back(dn1, gain0, z0, r0)
    dr_ref[...] = dr1
    da = dr1.astype(BF)
    do = dot(da, wo[...], NT).astype(BF)
    for h in range(16):
        lanes = slice(64 * h, 64 * h + 64)
        do_ref[h] = jnp.concatenate([do[:64, lanes], do[64:, lanes]], axis=1)
    cpay[:, 4096:5120] = da
    zpay[:, 1024:2048] = dm
    for r, (ref, at, gref, gat) in enumerate((
        (lown, 0, gpay, 0), (cpay, 5120, gpay, 1024), (lown, 512, zpay, 0), (cpay, 5632, zpay, 2048)
    )):
        few = pl.ds(pl.multiple_of(where[r] * 256, 256), 256)
        many = pl.ds(pl.multiple_of(where[r] * 1024, 1024), 1024)
        ref[:, at:at + 256] = nl[:, few]
        ref[:, at + 256:at + 512] = ob[:, few]
        gref[:, gat:gat + 1024] = gs[:, many]


def middle(o, tok, cot, lnf, lnp, shards, pieces):
    return pl.pallas_call(
        middle_kernel,
        out_shape=[
            shp((128, 1024), F32), shp((128, 1024), F32), shp((16, 64, 128), BF),
            shp((128, 3072), BF), shp((128, 2048), BF), shp((128, 6144), BF), shp((128, 1024), BF), shp((8, 1024), F32),
        ],
        in_specs=[VM] * 5 + [ANY] * 22,
        out_specs=[VM] * 8,
        scratch_shapes=[
            pltpu.VMEM((1024, 1024), BF),
            pltpu.VMEM((4, 1024, 1024), BF),
            pltpu.VMEM((32, 4, 32, 1024), BF),
            pltpu.VMEM((4, 128, 1024), F32),
            pltpu.VMEM((128, 4096), BF),
            pltpu.VMEM((128, 1024), BF),
            pltpu.VMEM((128, 1024), BF),
            DMA((2, 6)), DMA((2, 8, 3)),
        ],
        compiler_params=pltpu.CompilerParams(vmem_limit_bytes=LIMIT),
        cost_estimate=pl.CostEstimate(flops=10 << 30, bytes_accessed=32 << 20, transcendentals=2 << 20),
        name="middle",
    )(o, tok, cot, lnf, lnp, *shards[0], *shards[1], *pieces[0], *pieces[1])


def turn_kernel(do, cpay, lown, dor, own_a, plus_a, minus_a, own_b, plus_b, minus_b, rr, ll, lt, mid, sn, rn, ss, rs, ls, lo):
    zl, x, y, zh, co = place()
    flat = lax.axis_index("ctx") % 16
    core = device(zl, x, y, zh, 1 - co)
    bar = pltpu.get_barrier_semaphore()

    def greet_one(i, carry):
        pl.semaphore_signal(bar, inc=1, device_id={"ctx": zl * 16 + (flat + i) % 16}, device_id_type=MESH)
        return carry

    pl.semaphore_signal(bar, inc=1, device_id=core, device_id_type=MESH)
    lax.fori_loop(1, 16, greet_one, 0)
    local = [
        pltpu.make_async_copy(cpay.at[:, :5120], rr.at[0:128, :], ls.at[0]),
        pltpu.make_async_copy(lown, ll.at[0:128, :], ls.at[1]),
    ]
    for c in local:
        c.start()
    pl.semaphore_wait(bar, 16)

    def narrow_copy(i):
        p = (flat + i) % 16
        return pltpu.make_async_remote_copy(
            src_ref=do.at[p], dst_ref=dor.at[flat], send_sem=sn.at[i], recv_sem=rn.at[i],
            device_id={"ctx": zl * 16 + p}, device_id_type=MESH,
        )

    def start_one(i, carry):
        narrow_copy(i).start()
        return carry

    def wait_one(i, carry):
        narrow_copy(i).wait()
        return carry

    wire = Wire(ss, rs)
    near = [wire(cpay.at[:, 5120:], ll.at[128:256, :], core), wire(cpay.at[:, :5120], rr.at[128:256, :], core)]
    lax.fori_loop(1, 16, start_one, 0)
    home = pltpu.make_async_copy(do.at[flat], dor.at[flat], ls.at[2])
    home.start()
    for c in local:
        c.wait()
    for c in near:
        c.wait()
    for k in range(4):
        lt[256 * k:256 * k + 256, :] = ll[:, 256 * k:256 * k + 256].astype(F32).T.astype(BF)
    for z in range(2):
        mid[z, 0:256, :] = dot(lt[512 * z + 256:512 * z + 512, :], rr[:, 4096:5120]).astype(BF)
        for k in range(4):
            rows = slice(256 + 256 * k, 512 + 256 * k)
            mid[z, rows, :] = dot(lt[512 * z:512 * z + 256, :], rr[:, 1024 * k:1024 * k + 1024]).astype(BF)
    out = []
    for h, (at, own, plus, minus) in enumerate(((x, own_a, plus_a, minus_a), (y, own_b, plus_b, minus_b))):

        def rows(s, first, size):
            return pl.ds(pl.multiple_of(h * 640 + (at + s) % 4 * 160 + first, 16), size)

        for src, dst in (
            (rows(0, 0, 160), own),
            (rows(1, 0, 160), plus.at[:, :160]), (rows(2, 0, 80), plus.at[:, 160:]),
            (rows(3, 0, 160), minus.at[:, :160]), (rows(2, 80, 80), minus.at[:, 160:]),
        ):
            out.append(pltpu.make_async_copy(mid.at[:, src], dst, lo.at[len(out)]))
    for c in out:
        c.start()
    home.wait()
    lax.fori_loop(1, 16, wait_one, 0)
    for c in out:
        c.wait()


def turn(do, cpay, lown):
    return pl.pallas_call(
        turn_kernel,
        out_shape=[shp(do.shape, BF)] + [shp((2, 160, 1024), BF), shp((2, 240, 1024), BF), shp((2, 240, 1024), BF)] * 2,
        in_specs=[ANY] * 3,
        out_specs=[ANY] * 7,
        scratch_shapes=[
            pltpu.VMEM((256, 5120), BF), pltpu.VMEM((256, 1024), BF), pltpu.VMEM((1024, 256), BF),
            pltpu.VMEM((2, 1280, 1024), BF),
            DMA((16,)), DMA((16,)), DMA((2,)), DMA((2,)), DMA((3,)), DMA((10,)),
        ],
        compiler_params=pltpu.CompilerParams(collective_id=5, has_side_effects=True, vmem_limit_bytes=LIMIT),
        cost_estimate=pl.CostEstimate(flops=16 << 30, bytes_accessed=32 << 20, transcendentals=0),
        name="turn",
    )(do, cpay, lown)


class Spread:
    def __init__(self, wire, plus, minus, at, piece, bufs):
        self.wire, self.plus, self.minus, self.at, self.piece = wire, plus, minus, at, piece
        self.rp, self.rm, self.m, self.f = bufs

    def part(self, s, u):
        return self.piece((self.at + s) % 4, u)

    def start(self):
        self.a = self.wire(self.part(2, 0), self.m.at[0], self.plus)
        self.b = self.wire(self.part(2, 1), self.m.at[1], self.minus)
        self.c = self.wire(self.part(1, 1), self.rp.at[1], self.plus)
        self.d = self.wire(self.part(3, 0), self.rm.at[0], self.minus)

    def relay(self):
        self.a.wait_recv()
        self.f[0] = (self.part(1, 0)[...].astype(F32) + self.m[0].astype(F32)).astype(BF)
        self.e = self.wire(self.f.at[0], self.rp.at[0], self.plus)
        self.b.wait_recv()
        self.f[1] = (self.part(3, 1)[...].astype(F32) + self.m[1].astype(F32)).astype(BF)
        self.g = self.wire(self.f.at[1], self.rm.at[1], self.minus)

    def total(self):
        for c in (self.c, self.d, self.e, self.g):
            c.wait_recv()
        return [
            self.part(0, u)[...].astype(F32) + self.rp[u].astype(F32) + self.rm[u].astype(F32) for u in range(2)
        ]

    def sent(self):
        for c in (self.a, self.b, self.c, self.d, self.e, self.g):
            c.wait_send()


class Gather:
    def __init__(self, wire, plus, minus, at, block):
        self.wire, self.plus, self.minus, self.at, self.block = wire, plus, minus, at, block

    def send(self, s, u, peer):
        spot = self.block((self.at + s) % 4, u)
        return self.wire(spot, spot, peer)

    def start(self):
        self.p0 = self.send(0, 0, self.plus)
        self.m1 = self.send(0, 1, self.minus)
        self.p1 = self.send(0, 1, self.plus)
        self.m0 = self.send(0, 0, self.minus)

    def relay(self):
        self.p0.wait_recv()
        self.rp = self.send(3, 0, self.plus)
        self.m1.wait_recv()
        self.rm = self.send(1, 1, self.minus)

    def done(self):
        for c in (self.p1, self.m0, self.rp, self.rm):
            c.wait()
        for c in (self.p0, self.m1):
            c.wait_send()


class DirectSpread:
    def __init__(self, wire, peers, at, piece, bufs):
        self.wire, self.peers, self.at, self.piece, self.bufs = wire, peers, at, piece, bufs

    def start(self):
        self.copies = []
        for s in range(3):
            for u in range(2):
                src = self.piece((self.at + s + 1) % 4, u)
                self.copies.append(self.wire(src, self.bufs[s].at[u], self.peers[s]))

    def relay(self):
        pass

    def total(self):
        for c in self.copies:
            c.wait_recv()
        out = []
        for u in range(2):
            total = self.piece(self.at, u)[...].astype(F32)
            for s in range(3):
                total += self.bufs[s][u].astype(F32)
            out.append(total)
        return out

    def sent(self):
        for c in self.copies:
            c.wait_send()


class DirectGather:
    def __init__(self, wire, peers, at, block):
        self.wire, self.peers, self.at, self.block = wire, peers, at, block

    def start(self):
        self.copies = []
        for u in range(2):
            spot = self.block(self.at, u)
            for p in self.peers:
                self.copies.append(self.wire(spot, spot, p))

    def relay(self):
        pass

    def done(self):
        for c in self.copies:
            c.wait()


class Sum:
    direct = False

    def cut(self, g, rows):
        return g.at[rows]

    def __init__(self, g, hc, refs, wire, where, xp, yp, zp):
        bufs1, s1, bufs2, s2, self.r3, full = refs[:4], refs[4], refs[5:9], refs[9], refs[10], refs[11]
        zl, x, y, zh, co = where
        self.wire, self.zp, self.zl = wire, zp, zl
        self.s1, self.s2, self.last, self.full = s1, s2, s2, full
        hh = hc // 2
        first, second = (xp, yp), (yp, xp)
        self.at1, self.at2 = (x, y), (y, x)
        self.peers = [(first[h][0], first[h][2]) for h in range(2)]

        def rows(h, k, u):
            return pl.ds(pl.multiple_of(h * 4 * hc + k * hc + u * hh, 16), hh)

        def cols(k, width):
            return pl.ds(pl.multiple_of(k * width, 128), width)

        self.rows, self.cols = rows, cols

        def one(h):
            return lambda k, u: self.cut(g, rows(h, k, u))

        def two(h):
            return lambda k, u: s1.at[h, u, :, cols(k, 256)]

        def five(h):
            return lambda k, u: full.at[rows(h, self.at1[h], u), cols(k, 256)]

        def six(h):
            return lambda k, u: full.at[rows(h, k, u)]

        def ends(peers):
            return wire, peers[0], peers[2]

        if g is not None:
            self.one = [Spread(*ends(first[h]), self.at1[h], one(h), [r.at[h] for r in bufs1]) for h in range(2)]
        if self.direct:
            self.two = [DirectSpread(wire, second[h], self.at2[h], two(h), [r.at[h] for r in bufs2]) for h in range(2)]
            self.five = [DirectGather(wire, second[h], self.at2[h], five(h)) for h in range(2)]
        else:
            self.two = [Spread(*ends(second[h]), self.at2[h], two(h), [r.at[h] for r in bufs2]) for h in range(2)]
            self.five = [Gather(*ends(second[h]), self.at2[h], five(h)) for h in range(2)]
        self.six = [Gather(*ends(first[h]), self.at1[h], six(h)) for h in range(2)]

    def begin(self):
        for t in self.one:
            t.start()

    def relay(self):
        for t in self.one:
            t.relay()

    def totals(self, h):
        return self.one[h].total()

    def across(self):
        pass

    def settle(self):
        for t in self.one:
            t.sent()

    def steps(self):
        self.begin()
        yield
        self.relay()
        yield
        for h in range(2):
            for u, total in enumerate(self.totals(h)):
                self.s1[h, u] = total.astype(BF)
            self.two[h].start()
        yield
        for t in self.two:
            t.relay()
        yield
        for h in range(2):
            for u, total in enumerate(self.two[h].total()):
                self.s2[h, u] = total.astype(BF)
        self.across()
        yield
        three = []
        for h in range(2):
            self.ready(h)
            three.append(self.wire(self.last.at[h, :, :, self.cols(1 - self.zl, 128)], self.r3.at[h], self.zp))
        yield
        four = []
        for h in range(2):
            three[h].wait_recv()
            for u in range(2):
                total = self.last[h, u, :, self.cols(self.zl, 128)].astype(F32) + self.r3[h, u].astype(F32)
                spot = self.full.at[self.rows(h, self.at1[h], u), self.cols(self.at2[h] * 2 + self.zl, 128)]
                spot[...] = total.astype(BF)
                four.append(self.wire(spot, spot, self.zp))
        yield
        for h in range(2):
            four[2 * h].wait()
            four[2 * h + 1].wait()
            self.five[h].start()
        yield
        for t in self.five:
            t.relay()
        yield
        for h in range(2):
            self.five[h].done()
            self.six[h].start()
        yield
        for t in self.six:
            t.relay()
        yield
        for t in self.two:
            t.sent()
        for c in three:
            c.wait_send()
        self.settle()
        for t in self.six:
            t.done()
        yield

    def ready(self, h):
        pass


class PairSum(Sum):
    direct = True

    def cut(self, g, rows):
        return g.at[:, rows]

    def __init__(self, g, hc, refs, wire, where, xp, yp, zp, far):
        self.rf, self.s3 = refs[:2]
        super().__init__(g, hc, refs[2:], wire, where, xp, yp, zp)
        self.far, self.hh, self.last = far, hc // 2, self.s3

    def totals(self, h):
        return [t.reshape(2 * self.hh, 1024) for t in self.one[h].total()]

    def across(self):
        self.crossed = [self.wire(self.s2.at[h, :, self.hh:], self.rf.at[h], self.far) for h in range(2)]

    def ready(self, h):
        self.crossed[h].wait_recv()
        for u in range(2):
            self.s3[h, u] = (self.s2[h, u, :self.hh].astype(F32) + self.rf[h, u].astype(F32)).astype(BF)

    def settle(self):
        for t in self.one:
            t.sent()
        for c in self.crossed:
            c.wait_send()


class BegunSum(PairSum):
    direct = False

    def __init__(self, hc, refs, wire, where, xp, yp, zp, far, own, plus, minus):
        self.own, self.fwd = refs[:2]
        super().__init__(None, hc, list(refs[2:4]) + [None] * 4 + list(refs[4:]), wire, where, xp, yp, zp, far)
        self.plus, self.minus = plus, minus

    def begin(self):
        hc = 2 * self.hh
        self.passed = []
        for h in range(2):
            plus, minus = self.peers[h]
            self.passed.append((
                self.wire(self.plus[h].at[:, hc:], self.fwd.at[h, 0], plus),
                self.wire(self.minus[h].at[:, hc:], self.fwd.at[h, 1], minus),
            ))

    def relay(self):
        pass

    def totals(self, h):
        hh = self.hh
        for c in self.passed[h]:
            c.wait_recv()
        out = []
        for u in range(2):
            rows = slice(u * hh, u * hh + hh)
            total = self.own[h, 0, :, rows].astype(F32) + self.own[h, 1, :, rows].astype(F32)
            total += self.own[h, 2, :, rows].astype(F32) + self.fwd[h, u].astype(F32)
            out.append(total.reshape(2 * hh, 1024))
        return out

    def settle(self):
        for c in self.crossed:
            c.wait_send()
        for pair in self.passed:
            for c in pair:
                c.wait_send()


class FirstSum:
    def __init__(self, g, refs, wire, where, xp, yp, zp):
        bufs1, s1, bufs2, rz, half, full = refs[:4], refs[4], refs[5:9], refs[9], refs[10], refs[11]
        zl, x, y, zh, co = where
        self.g, self.wire, self.zp, self.zl = g, wire, zp, zl
        self.s1, self.rz, self.half, self.full = s1, rz, half, full
        first, second = (xp, yp), (yp, xp)
        self.at1, self.at2 = (x, y), (y, x)

        def cols(k):
            return pl.ds(pl.multiple_of(k * 256, 128), 256)

        def one(h):
            return lambda k, u: half.at[pl.ds(pl.multiple_of(h * 256 + k * 64 + u * 32, 32), 32)]

        def two(h):
            return lambda k, u: s1.at[h, u, :, cols(k)]

        def rows(h, k, z):
            return pl.ds(pl.multiple_of(z * 512 + h * 256 + k * 64, 64), 64)

        def five(h):
            return lambda k, z: full.at[rows(h, self.at1[h], z), cols(k)]

        def six(h):
            return lambda k, z: full.at[rows(h, k, z)]

        self.spot = lambda h: full.at[rows(h, self.at1[h], zl), cols(self.at2[h])]
        self.one = [Spread(wire, first[h][0], first[h][2], self.at1[h], one(h), [r.at[h] for r in bufs1]) for h in range(2)]
        self.two = [DirectSpread(wire, second[h], self.at2[h], two(h), [r.at[h] for r in bufs2]) for h in range(2)]
        self.five = [Gather(wire, second[h][0], second[h][2], self.at2[h], five(h)) for h in range(2)]
        self.six = [Gather(wire, first[h][0], first[h][2], self.at1[h], six(h)) for h in range(2)]

    def steps(self):
        zs = []
        for h in range(2):
            src = self.g.at[pl.ds(pl.multiple_of((1 - self.zl) * 512 + h * 256, 256), 256)]
            zs.append(self.wire(src, self.rz.at[h], self.zp))
        yield
        for h in range(2):
            zs[h].wait_recv()
            mine = self.g[pl.ds(pl.multiple_of(self.zl * 512 + h * 256, 256), 256), :]
            self.half[256 * h:256 * h + 256, :] = (mine.astype(F32) + self.rz[h].astype(F32)).astype(BF)
            self.one[h].start()
        yield
        for t in self.one:
            t.relay()
        yield
        for h in range(2):
            for u, total in enumerate(self.one[h].total()):
                self.s1[h, u] = total.astype(BF)
            self.two[h].start()
        yield
        four = []
        for h in range(2):
            spot = self.spot(h)
            spot[...] = jnp.concatenate(self.two[h].total(), axis=0).astype(BF)
            four.append(self.wire(spot, spot, self.zp))
        yield
        for h in range(2):
            four[h].wait()
            self.five[h].start()
        yield
        for t in self.five:
            t.relay()
        yield
        for h in range(2):
            self.five[h].done()
            self.six[h].start()
        yield
        for t in self.six:
            t.relay()
        yield
        for t in self.one + self.two:
            t.sent()
        for c in zs:
            c.wait_send()
        for t in self.six:
            t.done()
        yield


SUM_COPIES = 2 + 12 + 12 + 2 + 12 + 12


BEGUN_COPIES = 4 + 12 + 2 + 2 + 4 + 12 + 12
PAIR_COPIES = 12 + 12 + 2 + 2 + 4 + 12 + 12


def first_scratch():
    return (
        [pltpu.VMEM((2, 2, 32, 1024), BF)] * 5
        + [pltpu.VMEM((2, 2, 32, 256), BF)] * 4
        + [pltpu.VMEM((2, 256, 1024), BF), pltpu.VMEM((512, 1024), BF)]
    )


def pair_scratch(rows, begun):
    hh = rows // 16
    begin = [pltpu.VMEM((2, 3, 2, 2 * hh, 1024), BF), pltpu.VMEM((2, 2, 2, hh, 1024), BF)]
    first = [pltpu.VMEM((2, 2, 2, hh, 1024), BF)] * 4
    return (
        (begin if begun else [])
        + [pltpu.VMEM((2, 2, hh, 256), BF)] * 2
        + ([] if begun else first)
        + [pltpu.VMEM((2, 2, 2 * hh, 1024), BF)]
        + [pltpu.VMEM((2, 2, 2 * hh, 256), BF)] * 4
        + [pltpu.VMEM((2, 2, 2 * hh, 256), BF), pltpu.VMEM((2, 2, hh, 128), BF)]
    )


def finish_kernel(*refs):
    dkvp, dqp, dr_ref, gb, wall, gpay, zpay, zr, xs, x_ref = refs[:10]
    got = ((refs[10], refs[13]), (refs[11], refs[14]), (refs[12], refs[15]))

    gt, io_full, u_full, tail_full, s_vec = refs[16:21]
    io_refs = list(refs[21:32]) + [io_full]
    u_refs, tail_refs = list(refs[32:43]) + [u_full], list(refs[43:56]) + [tail_full]
    (dkv, zb, sb, dq, weights, ll2, rr2, lt2, mid, pay, ll, rr, tail, v0, vf, v1, vx, vy, vz, tx, ty,
     sz, rz, sw, rw, sn, rn, ss, rs, ls, lw) = refs[56:]
    scale = 1.0 / math.sqrt(16384)
    where = place()
    zl, x, y, zh, co = where
    w = zh * 2 + co
    me = lax.axis_index("ctx")
    flat = me % 16
    core = device(zl, x, y, zh, 1 - co)
    far = device(zl, x, y, 1 - zh, co)
    xp = [device(zl, (x + s) % 4, y, zh, co) for s in (1, 2, 3)]
    yp = [device(zl, x, (y + s) % 4, zh, co) for s in (1, 2, 3)]
    zp = device(1 - zl, x, y, zh, co)
    bar = pltpu.get_barrier_semaphore()

    def greet_one(i, carry):
        pl.semaphore_signal(bar, inc=1, device_id={"ctx": zl * 16 + (flat + i) % 16}, device_id_type=MESH)
        return carry

    for p in (core, far, zp):
        pl.semaphore_signal(bar, inc=1, device_id=p, device_id_type=MESH)
    lax.fori_loop(1, 16, greet_one, 0)

    mine = [pl.ds(pl.multiple_of(k * 256, 256), 256) for k in (w, (1 - zh) * 2 + co)]
    parts = []
    for h in range(2):
        for n in range(3):
            parts.append(pltpu.make_async_copy(got[n][h].at[:, :160], io_refs[0].at[h, n], ls.at[10 + 3 * h + n]))
    local = [
        pltpu.make_async_copy(gpay.at[:, :1024], ll2.at[0:128, :], ls.at[0]),
        pltpu.make_async_copy(zpay.at[:, 1024:2048], rr2.at[0:128, :], ls.at[1]),
        pltpu.make_async_copy(zr.at[:, :1024], ll2.at[256:384, :], ls.at[2]),
        pltpu.make_async_copy(zr.at[:, 1024:2048], rr2.at[256:384, :], ls.at[3]),
    ]
    for k in range(2):
        cols = slice(256 * k, 256 * k + 256)
        local.append(pltpu.make_async_copy(x_ref.at[:, mine[k]], ll.at[0:128, cols], ls.at[4 + k]))
        local.append(pltpu.make_async_copy(xs.at[k], ll.at[128:256, cols], ls.at[6 + k]))
    for c in local + parts:
        c.start()
    loads = [pltpu.make_async_copy(wall, weights, lw.at[0])]
    loads[0].start()
    pl.semaphore_wait(bar, 18)

    def narrow_copy(i):
        p = (flat + i) % 16
        return pltpu.make_async_remote_copy(
            src_ref=dqp.at[p], dst_ref=dq.at[flat], send_sem=sn.at[i], recv_sem=rn.at[i],
            device_id={"ctx": zl * 16 + p}, device_id_type=MESH,
        )

    def z_copy(i):
        return pltpu.make_async_remote_copy(
            src_ref=dkvp.at[(1 - zl) * 16 + (flat + i) % 16], dst_ref=zb.at[i], send_sem=sz.at[i], recv_sem=rz.at[i],
            device_id=zp, device_id_type=MESH,
        )

    def wide_copy(i):
        p = (flat + i) % 16
        return pltpu.make_async_remote_copy(
            src_ref=sb.at[i], dst_ref=dkv.at[flat], send_sem=sw.at[i], recv_sem=rw.at[i],
            device_id={"ctx": zl * 16 + p}, device_id_type=MESH,
        )

    def start(make):
        def one(i, carry):
            make(i).start()
            return carry
        return one

    def wait(make):
        def one(i, carry):
            make(i).wait()
            return carry
        return one

    def both(i):
        z_copy(i).wait_recv()
        return (dkvp[zl * 16 + (flat + i) % 16].astype(F32) + zb[i].astype(F32)).astype(BF)

    def pass_on(i, carry):
        sb[i] = both(i)
        wide_copy(i).start()
        return carry

    def sent(i, carry):
        z_copy(i).wait_send()
        return carry

    lax.fori_loop(1, 16, start(z_copy), 0)
    z_copy(0).start()
    lax.fori_loop(1, 16, start(narrow_copy), 0)
    home = [pltpu.make_async_copy(dqp.at[flat], dq.at[flat], ls.at[9])]
    for c in home:
        c.start()
    wire = Wire(ss, rs)
    near = [
        wire(gpay.at[:, 1024:], ll2.at[128:256, :], core),
        wire(zpay.at[:, 1024:2048], rr2.at[128:256, :], core),
        wire(zr.at[:, 2048:], ll2.at[384:512, :], core),
        wire(zr.at[:, 1024:2048], rr2.at[384:512, :], core),
    ]
    io = BegunSum(160, io_refs, wire, where, xp, yp, zp, far, *got).steps()
    big = FirstSum(mid, u_refs, wire, where, xp, yp, zp).steps()
    small = PairSum(tail, 96, tail_refs, wire, where, xp, yp, zp, far).steps()
    next(io)
    next(io)
    for c in local:
        c.wait()
    lt = ll[...].astype(F32).T.astype(BF)
    for c in near:
        c.wait()
    for k in range(4):
        lt2[256 * k:256 * k + 256, :] = ll2[:, 256 * k:256 * k + 256].astype(F32).T.astype(BF)
    for k in range(4):
        rows = slice(256 * k, 256 * k + 256)
        mid[rows, :] = dot(lt2[rows, :], rr2[...]).astype(BF)
    next(big)
    lax.fori_loop(1, 16, pass_on, 0)
    dkv[flat] = both(0)
    for c in parts:
        c.wait()
    next(io)

    for c in home:
        c.wait()
    lax.fori_loop(1, 16, wait(wide_copy), 0)
    lax.fori_loop(1, 16, wait(narrow_copy), 0)
    lax.fori_loop(0, 16, sent, 0)
    for h in range(16):
        lanes = slice(64 * h, 64 * h + 64)
        pair = dq[h]
        pay[:64, lanes] = pair[:, :64]
        pay[64:128, lanes] = pair[:, 64:]
        pair = dkv[h]
        pay[:128, 1024 + 64 * h:1088 + 64 * h] = pair[:, :64]
        pay[:128, 2048 + 64 * h:2112 + 64 * h] = pair[:, 64:]
    pay[128:144, :1024] = jnp.concatenate([gb[...], jnp.zeros((8, 1024), F32)], axis=0).astype(BF)
    pay[128:144, 1024:] = jnp.zeros((16, 2048), BF)
    to_core = wire(pay, rr, core)
    next(io)
    for c in loads:
        c.wait()
    for k in range(4):
        cols = slice(256 * k, 256 * k + 256)
        total = dr_ref[:, cols]
        for m in range(3):
            total += dot(pay[:128, 1024 * m:1024 * m + 1024], weights[k, m], NT)
        gt[:, cols] = total
    next(io)
    to_core.wait_recv()
    for z in range(2):
        for m in range(3):
            cols = slice(1024 * m, 1024 * m + 1024)
            total = dot(lt[256 * z:256 * z + 256, :128], pay[:128, cols])
            total += dot(lt[256 * z:256 * z + 256, 128:], rr[:128, cols])
            tail[z, 256 * m:256 * m + 256, :] = total.astype(BF)
    next(small)
    for z in range(2):
        v0[z] = (pay[128:144, mine[z]].astype(F32) + rr[128:144, mine[z]].astype(F32))[:8]
    vfar = wire(v0.at[1], vf, far)
    next(big)
    next(io)
    next(small)
    next(big)
    next(io)
    vfar.wait_recv()
    v1[...] = v0[0] + vf[...]
    vone = [wire(v1, vx.at[s], xp[s]) for s in range(3)]
    next(small)
    next(io)
    next(big)
    next(small)
    next(io)
    for c in vone:
        c.wait_recv()
    tx[...] = v1[...] + vx[0] + vx[1] + vx[2]
    vtwo = [wire(tx, vy.at[s], yp[s]) for s in range(3)]
    next(small)
    next(big)
    next(io)
    next(small)
    next(big)
    for c in vtwo:
        c.wait_recv()
    ty[...] = tx[...] + vy[0] + vy[1] + vy[2]
    vthree = wire(ty, vz, zp)
    next(small)
    next(big)
    next(small)
    next(big)
    next(io)
    next(small)
    next(small)
    next(big)
    vthree.wait()
    s_vec[...] = (ty[...] + vz[...]) * scale
    for c in vone + vtwo + [to_core, vfar]:
        c.wait_send()
    next(small)
    next(io)
    next(big)
    next(small)


def finish(dkvp, dqp, dr, gb, wall, gpay, zpay, zr, xs, tok, parts):
    n = SUM_COPIES + BEGUN_COPIES + PAIR_COPIES + 4 + 2 + 7
    return pl.pallas_call(
        finish_kernel,
        out_shape=[
            shp((128, 1024), F32), shp((1280, 1024), BF), shp((1024, 1024), BF), shp((768, 1024), BF), shp((8, 256), F32),
        ],
        in_specs=[VM, ANY, VM, VM] + [ANY] * 12,
        out_specs=[VM] * 5,
        scratch_shapes=pair_scratch(1280, True) + first_scratch() + pair_scratch(768, False) + [
            pltpu.VMEM((16, 128, 128), BF), pltpu.VMEM((16, 128, 128), BF), pltpu.VMEM((16, 128, 128), BF),
            pltpu.VMEM((16, 64, 128), BF), pltpu.VMEM((4, 3, 256, 1024), BF),
            pltpu.VMEM((512, 1024), BF), pltpu.VMEM((512, 1024), BF), pltpu.VMEM((1024, 512), BF),
            pltpu.VMEM((1024, 1024), BF), pltpu.VMEM((144, 3072), BF),
            pltpu.VMEM((256, 512), BF), pltpu.VMEM((144, 3072), BF), pltpu.VMEM((2, 768, 1024), BF),
            pltpu.VMEM((2, 8, 256), F32), pltpu.VMEM((8, 256), F32), pltpu.VMEM((8, 256), F32),
            pltpu.VMEM((3, 8, 256), F32), pltpu.VMEM((3, 8, 256), F32),
            pltpu.VMEM((8, 256), F32), pltpu.VMEM((8, 256), F32), pltpu.VMEM((8, 256), F32),
            DMA((16,)), DMA((16,)), DMA((16,)), DMA((16,)), DMA((16,)), DMA((16,)),
            DMA((n,)), DMA((n,)), DMA((16,)), DMA((1,)),
        ],
        compiler_params=pltpu.CompilerParams(collective_id=6, has_side_effects=True, vmem_limit_bytes=LIMIT),
        name="finish",
    )(dkvp, dqp, dr, gb, wall, gpay, zpay, zr, xs, tok, *parts)


def scale_kernel(o, i0, i1, i2, i3, u, q, k, v, out_q, out_k, out_v, out_o, out_i, out_u):
    scale = 1.0 / math.sqrt(16384)
    for src, dst in ((q, out_q), (k, out_k), (v, out_v), (o, out_o), (u, out_u)):
        dst[...] = src[...].astype(F32) * scale
    for n, src in enumerate((i0, i1, i2, i3)):
        out_i[:, 1024 * n:1024 * n + 1024] = src[...].astype(F32) * scale


def scaled(io, u, tail):
    def rows(first, n=32):
        return pl.BlockSpec((n, 1024), lambda j: (first // n + j, 0))

    return pl.pallas_call(
        scale_kernel,
        grid=(8,),
        out_shape=[shp((256, 1024), F32)] * 4 + [shp((256, 4096), F32), shp((1024, 1024), F32)],
        in_specs=[rows(0)] + [rows(256 + 256 * k) for k in range(4)] + [rows(0, 128)] + [rows(256 * k) for k in range(3)],
        out_specs=[rows(0)] * 4 + [pl.BlockSpec((32, 4096), lambda j: (j, 0)), rows(0, 128)],
        compiler_params=pltpu.CompilerParams(vmem_limit_bytes=LIMIT),
        name="scaled",
    )(*[io] * 5, u, *[tail] * 3)


FLIP_CORE = [(0, 1), (1, 0), (2, 3), (3, 2)]
FLIP_FAR = [(0, 2), (2, 0), (1, 3), (3, 1)]


def along_x(s):
    return [(c, c // 16 * 16 + (c // 4 + s) % 4 * 4 + c % 4) for c in range(32)]


def along_y(s):
    return [(c, c // 4 * 4 + (c + s) % 4) for c in range(32)]


def body(
    tokens, w_query, w_key, w_value, w_output, w_inner, w_outer, ln_gain, ln_bias, block_mask, block_pairs, cotangent,
):
    tok = tokens.reshape(128, 1024)
    cot = cotangent.reshape(128, 1024)
    lnp = jnp.concatenate([ln_gain, ln_bias, jnp.zeros((4, 256), F32)], axis=0)
    blk = block_pairs.reshape(-1)
    own = (w_query, w_key, w_value)
    outer = w_outer.reshape(8, 4, 32, 1024)
    wall, xs, lnf, *rest = front(tok, own, lnp, w_output, w_inner, outer)
    core_shard, (qa, qb, x2, y2, diag_a, diag_b, kvr, qr) = rest[:3], rest[3:]
    x1, x3 = (lax.ppermute(qa, "ctx", along_x(s)) for s in (1, 3))
    y1, y3 = (lax.ppermute(qb, "ctx", along_y(s)) for s in (1, 3))
    o, ot, lse = attend(blk, block_mask, kvr, qr)
    x1, x2, x3, y1, y2, y3, o = lax.optimization_barrier((x1, x2, x3, y1, y2, y3, o))
    far = [qa, x1, x2, x3, qb, y1, y2, y3]
    d1, d2, d3, e1, e2, e3 = (lax.ppermute(p, "wsh", FLIP_CORE) for p in (x1, x2, x3, y1, y2, y3))
    diag = [diag_a, d1, d2, d3, diag_b, e1, e2, e3]
    (o_back,) = exchange(None, o, 3)
    y_out, dr1, do, zpay, gpay, cpay, lown, gb = middle(
        o_back, tok, cot, lnf, lnp, ((w_output, w_inner, outer), core_shard), (far, diag)
    )
    zr = lax.ppermute(zpay, "wsh", FLIP_FAR)
    dor, own_a, plus_a, minus_a, own_b, plus_b, minus_b = turn(do, cpay, lown)
    plus_a = lax.ppermute(plus_a, "ctx", along_x(1))
    minus_a = lax.ppermute(minus_a, "ctx", along_x(3))
    plus_b = lax.ppermute(plus_b, "ctx", along_y(1))
    minus_b = lax.ppermute(minus_b, "ctx", along_y(3))
    dkvp, dqp = attend_back(blk, block_mask, kvr, qr, dor, ot, lse)
    zr, plus_a, minus_a, plus_b, minus_b, dkvp = lax.optimization_barrier((zr, plus_a, minus_a, plus_b, minus_b, dkvp))
    grad_tok, io, u, tail, s_vec = finish(
        dkvp, dqp, dr1, gb, wall, gpay, zpay, zr, xs, tok, (own_a, plus_a, minus_a, own_b, plus_b, minus_b)
    )
    s_q, s_k, s_v, s_o, s_i, s_u = scaled(io, u, tail)
    out_shape = tokens.shape
    return (
        y_out.reshape(out_shape), grad_tok.reshape(out_shape), s_q, s_k, s_v, s_o, s_i, s_u, s_vec[0:2], s_vec[2:4],
    )


def solution(mesh):
    return jax.shard_map(
        body,
        mesh=mesh,
        in_specs=(
            P("wsh", "ctx", None, None),
            P("wsh", None), P("wsh", None), P("wsh", None), P("wsh", None), P("wsh", None), P("wsh", None),
            P(None, "wsh"), P(None, "wsh"),
            P("wsh", None, None),
            P(),
            P("wsh", "ctx", None, None),
        ),
        out_specs=(
            P("wsh", "ctx", None, None), P("wsh", "ctx", None, None),
            P("wsh", None), P("wsh", None), P("wsh", None), P("wsh", None), P("wsh", None), P("wsh", None),
            P(None, "wsh"), P(None, "wsh"),
        ),
        check_vma=False,
    )
```

```python
import math

import jax
import jax.numpy as jnp
from jax import lax
from jax.experimental import pallas as pl
from jax.experimental.pallas import tpu as pltpu
from jax.sharding import PartitionSpec as P

MESH = pl.DeviceIdType.MESH
BF = jnp.bfloat16
F32 = jnp.float32
ANY = pl.BlockSpec(memory_space=pl.ANY)
VM = pl.BlockSpec(memory_space=pltpu.VMEM)
SM = pl.BlockSpec(memory_space=pltpu.SMEM)
DMA = pltpu.SemaphoreType.DMA
LIMIT = 56 * 1024 * 1024
EPS = 1e-05
NEG = -1e30


def shp(shape, dtype):
    return jax.ShapeDtypeStruct(shape, dtype)


def dot(a, b, dims=((1,), (0,))):
    return lax.dot_general(a, b, (dims, ((), ())), preferred_element_type=F32)


NN = ((1,), (0,))
NT = ((1,), (1,))
TN = ((0,), (0,))


def place():
    c = lax.axis_index("ctx")
    w = lax.axis_index("wsh")
    return c // 16, (c // 4) % 4, c % 4, w // 2, w % 2


def device(zl, x, y, zh, co):
    return {"ctx": zl * 16 + x * 4 + y, "wsh": zh * 2 + co}


def greet(peers):
    bar = pltpu.get_barrier_semaphore()
    for p in peers:
        pl.semaphore_signal(bar, inc=1, device_id=p, device_id_type=MESH)
    pl.semaphore_wait(bar, len(peers))


class Wire:
    def __init__(self, send, recv):
        self.send, self.recv, self.n = send, recv, 0

    def __call__(self, src, dst, peer):
        k = self.n
        self.n += 1
        copy = pltpu.make_async_remote_copy(
            src_ref=src, dst_ref=dst, send_sem=self.send.at[k], recv_sem=self.recv.at[k],
            device_id=peer, device_id_type=MESH,
        )
        copy.start()
        return copy


def front_kernel(*refs):
    x_ref, wq, wk, wv, x_any, ln_ref, wo, wi, wu = refs[:9]
    wall, xs, lnf, co_ref, ci_ref, cu_ref, qa_ref, qb_ref, x2_ref, y2_ref, da_ref, db_ref, kvr, qr = refs[9:23]
    weights, acc, kvp, qp, ss, rs, sw, rw, sf, rf, sn, rn, ls = refs[23:]
    zl, x, y, zh, co = place()
    me = zh * 2 + co
    slots = [me, zh * 2 + 1 - co, (1 - zh) * 2 + co, (1 - zh) * 2 + 1 - co]
    here = lax.axis_index("ctx")
    flat = here % 16
    core = device(zl, x, y, zh, 1 - co)
    far = device(zl, x, y, 1 - zh, co)
    diag = device(zl, x, y, 1 - zh, 1 - co)
    zp = device(1 - zl, x, y, zh, co)
    xp = [device(zl, (x + s) % 4, y, zh, co) for s in (1, 2, 3)]
    yp = [device(zl, x, (y + s) % 4, zh, co) for s in (1, 2, 3)]
    bar = pltpu.get_barrier_semaphore()

    def greet_one(i, carry):
        pl.semaphore_signal(bar, inc=1, device_id={"ctx": zl * 16 + (flat + i) % 16}, device_id_type=MESH)
        return carry

    for p in (far, core, diag, zp):
        pl.semaphore_signal(bar, inc=1, device_id=p, device_id_type=MESH)
    lax.fori_loop(1, 16, greet_one, 0)
    ws = (wq, wk, wv)
    local = [pltpu.make_async_copy(ws[m], weights.at[me, m], ls.at[m]) for m in range(3)]
    for c in local:
        c.start()
    pl.semaphore_wait(bar, 19)
    wire = Wire(ss, rs)
    rows_a = pl.ds(pl.multiple_of(x * 32, 32), 32)
    rows_b = pl.ds(pl.multiple_of(128 + y * 32, 32), 32)
    first_a, first_b = [], []
    for m in range(3):
        first_a.append(wire(ws[m].at[rows_a], weights.at[me, m, rows_a], far))
        first_b.append(wire(ws[m].at[rows_b], weights.at[me, m, rows_b], far))
    near = [wire(ws[m], weights.at[me, m], core) for m in range(3)]
    quarters = []
    for ref, k, n in ((qa_ref, x, y), (qb_ref, 4 + y, x)):
        rows = pl.ds(pl.multiple_of(k * 32, 32), 32)
        cols = pl.ds(pl.multiple_of(n * 256, 256), 256)
        quarters.append(wire(wo.at[rows, cols], ref.at[0, :, cols], far))
        for b in range(4):
            at = pl.ds(pl.multiple_of(1024 * b + n * 256, 256), 256)
            quarters.append(wire(wi.at[rows, at], ref.at[1 + b, :, cols], far))
        quarters.append(wire(wu.at[k, :, :, cols], ref.at[5:9, :, cols], far))
    rest = []
    for p in (core, far, diag):
        rest.append(wire(ln_ref, lnf.at[me], p))
    for n, idx in enumerate((slots[1], slots[3])):
        rest.append(wire(x_any.at[:, pl.ds(pl.multiple_of(idx * 256, 256), 256)], xs.at[n], core))

    def add(k, fresh):
        cols = x_ref[:, pl.ds(pl.multiple_of(slots[k] * 256, 256), 256)]
        for m in range(3):
            part = dot(cols, weights[slots[k], m])
            acc[m] = part if fresh else acc[m] + part

    for c in first_a:
        c.wait_recv()
    second = []
    for m in range(3):
        part = weights.at[slots[2], m, rows_a]
        for p in xp:
            second.append(wire(part, part, p))
    for c in first_b:
        c.wait_recv()
    for m in range(3):
        part = weights.at[slots[2], m, rows_b]
        for p in yp:
            second.append(wire(part, part, p))
    for c in local:
        c.wait()
    add(0, True)
    for c in near:
        c.wait_recv()
    add(1, False)
    for c in second:
        c.wait_recv()
    last = [wire(weights.at[slots[2], m], weights.at[slots[2], m], core) for m in range(3)]
    add(2, False)
    for c in last:
        c.wait_recv()
    add(3, False)
    keep = pltpu.make_async_copy(weights, wall, ls.at[0])
    keep.start()
    for j in range(8):
        lanes = slice(128 * j, 128 * j + 128)
        q = (acc[0, :, lanes].astype(BF).astype(F32) * 0.125).astype(BF)
        k = acc[1, :, lanes].astype(BF)
        v = acc[2, :, lanes].astype(BF)
        for u in range(2):
            part = slice(64 * u, 64 * u + 64)
            kvp[2 * j + u] = jnp.concatenate([k[:, part], v[:, part]], axis=1)
            qp[2 * j + u] = jnp.concatenate([q[:64, part], q[64:, part]], axis=1)

    def plane(i):
        return {"ctx": zl * 16 + (flat + i) % 16}

    def wide_copy(i):
        return pltpu.make_async_remote_copy(
            src_ref=kvp.at[(flat + i) % 16], dst_ref=kvr.at[here], send_sem=sw.at[i], recv_sem=rw.at[i],
            device_id=plane(i), device_id_type=MESH,
        )

    def narrow_copy(i):
        return pltpu.make_async_remote_copy(
            src_ref=qp.at[(flat + i) % 16], dst_ref=qr.at[flat], send_sem=sn.at[i], recv_sem=rn.at[i],
            device_id=plane(i), device_id_type=MESH,
        )

    def pass_copy(i):
        spot = kvr.at[zl * 16 + (flat + 16 - i) % 16]
        return pltpu.make_async_remote_copy(
            src_ref=spot, dst_ref=spot, send_sem=sf.at[i], recv_sem=rf.at[i], device_id=zp, device_id_type=MESH,
        )

    def start_wide(i, carry):
        wide_copy(i).start()
        return carry

    def start_narrow(i, carry):
        narrow_copy(i).start()
        return carry

    def pass_on(i, carry):
        wide_copy(i).wait_recv()
        pass_copy(i).start()
        return carry

    def wait_all(i, carry):
        wide_copy(i).wait_send()
        narrow_copy(i).wait()
        pass_copy(i).wait()
        return carry

    to_z = wire(kvp.at[flat], kvr.at[here], zp)
    lax.fori_loop(1, 16, start_wide, 0)
    lax.fori_loop(1, 16, start_narrow, 0)
    home = [
        pltpu.make_async_copy(kvp.at[flat], kvr.at[here], ls.at[1]),
        pltpu.make_async_copy(qp.at[flat], qr.at[flat], ls.at[2]),
    ]
    for c in home:
        c.start()
    for c in quarters:
        c.wait_recv()
    subs = []
    for ref, n, peers in ((qa_ref, y, yp), (qb_ref, x, xp)):
        spot = ref.at[:, :, pl.ds(pl.multiple_of(n * 256, 256), 256)]
        for p in peers:
            subs.append(wire(spot, spot, p))
    for src, dst in ((wo, co_ref), (wi, ci_ref), (wu, cu_ref)):
        rest.append(wire(src, dst, core))
    lax.fori_loop(1, 16, pass_on, 0)
    for c in subs:
        c.wait_recv()
    for src, dst, p in ((qa_ref, x2_ref, xp[1]), (qb_ref, y2_ref, yp[1]), (qa_ref, da_ref, core), (qb_ref, db_ref, core)):
        rest.append(wire(src, dst, p))
    for c in home:
        c.wait()
    keep.wait()
    lax.fori_loop(1, 16, wait_all, 0)
    to_z.wait()
    for c in first_a + first_b + near + second + last + quarters + subs:
        c.wait_send()
    for c in rest:
        c.wait()


def front(tok, own, lnp, wo, wi, wu):
    n = 6 + 3 + 12 + 3 + 2 + 18 + 3 + 1 + 6 + 3 + 4
    piece = shp((9, 32, 1024), BF)
    return pl.pallas_call(
        front_kernel,
        out_shape=[shp((4, 3, 256, 1024), BF), shp((2, 128, 256), BF), shp((4, 8, 256), F32)]
        + [shp(wo.shape, BF), shp(wi.shape, BF), shp(wu.shape, BF)] + [piece] * 6
        + [shp((32, 128, 128), BF), shp((16, 64, 128), BF)],
        in_specs=[VM] + [ANY] * 8,
        out_specs=[ANY] * 14,
        scratch_shapes=[
            pltpu.VMEM((4, 3, 256, 1024), BF), pltpu.VMEM((3, 128, 1024), F32),
            pltpu.VMEM((16, 128, 128), BF), pltpu.VMEM((16, 64, 128), BF),
            DMA((n,)), DMA((n,)), DMA((16,)), DMA((16,)), DMA((16,)), DMA((16,)), DMA((16,)), DMA((16,)), DMA((3,)),
        ],
        compiler_params=pltpu.CompilerParams(collective_id=1, has_side_effects=True, vmem_limit_bytes=LIMIT),
        cost_estimate=pl.CostEstimate(flops=16 << 30, bytes_accessed=32 << 20, transcendentals=0),
        name="front",
    )(tok, *own, tok, lnp, wo, wi, wu)


def attention_setup(blk, mask, kvr, qr, kvs, kaug, kvt, bias, qs, inv, order, oblk):
    first = (lax.axis_index("ctx") // 16) * 32

    def note(s, carry):
        inv[blk[s]] = s
        return carry

    lax.fori_loop(0, 64, note, 0)

    def pick(b, count):
        local = inv[b] - first
        order[count] = local
        oblk[count] = b
        mine = jnp.logical_and(local >= 0, local < 32)
        return count + mine.astype(jnp.int32)

    lax.fori_loop(0, 64, pick, 0)
    for s in range(64):
        at = pl.ds(pl.multiple_of(blk[s] * 64, 64), 64)
        kvs[at, :] = kvr[s // 2, (s % 2) * 64:(s % 2) * 64 + 64, :]
    for j in range(16):
        pair = qr[j]
        qs[2 * j] = pair[:, :64]
        qs[2 * j + 1] = pair[:, 64:]
    rows = lax.broadcasted_iota(jnp.int32, (512, 64), 0) // 64
    lanes = lax.broadcasted_iota(jnp.int32, (512, 64), 1)
    for c in range(8):
        part = kvs[512 * c:512 * c + 512, :]
        hot = jnp.where(rows + 8 * c == lanes, 1.0, 0.0).astype(BF)
        kaug[512 * c:512 * c + 512, :] = jnp.concatenate([part[:, :64], hot], axis=1)
        kvt[c] = part.astype(F32).T.astype(BF)
    qi = lax.broadcasted_iota(jnp.int32, (64, 64), 0)
    ki = lax.broadcasted_iota(jnp.int32, (64, 64), 1)
    bias[...] = jnp.where(jnp.logical_and(mask[0] != 0, ki < qi), 0.0, NEG)


def triangle():
    key = lax.broadcasted_iota(jnp.int32, (64, 256), 0)
    query = lax.broadcasted_iota(jnp.int32, (64, 256), 1) % 64
    return key <= query


def attend_kernel(blk, mask, kvr, qr, o_ref, ot_ref, lse_ref, kvs, kaug, kvt, bias, qs, qa, os, inv, order, oblk):
    attention_setup(blk, mask, kvr, qr, kvs, kaug, kvt, bias, qs, inv, order, oblk)

    def tile(g, carry):
        score, vals = [], []
        for u in range(4):
            i = oblk[4 * g + u]
            q = qs[order[4 * g + u]]
            row = jnp.broadcast_to(bias[pl.ds(i, 1), :], (64, 64)).astype(BF)
            qa[64 * u:64 * u + 64, :] = jnp.concatenate([q, row], axis=1)
            kv = kvs[pl.ds(pl.multiple_of(i * 64, 64), 64), :]
            score.append(dot(kv[:, :64], q, NT))
            vals.append(kv[:, 64:])
        s = jnp.where(triangle(), jnp.concatenate(score, axis=1), NEG)
        top = jnp.max(s, axis=0, keepdims=True)
        p = jnp.exp(s - top)
        total = jnp.sum(p, axis=0, keepdims=True)
        pb = p.astype(BF)
        mix = jnp.concatenate([dot(vals[u], pb[:, 64 * u:64 * u + 64], TN) for u in range(4)], axis=1)
        queries = qa[...]

        def chunk(c, state):
            top, total, mix = state
            keys = kaug[pl.ds(pl.multiple_of(c * 512, 512), 512), :]
            s = dot(keys, queries, NT)
            new = jnp.maximum(top, jnp.max(s, axis=0, keepdims=True))
            shrink = jnp.exp(top - new)
            p = jnp.exp(s - new)
            total = total * shrink + jnp.sum(p, axis=0, keepdims=True)
            mix = mix * shrink + dot(kvt[c, 64:, :], p.astype(BF))
            return new, total, mix

        chunks = (oblk[4 * g + 3] + 7) // 8
        def pair(c, state):
            top, total, mix = state
            parts = [dot(kaug[pl.ds(pl.multiple_of(c * 1024 + 512 * k, 512), 512), :], queries, NT) for k in range(2)]
            new = top
            for s in parts:
                new = jnp.maximum(new, jnp.max(s, axis=0, keepdims=True))
            shrink = jnp.exp(top - new)
            total, mix = total * shrink, mix * shrink
            for k, s in enumerate(parts):
                p = jnp.exp(s - new)
                total += jnp.sum(p, axis=0, keepdims=True)
                mix += dot(kvt[2 * c + k, 64:, :], p.astype(BF))
            return new, total, mix

        top, total, mix = lax.fori_loop(0, chunks // 2, pair, (top, total, mix))
        top, total, mix = lax.fori_loop(chunks // 2 * 2, chunks, chunk, (top, total, mix))
        out = mix / total
        ot_ref[g] = out
        lse_ref[g] = top + jnp.log(total)
        back = out.T.astype(BF)
        for u in range(4):
            os[order[4 * g + u]] = back[64 * u:64 * u + 64, :]
        return carry

    lax.fori_loop(0, 8, tile, 0)
    for j in range(16):
        o_ref[j] = jnp.concatenate([os[2 * j], os[2 * j + 1]], axis=1)


def attention_scratch():
    return [
        pltpu.VMEM((4096, 128), BF),
        pltpu.VMEM((4096, 128), BF),
        pltpu.VMEM((8, 128, 512), BF),
        pltpu.VMEM((64, 64), F32),
        pltpu.VMEM((32, 64, 64), BF),
        pltpu.VMEM((256, 128), BF),
        pltpu.VMEM((32, 64, 64), BF),
        pltpu.SMEM((64,), jnp.int32),
        pltpu.SMEM((72,), jnp.int32),
        pltpu.SMEM((72,), jnp.int32),
    ]


def attend(blk, mask, kvr, qr):
    return pl.pallas_call(
        attend_kernel,
        out_shape=[shp((16, 64, 128), BF), shp((8, 64, 256), F32), shp((8, 1, 256), F32)],
        in_specs=[SM, VM, VM, VM],
        out_specs=[VM] * 3,
        scratch_shapes=attention_scratch(),
        compiler_params=pltpu.CompilerParams(vmem_limit_bytes=LIMIT),
        cost_estimate=pl.CostEstimate(flops=10 << 30, bytes_accessed=32 << 20, transcendentals=4 << 20),
        name="attend",
    )(blk, mask, kvr, qr)


def attend_back_kernel(
    blk, mask, kvr, qr, dor, ot_ref, lse_ref, dkv_ref, dq_ref,
    kvs, kaug, kvt, bias, qs, qa, dqs, inv, order, oblk, dos, qz, dz, dkv,
):
    attention_setup(blk, mask, kvr, qr, kvs, kaug, kvt, bias, qs, inv, order, oblk)
    for j in range(16):
        pair = dor[j]
        dos[2 * j] = pair[:, :64]
        dos[2 * j + 1] = pair[:, 64:]
    dkv[...] = jnp.zeros_like(dkv)
    zero = jnp.zeros((64, 64), BF)

    def tile(g, carry):
        score, dprob, places, keys_own, q_own, d_own = [], [], [], [], [], []
        for u in range(4):
            i = oblk[4 * g + u]
            q = qs[order[4 * g + u]]
            do = dos[order[4 * g + u]]
            rows = slice(64 * u, 64 * u + 64)
            row = jnp.broadcast_to(bias[pl.ds(i, 1), :], (64, 64)).astype(BF)
            qa[rows, :] = jnp.concatenate([q, row], axis=1)
            qz[rows, :] = jnp.concatenate([q, zero], axis=1)
            dz[rows, :] = jnp.concatenate([zero, do], axis=1)
            at = pl.ds(pl.multiple_of(i * 64, 64), 64)
            kv = kvs[at, :]
            score.append(dot(kv[:, :64], q, NT))
            dprob.append(dot(kv[:, 64:], do, NT))
            places.append(at)
            keys_own.append(kv[:, :64])
            q_own.append(q)
            d_own.append(do)
        lse = lse_ref[g]
        queries = qa[...]
        qpad = qz[...]
        dpad = dz[...]
        dot_t = dpad[:, 64:].astype(F32).T
        delta = jnp.sum(ot_ref[g] * dot_t, axis=0, keepdims=True)
        s = jnp.where(triangle(), jnp.concatenate(score, axis=1), NEG)
        p = jnp.exp(s - lse)
        ds = (p * (jnp.concatenate(dprob, axis=1) - delta)).astype(BF)
        pb = p.astype(BF)
        dq = []
        for u in range(4):
            lanes = slice(64 * u, 64 * u + 64)
            grad = jnp.concatenate([dot(ds[:, lanes], q_own[u]), dot(pb[:, lanes], d_own[u])], axis=1)
            dkv[places[u], :] += grad
            dq.append(dot(keys_own[u], ds[:, lanes], TN))

        def chunk(c, dq):
            at = pl.ds(pl.multiple_of(c * 512, 512), 512)
            p = jnp.exp(dot(kaug[at, :], queries, NT) - lse)
            dp = dot(kvs[at, :], dpad, NT)
            ds = (p * (dp - delta)).astype(BF)
            dkv[at, :] += dot(ds, qpad) + dot(p.astype(BF), dpad)
            return dq + dot(kvt[c, :64, :], ds)

        chunks = (oblk[4 * g + 3] + 7) // 8
        dq = lax.fori_loop(0, chunks // 2, lambda c, dq: chunk(2 * c + 1, chunk(2 * c, dq)), jnp.concatenate(dq, axis=1))
        dq = lax.fori_loop(chunks // 2 * 2, chunks, chunk, dq)
        back = (dq * 0.125).T.astype(BF)
        for u in range(4):
            dqs[order[4 * g + u]] = back[64 * u:64 * u + 64, :]
        return carry

    lax.fori_loop(0, 8, tile, 0)
    for j in range(16):
        dq_ref[j] = jnp.concatenate([dqs[2 * j], dqs[2 * j + 1]], axis=1)
    for s in range(64):
        at = pl.ds(pl.multiple_of(blk[s] * 64, 64), 64)
        dkv_ref[s // 2, (s % 2) * 64:(s % 2) * 64 + 64, :] = dkv[at, :].astype(BF)


def attend_back(blk, mask, kvr, qr, dor, ot, lse):
    return pl.pallas_call(
        attend_back_kernel,
        out_shape=[shp((32, 128, 128), BF), shp((16, 64, 128), BF)],
        in_specs=[SM] + [VM] * 6,
        out_specs=[VM] * 2,
        scratch_shapes=attention_scratch()
        + [
            pltpu.VMEM((32, 64, 64), BF),
            pltpu.VMEM((256, 128), BF),
            pltpu.VMEM((256, 128), BF),
            pltpu.VMEM((4096, 128), F32),
        ],
        compiler_params=pltpu.CompilerParams(vmem_limit_bytes=LIMIT),
        cost_estimate=pl.CostEstimate(flops=1 << 30, bytes_accessed=4 << 20, transcendentals=0),
        name="attend_back",
    )(blk, mask, kvr, qr, dor, ot, lse)


def norm_parts(v):
    center = v - jnp.mean(v, axis=1, keepdims=True)
    r = lax.rsqrt(jnp.mean(center * center, axis=1, keepdims=True) + EPS)
    return center * r, r


def norm_back(e, gain, z, r):
    g = e * gain
    return r * (g - jnp.mean(g, axis=1, keepdims=True) - z * jnp.mean(g * z, axis=1, keepdims=True))


def heart_kernel(*refs):
    o_ref, x_ref, e_ref, ln_ref, ln_own = refs[:5]
    shards = (refs[5:8], refs[8:11])
    parts, diag_a, diag_b = refs[11:19], refs[19], refs[20]
    y_ref, dr_ref, zpay, gpay, gb_ref, dor = refs[21:27]
    cuts = (refs[27:30], refs[30:33])
    (wo, wi, wu, us, gs, nl, ob, orx, dos, rr, ll, cl, lt, mid,
     sw, sp, ss, rs, send_o, recv_o, send_do, recv_do, ls, lo) = refs[33:]
    zl, x, y, zh, co = place()
    w = zh * 2 + co
    flat = lax.axis_index("ctx") % 16
    where = [w, zh * 2 + 1 - co, (1 - zh) * 2 + co, (1 - zh) * 2 + 1 - co]
    core = device(zl, x, y, zh, 1 - co)
    bar = pltpu.get_barrier_semaphore()

    def plane(i):
        return {"ctx": zl * 16 + (flat + i) % 16}

    def greet_one(i, carry):
        pl.semaphore_signal(bar, inc=1, device_id=plane(i), device_id_type=MESH)
        return carry

    pl.semaphore_signal(bar, inc=1, device_id=core, device_id_type=MESH)
    lax.fori_loop(1, 16, greet_one, 0)
    copies = [[], [], []]
    for r, (a, b, c) in enumerate(shards):
        rows = pl.ds(pl.multiple_of(where[r] * 256, 256), 256)
        copies[0].append(pltpu.make_async_copy(a, wo.at[rows], sw.at[r, 0]))
        for k in range(4):
            cols = slice(1024 * k, 1024 * k + 1024)
            copies[1].append(pltpu.make_async_copy(b.at[:, cols], wi.at[k, rows], sw.at[r, 1 + k]))
        groups = pl.ds(where[r] * 8, 8)
        copies[2].append(pltpu.make_async_copy(c, wu.at[groups], sw.at[r, 5]))

    def spots(t, h, q):
        rows = pl.ds(pl.multiple_of(t * 256 + h * 128 + q * 32, 32), 32)
        return wo.at[rows], wi.at[:, rows], wu.at[t * 8 + h * 4 + q]

    quarters = [(parts[s], 0, (x + 4 - s) % 4) for s in range(4)]
    quarters += [(parts[4 + s], 1, (y + 4 - s) % 4) for s in range(4)]
    held = [(where[2],) + q for q in quarters] + [(where[3], diag_a, 0, x), (where[3], diag_b, 1, y)]
    for n, (t, ref, h, q) in enumerate(held):
        to = spots(t, h, q)
        for k, src in enumerate((ref.at[0], ref.at[1:5], ref.at[5:9])):
            copies[k].append(pltpu.make_async_copy(src, to[k], sp.at[n, k]))
    for group in copies:
        for c in group:
            c.start()
    pl.semaphore_wait(bar, 16)
    wire = Wire(ss, rs)

    def over(src, dst, send, recv):
        def copy(i):
            return pltpu.make_async_remote_copy(
                src_ref=src.at[(flat + i) % 16], dst_ref=dst.at[flat], send_sem=send.at[i], recv_sem=recv.at[i],
                device_id=plane(i), device_id_type=MESH,
            )

        def start_one(i, carry):
            copy(i).start()
            return carry

        def wait_one(i, carry):
            copy(i).wait()
            return carry

        return start_one, wait_one

    start_o, wait_o = over(o_ref, orx, send_o, recv_o)
    lax.fori_loop(1, 16, start_o, 0)
    home = pltpu.make_async_copy(o_ref.at[flat], orx.at[flat], ls.at[0])
    home.start()
    shared = [[], [], []]
    for k in range(3):
        for n in (1, 2, 3, 5, 6, 7):
            ref, h, q = quarters[n]
            src = (ref.at[0], ref.at[1:5], ref.at[5:9])[k]
            shared[k].append(wire(src, spots(where[2], h, q)[k], core))

    def loaded(k):
        for c in copies[k]:
            c.wait()
        for c in shared[k]:
            c.wait_recv()

    home.wait()
    lax.fori_loop(1, 16, wait_o, 0)
    ln = jnp.concatenate([jnp.where(w == k, ln_own[...], ln_ref[k]) for k in range(4)], axis=1)
    gain0, gain1, bias0, bias1 = (ln[k:k + 1, :] for k in range(4))
    for h in range(16):
        pair = orx[h]
        ob[:64, 64 * h:64 * h + 64] = pair[:, :64]
        ob[64:, 64 * h:64 * h + 64] = pair[:, 64:]
    loaded(0)
    z0, r0 = norm_parts(x_ref[...].astype(F32) + dot(ob[...], wo[...]))
    n1 = z0 * gain0 + bias0
    nl[...] = n1.astype(BF)
    loaded(1)

    half = math.sqrt(0.5)

    def up(c, carry):
        u = dot(nl[...], wi[c])
        us[c] = u
        gs[:, pl.ds(pl.multiple_of(c * 1024, 1024), 1024)] = (0.5 * u * (1.0 + lax.erf(u * half))).astype(BF)
        return carry

    lax.fori_loop(0, 4, up, 0)
    loaded(2)

    def down(c, total):
        cols = pl.ds(pl.multiple_of(c * 1024, 1024), 1024)
        return total + dot(gs[:, cols], wu[pl.ds(c * 8, 8)].reshape(1024, 1024))

    r2 = lax.fori_loop(0, 4, down, n1)
    z1, r1 = norm_parts(r2)
    y_ref[...] = z1 * gain1 + bias1
    e = e_ref[...].astype(F32)
    dr2 = norm_back(e, gain1, z1, r1)
    dm = dr2.astype(BF)
    gb_ref[1:2, :] = jnp.sum(e * z1, axis=0, keepdims=True)
    gb_ref[3:4, :] = jnp.sum(e, axis=0, keepdims=True)

    def back(c, total):
        u = us[c]
        dg = dot(dm, wu[pl.ds(c * 8, 8)].reshape(1024, 1024), NT)
        slope = 0.5 * (1.0 + lax.erf(u * half)) + u * (jnp.exp(-0.5 * u * u) * (1.0 / math.sqrt(2 * math.pi)))
        du = (dg * slope).astype(BF)
        rr[0:128, 1024 * c:1024 * c + 1024] = du
        return total + dot(du, wi[c], NT)

    few = [pl.ds(pl.multiple_of(where[r] * 256, 256), 256) for r in range(4)]
    many = [pl.ds(pl.multiple_of(where[r] * 1024, 1024), 1024) for r in range(4)]
    for ref, rows, at, r in ((ll, 128, 0, 0), (ll, 128, 512, 2), (cl, 128, 0, 1), (cl, 128, 512, 3)):
        ref[:rows, at:at + 256] = nl[:, few[r]]
        ref[:rows, at + 256:at + 512] = ob[:, few[r]]
    near = [wire(cl, ll.at[128:256, :], core)]
    dn1 = dr2
    for c in range(4):
        dn1 = back(c, dn1)
        cols = slice(1024 * c, 1024 * c + 1024)
        near.append(wire(rr.at[0:128, cols], rr.at[128:256, cols], core))
    gb_ref[0:1, :] = jnp.sum(dn1 * z0, axis=0, keepdims=True)
    gb_ref[2:3, :] = jnp.sum(dn1, axis=0, keepdims=True)
    gb_ref[4:8, :] = jnp.zeros((4, 1024), F32)
    dr1 = norm_back(dn1, gain0, z0, r0)
    dr_ref[...] = dr1
    da = dr1.astype(BF)
    rr[0:128, 4096:5120] = da
    near.append(wire(rr.at[0:128, 4096:5120], rr.at[128:256, 4096:5120], core))
    do = dot(da, wo[...], NT).astype(BF)
    for h in range(16):
        lanes = slice(64 * h, 64 * h + 64)
        dos[h] = jnp.concatenate([do[:64, lanes], do[64:, lanes]], axis=1)
    start_do, wait_do = over(dos, dor, send_do, recv_do)
    lax.fori_loop(1, 16, start_do, 0)
    home = pltpu.make_async_copy(dos.at[flat], dor.at[flat], ls.at[1])
    home.start()
    zpay[:, 1024:2048] = dm
    for r, (ref, at) in enumerate(((gpay, 0), (gpay, 1024), (zpay, 0), (zpay, 2048))):
        ref[:, at:at + 1024] = gs[:, many[r]]
    for c in near:
        c.wait_recv()
    for k in range(4):
        lt[256 * k:256 * k + 256, :] = ll[:, 256 * k:256 * k + 256].astype(F32).T.astype(BF)
    out = []
    for z in range(2):
        mid[z, 0:256, :] = dot(lt[512 * z + 256:512 * z + 512, :], rr[:, 4096:5120]).astype(BF)
        for k in range(4):
            rows = slice(256 + 256 * k, 512 + 256 * k)
            mid[z, rows, :] = dot(lt[512 * z:512 * z + 256, :], rr[:, 1024 * k:1024 * k + 1024]).astype(BF)
    for h, (at, (own, plus, minus)) in enumerate(zip((x, y), cuts)):

        def rows(s, first, size):
            return pl.ds(pl.multiple_of(h * 640 + (at + s) % 4 * 160 + first, 16), size)

        for src, dst in (
            (rows(0, 0, 160), own),
            (rows(1, 0, 160), plus.at[:, :160]), (rows(2, 0, 80), plus.at[:, 160:]),
            (rows(3, 0, 160), minus.at[:, :160]), (rows(2, 80, 80), minus.at[:, 160:]),
        ):
            out.append(pltpu.make_async_copy(mid.at[:, src], dst, lo.at[len(out)]))
    for c in out:
        c.start()
    home.wait()
    lax.fori_loop(1, 16, wait_do, 0)
    for c in near:
        c.wait_send()
    for group in shared:
        for c in group:
            c.wait_send()
    for c in out:
        c.wait()


def heart(o, tok, cot, lnf, lnp, shards, parts, diag_a, diag_b):
    cut = [shp((2, 160, 1024), BF), shp((2, 240, 1024), BF), shp((2, 240, 1024), BF)]
    n = 18 + 6
    return pl.pallas_call(
        heart_kernel,
        out_shape=[
            shp((128, 1024), F32), shp((128, 1024), F32),
            shp((128, 3072), BF), shp((128, 2048), BF), shp((8, 1024), F32), shp((16, 64, 128), BF),
        ] + cut + cut,
        in_specs=[ANY] + [VM] * 4 + [ANY] * 16,
        out_specs=[VM] * 5 + [ANY] * 7,
        scratch_shapes=[
            pltpu.VMEM((1024, 1024), BF),
            pltpu.VMEM((4, 1024, 1024), BF),
            pltpu.VMEM((32, 4, 32, 1024), BF),
            pltpu.VMEM((4, 128, 1024), F32),
            pltpu.VMEM((128, 4096), BF),
            pltpu.VMEM((128, 1024), BF),
            pltpu.VMEM((128, 1024), BF),
            pltpu.VMEM((16, 64, 128), BF),
            pltpu.VMEM((16, 64, 128), BF),
            pltpu.VMEM((256, 5120), BF),
            pltpu.VMEM((256, 1024), BF),
            pltpu.VMEM((128, 1024), BF),
            pltpu.VMEM((1024, 256), BF),
            pltpu.VMEM((2, 1280, 1024), BF),
            DMA((2, 6)), DMA((10, 3)), DMA((n,)), DMA((n,)), DMA((16,)), DMA((16,)), DMA((16,)), DMA((16,)),
            DMA((2,)), DMA((10,)),
        ],
        compiler_params=pltpu.CompilerParams(collective_id=5, has_side_effects=True, vmem_limit_bytes=LIMIT),
        cost_estimate=pl.CostEstimate(flops=16 << 30, bytes_accessed=32 << 20, transcendentals=2 << 20),
        name="heart",
    )(o, tok, cot, lnf, lnp, *shards[0], *shards[1], *parts, diag_a, diag_b)


class Spread:
    def __init__(self, wire, plus, minus, at, piece, bufs):
        self.wire, self.plus, self.minus, self.at, self.piece = wire, plus, minus, at, piece
        self.rp, self.rm, self.m, self.f = bufs

    def part(self, s, u):
        return self.piece((self.at + s) % 4, u)

    def start(self):
        self.a = self.wire(self.part(2, 0), self.m.at[0], self.plus)
        self.b = self.wire(self.part(2, 1), self.m.at[1], self.minus)
        self.c = self.wire(self.part(1, 1), self.rp.at[1], self.plus)
        self.d = self.wire(self.part(3, 0), self.rm.at[0], self.minus)

    def relay(self):
        self.a.wait_recv()
        self.f[0] = (self.part(1, 0)[...].astype(F32) + self.m[0].astype(F32)).astype(BF)
        self.e = self.wire(self.f.at[0], self.rp.at[0], self.plus)
        self.b.wait_recv()
        self.f[1] = (self.part(3, 1)[...].astype(F32) + self.m[1].astype(F32)).astype(BF)
        self.g = self.wire(self.f.at[1], self.rm.at[1], self.minus)

    def total(self):
        for c in (self.c, self.d, self.e, self.g):
            c.wait_recv()
        return [
            self.part(0, u)[...].astype(F32) + self.rp[u].astype(F32) + self.rm[u].astype(F32) for u in range(2)
        ]

    def sent(self):
        for c in (self.a, self.b, self.c, self.d, self.e, self.g):
            c.wait_send()


class Gather:
    def __init__(self, wire, plus, minus, at, block):
        self.wire, self.plus, self.minus, self.at, self.block = wire, plus, minus, at, block

    def send(self, s, u, peer):
        spot = self.block((self.at + s) % 4, u)
        return self.wire(spot, spot, peer)

    def start(self):
        self.p0 = self.send(0, 0, self.plus)
        self.m1 = self.send(0, 1, self.minus)
        self.p1 = self.send(0, 1, self.plus)
        self.m0 = self.send(0, 0, self.minus)

    def relay(self):
        self.p0.wait_recv()
        self.rp = self.send(3, 0, self.plus)
        self.m1.wait_recv()
        self.rm = self.send(1, 1, self.minus)

    def done(self):
        for c in (self.p1, self.m0, self.rp, self.rm):
            c.wait()
        for c in (self.p0, self.m1):
            c.wait_send()


class DirectSpread:
    def __init__(self, wire, peers, at, piece, bufs):
        self.wire, self.peers, self.at, self.piece, self.bufs = wire, peers, at, piece, bufs

    def start(self):
        self.copies = []
        for s in range(3):
            for u in range(2):
                src = self.piece((self.at + s + 1) % 4, u)
                self.copies.append(self.wire(src, self.bufs[s].at[u], self.peers[s]))

    def relay(self):
        pass

    def total(self):
        for c in self.copies:
            c.wait_recv()
        out = []
        for u in range(2):
            total = self.piece(self.at, u)[...].astype(F32)
            for s in range(3):
                total += self.bufs[s][u].astype(F32)
            out.append(total)
        return out

    def sent(self):
        for c in self.copies:
            c.wait_send()


class DirectGather:
    def __init__(self, wire, peers, at, block):
        self.wire, self.peers, self.at, self.block = wire, peers, at, block

    def start(self):
        self.copies = []
        for u in range(2):
            spot = self.block(self.at, u)
            for p in self.peers:
                self.copies.append(self.wire(spot, spot, p))

    def relay(self):
        pass

    def done(self):
        for c in self.copies:
            c.wait()


class Sum:
    direct = False

    def cut(self, g, rows):
        return g.at[rows]

    def __init__(self, g, hc, refs, wire, where, xp, yp, zp):
        bufs1, s1, bufs2, s2, self.r3, full = refs[:4], refs[4], refs[5:9], refs[9], refs[10], refs[11]
        zl, x, y, zh, co = where
        self.wire, self.zp, self.zl = wire, zp, zl
        self.s1, self.s2, self.last, self.full = s1, s2, s2, full
        hh = hc // 2
        first, second = (xp, yp), (yp, xp)
        self.at1, self.at2 = (x, y), (y, x)
        self.peers = [(first[h][0], first[h][2]) for h in range(2)]

        def rows(h, k, u):
            return pl.ds(pl.multiple_of(h * 4 * hc + k * hc + u * hh, 16), hh)

        def cols(k, width):
            return pl.ds(pl.multiple_of(k * width, 128), width)

        self.rows, self.cols = rows, cols

        def one(h):
            return lambda k, u: self.cut(g, rows(h, k, u))

        def two(h):
            return lambda k, u: s1.at[h, u, :, cols(k, 256)]

        def five(h):
            return lambda k, u: full.at[rows(h, self.at1[h], u), cols(k, 256)]

        def six(h):
            return lambda k, u: full.at[rows(h, k, u)]

        def ends(peers):
            return wire, peers[0], peers[2]

        if g is not None:
            self.one = [Spread(*ends(first[h]), self.at1[h], one(h), [r.at[h] for r in bufs1]) for h in range(2)]
        if self.direct:
            self.two = [DirectSpread(wire, second[h], self.at2[h], two(h), [r.at[h] for r in bufs2]) for h in range(2)]
            self.five = [DirectGather(wire, second[h], self.at2[h], five(h)) for h in range(2)]
        else:
            self.two = [Spread(*ends(second[h]), self.at2[h], two(h), [r.at[h] for r in bufs2]) for h in range(2)]
            self.five = [Gather(*ends(second[h]), self.at2[h], five(h)) for h in range(2)]
        self.six = [Gather(*ends(first[h]), self.at1[h], six(h)) for h in range(2)]

    def begin(self):
        for t in self.one:
            t.start()

    def relay(self):
        for t in self.one:
            t.relay()

    def totals(self, h):
        return self.one[h].total()

    def across(self):
        pass

    def settle(self):
        for t in self.one:
            t.sent()

    def steps(self):
        self.begin()
        yield
        self.relay()
        yield
        for h in range(2):
            for u, total in enumerate(self.totals(h)):
                self.s1[h, u] = total.astype(BF)
            self.two[h].start()
        yield
        for t in self.two:
            t.relay()
        yield
        for h in range(2):
            for u, total in enumerate(self.two[h].total()):
                self.s2[h, u] = total.astype(BF)
        self.across()
        yield
        three = []
        for h in range(2):
            self.ready(h)
            three.append(self.wire(self.last.at[h, :, :, self.cols(1 - self.zl, 128)], self.r3.at[h], self.zp))
        yield
        four = []
        for h in range(2):
            three[h].wait_recv()
            for u in range(2):
                total = self.last[h, u, :, self.cols(self.zl, 128)].astype(F32) + self.r3[h, u].astype(F32)
                spot = self.full.at[self.rows(h, self.at1[h], u), self.cols(self.at2[h] * 2 + self.zl, 128)]
                spot[...] = total.astype(BF)
                four.append(self.wire(spot, spot, self.zp))
        yield
        for h in range(2):
            four[2 * h].wait()
            four[2 * h + 1].wait()
            self.five[h].start()
        yield
        for t in self.five:
            t.relay()
        yield
        for h in range(2):
            self.five[h].done()
            self.six[h].start()
        yield
        for t in self.six:
            t.relay()
        yield
        for t in self.two:
            t.sent()
        for c in three:
            c.wait_send()
        self.settle()
        for t in self.six:
            t.done()
        yield

    def ready(self, h):
        pass


class PairSum(Sum):
    direct = True

    def cut(self, g, rows):
        return g.at[:, rows]

    def __init__(self, g, hc, refs, wire, where, xp, yp, zp, far):
        self.rf, self.s3 = refs[:2]
        super().__init__(g, hc, refs[2:], wire, where, xp, yp, zp)
        self.far, self.hh, self.last = far, hc // 2, self.s3

    def totals(self, h):
        return [t.reshape(2 * self.hh, 1024) for t in self.one[h].total()]

    def across(self):
        self.crossed = [self.wire(self.s2.at[h, :, self.hh:], self.rf.at[h], self.far) for h in range(2)]

    def ready(self, h):
        self.crossed[h].wait_recv()
        for u in range(2):
            self.s3[h, u] = (self.s2[h, u, :self.hh].astype(F32) + self.rf[h, u].astype(F32)).astype(BF)

    def settle(self):
        for t in self.one:
            t.sent()
        for c in self.crossed:
            c.wait_send()


class BegunSum(PairSum):
    direct = False

    def __init__(self, hc, refs, wire, where, xp, yp, zp, far, own, plus, minus):
        self.own, self.fwd = refs[:2]
        super().__init__(None, hc, list(refs[2:4]) + [None] * 4 + list(refs[4:]), wire, where, xp, yp, zp, far)
        self.plus, self.minus = plus, minus

    def begin(self):
        hc = 2 * self.hh
        self.passed = []
        for h in range(2):
            plus, minus = self.peers[h]
            self.passed.append((
                self.wire(self.plus[h].at[:, hc:], self.fwd.at[h, 0], plus),
                self.wire(self.minus[h].at[:, hc:], self.fwd.at[h, 1], minus),
            ))

    def relay(self):
        pass

    def totals(self, h):
        hh = self.hh
        for c in self.passed[h]:
            c.wait_recv()
        out = []
        for u in range(2):
            rows = slice(u * hh, u * hh + hh)
            total = self.own[h, 0, :, rows].astype(F32) + self.own[h, 1, :, rows].astype(F32)
            total += self.own[h, 2, :, rows].astype(F32) + self.fwd[h, u].astype(F32)
            out.append(total.reshape(2 * hh, 1024))
        return out

    def settle(self):
        for c in self.crossed:
            c.wait_send()
        for pair in self.passed:
            for c in pair:
                c.wait_send()


class FirstSum:
    def __init__(self, g, refs, wire, where, xp, yp, zp):
        bufs1, s1, bufs2, rz, half, full = refs[:4], refs[4], refs[5:9], refs[9], refs[10], refs[11]
        zl, x, y, zh, co = where
        self.g, self.wire, self.zp, self.zl = g, wire, zp, zl
        self.s1, self.rz, self.half, self.full = s1, rz, half, full
        first, second = (xp, yp), (yp, xp)
        self.at1, self.at2 = (x, y), (y, x)

        def cols(k):
            return pl.ds(pl.multiple_of(k * 256, 128), 256)

        def one(h):
            return lambda k, u: half.at[pl.ds(pl.multiple_of(h * 256 + k * 64 + u * 32, 32), 32)]

        def two(h):
            return lambda k, u: s1.at[h, u, :, cols(k)]

        def rows(h, k, z):
            return pl.ds(pl.multiple_of(z * 512 + h * 256 + k * 64, 64), 64)

        def five(h):
            return lambda k, z: full.at[rows(h, self.at1[h], z), cols(k)]

        def six(h):
            return lambda k, z: full.at[rows(h, k, z)]

        self.spot = lambda h: full.at[rows(h, self.at1[h], zl), cols(self.at2[h])]
        self.one = [Spread(wire, first[h][0], first[h][2], self.at1[h], one(h), [r.at[h] for r in bufs1]) for h in range(2)]
        self.two = [DirectSpread(wire, second[h], self.at2[h], two(h), [r.at[h] for r in bufs2]) for h in range(2)]
        self.five = [Gather(wire, second[h][0], second[h][2], self.at2[h], five(h)) for h in range(2)]
        self.six = [Gather(wire, first[h][0], first[h][2], self.at1[h], six(h)) for h in range(2)]

    def steps(self):
        zs = []
        for h in range(2):
            src = self.g.at[pl.ds(pl.multiple_of((1 - self.zl) * 512 + h * 256, 256), 256)]
            zs.append(self.wire(src, self.rz.at[h], self.zp))
        yield
        for h in range(2):
            zs[h].wait_recv()
            mine = self.g[pl.ds(pl.multiple_of(self.zl * 512 + h * 256, 256), 256), :]
            self.half[256 * h:256 * h + 256, :] = (mine.astype(F32) + self.rz[h].astype(F32)).astype(BF)
            self.one[h].start()
        yield
        for t in self.one:
            t.relay()
        yield
        for h in range(2):
            for u, total in enumerate(self.one[h].total()):
                self.s1[h, u] = total.astype(BF)
            self.two[h].start()
        yield
        four = []
        for h in range(2):
            spot = self.spot(h)
            spot[...] = jnp.concatenate(self.two[h].total(), axis=0).astype(BF)
            four.append(self.wire(spot, spot, self.zp))
        yield
        for h in range(2):
            four[h].wait()
            self.five[h].start()
        yield
        for t in self.five:
            t.relay()
        yield
        for h in range(2):
            self.five[h].done()
            self.six[h].start()
        yield
        for t in self.six:
            t.relay()
        yield
        for t in self.one + self.two:
            t.sent()
        for c in zs:
            c.wait_send()
        for t in self.six:
            t.done()
        yield


SUM_COPIES = 2 + 12 + 12 + 2 + 12 + 12


BEGUN_COPIES = 4 + 12 + 2 + 2 + 4 + 12 + 12
PAIR_COPIES = 12 + 12 + 2 + 2 + 4 + 12 + 12


def first_scratch():
    return (
        [pltpu.VMEM((2, 2, 32, 1024), BF)] * 5
        + [pltpu.VMEM((2, 2, 32, 256), BF)] * 4
        + [pltpu.VMEM((2, 256, 1024), BF), pltpu.VMEM((512, 1024), BF)]
    )


def pair_scratch(rows, begun):
    hh = rows // 16
    begin = [pltpu.VMEM((2, 3, 2, 2 * hh, 1024), BF), pltpu.VMEM((2, 2, 2, hh, 1024), BF)]
    first = [pltpu.VMEM((2, 2, 2, hh, 1024), BF)] * 4
    return (
        (begin if begun else [])
        + [pltpu.VMEM((2, 2, hh, 256), BF)] * 2
        + ([] if begun else first)
        + [pltpu.VMEM((2, 2, 2 * hh, 1024), BF)]
        + [pltpu.VMEM((2, 2, 2 * hh, 256), BF)] * 4
        + [pltpu.VMEM((2, 2, 2 * hh, 256), BF), pltpu.VMEM((2, 2, hh, 128), BF)]
    )


def finish_kernel(*refs):
    dkvp, dqp, dr_ref, gb, wall, gpay, zpay, zr, xs, x_ref = refs[:10]
    got = ((refs[10], refs[13]), (refs[11], refs[14]), (refs[12], refs[15]))

    gt, io_full, u_full, tail_full, s_vec = refs[16:21]
    io_refs = list(refs[21:32]) + [io_full]
    u_refs, tail_refs = list(refs[32:43]) + [u_full], list(refs[43:56]) + [tail_full]
    (dkv, zb, sb, dq, weights, ll2, rr2, lt2, mid, pay, ll, rr, tail, v0, vf, v1, vx, vy, vz, tx, ty,
     sz, rz, sw, rw, sn, rn, ss, rs, ls, lw) = refs[56:]
    scale = 1.0 / math.sqrt(16384)
    where = place()
    zl, x, y, zh, co = where
    w = zh * 2 + co
    me = lax.axis_index("ctx")
    flat = me % 16
    core = device(zl, x, y, zh, 1 - co)
    far = device(zl, x, y, 1 - zh, co)
    xp = [device(zl, (x + s) % 4, y, zh, co) for s in (1, 2, 3)]
    yp = [device(zl, x, (y + s) % 4, zh, co) for s in (1, 2, 3)]
    zp = device(1 - zl, x, y, zh, co)
    bar = pltpu.get_barrier_semaphore()

    def greet_one(i, carry):
        pl.semaphore_signal(bar, inc=1, device_id={"ctx": zl * 16 + (flat + i) % 16}, device_id_type=MESH)
        return carry

    for p in (core, far, zp):
        pl.semaphore_signal(bar, inc=1, device_id=p, device_id_type=MESH)
    lax.fori_loop(1, 16, greet_one, 0)

    mine = [pl.ds(pl.multiple_of(k * 256, 256), 256) for k in (w, (1 - zh) * 2 + co)]
    parts = []
    for h in range(2):
        for n in range(3):
            parts.append(pltpu.make_async_copy(got[n][h].at[:, :160], io_refs[0].at[h, n], ls.at[10 + 3 * h + n]))
    local = [
        pltpu.make_async_copy(gpay.at[:, :1024], ll2.at[0:128, :], ls.at[0]),
        pltpu.make_async_copy(zpay.at[:, 1024:2048], rr2.at[0:128, :], ls.at[1]),
        pltpu.make_async_copy(zr.at[:, :1024], ll2.at[256:384, :], ls.at[2]),
        pltpu.make_async_copy(zr.at[:, 1024:2048], rr2.at[256:384, :], ls.at[3]),
    ]
    for k in range(2):
        cols = slice(256 * k, 256 * k + 256)
        local.append(pltpu.make_async_copy(x_ref.at[:, mine[k]], ll.at[0:128, cols], ls.at[4 + k]))
        local.append(pltpu.make_async_copy(xs.at[k], ll.at[128:256, cols], ls.at[6 + k]))
    for c in local + parts:
        c.start()
    loads = [pltpu.make_async_copy(wall, weights, lw.at[0])]
    loads[0].start()
    pl.semaphore_wait(bar, 18)

    def narrow_copy(i):
        p = (flat + i) % 16
        return pltpu.make_async_remote_copy(
            src_ref=dqp.at[p], dst_ref=dq.at[flat], send_sem=sn.at[i], recv_sem=rn.at[i],
            device_id={"ctx": zl * 16 + p}, device_id_type=MESH,
        )

    def z_copy(i):
        return pltpu.make_async_remote_copy(
            src_ref=dkvp.at[(1 - zl) * 16 + (flat + i) % 16], dst_ref=zb.at[i], send_sem=sz.at[i], recv_sem=rz.at[i],
            device_id=zp, device_id_type=MESH,
        )

    def wide_copy(i):
        p = (flat + i) % 16
        return pltpu.make_async_remote_copy(
            src_ref=sb.at[i], dst_ref=dkv.at[flat], send_sem=sw.at[i], recv_sem=rw.at[i],
            device_id={"ctx": zl * 16 + p}, device_id_type=MESH,
        )

    def start(make):
        def one(i, carry):
            make(i).start()
            return carry
        return one

    def wait(make):
        def one(i, carry):
            make(i).wait()
            return carry
        return one

    def both(i):
        z_copy(i).wait_recv()
        return (dkvp[zl * 16 + (flat + i) % 16].astype(F32) + zb[i].astype(F32)).astype(BF)

    def pass_on(i, carry):
        sb[i] = both(i)
        wide_copy(i).start()
        return carry

    def sent(i, carry):
        z_copy(i).wait_send()
        return carry

    lax.fori_loop(1, 16, start(z_copy), 0)
    z_copy(0).start()
    lax.fori_loop(1, 16, start(narrow_copy), 0)
    home = [pltpu.make_async_copy(dqp.at[flat], dq.at[flat], ls.at[9])]
    for c in home:
        c.start()
    wire = Wire(ss, rs)
    near = [
        wire(gpay.at[:, 1024:], ll2.at[128:256, :], core),
        wire(zpay.at[:, 1024:2048], rr2.at[128:256, :], core),
        wire(zr.at[:, 2048:], ll2.at[384:512, :], core),
        wire(zr.at[:, 1024:2048], rr2.at[384:512, :], core),
    ]
    io = BegunSum(160, io_refs, wire, where, xp, yp, zp, far, *got).steps()
    big = FirstSum(mid, u_refs, wire, where, xp, yp, zp).steps()
    small = PairSum(tail, 96, tail_refs, wire, where, xp, yp, zp, far).steps()
    next(io)
    next(io)
    for c in local:
        c.wait()
    lt = ll[...].astype(F32).T.astype(BF)
    for c in near:
        c.wait()
    for k in range(4):
        lt2[256 * k:256 * k + 256, :] = ll2[:, 256 * k:256 * k + 256].astype(F32).T.astype(BF)
    for k in range(4):
        rows = slice(256 * k, 256 * k + 256)
        mid[rows, :] = dot(lt2[rows, :], rr2[...]).astype(BF)
    next(big)
    lax.fori_loop(1, 16, pass_on, 0)
    dkv[flat] = both(0)
    for c in parts:
        c.wait()
    next(io)

    for c in home:
        c.wait()
    lax.fori_loop(1, 16, wait(wide_copy), 0)
    lax.fori_loop(1, 16, wait(narrow_copy), 0)
    lax.fori_loop(0, 16, sent, 0)
    for h in range(16):
        lanes = slice(64 * h, 64 * h + 64)
        pair = dq[h]
        pay[:64, lanes] = pair[:, :64]
        pay[64:128, lanes] = pair[:, 64:]
        pair = dkv[h]
        pay[:128, 1024 + 64 * h:1088 + 64 * h] = pair[:, :64]
        pay[:128, 2048 + 64 * h:2112 + 64 * h] = pair[:, 64:]
    pay[128:144, :1024] = jnp.concatenate([gb[...], jnp.zeros((8, 1024), F32)], axis=0).astype(BF)
    pay[128:144, 1024:] = jnp.zeros((16, 2048), BF)
    to_core = wire(pay, rr, core)
    next(io)
    for c in loads:
        c.wait()
    for k in range(4):
        cols = slice(256 * k, 256 * k + 256)
        total = dr_ref[:, cols]
        for m in range(3):
            total += dot(pay[:128, 1024 * m:1024 * m + 1024], weights[k, m], NT)
        gt[:, cols] = total
    next(io)
    to_core.wait_recv()
    for z in range(2):
        for m in range(3):
            cols = slice(1024 * m, 1024 * m + 1024)
            total = dot(lt[256 * z:256 * z + 256, :128], pay[:128, cols])
            total += dot(lt[256 * z:256 * z + 256, 128:], rr[:128, cols])
            tail[z, 256 * m:256 * m + 256, :] = total.astype(BF)
    next(small)
    for z in range(2):
        v0[z] = (pay[128:144, mine[z]].astype(F32) + rr[128:144, mine[z]].astype(F32))[:8]
    vfar = wire(v0.at[1], vf, far)
    next(big)
    next(io)
    next(small)
    next(big)
    next(io)
    vfar.wait_recv()
    v1[...] = v0[0] + vf[...]
    vone = [wire(v1, vx.at[s], xp[s]) for s in range(3)]
    next(small)
    next(io)
    next(big)
    next(small)
    next(io)
    for c in vone:
        c.wait_recv()
    tx[...] = v1[...] + vx[0] + vx[1] + vx[2]
    vtwo = [wire(tx, vy.at[s], yp[s]) for s in range(3)]
    next(small)
    next(big)
    next(io)
    next(small)
    next(big)
    for c in vtwo:
        c.wait_recv()
    ty[...] = tx[...] + vy[0] + vy[1] + vy[2]
    vthree = wire(ty, vz, zp)
    next(small)
    next(big)
    next(small)
    next(big)
    next(io)
    next(small)
    next(small)
    next(big)
    vthree.wait()
    s_vec[...] = (ty[...] + vz[...]) * scale
    for c in vone + vtwo + [to_core, vfar]:
        c.wait_send()
    next(small)
    next(io)
    next(big)
    next(small)


def finish(dkvp, dqp, dr, gb, wall, gpay, zpay, zr, xs, tok, parts):
    n = SUM_COPIES + BEGUN_COPIES + PAIR_COPIES + 4 + 2 + 7
    return pl.pallas_call(
        finish_kernel,
        out_shape=[
            shp((128, 1024), F32), shp((1280, 1024), BF), shp((1024, 1024), BF), shp((768, 1024), BF), shp((8, 256), F32),
        ],
        in_specs=[VM, ANY, VM, VM] + [ANY] * 12,
        out_specs=[VM] * 5,
        scratch_shapes=pair_scratch(1280, True) + first_scratch() + pair_scratch(768, False) + [
            pltpu.VMEM((16, 128, 128), BF), pltpu.VMEM((16, 128, 128), BF), pltpu.VMEM((16, 128, 128), BF),
            pltpu.VMEM((16, 64, 128), BF), pltpu.VMEM((4, 3, 256, 1024), BF),
            pltpu.VMEM((512, 1024), BF), pltpu.VMEM((512, 1024), BF), pltpu.VMEM((1024, 512), BF),
            pltpu.VMEM((1024, 1024), BF), pltpu.VMEM((144, 3072), BF),
            pltpu.VMEM((256, 512), BF), pltpu.VMEM((144, 3072), BF), pltpu.VMEM((2, 768, 1024), BF),
            pltpu.VMEM((2, 8, 256), F32), pltpu.VMEM((8, 256), F32), pltpu.VMEM((8, 256), F32),
            pltpu.VMEM((3, 8, 256), F32), pltpu.VMEM((3, 8, 256), F32),
            pltpu.VMEM((8, 256), F32), pltpu.VMEM((8, 256), F32), pltpu.VMEM((8, 256), F32),
            DMA((16,)), DMA((16,)), DMA((16,)), DMA((16,)), DMA((16,)), DMA((16,)),
            DMA((n,)), DMA((n,)), DMA((16,)), DMA((1,)),
        ],
        compiler_params=pltpu.CompilerParams(collective_id=6, has_side_effects=True, vmem_limit_bytes=LIMIT),
        name="finish",
    )(dkvp, dqp, dr, gb, wall, gpay, zpay, zr, xs, tok, *parts)


def scale_kernel(o, i0, i1, i2, i3, u, q, k, v, out_q, out_k, out_v, out_o, out_i, out_u):
    scale = 1.0 / math.sqrt(16384)
    for src, dst in ((q, out_q), (k, out_k), (v, out_v), (o, out_o), (u, out_u)):
        dst[...] = src[...].astype(F32) * scale
    for n, src in enumerate((i0, i1, i2, i3)):
        out_i[:, 1024 * n:1024 * n + 1024] = src[...].astype(F32) * scale


def scaled(io, u, tail):
    def rows(first, n=32):
        return pl.BlockSpec((n, 1024), lambda j: (first // n + j, 0))

    return pl.pallas_call(
        scale_kernel,
        grid=(8,),
        out_shape=[shp((256, 1024), F32)] * 4 + [shp((256, 4096), F32), shp((1024, 1024), F32)],
        in_specs=[rows(0)] + [rows(256 + 256 * k) for k in range(4)] + [rows(0, 128)] + [rows(256 * k) for k in range(3)],
        out_specs=[rows(0)] * 4 + [pl.BlockSpec((32, 4096), lambda j: (j, 0)), rows(0, 128)],
        compiler_params=pltpu.CompilerParams(vmem_limit_bytes=LIMIT),
        name="scaled",
    )(*[io] * 5, u, *[tail] * 3)


FLIP_CORE = [(0, 1), (1, 0), (2, 3), (3, 2)]
FLIP_FAR = [(0, 2), (2, 0), (1, 3), (3, 1)]


def along_x(s):
    return [(c, c // 16 * 16 + (c // 4 + s) % 4 * 4 + c % 4) for c in range(32)]


def along_y(s):
    return [(c, c // 4 * 4 + (c + s) % 4) for c in range(32)]


def body(
    tokens, w_query, w_key, w_value, w_output, w_inner, w_outer, ln_gain, ln_bias, block_mask, block_pairs, cotangent,
):
    tok = tokens.reshape(128, 1024)
    cot = cotangent.reshape(128, 1024)
    lnp = jnp.concatenate([ln_gain, ln_bias, jnp.zeros((4, 256), F32)], axis=0)
    blk = block_pairs.reshape(-1)
    own = (w_query, w_key, w_value)
    outer = w_outer.reshape(8, 4, 32, 1024)
    wall, xs, lnf, *rest = front(tok, own, lnp, w_output, w_inner, outer)
    core_shard, (qa, qb, x2, y2, diag_a, diag_b, kvr, qr) = rest[:3], rest[3:]
    x1, x3 = (lax.ppermute(qa, "ctx", along_x(s)) for s in (1, 3))
    y1, y3 = (lax.ppermute(qb, "ctx", along_y(s)) for s in (1, 3))
    o, ot, lse = attend(blk, block_mask, kvr, qr)
    x1, x2, x3, y1, y2, y3, o = lax.optimization_barrier((x1, x2, x3, y1, y2, y3, o))
    far = [qa, x1, x2, x3, qb, y1, y2, y3]
    y_out, dr1, zpay, gpay, gb, dor, own_a, plus_a, minus_a, own_b, plus_b, minus_b = heart(
        o, tok, cot, lnf, lnp, ((w_output, w_inner, outer), core_shard), far, diag_a, diag_b
    )
    zr = lax.ppermute(zpay, "wsh", FLIP_FAR)
    plus_a = lax.ppermute(plus_a, "ctx", along_x(1))
    minus_a = lax.ppermute(minus_a, "ctx", along_x(3))
    plus_b = lax.ppermute(plus_b, "ctx", along_y(1))
    minus_b = lax.ppermute(minus_b, "ctx", along_y(3))
    dkvp, dqp = attend_back(blk, block_mask, kvr, qr, dor, ot, lse)
    zr, plus_a, minus_a, plus_b, minus_b, dkvp = lax.optimization_barrier((zr, plus_a, minus_a, plus_b, minus_b, dkvp))
    grad_tok, io, u, tail, s_vec = finish(
        dkvp, dqp, dr1, gb, wall, gpay, zpay, zr, xs, tok, (own_a, plus_a, minus_a, own_b, plus_b, minus_b)
    )
    s_q, s_k, s_v, s_o, s_i, s_u = scaled(io, u, tail)
    out_shape = tokens.shape
    return (
        y_out.reshape(out_shape), grad_tok.reshape(out_shape), s_q, s_k, s_v, s_o, s_i, s_u, s_vec[0:2], s_vec[2:4],
    )


def solution(mesh):
    return jax.shard_map(
        body,
        mesh=mesh,
        in_specs=(
            P("wsh", "ctx", None, None),
            P("wsh", None), P("wsh", None), P("wsh", None), P("wsh", None), P("wsh", None), P("wsh", None),
            P(None, "wsh"), P(None, "wsh"),
            P("wsh", None, None),
            P(),
            P("wsh", "ctx", None, None),
        ),
        out_specs=(
            P("wsh", "ctx", None, None), P("wsh", "ctx", None, None),
            P("wsh", None), P("wsh", None), P("wsh", None), P("wsh", None), P("wsh", None), P("wsh", None),
            P(None, "wsh"), P(None, "wsh"),
        ),
        check_vma=False,
    )
```

```python
import math

import jax
import jax.numpy as jnp
from jax import lax
from jax.experimental import pallas as pl
from jax.experimental.pallas import tpu as pltpu
from jax.sharding import PartitionSpec as P

MESH = pl.DeviceIdType.MESH
BF = jnp.bfloat16
F32 = jnp.float32
ANY = pl.BlockSpec(memory_space=pl.ANY)
VM = pl.BlockSpec(memory_space=pltpu.VMEM)
SM = pl.BlockSpec(memory_space=pltpu.SMEM)
DMA = pltpu.SemaphoreType.DMA
LIMIT = 56 * 1024 * 1024
EPS = 1e-05
NEG = -1e30


def shp(shape, dtype):
    return jax.ShapeDtypeStruct(shape, dtype)


def dot(a, b, dims=((1,), (0,))):
    return lax.dot_general(a, b, (dims, ((), ())), preferred_element_type=F32)


NN = ((1,), (0,))
NT = ((1,), (1,))
TN = ((0,), (0,))


def place():
    c = lax.axis_index("ctx")
    w = lax.axis_index("wsh")
    return c // 16, (c // 4) % 4, c % 4, w // 2, w % 2


def device(zl, x, y, zh, co):
    return {"ctx": zl * 16 + x * 4 + y, "wsh": zh * 2 + co}


def greet(peers):
    bar = pltpu.get_barrier_semaphore()
    for p in peers:
        pl.semaphore_signal(bar, inc=1, device_id=p, device_id_type=MESH)
    pl.semaphore_wait(bar, len(peers))


class Wire:
    def __init__(self, send, recv):
        self.send, self.recv, self.n = send, recv, 0

    def __call__(self, src, dst, peer):
        k = self.n
        self.n += 1
        copy = pltpu.make_async_remote_copy(
            src_ref=src, dst_ref=dst, send_sem=self.send.at[k], recv_sem=self.recv.at[k],
            device_id=peer, device_id_type=MESH,
        )
        copy.start()
        return copy


def front_kernel(*refs):
    x_ref, wq, wk, wv, x_any, ln_ref, wo, wi, wu = refs[:9]
    wall, xs, lnf, co_ref, ci_ref, cu_ref, qa_ref, qb_ref, da_ref, db_ref, kvr, qr = refs[9:21]
    weights, acc, kvp, qp, ss, rs, sw, rw, sf, rf, sn, rn, ls = refs[21:]
    zl, x, y, zh, co = place()
    me = zh * 2 + co
    slots = [me, zh * 2 + 1 - co, (1 - zh) * 2 + co, (1 - zh) * 2 + 1 - co]
    here = lax.axis_index("ctx")
    flat = here % 16
    core = device(zl, x, y, zh, 1 - co)
    far = device(zl, x, y, 1 - zh, co)
    diag = device(zl, x, y, 1 - zh, 1 - co)
    zp = device(1 - zl, x, y, zh, co)
    xp = [device(zl, (x + s) % 4, y, zh, co) for s in (1, 2, 3)]
    yp = [device(zl, x, (y + s) % 4, zh, co) for s in (1, 2, 3)]
    bar = pltpu.get_barrier_semaphore()

    def greet_one(i, carry):
        pl.semaphore_signal(bar, inc=1, device_id={"ctx": zl * 16 + (flat + i) % 16}, device_id_type=MESH)
        return carry

    for p in (far, core, diag, zp):
        pl.semaphore_signal(bar, inc=1, device_id=p, device_id_type=MESH)
    lax.fori_loop(1, 16, greet_one, 0)
    ws = (wq, wk, wv)
    local = [pltpu.make_async_copy(ws[m], weights.at[me, m], ls.at[m]) for m in range(3)]
    for c in local:
        c.start()
    pl.semaphore_wait(bar, 19)
    wire = Wire(ss, rs)
    rows_a = pl.ds(pl.multiple_of(x * 32, 32), 32)
    rows_b = pl.ds(pl.multiple_of(128 + y * 32, 32), 32)
    first_a, first_b = [], []
    for m in range(3):
        first_a.append(wire(ws[m].at[rows_a], weights.at[me, m, rows_a], far))
        first_b.append(wire(ws[m].at[rows_b], weights.at[me, m, rows_b], far))
    near = [wire(ws[m], weights.at[me, m], core) for m in range(3)]
    quarters = []
    for ref, k, n in ((qa_ref, x, y), (qb_ref, 4 + y, x)):
        rows = pl.ds(pl.multiple_of(k * 32, 32), 32)
        cols = pl.ds(pl.multiple_of(n * 256, 256), 256)
        quarters.append(wire(wo.at[rows, cols], ref.at[0, :, cols], far))
        for b in range(4):
            at = pl.ds(pl.multiple_of(1024 * b + n * 256, 256), 256)
            quarters.append(wire(wi.at[rows, at], ref.at[1 + b, :, cols], far))
        quarters.append(wire(wu.at[k, :, :, cols], ref.at[5:9, :, cols], far))
    rest = []
    for p in (core, far, diag):
        rest.append(wire(ln_ref, lnf.at[me], p))
    for n, idx in enumerate((slots[1], slots[3])):
        rest.append(wire(x_any.at[:, pl.ds(pl.multiple_of(idx * 256, 256), 256)], xs.at[n], core))

    def add(k, fresh):
        cols = x_ref[:, pl.ds(pl.multiple_of(slots[k] * 256, 256), 256)]
        for m in range(3):
            part = dot(cols, weights[slots[k], m])
            acc[m] = part if fresh else acc[m] + part

    for c in first_a:
        c.wait_recv()
    second = []
    for m in range(3):
        part = weights.at[slots[2], m, rows_a]
        for p in xp:
            second.append(wire(part, part, p))
    for c in first_b:
        c.wait_recv()
    for m in range(3):
        part = weights.at[slots[2], m, rows_b]
        for p in yp:
            second.append(wire(part, part, p))
    for c in local:
        c.wait()
    add(0, True)
    for c in near:
        c.wait_recv()
    add(1, False)
    for c in quarters:
        c.wait_recv()
    subs = []
    for ref, n, peers in ((qa_ref, y, yp), (qb_ref, x, xp)):
        spot = ref.at[:, :, pl.ds(pl.multiple_of(n * 256, 256), 256)]
        for p in peers:
            subs.append(wire(spot, spot, p))
    for c in second:
        c.wait_recv()
    last = [wire(weights.at[slots[2], m], weights.at[slots[2], m], core) for m in range(3)]
    add(2, False)
    for c in last:
        c.wait_recv()
    add(3, False)
    keep = pltpu.make_async_copy(weights, wall, ls.at[0])
    keep.start()
    for j in range(8):
        lanes = slice(128 * j, 128 * j + 128)
        q = (acc[0, :, lanes].astype(BF).astype(F32) * 0.125).astype(BF)
        k = acc[1, :, lanes].astype(BF)
        v = acc[2, :, lanes].astype(BF)
        for u in range(2):
            part = slice(64 * u, 64 * u + 64)
            kvp[2 * j + u] = jnp.concatenate([k[:, part], v[:, part]], axis=1)
            qp[2 * j + u] = jnp.concatenate([q[:64, part], q[64:, part]], axis=1)

    def plane(i):
        return {"ctx": zl * 16 + (flat + i) % 16}

    def wide_copy(i):
        return pltpu.make_async_remote_copy(
            src_ref=kvp.at[(flat + i) % 16], dst_ref=kvr.at[here], send_sem=sw.at[i], recv_sem=rw.at[i],
            device_id=plane(i), device_id_type=MESH,
        )

    def narrow_copy(i):
        return pltpu.make_async_remote_copy(
            src_ref=qp.at[(flat + i) % 16], dst_ref=qr.at[flat], send_sem=sn.at[i], recv_sem=rn.at[i],
            device_id=plane(i), device_id_type=MESH,
        )

    def pass_copy(i):
        spot = kvr.at[zl * 16 + (flat + 16 - i) % 16]
        return pltpu.make_async_remote_copy(
            src_ref=spot, dst_ref=spot, send_sem=sf.at[i], recv_sem=rf.at[i], device_id=zp, device_id_type=MESH,
        )

    def start_wide(i, carry):
        wide_copy(i).start()
        return carry

    def start_narrow(i, carry):
        narrow_copy(i).start()
        return carry

    def pass_on(i, carry):
        wide_copy(i).wait_recv()
        pass_copy(i).start()
        return carry

    def wait_all(i, carry):
        wide_copy(i).wait_send()
        narrow_copy(i).wait()
        pass_copy(i).wait()
        return carry

    to_z = wire(kvp.at[flat], kvr.at[here], zp)
    lax.fori_loop(1, 16, start_wide, 0)
    lax.fori_loop(1, 16, start_narrow, 0)
    home = [
        pltpu.make_async_copy(kvp.at[flat], kvr.at[here], ls.at[1]),
        pltpu.make_async_copy(qp.at[flat], qr.at[flat], ls.at[2]),
    ]
    for c in home:
        c.start()
    for src, dst in ((wo, co_ref), (wi, ci_ref), (wu, cu_ref)):
        rest.append(wire(src, dst, core))
    lax.fori_loop(1, 16, pass_on, 0)
    for c in subs:
        c.wait_recv()
    for src, dst in ((qa_ref, da_ref), (qb_ref, db_ref)):
        rest.append(wire(src, dst, core))
    for c in home:
        c.wait()
    keep.wait()
    lax.fori_loop(1, 16, wait_all, 0)
    to_z.wait()
    for c in first_a + first_b + near + second + last + quarters + subs:
        c.wait_send()
    for c in rest:
        c.wait()


def front(tok, own, lnp, wo, wi, wu):
    n = 6 + 3 + 12 + 3 + 2 + 18 + 3 + 1 + 6 + 3 + 2
    piece = shp((9, 32, 1024), BF)
    return pl.pallas_call(
        front_kernel,
        out_shape=[shp((4, 3, 256, 1024), BF), shp((2, 128, 256), BF), shp((4, 8, 256), F32)]
        + [shp(wo.shape, BF), shp(wi.shape, BF), shp(wu.shape, BF)] + [piece] * 4
        + [shp((32, 128, 128), BF), shp((16, 64, 128), BF)],
        in_specs=[VM] + [ANY] * 8,
        out_specs=[ANY] * 12,
        scratch_shapes=[
            pltpu.VMEM((4, 3, 256, 1024), BF), pltpu.VMEM((3, 128, 1024), F32),
            pltpu.VMEM((16, 128, 128), BF), pltpu.VMEM((16, 64, 128), BF),
            DMA((n,)), DMA((n,)), DMA((16,)), DMA((16,)), DMA((16,)), DMA((16,)), DMA((16,)), DMA((16,)), DMA((3,)),
        ],
        compiler_params=pltpu.CompilerParams(collective_id=1, has_side_effects=True, vmem_limit_bytes=LIMIT),
        cost_estimate=pl.CostEstimate(flops=16 << 30, bytes_accessed=32 << 20, transcendentals=0),
        name="front",
    )(tok, *own, tok, lnp, wo, wi, wu)


def attention_setup(blk, mask, kvr, qr, kvs, kaug, kvt, bias, qs, inv, order, oblk):
    first = (lax.axis_index("ctx") // 16) * 32

    def note(s, carry):
        inv[blk[s]] = s
        return carry

    lax.fori_loop(0, 64, note, 0)

    def pick(b, count):
        local = inv[b] - first
        order[count] = local
        oblk[count] = b
        mine = jnp.logical_and(local >= 0, local < 32)
        return count + mine.astype(jnp.int32)

    lax.fori_loop(0, 64, pick, 0)
    for s in range(64):
        at = pl.ds(pl.multiple_of(blk[s] * 64, 64), 64)
        kvs[at, :] = kvr[s // 2, (s % 2) * 64:(s % 2) * 64 + 64, :]
    for j in range(16):
        pair = qr[j]
        qs[2 * j] = pair[:, :64]
        qs[2 * j + 1] = pair[:, 64:]
    rows = lax.broadcasted_iota(jnp.int32, (512, 64), 0) // 64
    lanes = lax.broadcasted_iota(jnp.int32, (512, 64), 1)
    for c in range(8):
        part = kvs[512 * c:512 * c + 512, :]
        hot = jnp.where(rows + 8 * c == lanes, 1.0, 0.0).astype(BF)
        kaug[512 * c:512 * c + 512, :] = jnp.concatenate([part[:, :64], hot], axis=1)
        kvt[c] = part.astype(F32).T.astype(BF)
    qi = lax.broadcasted_iota(jnp.int32, (64, 64), 0)
    ki = lax.broadcasted_iota(jnp.int32, (64, 64), 1)
    bias[...] = jnp.where(jnp.logical_and(mask[0] != 0, ki < qi), 0.0, NEG)


def triangle():
    key = lax.broadcasted_iota(jnp.int32, (64, 256), 0)
    query = lax.broadcasted_iota(jnp.int32, (64, 256), 1) % 64
    return key <= query


def attend_kernel(blk, mask, kvr, qr, o_ref, ot_ref, lse_ref, kvs, kaug, kvt, bias, qs, qa, os, inv, order, oblk):
    attention_setup(blk, mask, kvr, qr, kvs, kaug, kvt, bias, qs, inv, order, oblk)

    def tile(g, carry):
        score, vals = [], []
        for u in range(4):
            i = oblk[4 * g + u]
            q = qs[order[4 * g + u]]
            row = jnp.broadcast_to(bias[pl.ds(i, 1), :], (64, 64)).astype(BF)
            qa[64 * u:64 * u + 64, :] = jnp.concatenate([q, row], axis=1)
            kv = kvs[pl.ds(pl.multiple_of(i * 64, 64), 64), :]
            score.append(dot(kv[:, :64], q, NT))
            vals.append(kv[:, 64:])
        s = jnp.where(triangle(), jnp.concatenate(score, axis=1), NEG)
        top = jnp.max(s, axis=0, keepdims=True)
        p = jnp.exp(s - top)
        total = jnp.sum(p, axis=0, keepdims=True)
        pb = p.astype(BF)
        mix = jnp.concatenate([dot(vals[u], pb[:, 64 * u:64 * u + 64], TN) for u in range(4)], axis=1)
        queries = qa[...]

        def chunk(c, state):
            top, total, mix = state
            keys = kaug[pl.ds(pl.multiple_of(c * 512, 512), 512), :]
            s = dot(keys, queries, NT)
            new = jnp.maximum(top, jnp.max(s, axis=0, keepdims=True))
            shrink = jnp.exp(top - new)
            p = jnp.exp(s - new)
            total = total * shrink + jnp.sum(p, axis=0, keepdims=True)
            mix = mix * shrink + dot(kvt[c, 64:, :], p.astype(BF))
            return new, total, mix

        chunks = (oblk[4 * g + 3] + 7) // 8
        def pair(c, state):
            top, total, mix = state
            parts = [dot(kaug[pl.ds(pl.multiple_of(c * 1024 + 512 * k, 512), 512), :], queries, NT) for k in range(2)]
            new = top
            for s in parts:
                new = jnp.maximum(new, jnp.max(s, axis=0, keepdims=True))
            shrink = jnp.exp(top - new)
            total, mix = total * shrink, mix * shrink
            for k, s in enumerate(parts):
                p = jnp.exp(s - new)
                total += jnp.sum(p, axis=0, keepdims=True)
                mix += dot(kvt[2 * c + k, 64:, :], p.astype(BF))
            return new, total, mix

        top, total, mix = lax.fori_loop(0, chunks // 2, pair, (top, total, mix))
        top, total, mix = lax.fori_loop(chunks // 2 * 2, chunks, chunk, (top, total, mix))
        out = mix / total
        ot_ref[g] = out
        lse_ref[g] = top + jnp.log(total)
        back = out.T.astype(BF)
        for u in range(4):
            os[order[4 * g + u]] = back[64 * u:64 * u + 64, :]
        return carry

    lax.fori_loop(0, 8, tile, 0)
    for j in range(16):
        o_ref[j] = jnp.concatenate([os[2 * j], os[2 * j + 1]], axis=1)


def attention_scratch():
    return [
        pltpu.VMEM((4096, 128), BF),
        pltpu.VMEM((4096, 128), BF),
        pltpu.VMEM((8, 128, 512), BF),
        pltpu.VMEM((64, 64), F32),
        pltpu.VMEM((32, 64, 64), BF),
        pltpu.VMEM((256, 128), BF),
        pltpu.VMEM((32, 64, 64), BF),
        pltpu.SMEM((64,), jnp.int32),
        pltpu.SMEM((72,), jnp.int32),
        pltpu.SMEM((72,), jnp.int32),
    ]


def attend(blk, mask, kvr, qr):
    return pl.pallas_call(
        attend_kernel,
        out_shape=[shp((16, 64, 128), BF), shp((8, 64, 256), F32), shp((8, 1, 256), F32)],
        in_specs=[SM, VM, VM, VM],
        out_specs=[VM] * 3,
        scratch_shapes=attention_scratch(),
        compiler_params=pltpu.CompilerParams(vmem_limit_bytes=LIMIT),
        cost_estimate=pl.CostEstimate(flops=10 << 30, bytes_accessed=32 << 20, transcendentals=4 << 20),
        name="attend",
    )(blk, mask, kvr, qr)


def attend_back_kernel(
    blk, mask, kvr, qr, dor, ot_ref, lse_ref, dkv_ref, dq_ref,
    kvs, kaug, kvt, bias, qs, qa, dqs, inv, order, oblk, dos, qz, dz, dkv,
):
    attention_setup(blk, mask, kvr, qr, kvs, kaug, kvt, bias, qs, inv, order, oblk)
    for j in range(16):
        pair = dor[j]
        dos[2 * j] = pair[:, :64]
        dos[2 * j + 1] = pair[:, 64:]
    dkv[...] = jnp.zeros_like(dkv)
    zero = jnp.zeros((64, 64), BF)

    def tile(g, carry):
        score, dprob, places, keys_own, q_own, d_own = [], [], [], [], [], []
        for u in range(4):
            i = oblk[4 * g + u]
            q = qs[order[4 * g + u]]
            do = dos[order[4 * g + u]]
            rows = slice(64 * u, 64 * u + 64)
            row = jnp.broadcast_to(bias[pl.ds(i, 1), :], (64, 64)).astype(BF)
            qa[rows, :] = jnp.concatenate([q, row], axis=1)
            qz[rows, :] = jnp.concatenate([q, zero], axis=1)
            dz[rows, :] = jnp.concatenate([zero, do], axis=1)
            at = pl.ds(pl.multiple_of(i * 64, 64), 64)
            kv = kvs[at, :]
            score.append(dot(kv[:, :64], q, NT))
            dprob.append(dot(kv[:, 64:], do, NT))
            places.append(at)
            keys_own.append(kv[:, :64])
            q_own.append(q)
            d_own.append(do)
        lse = lse_ref[g]
        queries = qa[...]
        qpad = qz[...]
        dpad = dz[...]
        dot_t = dpad[:, 64:].astype(F32).T
        delta = jnp.sum(ot_ref[g] * dot_t, axis=0, keepdims=True)
        s = jnp.where(triangle(), jnp.concatenate(score, axis=1), NEG)
        p = jnp.exp(s - lse)
        ds = (p * (jnp.concatenate(dprob, axis=1) - delta)).astype(BF)
        pb = p.astype(BF)
        dq = []
        for u in range(4):
            lanes = slice(64 * u, 64 * u + 64)
            grad = jnp.concatenate([dot(ds[:, lanes], q_own[u]), dot(pb[:, lanes], d_own[u])], axis=1)
            dkv[places[u], :] += grad
            dq.append(dot(keys_own[u], ds[:, lanes], TN))

        def chunk(c, dq):
            at = pl.ds(pl.multiple_of(c * 512, 512), 512)
            p = jnp.exp(dot(kaug[at, :], queries, NT) - lse)
            dp = dot(kvs[at, :], dpad, NT)
            ds = (p * (dp - delta)).astype(BF)
            dkv[at, :] += dot(ds, qpad) + dot(p.astype(BF), dpad)
            return dq + dot(kvt[c, :64, :], ds)

        chunks = (oblk[4 * g + 3] + 7) // 8
        dq = lax.fori_loop(0, chunks // 2, lambda c, dq: chunk(2 * c + 1, chunk(2 * c, dq)), jnp.concatenate(dq, axis=1))
        dq = lax.fori_loop(chunks // 2 * 2, chunks, chunk, dq)
        back = (dq * 0.125).T.astype(BF)
        for u in range(4):
            dqs[order[4 * g + u]] = back[64 * u:64 * u + 64, :]
        return carry

    lax.fori_loop(0, 8, tile, 0)
    for j in range(16):
        dq_ref[j] = jnp.concatenate([dqs[2 * j], dqs[2 * j + 1]], axis=1)
    for s in range(64):
        at = pl.ds(pl.multiple_of(blk[s] * 64, 64), 64)
        dkv_ref[s // 2, (s % 2) * 64:(s % 2) * 64 + 64, :] = dkv[at, :].astype(BF)


def attend_back(blk, mask, kvr, qr, dor, ot, lse):
    return pl.pallas_call(
        attend_back_kernel,
        out_shape=[shp((32, 128, 128), BF), shp((16, 64, 128), BF)],
        in_specs=[SM] + [VM] * 6,
        out_specs=[VM] * 2,
        scratch_shapes=attention_scratch()
        + [
            pltpu.VMEM((32, 64, 64), BF),
            pltpu.VMEM((256, 128), BF),
            pltpu.VMEM((256, 128), BF),
            pltpu.VMEM((4096, 128), F32),
        ],
        compiler_params=pltpu.CompilerParams(vmem_limit_bytes=LIMIT),
        cost_estimate=pl.CostEstimate(flops=1 << 30, bytes_accessed=4 << 20, transcendentals=0),
        name="attend_back",
    )(blk, mask, kvr, qr, dor, ot, lse)


def norm_parts(v):
    center = v - jnp.mean(v, axis=1, keepdims=True)
    r = lax.rsqrt(jnp.mean(center * center, axis=1, keepdims=True) + EPS)
    return center * r, r


def norm_back(e, gain, z, r):
    g = e * gain
    return r * (g - jnp.mean(g, axis=1, keepdims=True) - z * jnp.mean(g * z, axis=1, keepdims=True))


def heart_kernel(*refs):
    o_ref, x_ref, e_ref, ln_ref, ln_own = refs[:5]
    shards = (refs[5:8], refs[8:11])
    qa, x1, x3, qb, y1, y3, diag_a, diag_b = refs[11:19]
    y_ref, dr_ref, zpay, gpay, gb_ref, dor = refs[19:25]
    cuts = (refs[25:28], refs[28:31])
    (wo, wi, wu, us, gs, nl, ob, orx, dos, rr, ll, cl, lt, mid,
     sw, sp, ss, rs, send_o, recv_o, send_do, recv_do, ls, lo) = refs[31:]
    zl, x, y, zh, co = place()
    w = zh * 2 + co
    flat = lax.axis_index("ctx") % 16
    where = [w, zh * 2 + 1 - co, (1 - zh) * 2 + co, (1 - zh) * 2 + 1 - co]
    core = device(zl, x, y, zh, 1 - co)
    bar = pltpu.get_barrier_semaphore()

    def plane(i):
        return {"ctx": zl * 16 + (flat + i) % 16}

    def greet_one(i, carry):
        pl.semaphore_signal(bar, inc=1, device_id=plane(i), device_id_type=MESH)
        return carry

    pl.semaphore_signal(bar, inc=1, device_id=core, device_id_type=MESH)
    lax.fori_loop(1, 16, greet_one, 0)
    copies = [[], [], []]
    for r, (a, b, c) in enumerate(shards):
        rows = pl.ds(pl.multiple_of(where[r] * 256, 256), 256)
        copies[0].append(pltpu.make_async_copy(a, wo.at[rows], sw.at[r, 0]))
        for k in range(4):
            cols = slice(1024 * k, 1024 * k + 1024)
            copies[1].append(pltpu.make_async_copy(b.at[:, cols], wi.at[k, rows], sw.at[r, 1 + k]))
        groups = pl.ds(where[r] * 8, 8)
        copies[2].append(pltpu.make_async_copy(c, wu.at[groups], sw.at[r, 5]))

    def spots(t, h, q):
        rows = pl.ds(pl.multiple_of(t * 256 + h * 128 + q * 32, 32), 32)
        return wo.at[rows], wi.at[:, rows], wu.at[t * 8 + h * 4 + q]

    quarters = [(qa, 0, x), (x1, 0, (x + 3) % 4), (x3, 0, (x + 1) % 4)]
    quarters += [(qb, 1, y), (y1, 1, (y + 3) % 4), (y3, 1, (y + 1) % 4)]
    held = [(where[2],) + q for q in quarters] + [(where[3], diag_a, 0, x), (where[3], diag_b, 1, y)]
    for n, (t, ref, h, q) in enumerate(held):
        to = spots(t, h, q)
        for k, src in enumerate((ref.at[0], ref.at[1:5], ref.at[5:9])):
            copies[k].append(pltpu.make_async_copy(src, to[k], sp.at[n, k]))
    for group in copies:
        for c in group:
            c.start()
    pl.semaphore_wait(bar, 16)
    wire = Wire(ss, rs)

    def over(src, dst, send, recv):
        def copy(i):
            return pltpu.make_async_remote_copy(
                src_ref=src.at[(flat + i) % 16], dst_ref=dst.at[flat], send_sem=send.at[i], recv_sem=recv.at[i],
                device_id=plane(i), device_id_type=MESH,
            )

        def start_one(i, carry):
            copy(i).start()
            return carry

        def wait_one(i, carry):
            copy(i).wait()
            return carry

        return start_one, wait_one

    start_o, wait_o = over(o_ref, orx, send_o, recv_o)
    lax.fori_loop(1, 16, start_o, 0)
    home = pltpu.make_async_copy(o_ref.at[flat], orx.at[flat], ls.at[0])
    home.start()
    shared = [[], [], []]
    passed = [[], [], []]
    ends = (
        (device(zl, (x + 1) % 4, y, zh, co), device(zl, (x + 3) % 4, y, zh, co)),
        (device(zl, x, (y + 1) % 4, zh, co), device(zl, x, (y + 3) % 4, zh, co)),
    )
    for k in range(3):
        for h in range(2):
            ref, _, q = quarters[3 * h + (2 if k == 2 else 1)]
            src = (ref.at[0], ref.at[1:5], ref.at[5:9])[k]
            passed[k].append(wire(src, spots(where[2], h, q)[k], ends[h][1 if k == 2 else 0]))
    for k in range(3):
        for n in (1, 2, 4, 5):
            ref, h, q = quarters[n]
            src = (ref.at[0], ref.at[1:5], ref.at[5:9])[k]
            shared[k].append(wire(src, spots(where[2], h, q)[k], core))

    def loaded(k):
        for c in copies[k]:
            c.wait()
        for c in shared[k]:
            c.wait_recv()

    home.wait()
    lax.fori_loop(1, 16, wait_o, 0)
    for k in range(3):
        for h, at in enumerate((x, y)):
            passed[k][h].wait_recv()
            spot = spots(where[2], h, (at + 2) % 4)[k]
            shared[k].append(wire(spot, spot, core))
    ln = jnp.concatenate([jnp.where(w == k, ln_own[...], ln_ref[k]) for k in range(4)], axis=1)
    gain0, gain1, bias0, bias1 = (ln[k:k + 1, :] for k in range(4))
    for h in range(16):
        pair = orx[h]
        ob[:64, 64 * h:64 * h + 64] = pair[:, :64]
        ob[64:, 64 * h:64 * h + 64] = pair[:, 64:]
    loaded(0)
    z0, r0 = norm_parts(x_ref[...].astype(F32) + dot(ob[...], wo[...]))
    n1 = z0 * gain0 + bias0
    nl[...] = n1.astype(BF)
    loaded(1)

    half = math.sqrt(0.5)

    def up(c, carry):
        u = dot(nl[...], wi[c])
        us[c] = u
        gs[:, pl.ds(pl.multiple_of(c * 1024, 1024), 1024)] = (0.5 * u * (1.0 + lax.erf(u * half))).astype(BF)
        return carry

    lax.fori_loop(0, 4, up, 0)
    loaded(2)

    def down(c, total):
        cols = pl.ds(pl.multiple_of(c * 1024, 1024), 1024)
        return total + dot(gs[:, cols], wu[pl.ds(c * 8, 8)].reshape(1024, 1024))

    r2 = lax.fori_loop(0, 4, down, n1)
    z1, r1 = norm_parts(r2)
    y_ref[...] = z1 * gain1 + bias1
    e = e_ref[...].astype(F32)
    dr2 = norm_back(e, gain1, z1, r1)
    dm = dr2.astype(BF)
    gb_ref[1:2, :] = jnp.sum(e * z1, axis=0, keepdims=True)
    gb_ref[3:4, :] = jnp.sum(e, axis=0, keepdims=True)

    def back(c, total):
        u = us[c]
        dg = dot(dm, wu[pl.ds(c * 8, 8)].reshape(1024, 1024), NT)
        slope = 0.5 * (1.0 + lax.erf(u * half)) + u * (jnp.exp(-0.5 * u * u) * (1.0 / math.sqrt(2 * math.pi)))
        du = (dg * slope).astype(BF)
        rr[0:128, 1024 * c:1024 * c + 1024] = du
        return total + dot(du, wi[c], NT)

    few = [pl.ds(pl.multiple_of(where[r] * 256, 256), 256) for r in range(4)]
    many = [pl.ds(pl.multiple_of(where[r] * 1024, 1024), 1024) for r in range(4)]
    for ref, rows, at, r in ((ll, 128, 0, 0), (ll, 128, 512, 2), (cl, 128, 0, 1), (cl, 128, 512, 3)):
        ref[:rows, at:at + 256] = nl[:, few[r]]
        ref[:rows, at + 256:at + 512] = ob[:, few[r]]
    near = [wire(cl, ll.at[128:256, :], core)]
    dn1 = dr2
    for c in range(4):
        dn1 = back(c, dn1)
        cols = slice(1024 * c, 1024 * c + 1024)
        near.append(wire(rr.at[0:128, cols], rr.at[128:256, cols], core))
    gb_ref[0:1, :] = jnp.sum(dn1 * z0, axis=0, keepdims=True)
    gb_ref[2:3, :] = jnp.sum(dn1, axis=0, keepdims=True)
    gb_ref[4:8, :] = jnp.zeros((4, 1024), F32)
    dr1 = norm_back(dn1, gain0, z0, r0)
    dr_ref[...] = dr1
    da = dr1.astype(BF)
    rr[0:128, 4096:5120] = da
    near.append(wire(rr.at[0:128, 4096:5120], rr.at[128:256, 4096:5120], core))
    do = dot(da, wo[...], NT).astype(BF)
    for h in range(16):
        lanes = slice(64 * h, 64 * h + 64)
        dos[h] = jnp.concatenate([do[:64, lanes], do[64:, lanes]], axis=1)
    start_do, wait_do = over(dos, dor, send_do, recv_do)
    lax.fori_loop(1, 16, start_do, 0)
    home = pltpu.make_async_copy(dos.at[flat], dor.at[flat], ls.at[1])
    home.start()
    zpay[:, 1024:2048] = dm
    for r, (ref, at) in enumerate(((gpay, 0), (gpay, 1024), (zpay, 0), (zpay, 2048))):
        ref[:, at:at + 1024] = gs[:, many[r]]
    for c in near:
        c.wait_recv()
    for k in range(4):
        lt[256 * k:256 * k + 256, :] = ll[:, 256 * k:256 * k + 256].astype(F32).T.astype(BF)
    out = []
    for z in range(2):
        mid[z, 0:256, :] = dot(lt[512 * z + 256:512 * z + 512, :], rr[:, 4096:5120]).astype(BF)
        for k in range(4):
            rows = slice(256 + 256 * k, 512 + 256 * k)
            mid[z, rows, :] = dot(lt[512 * z:512 * z + 256, :], rr[:, 1024 * k:1024 * k + 1024]).astype(BF)
    for h, (at, (own, plus, minus)) in enumerate(zip((x, y), cuts)):

        def rows(s, first, size):
            return pl.ds(pl.multiple_of(h * 640 + (at + s) % 4 * 160 + first, 16), size)

        for src, dst in (
            (rows(0, 0, 160), own),
            (rows(1, 0, 160), plus.at[:, :160]), (rows(2, 0, 80), plus.at[:, 160:]),
            (rows(3, 0, 160), minus.at[:, :160]), (rows(2, 80, 80), minus.at[:, 160:]),
        ):
            out.append(pltpu.make_async_copy(mid.at[:, src], dst, lo.at[len(out)]))
    for c in out:
        c.start()
    home.wait()
    lax.fori_loop(1, 16, wait_do, 0)
    for c in near:
        c.wait_send()
    for group in shared + passed:
        for c in group:
            c.wait_send()
    for c in out:
        c.wait()


def heart(o, tok, cot, lnf, lnp, shards, parts):
    cut = [shp((2, 160, 1024), BF), shp((2, 240, 1024), BF), shp((2, 240, 1024), BF)]
    n = 12 + 6 + 6 + 6
    return pl.pallas_call(
        heart_kernel,
        out_shape=[
            shp((128, 1024), F32), shp((128, 1024), F32),
            shp((128, 3072), BF), shp((128, 2048), BF), shp((8, 1024), F32), shp((16, 64, 128), BF),
        ] + cut + cut,
        in_specs=[ANY] + [VM] * 4 + [ANY] * 14,
        out_specs=[VM] * 5 + [ANY] * 7,
        scratch_shapes=[
            pltpu.VMEM((1024, 1024), BF),
            pltpu.VMEM((4, 1024, 1024), BF),
            pltpu.VMEM((32, 4, 32, 1024), BF),
            pltpu.VMEM((4, 128, 1024), F32),
            pltpu.VMEM((128, 4096), BF),
            pltpu.VMEM((128, 1024), BF),
            pltpu.VMEM((128, 1024), BF),
            pltpu.VMEM((16, 64, 128), BF),
            pltpu.VMEM((16, 64, 128), BF),
            pltpu.VMEM((256, 5120), BF),
            pltpu.VMEM((256, 1024), BF),
            pltpu.VMEM((128, 1024), BF),
            pltpu.VMEM((1024, 256), BF),
            pltpu.VMEM((2, 1280, 1024), BF),
            DMA((2, 6)), DMA((8, 3)), DMA((n,)), DMA((n,)), DMA((16,)), DMA((16,)), DMA((16,)), DMA((16,)),
            DMA((2,)), DMA((10,)),
        ],
        compiler_params=pltpu.CompilerParams(collective_id=5, has_side_effects=True, vmem_limit_bytes=LIMIT),
        cost_estimate=pl.CostEstimate(flops=16 << 30, bytes_accessed=32 << 20, transcendentals=2 << 20),
        name="heart",
    )(o, tok, cot, lnf, lnp, *shards[0], *shards[1], *parts)


class Spread:
    def __init__(self, wire, plus, minus, at, piece, bufs):
        self.wire, self.plus, self.minus, self.at, self.piece = wire, plus, minus, at, piece
        self.rp, self.rm, self.m, self.f = bufs

    def part(self, s, u):
        return self.piece((self.at + s) % 4, u)

    def start(self):
        self.a = self.wire(self.part(2, 0), self.m.at[0], self.plus)
        self.b = self.wire(self.part(2, 1), self.m.at[1], self.minus)
        self.c = self.wire(self.part(1, 1), self.rp.at[1], self.plus)
        self.d = self.wire(self.part(3, 0), self.rm.at[0], self.minus)

    def relay(self):
        self.a.wait_recv()
        self.f[0] = (self.part(1, 0)[...].astype(F32) + self.m[0].astype(F32)).astype(BF)
        self.e = self.wire(self.f.at[0], self.rp.at[0], self.plus)
        self.b.wait_recv()
        self.f[1] = (self.part(3, 1)[...].astype(F32) + self.m[1].astype(F32)).astype(BF)
        self.g = self.wire(self.f.at[1], self.rm.at[1], self.minus)

    def total(self):
        for c in (self.c, self.d, self.e, self.g):
            c.wait_recv()
        return [
            self.part(0, u)[...].astype(F32) + self.rp[u].astype(F32) + self.rm[u].astype(F32) for u in range(2)
        ]

    def sent(self):
        for c in (self.a, self.b, self.c, self.d, self.e, self.g):
            c.wait_send()


class Gather:
    def __init__(self, wire, plus, minus, at, block):
        self.wire, self.plus, self.minus, self.at, self.block = wire, plus, minus, at, block

    def send(self, s, u, peer):
        spot = self.block((self.at + s) % 4, u)
        return self.wire(spot, spot, peer)

    def start(self):
        self.p0 = self.send(0, 0, self.plus)
        self.m1 = self.send(0, 1, self.minus)
        self.p1 = self.send(0, 1, self.plus)
        self.m0 = self.send(0, 0, self.minus)

    def relay(self):
        self.p0.wait_recv()
        self.rp = self.send(3, 0, self.plus)
        self.m1.wait_recv()
        self.rm = self.send(1, 1, self.minus)

    def done(self):
        for c in (self.p1, self.m0, self.rp, self.rm):
            c.wait()
        for c in (self.p0, self.m1):
            c.wait_send()


class DirectSpread:
    def __init__(self, wire, peers, at, piece, bufs):
        self.wire, self.peers, self.at, self.piece, self.bufs = wire, peers, at, piece, bufs

    def start(self):
        self.copies = []
        for s in range(3):
            for u in range(2):
                src = self.piece((self.at + s + 1) % 4, u)
                self.copies.append(self.wire(src, self.bufs[s].at[u], self.peers[s]))

    def relay(self):
        pass

    def total(self):
        for c in self.copies:
            c.wait_recv()
        out = []
        for u in range(2):
            total = self.piece(self.at, u)[...].astype(F32)
            for s in range(3):
                total += self.bufs[s][u].astype(F32)
            out.append(total)
        return out

    def sent(self):
        for c in self.copies:
            c.wait_send()


class DirectGather:
    def __init__(self, wire, peers, at, block):
        self.wire, self.peers, self.at, self.block = wire, peers, at, block

    def start(self):
        self.copies = []
        for u in range(2):
            spot = self.block(self.at, u)
            for p in self.peers:
                self.copies.append(self.wire(spot, spot, p))

    def relay(self):
        pass

    def done(self):
        for c in self.copies:
            c.wait()


class Sum:
    direct = False

    def cut(self, g, rows):
        return g.at[rows]

    def __init__(self, g, hc, refs, wire, where, xp, yp, zp):
        bufs1, s1, bufs2, s2, self.r3, full = refs[:4], refs[4], refs[5:9], refs[9], refs[10], refs[11]
        zl, x, y, zh, co = where
        self.wire, self.zp, self.zl = wire, zp, zl
        self.s1, self.s2, self.last, self.full = s1, s2, s2, full
        hh = hc // 2
        first, second = (xp, yp), (yp, xp)
        self.at1, self.at2 = (x, y), (y, x)
        self.peers = [(first[h][0], first[h][2]) for h in range(2)]

        def rows(h, k, u):
            return pl.ds(pl.multiple_of(h * 4 * hc + k * hc + u * hh, 16), hh)

        def cols(k, width):
            return pl.ds(pl.multiple_of(k * width, 128), width)

        self.rows, self.cols = rows, cols

        def one(h):
            return lambda k, u: self.cut(g, rows(h, k, u))

        def two(h):
            return lambda k, u: s1.at[h, u, :, cols(k, 256)]

        def five(h):
            return lambda k, u: full.at[rows(h, self.at1[h], u), cols(k, 256)]

        def six(h):
            return lambda k, u: full.at[rows(h, k, u)]

        def ends(peers):
            return wire, peers[0], peers[2]

        if g is not None:
            self.one = [Spread(*ends(first[h]), self.at1[h], one(h), [r.at[h] for r in bufs1]) for h in range(2)]
        if self.direct:
            self.two = [DirectSpread(wire, second[h], self.at2[h], two(h), [r.at[h] for r in bufs2]) for h in range(2)]
            self.five = [DirectGather(wire, second[h], self.at2[h], five(h)) for h in range(2)]
        else:
            self.two = [Spread(*ends(second[h]), self.at2[h], two(h), [r.at[h] for r in bufs2]) for h in range(2)]
            self.five = [Gather(*ends(second[h]), self.at2[h], five(h)) for h in range(2)]
        self.six = [Gather(*ends(first[h]), self.at1[h], six(h)) for h in range(2)]

    def begin(self):
        for t in self.one:
            t.start()

    def relay(self):
        for t in self.one:
            t.relay()

    def totals(self, h):
        return self.one[h].total()

    def across(self):
        pass

    def settle(self):
        for t in self.one:
            t.sent()

    def steps(self):
        self.begin()
        yield
        self.relay()
        yield
        for h in range(2):
            for u, total in enumerate(self.totals(h)):
                self.s1[h, u] = total.astype(BF)
            self.two[h].start()
        yield
        for t in self.two:
            t.relay()
        yield
        for h in range(2):
            for u, total in enumerate(self.two[h].total()):
                self.s2[h, u] = total.astype(BF)
        self.across()
        yield
        three = []
        for h in range(2):
            self.ready(h)
            three.append(self.wire(self.last.at[h, :, :, self.cols(1 - self.zl, 128)], self.r3.at[h], self.zp))
        yield
        four = []
        for h in range(2):
            three[h].wait_recv()
            for u in range(2):
                total = self.last[h, u, :, self.cols(self.zl, 128)].astype(F32) + self.r3[h, u].astype(F32)
                spot = self.full.at[self.rows(h, self.at1[h], u), self.cols(self.at2[h] * 2 + self.zl, 128)]
                spot[...] = total.astype(BF)
                four.append(self.wire(spot, spot, self.zp))
        yield
        for h in range(2):
            four[2 * h].wait()
            four[2 * h + 1].wait()
            self.five[h].start()
        yield
        for t in self.five:
            t.relay()
        yield
        for h in range(2):
            self.five[h].done()
            self.six[h].start()
        yield
        for t in self.six:
            t.relay()
        yield
        for t in self.two:
            t.sent()
        for c in three:
            c.wait_send()
        self.settle()
        for t in self.six:
            t.done()
        yield

    def ready(self, h):
        pass


class PairSum(Sum):
    direct = True

    def cut(self, g, rows):
        return g.at[:, rows]

    def __init__(self, g, hc, refs, wire, where, xp, yp, zp, far):
        self.rf, self.s3 = refs[:2]
        super().__init__(g, hc, refs[2:], wire, where, xp, yp, zp)
        self.far, self.hh, self.last = far, hc // 2, self.s3

    def totals(self, h):
        return [t.reshape(2 * self.hh, 1024) for t in self.one[h].total()]

    def across(self):
        self.crossed = [self.wire(self.s2.at[h, :, self.hh:], self.rf.at[h], self.far) for h in range(2)]

    def ready(self, h):
        self.crossed[h].wait_recv()
        for u in range(2):
            self.s3[h, u] = (self.s2[h, u, :self.hh].astype(F32) + self.rf[h, u].astype(F32)).astype(BF)

    def settle(self):
        for t in self.one:
            t.sent()
        for c in self.crossed:
            c.wait_send()


class BegunSum(PairSum):
    direct = False

    def __init__(self, hc, refs, wire, where, xp, yp, zp, far, own, plus, minus):
        self.own, self.fwd = refs[:2]
        super().__init__(None, hc, list(refs[2:4]) + [None] * 4 + list(refs[4:]), wire, where, xp, yp, zp, far)
        self.plus, self.minus = plus, minus

    def begin(self):
        hc = 2 * self.hh
        self.passed = []
        for h in range(2):
            plus, minus = self.peers[h]
            self.passed.append((
                self.wire(self.plus[h].at[:, hc:], self.fwd.at[h, 0], plus),
                self.wire(self.minus[h].at[:, hc:], self.fwd.at[h, 1], minus),
            ))

    def relay(self):
        pass

    def totals(self, h):
        hh = self.hh
        for c in self.passed[h]:
            c.wait_recv()
        out = []
        for u in range(2):
            rows = slice(u * hh, u * hh + hh)
            total = self.own[h, 0, :, rows].astype(F32) + self.own[h, 1, :, rows].astype(F32)
            total += self.own[h, 2, :, rows].astype(F32) + self.fwd[h, u].astype(F32)
            out.append(total.reshape(2 * hh, 1024))
        return out

    def settle(self):
        for c in self.crossed:
            c.wait_send()
        for pair in self.passed:
            for c in pair:
                c.wait_send()


class FirstSum:
    def __init__(self, g, refs, wire, where, xp, yp, zp):
        bufs1, s1, bufs2, rz, half, full = refs[:4], refs[4], refs[5:9], refs[9], refs[10], refs[11]
        zl, x, y, zh, co = where
        self.g, self.wire, self.zp, self.zl = g, wire, zp, zl
        self.s1, self.rz, self.half, self.full = s1, rz, half, full
        first, second = (xp, yp), (yp, xp)
        self.at1, self.at2 = (x, y), (y, x)

        def cols(k):
            return pl.ds(pl.multiple_of(k * 256, 128), 256)

        def one(h):
            return lambda k, u: half.at[pl.ds(pl.multiple_of(h * 256 + k * 64 + u * 32, 32), 32)]

        def two(h):
            return lambda k, u: s1.at[h, u, :, cols(k)]

        def rows(h, k, z):
            return pl.ds(pl.multiple_of(z * 512 + h * 256 + k * 64, 64), 64)

        def five(h):
            return lambda k, z: full.at[rows(h, self.at1[h], z), cols(k)]

        def six(h):
            return lambda k, z: full.at[rows(h, k, z)]

        self.spot = lambda h: full.at[rows(h, self.at1[h], zl), cols(self.at2[h])]
        self.one = [Spread(wire, first[h][0], first[h][2], self.at1[h], one(h), [r.at[h] for r in bufs1]) for h in range(2)]
        self.two = [DirectSpread(wire, second[h], self.at2[h], two(h), [r.at[h] for r in bufs2]) for h in range(2)]
        self.five = [Gather(wire, second[h][0], second[h][2], self.at2[h], five(h)) for h in range(2)]
        self.six = [Gather(wire, first[h][0], first[h][2], self.at1[h], six(h)) for h in range(2)]

    def steps(self):
        zs = []
        for h in range(2):
            src = self.g.at[pl.ds(pl.multiple_of((1 - self.zl) * 512 + h * 256, 256), 256)]
            zs.append(self.wire(src, self.rz.at[h], self.zp))
        yield
        for h in range(2):
            zs[h].wait_recv()
            mine = self.g[pl.ds(pl.multiple_of(self.zl * 512 + h * 256, 256), 256), :]
            self.half[256 * h:256 * h + 256, :] = (mine.astype(F32) + self.rz[h].astype(F32)).astype(BF)
            self.one[h].start()
        yield
        for t in self.one:
            t.relay()
        yield
        for h in range(2):
            for u, total in enumerate(self.one[h].total()):
                self.s1[h, u] = total.astype(BF)
            self.two[h].start()
        yield
        four = []
        for h in range(2):
            spot = self.spot(h)
            spot[...] = jnp.concatenate(self.two[h].total(), axis=0).astype(BF)
            four.append(self.wire(spot, spot, self.zp))
        yield
        for h in range(2):
            four[h].wait()
            self.five[h].start()
        yield
        for t in self.five:
            t.relay()
        yield
        for h in range(2):
            self.five[h].done()
            self.six[h].start()
        yield
        for t in self.six:
            t.relay()
        yield
        for t in self.one + self.two:
            t.sent()
        for c in zs:
            c.wait_send()
        for t in self.six:
            t.done()
        yield


SUM_COPIES = 2 + 12 + 12 + 2 + 12 + 12


BEGUN_COPIES = 4 + 12 + 2 + 2 + 4 + 12 + 12
PAIR_COPIES = 12 + 12 + 2 + 2 + 4 + 12 + 12


def first_scratch():
    return (
        [pltpu.VMEM((2, 2, 32, 1024), BF)] * 5
        + [pltpu.VMEM((2, 2, 32, 256), BF)] * 4
        + [pltpu.VMEM((2, 256, 1024), BF), pltpu.VMEM((512, 1024), BF)]
    )


def pair_scratch(rows, begun):
    hh = rows // 16
    begin = [pltpu.VMEM((2, 3, 2, 2 * hh, 1024), BF), pltpu.VMEM((2, 2, 2, hh, 1024), BF)]
    first = [pltpu.VMEM((2, 2, 2, hh, 1024), BF)] * 4
    return (
        (begin if begun else [])
        + [pltpu.VMEM((2, 2, hh, 256), BF)] * 2
        + ([] if begun else first)
        + [pltpu.VMEM((2, 2, 2 * hh, 1024), BF)]
        + [pltpu.VMEM((2, 2, 2 * hh, 256), BF)] * 4
        + [pltpu.VMEM((2, 2, 2 * hh, 256), BF), pltpu.VMEM((2, 2, hh, 128), BF)]
    )


def finish_kernel(*refs):
    dkvp, dqp, dr_ref, gb, wall, gpay, zpay, zr, xs, x_ref = refs[:10]
    got = ((refs[10], refs[13]), (refs[11], refs[14]), (refs[12], refs[15]))

    gt, io_full, u_full, tail_full, s_vec = refs[16:21]
    io_refs = list(refs[21:32]) + [io_full]
    u_refs, tail_refs = list(refs[32:43]) + [u_full], list(refs[43:56]) + [tail_full]
    (dkv, zb, sb, dq, weights, ll2, rr2, lt2, mid, pay, ll, rr, tail, v0, vf, v1, vx, vy, vz, tx, ty,
     sz, rz, sw, rw, sn, rn, ss, rs, ls, lw) = refs[56:]
    scale = 1.0 / math.sqrt(16384)
    where = place()
    zl, x, y, zh, co = where
    w = zh * 2 + co
    me = lax.axis_index("ctx")
    flat = me % 16
    core = device(zl, x, y, zh, 1 - co)
    far = device(zl, x, y, 1 - zh, co)
    xp = [device(zl, (x + s) % 4, y, zh, co) for s in (1, 2, 3)]
    yp = [device(zl, x, (y + s) % 4, zh, co) for s in (1, 2, 3)]
    zp = device(1 - zl, x, y, zh, co)
    bar = pltpu.get_barrier_semaphore()

    def greet_one(i, carry):
        pl.semaphore_signal(bar, inc=1, device_id={"ctx": zl * 16 + (flat + i) % 16}, device_id_type=MESH)
        return carry

    for p in (core, far, zp):
        pl.semaphore_signal(bar, inc=1, device_id=p, device_id_type=MESH)
    lax.fori_loop(1, 16, greet_one, 0)

    mine = [pl.ds(pl.multiple_of(k * 256, 256), 256) for k in (w, (1 - zh) * 2 + co)]
    parts = []
    for h in range(2):
        for n in range(3):
            parts.append(pltpu.make_async_copy(got[n][h].at[:, :160], io_refs[0].at[h, n], ls.at[10 + 3 * h + n]))
    local = [
        pltpu.make_async_copy(gpay.at[:, :1024], ll2.at[0:128, :], ls.at[0]),
        pltpu.make_async_copy(zpay.at[:, 1024:2048], rr2.at[0:128, :], ls.at[1]),
        pltpu.make_async_copy(zr.at[:, :1024], ll2.at[256:384, :], ls.at[2]),
        pltpu.make_async_copy(zr.at[:, 1024:2048], rr2.at[256:384, :], ls.at[3]),
    ]
    for k in range(2):
        cols = slice(256 * k, 256 * k + 256)
        local.append(pltpu.make_async_copy(x_ref.at[:, mine[k]], ll.at[0:128, cols], ls.at[4 + k]))
        local.append(pltpu.make_async_copy(xs.at[k], ll.at[128:256, cols], ls.at[6 + k]))
    for c in local + parts:
        c.start()
    loads = [pltpu.make_async_copy(wall, weights, lw.at[0])]
    loads[0].start()
    pl.semaphore_wait(bar, 18)

    def narrow_copy(i):
        p = (flat + i) % 16
        return pltpu.make_async_remote_copy(
            src_ref=dqp.at[p], dst_ref=dq.at[flat], send_sem=sn.at[i], recv_sem=rn.at[i],
            device_id={"ctx": zl * 16 + p}, device_id_type=MESH,
        )

    def z_copy(i):
        return pltpu.make_async_remote_copy(
            src_ref=dkvp.at[(1 - zl) * 16 + (flat + i) % 16], dst_ref=zb.at[i], send_sem=sz.at[i], recv_sem=rz.at[i],
            device_id=zp, device_id_type=MESH,
        )

    def wide_copy(i):
        p = (flat + i) % 16
        return pltpu.make_async_remote_copy(
            src_ref=sb.at[i], dst_ref=dkv.at[flat], send_sem=sw.at[i], recv_sem=rw.at[i],
            device_id={"ctx": zl * 16 + p}, device_id_type=MESH,
        )

    def start(make):
        def one(i, carry):
            make(i).start()
            return carry
        return one

    def wait(make):
        def one(i, carry):
            make(i).wait()
            return carry
        return one

    def both(i):
        z_copy(i).wait_recv()
        return (dkvp[zl * 16 + (flat + i) % 16].astype(F32) + zb[i].astype(F32)).astype(BF)

    def pass_on(i, carry):
        sb[i] = both(i)
        wide_copy(i).start()
        return carry

    def sent(i, carry):
        z_copy(i).wait_send()
        return carry

    lax.fori_loop(1, 16, start(z_copy), 0)
    z_copy(0).start()
    lax.fori_loop(1, 16, start(narrow_copy), 0)
    home = [pltpu.make_async_copy(dqp.at[flat], dq.at[flat], ls.at[9])]
    for c in home:
        c.start()
    wire = Wire(ss, rs)
    near = [
        wire(gpay.at[:, 1024:], ll2.at[128:256, :], core),
        wire(zpay.at[:, 1024:2048], rr2.at[128:256, :], core),
        wire(zr.at[:, 2048:], ll2.at[384:512, :], core),
        wire(zr.at[:, 1024:2048], rr2.at[384:512, :], core),
    ]
    io = BegunSum(160, io_refs, wire, where, xp, yp, zp, far, *got).steps()
    big = FirstSum(mid, u_refs, wire, where, xp, yp, zp).steps()
    small = PairSum(tail, 96, tail_refs, wire, where, xp, yp, zp, far).steps()
    next(io)
    next(io)
    for c in local:
        c.wait()
    lt = ll[...].astype(F32).T.astype(BF)
    for c in near:
        c.wait()
    for k in range(4):
        lt2[256 * k:256 * k + 256, :] = ll2[:, 256 * k:256 * k + 256].astype(F32).T.astype(BF)
    for k in range(4):
        rows = slice(256 * k, 256 * k + 256)
        mid[rows, :] = dot(lt2[rows, :], rr2[...]).astype(BF)
    lax.fori_loop(1, 16, pass_on, 0)
    dkv[flat] = both(0)
    next(big)
    for c in parts:
        c.wait()
    next(io)

    for c in home:
        c.wait()
    lax.fori_loop(1, 16, wait(wide_copy), 0)
    lax.fori_loop(1, 16, wait(narrow_copy), 0)
    lax.fori_loop(0, 16, sent, 0)
    for h in range(16):
        lanes = slice(64 * h, 64 * h + 64)
        pair = dq[h]
        pay[:64, lanes] = pair[:, :64]
        pay[64:128, lanes] = pair[:, 64:]
        pair = dkv[h]
        pay[:128, 1024 + 64 * h:1088 + 64 * h] = pair[:, :64]
        pay[:128, 2048 + 64 * h:2112 + 64 * h] = pair[:, 64:]
    pay[128:144, :1024] = jnp.concatenate([gb[...], jnp.zeros((8, 1024), F32)], axis=0).astype(BF)
    pay[128:144, 1024:] = jnp.zeros((16, 2048), BF)
    to_core = wire(pay, rr, core)
    next(io)
    for c in loads:
        c.wait()
    for k in range(4):
        cols = slice(256 * k, 256 * k + 256)
        total = dr_ref[:, cols]
        for m in range(3):
            total += dot(pay[:128, 1024 * m:1024 * m + 1024], weights[k, m], NT)
        gt[:, cols] = total
    next(io)
    to_core.wait_recv()
    for z in range(2):
        for m in range(3):
            cols = slice(1024 * m, 1024 * m + 1024)
            total = dot(lt[256 * z:256 * z + 256, :128], pay[:128, cols])
            total += dot(lt[256 * z:256 * z + 256, 128:], rr[:128, cols])
            tail[z, 256 * m:256 * m + 256, :] = total.astype(BF)
    next(small)
    for z in range(2):
        v0[z] = (pay[128:144, mine[z]].astype(F32) + rr[128:144, mine[z]].astype(F32))[:8]
    vfar = wire(v0.at[1], vf, far)
    next(big)
    next(io)
    next(small)
    next(big)
    next(io)
    vfar.wait_recv()
    v1[...] = v0[0] + vf[...]
    vone = [wire(v1, vx.at[s], xp[s]) for s in range(3)]
    next(small)
    next(io)
    next(big)
    next(small)
    next(io)
    for c in vone:
        c.wait_recv()
    tx[...] = v1[...] + vx[0] + vx[1] + vx[2]
    vtwo = [wire(tx, vy.at[s], yp[s]) for s in range(3)]
    next(small)
    next(big)
    next(io)
    next(small)
    next(big)
    for c in vtwo:
        c.wait_recv()
    ty[...] = tx[...] + vy[0] + vy[1] + vy[2]
    vthree = wire(ty, vz, zp)
    next(small)
    next(big)
    next(small)
    next(big)
    next(io)
    next(small)
    next(small)
    next(big)
    vthree.wait()
    s_vec[...] = (ty[...] + vz[...]) * scale
    for c in vone + vtwo + [to_core, vfar]:
        c.wait_send()
    next(small)
    next(io)
    next(big)
    next(small)


def finish(dkvp, dqp, dr, gb, wall, gpay, zpay, zr, xs, tok, parts):
    n = SUM_COPIES + BEGUN_COPIES + PAIR_COPIES + 4 + 2 + 7
    return pl.pallas_call(
        finish_kernel,
        out_shape=[
            shp((128, 1024), F32), shp((1280, 1024), BF), shp((1024, 1024), BF), shp((768, 1024), BF), shp((8, 256), F32),
        ],
        in_specs=[VM, ANY, VM, VM] + [ANY] * 12,
        out_specs=[VM] * 5,
        scratch_shapes=pair_scratch(1280, True) + first_scratch() + pair_scratch(768, False) + [
            pltpu.VMEM((16, 128, 128), BF), pltpu.VMEM((16, 128, 128), BF), pltpu.VMEM((16, 128, 128), BF),
            pltpu.VMEM((16, 64, 128), BF), pltpu.VMEM((4, 3, 256, 1024), BF),
            pltpu.VMEM((512, 1024), BF), pltpu.VMEM((512, 1024), BF), pltpu.VMEM((1024, 512), BF),
            pltpu.VMEM((1024, 1024), BF), pltpu.VMEM((144, 3072), BF),
            pltpu.VMEM((256, 512), BF), pltpu.VMEM((144, 3072), BF), pltpu.VMEM((2, 768, 1024), BF),
            pltpu.VMEM((2, 8, 256), F32), pltpu.VMEM((8, 256), F32), pltpu.VMEM((8, 256), F32),
            pltpu.VMEM((3, 8, 256), F32), pltpu.VMEM((3, 8, 256), F32),
            pltpu.VMEM((8, 256), F32), pltpu.VMEM((8, 256), F32), pltpu.VMEM((8, 256), F32),
            DMA((16,)), DMA((16,)), DMA((16,)), DMA((16,)), DMA((16,)), DMA((16,)),
            DMA((n,)), DMA((n,)), DMA((16,)), DMA((1,)),
        ],
        compiler_params=pltpu.CompilerParams(collective_id=6, has_side_effects=True, vmem_limit_bytes=LIMIT),
        name="finish",
    )(dkvp, dqp, dr, gb, wall, gpay, zpay, zr, xs, tok, *parts)


def scale_kernel(o, i0, i1, i2, i3, u, q, k, v, out_q, out_k, out_v, out_o, out_i, out_u):
    scale = 1.0 / math.sqrt(16384)
    for src, dst in ((q, out_q), (k, out_k), (v, out_v), (o, out_o), (u, out_u)):
        dst[...] = src[...].astype(F32) * scale
    for n, src in enumerate((i0, i1, i2, i3)):
        out_i[:, 1024 * n:1024 * n + 1024] = src[...].astype(F32) * scale


def scaled(io, u, tail):
    def rows(first, n=32):
        return pl.BlockSpec((n, 1024), lambda j: (first // n + j, 0))

    return pl.pallas_call(
        scale_kernel,
        grid=(8,),
        out_shape=[shp((256, 1024), F32)] * 4 + [shp((256, 4096), F32), shp((1024, 1024), F32)],
        in_specs=[rows(0)] + [rows(256 + 256 * k) for k in range(4)] + [rows(0, 128)] + [rows(256 * k) for k in range(3)],
        out_specs=[rows(0)] * 4 + [pl.BlockSpec((32, 4096), lambda j: (j, 0)), rows(0, 128)],
        compiler_params=pltpu.CompilerParams(vmem_limit_bytes=LIMIT),
        name="scaled",
    )(*[io] * 5, u, *[tail] * 3)


FLIP_CORE = [(0, 1), (1, 0), (2, 3), (3, 2)]
FLIP_FAR = [(0, 2), (2, 0), (1, 3), (3, 1)]


def along_x(s):
    return [(c, c // 16 * 16 + (c // 4 + s) % 4 * 4 + c % 4) for c in range(32)]


def along_y(s):
    return [(c, c // 4 * 4 + (c + s) % 4) for c in range(32)]


def body(
    tokens, w_query, w_key, w_value, w_output, w_inner, w_outer, ln_gain, ln_bias, block_mask, block_pairs, cotangent,
):
    tok = tokens.reshape(128, 1024)
    cot = cotangent.reshape(128, 1024)
    lnp = jnp.concatenate([ln_gain, ln_bias, jnp.zeros((4, 256), F32)], axis=0)
    blk = block_pairs.reshape(-1)
    own = (w_query, w_key, w_value)
    outer = w_outer.reshape(8, 4, 32, 1024)
    wall, xs, lnf, *rest = front(tok, own, lnp, w_output, w_inner, outer)
    core_shard, (qa, qb, diag_a, diag_b, kvr, qr) = rest[:3], rest[3:]
    x1, x3 = (lax.ppermute(qa, "ctx", along_x(s)) for s in (1, 3))
    y1, y3 = (lax.ppermute(qb, "ctx", along_y(s)) for s in (1, 3))
    o, ot, lse = attend(blk, block_mask, kvr, qr)
    x1, x3, y1, y3, o = lax.optimization_barrier((x1, x3, y1, y3, o))
    y_out, dr1, zpay, gpay, gb, dor, own_a, plus_a, minus_a, own_b, plus_b, minus_b = heart(
        o, tok, cot, lnf, lnp, ((w_output, w_inner, outer), core_shard), (qa, x1, x3, qb, y1, y3, diag_a, diag_b)
    )
    zr = lax.ppermute(zpay, "wsh", FLIP_FAR)
    plus_a = lax.ppermute(plus_a, "ctx", along_x(1))
    minus_a = lax.ppermute(minus_a, "ctx", along_x(3))
    plus_b = lax.ppermute(plus_b, "ctx", along_y(1))
    minus_b = lax.ppermute(minus_b, "ctx", along_y(3))
    dkvp, dqp = attend_back(blk, block_mask, kvr, qr, dor, ot, lse)
    zr, plus_a, minus_a, plus_b, minus_b, dkvp = lax.optimization_barrier((zr, plus_a, minus_a, plus_b, minus_b, dkvp))
    grad_tok, io, u, tail, s_vec = finish(
        dkvp, dqp, dr1, gb, wall, gpay, zpay, zr, xs, tok, (own_a, plus_a, minus_a, own_b, plus_b, minus_b)
    )
    s_q, s_k, s_v, s_o, s_i, s_u = scaled(io, u, tail)
    out_shape = tokens.shape
    return (
        y_out.reshape(out_shape), grad_tok.reshape(out_shape), s_q, s_k, s_v, s_o, s_i, s_u, s_vec[0:2], s_vec[2:4],
    )


def solution(mesh):
    return jax.shard_map(
        body,
        mesh=mesh,
        in_specs=(
            P("wsh", "ctx", None, None),
            P("wsh", None), P("wsh", None), P("wsh", None), P("wsh", None), P("wsh", None), P("wsh", None),
            P(None, "wsh"), P(None, "wsh"),
            P("wsh", None, None),
            P(),
            P("wsh", "ctx", None, None),
        ),
        out_specs=(
            P("wsh", "ctx", None, None), P("wsh", "ctx", None, None),
            P("wsh", None), P("wsh", None), P("wsh", None), P("wsh", None), P("wsh", None), P("wsh", None),
            P(None, "wsh"), P(None, "wsh"),
        ),
        check_vma=False,
    )
```

```python
import math

import jax
import jax.numpy as jnp
from jax import lax
from jax.experimental import pallas as pl
from jax.experimental.pallas import tpu as pltpu
from jax.sharding import PartitionSpec as P

MESH = pl.DeviceIdType.MESH
BF = jnp.bfloat16
F32 = jnp.float32
ANY = pl.BlockSpec(memory_space=pl.ANY)
VM = pl.BlockSpec(memory_space=pltpu.VMEM)
SM = pl.BlockSpec(memory_space=pltpu.SMEM)
DMA = pltpu.SemaphoreType.DMA
LIMIT = 56 * 1024 * 1024
EPS = 1e-05
NEG = -1e30


def shp(shape, dtype):
    return jax.ShapeDtypeStruct(shape, dtype)


def dot(a, b, dims=((1,), (0,))):
    return lax.dot_general(a, b, (dims, ((), ())), preferred_element_type=F32)


NN = ((1,), (0,))
NT = ((1,), (1,))
TN = ((0,), (0,))


def place():
    c = lax.axis_index("ctx")
    w = lax.axis_index("wsh")
    return c // 16, (c // 4) % 4, c % 4, w // 2, w % 2


def device(zl, x, y, zh, co):
    return {"ctx": zl * 16 + x * 4 + y, "wsh": zh * 2 + co}


def greet(peers):
    bar = pltpu.get_barrier_semaphore()
    for p in peers:
        pl.semaphore_signal(bar, inc=1, device_id=p, device_id_type=MESH)
    pl.semaphore_wait(bar, len(peers))


class Wire:
    def __init__(self, send, recv):
        self.send, self.recv, self.n = send, recv, 0

    def __call__(self, src, dst, peer):
        k = self.n
        self.n += 1
        copy = pltpu.make_async_remote_copy(
            src_ref=src, dst_ref=dst, send_sem=self.send.at[k], recv_sem=self.recv.at[k],
            device_id=peer, device_id_type=MESH,
        )
        copy.start()
        return copy


def front_kernel(*refs):
    x_ref, wq, wk, wv, x_any, ln_ref, wo, wi, wu = refs[:9]
    wall, xs, lnf, co_ref, ci_ref, cu_ref, qa_ref, qb_ref, da_ref, db_ref, kvr, qr = refs[9:21]
    weights, acc, kvp, qp, ss, rs, sw, rw, sf, rf, sn, rn, ls = refs[21:]
    zl, x, y, zh, co = place()
    me = zh * 2 + co
    slots = [me, zh * 2 + 1 - co, (1 - zh) * 2 + co, (1 - zh) * 2 + 1 - co]
    here = lax.axis_index("ctx")
    flat = here % 16
    core = device(zl, x, y, zh, 1 - co)
    far = device(zl, x, y, 1 - zh, co)
    diag = device(zl, x, y, 1 - zh, 1 - co)
    zp = device(1 - zl, x, y, zh, co)
    xp = [device(zl, (x + s) % 4, y, zh, co) for s in (1, 2, 3)]
    yp = [device(zl, x, (y + s) % 4, zh, co) for s in (1, 2, 3)]
    bar = pltpu.get_barrier_semaphore()

    def greet_one(i, carry):
        pl.semaphore_signal(bar, inc=1, device_id={"ctx": zl * 16 + (flat + i) % 16}, device_id_type=MESH)
        return carry

    for p in (far, core, diag, zp):
        pl.semaphore_signal(bar, inc=1, device_id=p, device_id_type=MESH)
    lax.fori_loop(1, 16, greet_one, 0)
    ws = (wq, wk, wv)
    local = [pltpu.make_async_copy(ws[m], weights.at[me, m], ls.at[m]) for m in range(3)]
    for c in local:
        c.start()
    pl.semaphore_wait(bar, 19)
    wire = Wire(ss, rs)
    rows_a = pl.ds(pl.multiple_of(x * 32, 32), 32)
    rows_b = pl.ds(pl.multiple_of(128 + y * 32, 32), 32)
    first_a, first_b = [], []
    for m in range(3):
        first_a.append(wire(ws[m].at[rows_a], weights.at[me, m, rows_a], far))
        first_b.append(wire(ws[m].at[rows_b], weights.at[me, m, rows_b], far))
    near = [wire(ws[m], weights.at[me, m], core) for m in range(3)]
    quarters = []
    for ref, k, n in ((qa_ref, x, y), (qb_ref, 4 + y, x)):
        rows = pl.ds(pl.multiple_of(k * 32, 32), 32)
        cols = pl.ds(pl.multiple_of(n * 256, 256), 256)
        quarters.append(wire(wo.at[rows, cols], ref.at[0, :, cols], far))
        for b in range(4):
            at = pl.ds(pl.multiple_of(1024 * b + n * 256, 256), 256)
            quarters.append(wire(wi.at[rows, at], ref.at[1 + b, :, cols], far))
        quarters.append(wire(wu.at[k, :, :, cols], ref.at[5:9, :, cols], far))
    rest = []
    for p in (core, far, diag):
        rest.append(wire(ln_ref, lnf.at[me], p))
    for n, idx in enumerate((slots[1], slots[3])):
        rest.append(wire(x_any.at[:, pl.ds(pl.multiple_of(idx * 256, 256), 256)], xs.at[n], core))

    def add(k, fresh):
        cols = x_ref[:, pl.ds(pl.multiple_of(slots[k] * 256, 256), 256)]
        for m in range(3):
            part = dot(cols, weights[slots[k], m])
            acc[m] = part if fresh else acc[m] + part

    for c in first_a:
        c.wait_recv()
    second = []
    for m in range(3):
        part = weights.at[slots[2], m, rows_a]
        for p in xp:
            second.append(wire(part, part, p))
    for c in first_b:
        c.wait_recv()
    for m in range(3):
        part = weights.at[slots[2], m, rows_b]
        for p in yp:
            second.append(wire(part, part, p))
    for c in local:
        c.wait()
    add(0, True)
    for c in near:
        c.wait_recv()
    add(1, False)
    for c in quarters:
        c.wait_recv()
    subs = []
    for ref, n, peers in ((qa_ref, y, yp), (qb_ref, x, xp)):
        spot = ref.at[:, :, pl.ds(pl.multiple_of(n * 256, 256), 256)]
        for p in peers:
            subs.append(wire(spot, spot, p))
    for c in second:
        c.wait_recv()
    last = [wire(weights.at[slots[2], m], weights.at[slots[2], m], core) for m in range(3)]
    add(2, False)
    for c in last:
        c.wait_recv()
    add(3, False)
    keep = pltpu.make_async_copy(weights, wall, ls.at[0])
    keep.start()
    for j in range(8):
        lanes = slice(128 * j, 128 * j + 128)
        q = (acc[0, :, lanes].astype(BF).astype(F32) * 0.125).astype(BF)
        k = acc[1, :, lanes].astype(BF)
        v = acc[2, :, lanes].astype(BF)
        for u in range(2):
            part = slice(64 * u, 64 * u + 64)
            kvp[2 * j + u] = jnp.concatenate([k[:, part], v[:, part]], axis=1)
            qp[2 * j + u] = jnp.concatenate([q[:64, part], q[64:, part]], axis=1)

    def plane(i):
        return {"ctx": zl * 16 + (flat + i) % 16}

    def wide_copy(i):
        return pltpu.make_async_remote_copy(
            src_ref=kvp.at[(flat + i) % 16], dst_ref=kvr.at[here], send_sem=sw.at[i], recv_sem=rw.at[i],
            device_id=plane(i), device_id_type=MESH,
        )

    def narrow_copy(i):
        return pltpu.make_async_remote_copy(
            src_ref=qp.at[(flat + i) % 16], dst_ref=qr.at[flat], send_sem=sn.at[i], recv_sem=rn.at[i],
            device_id=plane(i), device_id_type=MESH,
        )

    def pass_copy(i):
        spot = kvr.at[zl * 16 + (flat + 16 - i) % 16]
        return pltpu.make_async_remote_copy(
            src_ref=spot, dst_ref=spot, send_sem=sf.at[i], recv_sem=rf.at[i], device_id=zp, device_id_type=MESH,
        )

    def start_wide(i, carry):
        wide_copy(i).start()
        return carry

    def start_narrow(i, carry):
        narrow_copy(i).start()
        return carry

    def pass_on(i, carry):
        wide_copy(i).wait_recv()
        pass_copy(i).start()
        return carry

    def wait_all(i, carry):
        wide_copy(i).wait_send()
        narrow_copy(i).wait()
        pass_copy(i).wait()
        return carry

    to_z = wire(kvp.at[flat], kvr.at[here], zp)
    lax.fori_loop(1, 16, start_wide, 0)
    lax.fori_loop(1, 16, start_narrow, 0)
    home = [
        pltpu.make_async_copy(kvp.at[flat], kvr.at[here], ls.at[1]),
        pltpu.make_async_copy(qp.at[flat], qr.at[flat], ls.at[2]),
    ]
    for c in home:
        c.start()
    for src, dst in ((wo, co_ref), (wi, ci_ref), (wu, cu_ref)):
        rest.append(wire(src, dst, core))
    lax.fori_loop(1, 16, pass_on, 0)
    for c in subs:
        c.wait_recv()
    for src, dst in ((qa_ref, da_ref), (qb_ref, db_ref)):
        rest.append(wire(src, dst, core))
    for c in home:
        c.wait()
    keep.wait()
    lax.fori_loop(1, 16, wait_all, 0)
    to_z.wait()
    for c in first_a + first_b + near + second + last + quarters + subs:
        c.wait_send()
    for c in rest:
        c.wait()


def front(tok, own, lnp, wo, wi, wu):
    n = 6 + 3 + 12 + 3 + 2 + 18 + 3 + 1 + 6 + 3 + 2
    piece = shp((9, 32, 1024), BF)
    return pl.pallas_call(
        front_kernel,
        out_shape=[shp((4, 3, 256, 1024), BF), shp((2, 128, 256), BF), shp((4, 8, 256), F32)]
        + [shp(wo.shape, BF), shp(wi.shape, BF), shp(wu.shape, BF)] + [piece] * 4
        + [shp((32, 128, 128), BF), shp((16, 64, 128), BF)],
        in_specs=[VM] + [ANY] * 8,
        out_specs=[ANY] * 12,
        scratch_shapes=[
            pltpu.VMEM((4, 3, 256, 1024), BF), pltpu.VMEM((3, 128, 1024), F32),
            pltpu.VMEM((16, 128, 128), BF), pltpu.VMEM((16, 64, 128), BF),
            DMA((n,)), DMA((n,)), DMA((16,)), DMA((16,)), DMA((16,)), DMA((16,)), DMA((16,)), DMA((16,)), DMA((3,)),
        ],
        compiler_params=pltpu.CompilerParams(collective_id=1, has_side_effects=True, vmem_limit_bytes=LIMIT),
        cost_estimate=pl.CostEstimate(flops=16 << 30, bytes_accessed=32 << 20, transcendentals=0),
        name="front",
    )(tok, *own, tok, lnp, wo, wi, wu)


def attention_setup(blk, mask, kvr, qr, kvs, kaug, kvt, bias, qs, inv, order, oblk):
    first = (lax.axis_index("ctx") // 16) * 32

    def note(s, carry):
        inv[blk[s]] = s
        return carry

    lax.fori_loop(0, 64, note, 0)

    def pick(b, count):
        local = inv[b] - first
        order[count] = local
        oblk[count] = b
        mine = jnp.logical_and(local >= 0, local < 32)
        return count + mine.astype(jnp.int32)

    lax.fori_loop(0, 64, pick, 0)
    for s in range(64):
        at = pl.ds(pl.multiple_of(blk[s] * 64, 64), 64)
        kvs[at, :] = kvr[s // 2, (s % 2) * 64:(s % 2) * 64 + 64, :]
    for j in range(16):
        pair = qr[j]
        qs[2 * j] = pair[:, :64]
        qs[2 * j + 1] = pair[:, 64:]
    rows = lax.broadcasted_iota(jnp.int32, (512, 64), 0) // 64
    lanes = lax.broadcasted_iota(jnp.int32, (512, 64), 1)
    for c in range(8):
        part = kvs[512 * c:512 * c + 512, :]
        hot = jnp.where(rows + 8 * c == lanes, 1.0, 0.0).astype(BF)
        kaug[512 * c:512 * c + 512, :] = jnp.concatenate([part[:, :64], hot], axis=1)
        kvt[c] = part.astype(F32).T.astype(BF)
    qi = lax.broadcasted_iota(jnp.int32, (64, 64), 0)
    ki = lax.broadcasted_iota(jnp.int32, (64, 64), 1)
    bias[...] = jnp.where(jnp.logical_and(mask[0] != 0, ki < qi), 0.0, NEG)


def triangle():
    key = lax.broadcasted_iota(jnp.int32, (64, 256), 0)
    query = lax.broadcasted_iota(jnp.int32, (64, 256), 1) % 64
    return key <= query


def attend_kernel(
    blk, mask, kvr, qr, o_ref, ot_ref, lse_ref, kvs, kaug, kvt, bias, qs, qa, os, inv, order, oblk, tops, totals, mixes
):
    attention_setup(blk, mask, kvr, qr, kvs, kaug, kvt, bias, qs, inv, order, oblk)

    def diagonal(g):
        score, vals = [], []
        for u in range(4):
            i = oblk[4 * g + u]
            q = qs[order[4 * g + u]]
            row = jnp.broadcast_to(bias[pl.ds(i, 1), :], (64, 64)).astype(BF)
            qa[g, 64 * u:64 * u + 64, :] = jnp.concatenate([q, row], axis=1)
            kv = kvs[pl.ds(pl.multiple_of(i * 64, 64), 64), :]
            score.append(dot(kv[:, :64], q, NT))
            vals.append(kv[:, 64:])
        s = jnp.where(triangle(), jnp.concatenate(score, axis=1), NEG)
        top = jnp.max(s, axis=0, keepdims=True)
        p = jnp.exp(s - top)
        total = jnp.sum(p, axis=0, keepdims=True)
        pb = p.astype(BF)
        mix = jnp.concatenate([dot(vals[u], pb[:, 64 * u:64 * u + 64], TN) for u in range(4)], axis=1)
        tops[g], totals[g], mixes[g] = top, total, mix

    def diagonals(k, carry):
        for j in range(4):
            diagonal(4 * k + j)
        return carry

    lax.fori_loop(0, 2, diagonals, 0)

    def tile(g, carry):
        top, total, mix = tops[g], totals[g], mixes[g]
        queries = qa[g]

        def chunk(c, state):
            top, total, mix = state
            keys = kaug[pl.ds(pl.multiple_of(c * 512, 512), 512), :]
            s = dot(keys, queries, NT)
            new = jnp.maximum(top, jnp.max(s, axis=0, keepdims=True))
            shrink = jnp.exp(top - new)
            p = jnp.exp(s - new)
            total = total * shrink + jnp.sum(p, axis=0, keepdims=True)
            mix = mix * shrink + dot(kvt[c, 64:, :], p.astype(BF))
            return new, total, mix

        chunks = (oblk[4 * g + 3] + 7) // 8
        def pair(c, state):
            top, total, mix = state
            parts = [dot(kaug[pl.ds(pl.multiple_of(c * 1024 + 512 * k, 512), 512), :], queries, NT) for k in range(2)]
            new = top
            for s in parts:
                new = jnp.maximum(new, jnp.max(s, axis=0, keepdims=True))
            shrink = jnp.exp(top - new)
            total, mix = total * shrink, mix * shrink
            for k, s in enumerate(parts):
                p = jnp.exp(s - new)
                total += jnp.sum(p, axis=0, keepdims=True)
                mix += dot(kvt[2 * c + k, 64:, :], p.astype(BF))
            return new, total, mix

        top, total, mix = lax.fori_loop(0, chunks // 2, pair, (top, total, mix))
        top, total, mix = lax.fori_loop(chunks // 2 * 2, chunks, chunk, (top, total, mix))
        out = mix / total
        ot_ref[g] = out
        lse_ref[g] = top + jnp.log(total)
        back = out.T.astype(BF)
        for u in range(4):
            os[order[4 * g + u]] = back[64 * u:64 * u + 64, :]
        return carry

    lax.fori_loop(0, 8, tile, 0)
    for j in range(16):
        o_ref[j] = jnp.concatenate([os[2 * j], os[2 * j + 1]], axis=1)


def attention_scratch():
    return [
        pltpu.VMEM((4096, 128), BF),
        pltpu.VMEM((4096, 128), BF),
        pltpu.VMEM((8, 128, 512), BF),
        pltpu.VMEM((64, 64), F32),
        pltpu.VMEM((32, 64, 64), BF),
        pltpu.VMEM((8, 256, 128), BF),
        pltpu.VMEM((32, 64, 64), BF),
        pltpu.SMEM((64,), jnp.int32),
        pltpu.SMEM((72,), jnp.int32),
        pltpu.SMEM((72,), jnp.int32),
    ]


def attend(blk, mask, kvr, qr):
    return pl.pallas_call(
        attend_kernel,
        out_shape=[shp((16, 64, 128), BF), shp((8, 64, 256), F32), shp((8, 1, 256), F32)],
        in_specs=[SM, VM, VM, VM],
        out_specs=[VM] * 3,
        scratch_shapes=attention_scratch()
        + [pltpu.VMEM((8, 1, 256), F32), pltpu.VMEM((8, 1, 256), F32), pltpu.VMEM((8, 64, 256), F32)],
        compiler_params=pltpu.CompilerParams(vmem_limit_bytes=LIMIT),
        cost_estimate=pl.CostEstimate(flops=10 << 30, bytes_accessed=32 << 20, transcendentals=4 << 20),
        name="attend",
    )(blk, mask, kvr, qr)


def attend_back_kernel(
    blk, mask, kvr, qr, dor, ot_ref, lse_ref, dkv_ref, dq_ref,
    kvs, kaug, kvt, bias, qs, qa, dqs, inv, order, oblk, dos, qz, dz, dkv, deltas, dqt,
):
    attention_setup(blk, mask, kvr, qr, kvs, kaug, kvt, bias, qs, inv, order, oblk)
    for j in range(16):
        pair = dor[j]
        dos[2 * j] = pair[:, :64]
        dos[2 * j + 1] = pair[:, 64:]
    dkv[...] = jnp.zeros_like(dkv)
    zero = jnp.zeros((64, 64), BF)

    def diagonal(g):
        score, dprob, places, keys_own, q_own, d_own = [], [], [], [], [], []
        for u in range(4):
            i = oblk[4 * g + u]
            q = qs[order[4 * g + u]]
            do = dos[order[4 * g + u]]
            rows = slice(64 * u, 64 * u + 64)
            row = jnp.broadcast_to(bias[pl.ds(i, 1), :], (64, 64)).astype(BF)
            qa[g, rows, :] = jnp.concatenate([q, row], axis=1)
            qz[g, rows, :] = jnp.concatenate([q, zero], axis=1)
            dz[g, rows, :] = jnp.concatenate([zero, do], axis=1)
            at = pl.ds(pl.multiple_of(i * 64, 64), 64)
            kv = kvs[at, :]
            score.append(dot(kv[:, :64], q, NT))
            dprob.append(dot(kv[:, 64:], do, NT))
            places.append(at)
            keys_own.append(kv[:, :64])
            q_own.append(q)
            d_own.append(do)
        lse = lse_ref[g]
        dot_t = dz[g][:, 64:].astype(F32).T
        delta = jnp.sum(ot_ref[g] * dot_t, axis=0, keepdims=True)
        s = jnp.where(triangle(), jnp.concatenate(score, axis=1), NEG)
        p = jnp.exp(s - lse)
        ds = (p * (jnp.concatenate(dprob, axis=1) - delta)).astype(BF)
        pb = p.astype(BF)
        dq = []
        for u in range(4):
            lanes = slice(64 * u, 64 * u + 64)
            grad = jnp.concatenate([dot(ds[:, lanes], q_own[u]), dot(pb[:, lanes], d_own[u])], axis=1)
            dkv[places[u], :] += grad
            dq.append(dot(keys_own[u], ds[:, lanes], TN))
        deltas[g] = delta
        dqt[g] = jnp.concatenate(dq, axis=1)

    def diagonals(k, carry):
        for j in range(4):
            diagonal(4 * k + j)
        return carry

    lax.fori_loop(0, 2, diagonals, 0)

    def tile(g, carry):
        lse, delta = lse_ref[g], deltas[g]
        queries, qpad, dpad = qa[g], qz[g], dz[g]

        def chunk(c, dq):
            at = pl.ds(pl.multiple_of(c * 512, 512), 512)
            p = jnp.exp(dot(kaug[at, :], queries, NT) - lse)
            dp = dot(kvs[at, :], dpad, NT)
            ds = (p * (dp - delta)).astype(BF)
            dkv[at, :] += dot(ds, qpad) + dot(p.astype(BF), dpad)
            return dq + dot(kvt[c, :64, :], ds)

        chunks = (oblk[4 * g + 3] + 7) // 8
        dq = lax.fori_loop(0, chunks // 2, lambda c, dq: chunk(2 * c + 1, chunk(2 * c, dq)), dqt[g])
        dq = lax.fori_loop(chunks // 2 * 2, chunks, chunk, dq)
        back = (dq * 0.125).T.astype(BF)
        for u in range(4):
            dqs[order[4 * g + u]] = back[64 * u:64 * u + 64, :]
        return carry

    lax.fori_loop(0, 8, tile, 0)
    for j in range(16):
        dq_ref[j] = jnp.concatenate([dqs[2 * j], dqs[2 * j + 1]], axis=1)
    for s in range(64):
        at = pl.ds(pl.multiple_of(blk[s] * 64, 64), 64)
        dkv_ref[s // 2, (s % 2) * 64:(s % 2) * 64 + 64, :] = dkv[at, :].astype(BF)


def attend_back(blk, mask, kvr, qr, dor, ot, lse):
    return pl.pallas_call(
        attend_back_kernel,
        out_shape=[shp((32, 128, 128), BF), shp((16, 64, 128), BF)],
        in_specs=[SM] + [VM] * 6,
        out_specs=[VM] * 2,
        scratch_shapes=attention_scratch()
        + [
            pltpu.VMEM((32, 64, 64), BF),
            pltpu.VMEM((8, 256, 128), BF),
            pltpu.VMEM((8, 256, 128), BF),
            pltpu.VMEM((4096, 128), F32),
            pltpu.VMEM((8, 1, 256), F32),
            pltpu.VMEM((8, 64, 256), F32),
        ],
        compiler_params=pltpu.CompilerParams(vmem_limit_bytes=LIMIT),
        cost_estimate=pl.CostEstimate(flops=1 << 30, bytes_accessed=4 << 20, transcendentals=0),
        name="attend_back",
    )(blk, mask, kvr, qr, dor, ot, lse)


def norm_parts(v):
    center = v - jnp.mean(v, axis=1, keepdims=True)
    r = lax.rsqrt(jnp.mean(center * center, axis=1, keepdims=True) + EPS)
    return center * r, r


def norm_back(e, gain, z, r):
    g = e * gain
    return r * (g - jnp.mean(g, axis=1, keepdims=True) - z * jnp.mean(g * z, axis=1, keepdims=True))


def heart_kernel(*refs):
    o_ref, x_ref, e_ref, ln_ref, ln_own = refs[:5]
    shards = (refs[5:8], refs[8:11])
    qa, x1, x3, qb, y1, y3, diag_a, diag_b = refs[11:19]
    y_ref, dr_ref, zpay, gpay, gb_ref, dor = refs[19:25]
    cuts = (refs[25:28], refs[28:31])
    (wo, wi, wu, us, gs, nl, ob, orx, dos, rr, ll, cl, lt, mid,
     sw, sp, ss, rs, send_o, recv_o, send_do, recv_do, ls, lo) = refs[31:]
    zl, x, y, zh, co = place()
    w = zh * 2 + co
    flat = lax.axis_index("ctx") % 16
    where = [w, zh * 2 + 1 - co, (1 - zh) * 2 + co, (1 - zh) * 2 + 1 - co]
    core = device(zl, x, y, zh, 1 - co)
    bar = pltpu.get_barrier_semaphore()

    def plane(i):
        return {"ctx": zl * 16 + (flat + i) % 16}

    def greet_one(i, carry):
        pl.semaphore_signal(bar, inc=1, device_id=plane(i), device_id_type=MESH)
        return carry

    pl.semaphore_signal(bar, inc=1, device_id=core, device_id_type=MESH)
    lax.fori_loop(1, 16, greet_one, 0)
    copies = [[], [], []]
    for r, (a, b, c) in enumerate(shards):
        rows = pl.ds(pl.multiple_of(where[r] * 256, 256), 256)
        copies[0].append(pltpu.make_async_copy(a, wo.at[rows], sw.at[r, 0]))
        for k in range(4):
            cols = slice(1024 * k, 1024 * k + 1024)
            copies[1].append(pltpu.make_async_copy(b.at[:, cols], wi.at[k, rows], sw.at[r, 1 + k]))
        groups = pl.ds(where[r] * 8, 8)
        copies[2].append(pltpu.make_async_copy(c, wu.at[groups], sw.at[r, 5]))

    def spots(t, h, q):
        rows = pl.ds(pl.multiple_of(t * 256 + h * 128 + q * 32, 32), 32)
        return wo.at[rows], wi.at[:, rows], wu.at[t * 8 + h * 4 + q]

    quarters = [(qa, 0, x), (x1, 0, (x + 3) % 4), (x3, 0, (x + 1) % 4)]
    quarters += [(qb, 1, y), (y1, 1, (y + 3) % 4), (y3, 1, (y + 1) % 4)]
    held = [(where[2],) + q for q in quarters] + [(where[3], diag_a, 0, x), (where[3], diag_b, 1, y)]
    for n, (t, ref, h, q) in enumerate(held):
        to = spots(t, h, q)
        for k, src in enumerate((ref.at[0], ref.at[1:5], ref.at[5:9])):
            copies[k].append(pltpu.make_async_copy(src, to[k], sp.at[n, k]))
    for group in copies:
        for c in group:
            c.start()
    pl.semaphore_wait(bar, 16)
    wire = Wire(ss, rs)

    def over(src, dst, send, recv):
        def copy(i):
            return pltpu.make_async_remote_copy(
                src_ref=src.at[(flat + i) % 16], dst_ref=dst.at[flat], send_sem=send.at[i], recv_sem=recv.at[i],
                device_id=plane(i), device_id_type=MESH,
            )

        def start_one(i, carry):
            copy(i).start()
            return carry

        def wait_one(i, carry):
            copy(i).wait()
            return carry

        return start_one, wait_one

    start_o, wait_o = over(o_ref, orx, send_o, recv_o)
    lax.fori_loop(1, 16, start_o, 0)
    home = pltpu.make_async_copy(o_ref.at[flat], orx.at[flat], ls.at[0])
    home.start()
    shared = [[], [], []]
    passed = [[], [], []]
    ends = (
        (device(zl, (x + 1) % 4, y, zh, co), device(zl, (x + 3) % 4, y, zh, co)),
        (device(zl, x, (y + 1) % 4, zh, co), device(zl, x, (y + 3) % 4, zh, co)),
    )
    for k in range(3):
        for h in range(2):
            (one, _, q1), (three, _, q3) = quarters[3 * h + 1], quarters[3 * h + 2]
            up_to, down_to = spots(where[2], h, q1)[k], spots(where[2], h, q3)[k]
            if k == 0:
                passed[k].append([wire(one.at[0], up_to, ends[h][0])])
            else:
                first = 4 * k - 3
                passed[k].append([
                    wire(one.at[first:first + 2], up_to.at[0:2], ends[h][0]),
                    wire(three.at[first + 2:first + 4], down_to.at[2:4], ends[h][1]),
                ])
    for k in range(3):
        for n in (1, 2, 4, 5):
            ref, h, q = quarters[n]
            src = (ref.at[0], ref.at[1:5], ref.at[5:9])[k]
            shared[k].append(wire(src, spots(where[2], h, q)[k], core))

    def loaded(k):
        for c in copies[k]:
            c.wait()
        for c in shared[k]:
            c.wait_recv()

    home.wait()
    lax.fori_loop(1, 16, wait_o, 0)

    def pass_on(k):
        for h, at in enumerate((x, y)):
            for c in passed[k][h]:
                c.wait_recv()
            spot = spots(where[2], h, (at + 2) % 4)[k]
            shared[k].append(wire(spot, spot, core))

    pass_on(0)
    ln = jnp.concatenate([jnp.where(w == k, ln_own[...], ln_ref[k]) for k in range(4)], axis=1)
    gain0, gain1, bias0, bias1 = (ln[k:k + 1, :] for k in range(4))
    for h in range(16):
        pair = orx[h]
        ob[:64, 64 * h:64 * h + 64] = pair[:, :64]
        ob[64:, 64 * h:64 * h + 64] = pair[:, 64:]
    loaded(0)
    z0, r0 = norm_parts(x_ref[...].astype(F32) + dot(ob[...], wo[...]))
    n1 = z0 * gain0 + bias0
    nl[...] = n1.astype(BF)
    pass_on(1)
    loaded(1)
    pass_on(2)

    half = math.sqrt(0.5)

    def up(c, carry):
        u = dot(nl[...], wi[c])
        us[c] = u
        gs[:, pl.ds(pl.multiple_of(c * 1024, 1024), 1024)] = (0.5 * u * (1.0 + lax.erf(u * half))).astype(BF)
        return carry

    lax.fori_loop(0, 4, up, 0)
    loaded(2)

    def down(c, total):
        cols = pl.ds(pl.multiple_of(c * 1024, 1024), 1024)
        return total + dot(gs[:, cols], wu[pl.ds(c * 8, 8)].reshape(1024, 1024))

    r2 = lax.fori_loop(0, 4, down, n1)
    z1, r1 = norm_parts(r2)
    y_ref[...] = z1 * gain1 + bias1
    e = e_ref[...].astype(F32)
    dr2 = norm_back(e, gain1, z1, r1)
    dm = dr2.astype(BF)
    gb_ref[1:2, :] = jnp.sum(e * z1, axis=0, keepdims=True)
    gb_ref[3:4, :] = jnp.sum(e, axis=0, keepdims=True)

    def back(c, total):
        u = us[c]
        dg = dot(dm, wu[pl.ds(c * 8, 8)].reshape(1024, 1024), NT)
        slope = 0.5 * (1.0 + lax.erf(u * half)) + u * (jnp.exp(-0.5 * u * u) * (1.0 / math.sqrt(2 * math.pi)))
        du = (dg * slope).astype(BF)
        rr[0:128, 1024 * c:1024 * c + 1024] = du
        return total + dot(du, wi[c], NT)

    few = [pl.ds(pl.multiple_of(where[r] * 256, 256), 256) for r in range(4)]
    many = [pl.ds(pl.multiple_of(where[r] * 1024, 1024), 1024) for r in range(4)]
    for ref, rows, at, r in ((ll, 128, 0, 0), (ll, 128, 512, 2), (cl, 128, 0, 1), (cl, 128, 512, 3)):
        ref[:rows, at:at + 256] = nl[:, few[r]]
        ref[:rows, at + 256:at + 512] = ob[:, few[r]]
    near = [wire(cl, ll.at[128:256, :], core)]
    dn1 = dr2
    for c in range(4):
        dn1 = back(c, dn1)
        cols = slice(1024 * c, 1024 * c + 1024)
        near.append(wire(rr.at[0:128, cols], rr.at[128:256, cols], core))
    gb_ref[0:1, :] = jnp.sum(dn1 * z0, axis=0, keepdims=True)
    gb_ref[2:3, :] = jnp.sum(dn1, axis=0, keepdims=True)
    gb_ref[4:8, :] = jnp.zeros((4, 1024), F32)
    dr1 = norm_back(dn1, gain0, z0, r0)
    dr_ref[...] = dr1
    da = dr1.astype(BF)
    rr[0:128, 4096:5120] = da
    near.append(wire(rr.at[0:128, 4096:5120], rr.at[128:256, 4096:5120], core))
    do = dot(da, wo[...], NT).astype(BF)
    for h in range(16):
        lanes = slice(64 * h, 64 * h + 64)
        dos[h] = jnp.concatenate([do[:64, lanes], do[64:, lanes]], axis=1)
    start_do, wait_do = over(dos, dor, send_do, recv_do)
    lax.fori_loop(1, 16, start_do, 0)
    home = pltpu.make_async_copy(dos.at[flat], dor.at[flat], ls.at[1])
    home.start()
    zpay[:, 1024:2048] = dm
    for r, (ref, at) in enumerate(((gpay, 0), (gpay, 1024), (zpay, 0), (zpay, 2048))):
        ref[:, at:at + 1024] = gs[:, many[r]]
    for c in near:
        c.wait_recv()
    for k in range(4):
        lt[256 * k:256 * k + 256, :] = ll[:, 256 * k:256 * k + 256].astype(F32).T.astype(BF)
    out = []
    for z in range(2):
        mid[z, 0:256, :] = dot(lt[512 * z + 256:512 * z + 512, :], rr[:, 4096:5120]).astype(BF)
        for k in range(4):
            rows = slice(256 + 256 * k, 512 + 256 * k)
            mid[z, rows, :] = dot(lt[512 * z:512 * z + 256, :], rr[:, 1024 * k:1024 * k + 1024]).astype(BF)
    for h, (at, (own, plus, minus)) in enumerate(zip((x, y), cuts)):

        def rows(s, first, size):
            return pl.ds(pl.multiple_of(h * 640 + (at + s) % 4 * 160 + first, 16), size)

        for src, dst in (
            (rows(0, 0, 160), own),
            (rows(1, 0, 160), plus.at[:, :160]), (rows(2, 0, 80), plus.at[:, 160:]),
            (rows(3, 0, 160), minus.at[:, :160]), (rows(2, 80, 80), minus.at[:, 160:]),
        ):
            out.append(pltpu.make_async_copy(mid.at[:, src], dst, lo.at[len(out)]))
    for c in out:
        c.start()
    home.wait()
    lax.fori_loop(1, 16, wait_do, 0)
    for c in near:
        c.wait_send()
    for group in shared + [c for k in range(3) for c in passed[k]]:
        for c in group:
            c.wait_send()
    for c in out:
        c.wait()


def heart(o, tok, cot, lnf, lnp, shards, parts):
    cut = [shp((2, 160, 1024), BF), shp((2, 240, 1024), BF), shp((2, 240, 1024), BF)]
    n = 12 + 10 + 6 + 6
    return pl.pallas_call(
        heart_kernel,
        out_shape=[
            shp((128, 1024), F32), shp((128, 1024), F32),
            shp((128, 3072), BF), shp((128, 2048), BF), shp((8, 1024), F32), shp((16, 64, 128), BF),
        ] + cut + cut,
        in_specs=[ANY] + [VM] * 4 + [ANY] * 14,
        out_specs=[VM] * 5 + [ANY] * 7,
        scratch_shapes=[
            pltpu.VMEM((1024, 1024), BF),
            pltpu.VMEM((4, 1024, 1024), BF),
            pltpu.VMEM((32, 4, 32, 1024), BF),
            pltpu.VMEM((4, 128, 1024), F32),
            pltpu.VMEM((128, 4096), BF),
            pltpu.VMEM((128, 1024), BF),
            pltpu.VMEM((128, 1024), BF),
            pltpu.VMEM((16, 64, 128), BF),
            pltpu.VMEM((16, 64, 128), BF),
            pltpu.VMEM((256, 5120), BF),
            pltpu.VMEM((256, 1024), BF),
            pltpu.VMEM((128, 1024), BF),
            pltpu.VMEM((1024, 256), BF),
            pltpu.VMEM((2, 1280, 1024), BF),
            DMA((2, 6)), DMA((8, 3)), DMA((n,)), DMA((n,)), DMA((16,)), DMA((16,)), DMA((16,)), DMA((16,)),
            DMA((2,)), DMA((10,)),
        ],
        compiler_params=pltpu.CompilerParams(collective_id=5, has_side_effects=True, vmem_limit_bytes=LIMIT),
        cost_estimate=pl.CostEstimate(flops=16 << 30, bytes_accessed=32 << 20, transcendentals=2 << 20),
        name="heart",
    )(o, tok, cot, lnf, lnp, *shards[0], *shards[1], *parts)


class Spread:
    def __init__(self, wire, plus, minus, at, piece, bufs):
        self.wire, self.plus, self.minus, self.at, self.piece = wire, plus, minus, at, piece
        self.rp, self.rm, self.m, self.f = bufs

    def part(self, s, u):
        return self.piece((self.at + s) % 4, u)

    def start(self):
        self.a = self.wire(self.part(2, 0), self.m.at[0], self.plus)
        self.b = self.wire(self.part(2, 1), self.m.at[1], self.minus)
        self.c = self.wire(self.part(1, 1), self.rp.at[1], self.plus)
        self.d = self.wire(self.part(3, 0), self.rm.at[0], self.minus)

    def relay(self):
        self.a.wait_recv()
        self.f[0] = (self.part(1, 0)[...].astype(F32) + self.m[0].astype(F32)).astype(BF)
        self.e = self.wire(self.f.at[0], self.rp.at[0], self.plus)
        self.b.wait_recv()
        self.f[1] = (self.part(3, 1)[...].astype(F32) + self.m[1].astype(F32)).astype(BF)
        self.g = self.wire(self.f.at[1], self.rm.at[1], self.minus)

    def total(self):
        for c in (self.c, self.d, self.e, self.g):
            c.wait_recv()
        return [
            self.part(0, u)[...].astype(F32) + self.rp[u].astype(F32) + self.rm[u].astype(F32) for u in range(2)
        ]

    def sent(self):
        for c in (self.a, self.b, self.c, self.d, self.e, self.g):
            c.wait_send()


class Gather:
    def __init__(self, wire, plus, minus, at, block):
        self.wire, self.plus, self.minus, self.at, self.block = wire, plus, minus, at, block

    def send(self, s, u, peer):
        spot = self.block((self.at + s) % 4, u)
        return self.wire(spot, spot, peer)

    def start(self):
        self.p0 = self.send(0, 0, self.plus)
        self.m1 = self.send(0, 1, self.minus)
        self.p1 = self.send(0, 1, self.plus)
        self.m0 = self.send(0, 0, self.minus)

    def relay(self):
        self.p0.wait_recv()
        self.rp = self.send(3, 0, self.plus)
        self.m1.wait_recv()
        self.rm = self.send(1, 1, self.minus)

    def done(self):
        for c in (self.p1, self.m0, self.rp, self.rm):
            c.wait()
        for c in (self.p0, self.m1):
            c.wait_send()


class DirectSpread:
    def __init__(self, wire, peers, at, piece, bufs):
        self.wire, self.peers, self.at, self.piece, self.bufs = wire, peers, at, piece, bufs

    def start(self):
        self.copies = []
        for s in range(3):
            for u in range(2):
                src = self.piece((self.at + s + 1) % 4, u)
                self.copies.append(self.wire(src, self.bufs[s].at[u], self.peers[s]))

    def relay(self):
        pass

    def total(self):
        for c in self.copies:
            c.wait_recv()
        out = []
        for u in range(2):
            total = self.piece(self.at, u)[...].astype(F32)
            for s in range(3):
                total += self.bufs[s][u].astype(F32)
            out.append(total)
        return out

    def sent(self):
        for c in self.copies:
            c.wait_send()


class DirectGather:
    def __init__(self, wire, peers, at, block):
        self.wire, self.peers, self.at, self.block = wire, peers, at, block

    def start(self):
        self.copies = []
        for u in range(2):
            spot = self.block(self.at, u)
            for p in self.peers:
                self.copies.append(self.wire(spot, spot, p))

    def relay(self):
        pass

    def done(self):
        for c in self.copies:
            c.wait()


class Sum:
    direct = False

    def cut(self, g, rows):
        return g.at[rows]

    def __init__(self, g, hc, refs, wire, where, xp, yp, zp):
        bufs1, s1, bufs2, s2, self.r3, full = refs[:4], refs[4], refs[5:9], refs[9], refs[10], refs[11]
        zl, x, y, zh, co = where
        self.wire, self.zp, self.zl = wire, zp, zl
        self.s1, self.s2, self.last, self.full = s1, s2, s2, full
        hh = hc // 2
        first, second = (xp, yp), (yp, xp)
        self.at1, self.at2 = (x, y), (y, x)
        self.peers = [(first[h][0], first[h][2]) for h in range(2)]

        def rows(h, k, u):
            return pl.ds(pl.multiple_of(h * 4 * hc + k * hc + u * hh, 16), hh)

        def cols(k, width):
            return pl.ds(pl.multiple_of(k * width, 128), width)

        self.rows, self.cols = rows, cols

        def one(h):
            return lambda k, u: self.cut(g, rows(h, k, u))

        def two(h):
            return lambda k, u: s1.at[h, u, :, cols(k, 256)]

        def five(h):
            return lambda k, u: full.at[rows(h, self.at1[h], u), cols(k, 256)]

        def six(h):
            return lambda k, u: full.at[rows(h, k, u)]

        def ends(peers):
            return wire, peers[0], peers[2]

        if g is not None:
            self.one = [Spread(*ends(first[h]), self.at1[h], one(h), [r.at[h] for r in bufs1]) for h in range(2)]
        if self.direct:
            self.two = [DirectSpread(wire, second[h], self.at2[h], two(h), [r.at[h] for r in bufs2]) for h in range(2)]
            self.five = [DirectGather(wire, second[h], self.at2[h], five(h)) for h in range(2)]
        else:
            self.two = [Spread(*ends(second[h]), self.at2[h], two(h), [r.at[h] for r in bufs2]) for h in range(2)]
            self.five = [Gather(*ends(second[h]), self.at2[h], five(h)) for h in range(2)]
        self.six = [Gather(*ends(first[h]), self.at1[h], six(h)) for h in range(2)]

    def begin(self):
        for t in self.one:
            t.start()

    def relay(self):
        for t in self.one:
            t.relay()

    def totals(self, h):
        return self.one[h].total()

    def across(self):
        pass

    def settle(self):
        for t in self.one:
            t.sent()

    def steps(self):
        self.begin()
        yield
        self.relay()
        yield
        for h in range(2):
            for u, total in enumerate(self.totals(h)):
                self.s1[h, u] = total.astype(BF)
            self.two[h].start()
        yield
        for t in self.two:
            t.relay()
        yield
        for h in range(2):
            for u, total in enumerate(self.two[h].total()):
                self.s2[h, u] = total.astype(BF)
        self.across()
        yield
        three = []
        for h in range(2):
            self.ready(h)
            three.append(self.wire(self.last.at[h, :, :, self.cols(1 - self.zl, 128)], self.r3.at[h], self.zp))
        yield
        four = []
        for h in range(2):
            three[h].wait_recv()
            for u in range(2):
                total = self.last[h, u, :, self.cols(self.zl, 128)].astype(F32) + self.r3[h, u].astype(F32)
                spot = self.full.at[self.rows(h, self.at1[h], u), self.cols(self.at2[h] * 2 + self.zl, 128)]
                spot[...] = total.astype(BF)
                four.append(self.wire(spot, spot, self.zp))
        yield
        for h in range(2):
            four[2 * h].wait()
            four[2 * h + 1].wait()
            self.five[h].start()
        yield
        for t in self.five:
            t.relay()
        yield
        for h in range(2):
            self.five[h].done()
            self.six[h].start()
        yield
        for t in self.six:
            t.relay()
        yield
        for t in self.two:
            t.sent()
        for c in three:
            c.wait_send()
        self.settle()
        for t in self.six:
            t.done()
        yield

    def ready(self, h):
        pass


class PairSum(Sum):
    direct = True

    def cut(self, g, rows):
        return g.at[:, rows]

    def __init__(self, g, hc, refs, wire, where, xp, yp, zp, far):
        self.rf, self.s3 = refs[:2]
        super().__init__(g, hc, refs[2:], wire, where, xp, yp, zp)
        self.far, self.hh, self.last = far, hc // 2, self.s3

    def totals(self, h):
        return [t.reshape(2 * self.hh, 1024) for t in self.one[h].total()]

    def across(self):
        self.crossed = [self.wire(self.s2.at[h, :, self.hh:], self.rf.at[h], self.far) for h in range(2)]

    def ready(self, h):
        self.crossed[h].wait_recv()
        for u in range(2):
            self.s3[h, u] = (self.s2[h, u, :self.hh].astype(F32) + self.rf[h, u].astype(F32)).astype(BF)

    def settle(self):
        for t in self.one:
            t.sent()
        for c in self.crossed:
            c.wait_send()


class BegunSum(PairSum):
    direct = False

    def __init__(self, hc, refs, wire, where, xp, yp, zp, far, own, plus, minus):
        self.own, self.fwd = refs[:2]
        super().__init__(None, hc, list(refs[2:4]) + [None] * 4 + list(refs[4:]), wire, where, xp, yp, zp, far)
        self.plus, self.minus = plus, minus

    def begin(self):
        hc = 2 * self.hh
        self.passed = []
        for h in range(2):
            plus, minus = self.peers[h]
            self.passed.append((
                self.wire(self.plus[h].at[:, hc:], self.fwd.at[h, 0], plus),
                self.wire(self.minus[h].at[:, hc:], self.fwd.at[h, 1], minus),
            ))

    def relay(self):
        pass

    def totals(self, h):
        hh = self.hh
        for c in self.passed[h]:
            c.wait_recv()
        out = []
        for u in range(2):
            rows = slice(u * hh, u * hh + hh)
            total = self.own[h, 0, :, rows].astype(F32) + self.own[h, 1, :, rows].astype(F32)
            total += self.own[h, 2, :, rows].astype(F32) + self.fwd[h, u].astype(F32)
            out.append(total.reshape(2 * hh, 1024))
        return out

    def settle(self):
        for c in self.crossed:
            c.wait_send()
        for pair in self.passed:
            for c in pair:
                c.wait_send()


class FirstSum:
    def __init__(self, g, refs, wire, where, xp, yp, zp):
        bufs1, s1, bufs2, rz, half, full = refs[:4], refs[4], refs[5:9], refs[9], refs[10], refs[11]
        zl, x, y, zh, co = where
        self.g, self.wire, self.zp, self.zl = g, wire, zp, zl
        self.s1, self.rz, self.half, self.full = s1, rz, half, full
        first, second = (xp, yp), (yp, xp)
        self.at1, self.at2 = (x, y), (y, x)

        def cols(k):
            return pl.ds(pl.multiple_of(k * 256, 128), 256)

        def one(h):
            return lambda k, u: half.at[pl.ds(pl.multiple_of(h * 256 + k * 64 + u * 32, 32), 32)]

        def two(h):
            return lambda k, u: s1.at[h, u, :, cols(k)]

        def rows(h, k, z):
            return pl.ds(pl.multiple_of(z * 512 + h * 256 + k * 64, 64), 64)

        def five(h):
            return lambda k, z: full.at[rows(h, self.at1[h], z), cols(k)]

        def six(h):
            return lambda k, z: full.at[rows(h, k, z)]

        self.spot = lambda h: full.at[rows(h, self.at1[h], zl), cols(self.at2[h])]
        self.one = [Spread(wire, first[h][0], first[h][2], self.at1[h], one(h), [r.at[h] for r in bufs1]) for h in range(2)]
        self.two = [DirectSpread(wire, second[h], self.at2[h], two(h), [r.at[h] for r in bufs2]) for h in range(2)]
        self.five = [Gather(wire, second[h][0], second[h][2], self.at2[h], five(h)) for h in range(2)]
        self.six = [Gather(wire, first[h][0], first[h][2], self.at1[h], six(h)) for h in range(2)]

    def steps(self):
        zs = []
        for h in range(2):
            src = self.g.at[pl.ds(pl.multiple_of((1 - self.zl) * 512 + h * 256, 256), 256)]
            zs.append(self.wire(src, self.rz.at[h], self.zp))
        yield
        for h in range(2):
            zs[h].wait_recv()
            mine = self.g[pl.ds(pl.multiple_of(self.zl * 512 + h * 256, 256), 256), :]
            self.half[256 * h:256 * h + 256, :] = (mine.astype(F32) + self.rz[h].astype(F32)).astype(BF)
            self.one[h].start()
        yield
        for t in self.one:
            t.relay()
        yield
        for h in range(2):
            for u, total in enumerate(self.one[h].total()):
                self.s1[h, u] = total.astype(BF)
            self.two[h].start()
        yield
        four = []
        for h in range(2):
            spot = self.spot(h)
            spot[...] = jnp.concatenate(self.two[h].total(), axis=0).astype(BF)
            four.append(self.wire(spot, spot, self.zp))
        yield
        for h in range(2):
            four[h].wait()
            self.five[h].start()
        yield
        for t in self.five:
            t.relay()
        yield
        for h in range(2):
            self.five[h].done()
            self.six[h].start()
        yield
        for t in self.six:
            t.relay()
        yield
        for t in self.one + self.two:
            t.sent()
        for c in zs:
            c.wait_send()
        for t in self.six:
            t.done()
        yield


SUM_COPIES = 2 + 12 + 12 + 2 + 12 + 12


BEGUN_COPIES = 4 + 12 + 2 + 2 + 4 + 12 + 12
PAIR_COPIES = 12 + 12 + 2 + 2 + 4 + 12 + 12


def first_scratch():
    return (
        [pltpu.VMEM((2, 2, 32, 1024), BF)] * 5
        + [pltpu.VMEM((2, 2, 32, 256), BF)] * 4
        + [pltpu.VMEM((2, 256, 1024), BF), pltpu.VMEM((512, 1024), BF)]
    )


def pair_scratch(rows, begun):
    hh = rows // 16
    begin = [pltpu.VMEM((2, 3, 2, 2 * hh, 1024), BF), pltpu.VMEM((2, 2, 2, hh, 1024), BF)]
    first = [pltpu.VMEM((2, 2, 2, hh, 1024), BF)] * 4
    return (
        (begin if begun else [])
        + [pltpu.VMEM((2, 2, hh, 256), BF)] * 2
        + ([] if begun else first)
        + [pltpu.VMEM((2, 2, 2 * hh, 1024), BF)]
        + [pltpu.VMEM((2, 2, 2 * hh, 256), BF)] * 4
        + [pltpu.VMEM((2, 2, 2 * hh, 256), BF), pltpu.VMEM((2, 2, hh, 128), BF)]
    )


def finish_kernel(*refs):
    dkvp, dqp, dr_ref, gb, wall, gpay, zpay, zr, xs, x_ref = refs[:10]
    got = ((refs[10], refs[13]), (refs[11], refs[14]), (refs[12], refs[15]))

    gt, io_full, u_full, tail_full, s_vec = refs[16:21]
    io_refs = list(refs[21:32]) + [io_full]
    u_refs, tail_refs = list(refs[32:43]) + [u_full], list(refs[43:56]) + [tail_full]
    (dkv, zb, sb, dq, weights, ll2, rr2, lt2, mid, pay, ll, rr, tail, v0, vf, v1, vx, vy, vz, tx, ty,
     sz, rz, sw, rw, sn, rn, ss, rs, ls, lw) = refs[56:]
    scale = 1.0 / math.sqrt(16384)
    where = place()
    zl, x, y, zh, co = where
    w = zh * 2 + co
    me = lax.axis_index("ctx")
    flat = me % 16
    core = device(zl, x, y, zh, 1 - co)
    far = device(zl, x, y, 1 - zh, co)
    xp = [device(zl, (x + s) % 4, y, zh, co) for s in (1, 2, 3)]
    yp = [device(zl, x, (y + s) % 4, zh, co) for s in (1, 2, 3)]
    zp = device(1 - zl, x, y, zh, co)
    bar = pltpu.get_barrier_semaphore()

    def greet_one(i, carry):
        pl.semaphore_signal(bar, inc=1, device_id={"ctx": zl * 16 + (flat + i) % 16}, device_id_type=MESH)
        return carry

    for p in (core, far, zp):
        pl.semaphore_signal(bar, inc=1, device_id=p, device_id_type=MESH)
    lax.fori_loop(1, 16, greet_one, 0)

    mine = [pl.ds(pl.multiple_of(k * 256, 256), 256) for k in (w, (1 - zh) * 2 + co)]
    parts = []
    for h in range(2):
        for n in range(3):
            parts.append(pltpu.make_async_copy(got[n][h].at[:, :160], io_refs[0].at[h, n], ls.at[10 + 3 * h + n]))
    local = [
        pltpu.make_async_copy(gpay.at[:, :1024], ll2.at[0:128, :], ls.at[0]),
        pltpu.make_async_copy(zpay.at[:, 1024:2048], rr2.at[0:128, :], ls.at[1]),
        pltpu.make_async_copy(zr.at[:, :1024], ll2.at[256:384, :], ls.at[2]),
        pltpu.make_async_copy(zr.at[:, 1024:2048], rr2.at[256:384, :], ls.at[3]),
    ]
    for k in range(2):
        cols = slice(256 * k, 256 * k + 256)
        local.append(pltpu.make_async_copy(x_ref.at[:, mine[k]], ll.at[0:128, cols], ls.at[4 + k]))
        local.append(pltpu.make_async_copy(xs.at[k], ll.at[128:256, cols], ls.at[6 + k]))
    for c in local + parts:
        c.start()
    loads = [pltpu.make_async_copy(wall, weights, lw.at[0])]
    loads[0].start()
    pl.semaphore_wait(bar, 18)

    def narrow_copy(i):
        p = (flat + i) % 16
        return pltpu.make_async_remote_copy(
            src_ref=dqp.at[p], dst_ref=dq.at[flat], send_sem=sn.at[i], recv_sem=rn.at[i],
            device_id={"ctx": zl * 16 + p}, device_id_type=MESH,
        )

    def z_copy(i):
        return pltpu.make_async_remote_copy(
            src_ref=dkvp.at[(1 - zl) * 16 + (flat + i) % 16], dst_ref=zb.at[i], send_sem=sz.at[i], recv_sem=rz.at[i],
            device_id=zp, device_id_type=MESH,
        )

    def wide_copy(i):
        p = (flat + i) % 16
        return pltpu.make_async_remote_copy(
            src_ref=sb.at[i], dst_ref=dkv.at[flat], send_sem=sw.at[i], recv_sem=rw.at[i],
            device_id={"ctx": zl * 16 + p}, device_id_type=MESH,
        )

    def start(make):
        def one(i, carry):
            make(i).start()
            return carry
        return one

    def wait(make):
        def one(i, carry):
            make(i).wait()
            return carry
        return one

    def both(i):
        z_copy(i).wait_recv()
        return (dkvp[zl * 16 + (flat + i) % 16].astype(F32) + zb[i].astype(F32)).astype(BF)

    def pass_on(i, carry):
        sb[i] = both(i)
        wide_copy(i).start()
        return carry

    def sent(i, carry):
        z_copy(i).wait_send()
        return carry

    lax.fori_loop(1, 16, start(z_copy), 0)
    z_copy(0).start()
    lax.fori_loop(1, 16, start(narrow_copy), 0)
    home = [pltpu.make_async_copy(dqp.at[flat], dq.at[flat], ls.at[9])]
    for c in home:
        c.start()
    wire = Wire(ss, rs)
    near = [
        wire(gpay.at[:, 1024:], ll2.at[128:256, :], core),
        wire(zpay.at[:, 1024:2048], rr2.at[128:256, :], core),
        wire(zr.at[:, 2048:], ll2.at[384:512, :], core),
        wire(zr.at[:, 1024:2048], rr2.at[384:512, :], core),
    ]
    io = BegunSum(160, io_refs, wire, where, xp, yp, zp, far, *got).steps()
    big = FirstSum(mid, u_refs, wire, where, xp, yp, zp).steps()
    small = PairSum(tail, 96, tail_refs, wire, where, xp, yp, zp, far).steps()
    next(io)
    next(io)
    for c in local:
        c.wait()
    lt = ll[...].astype(F32).T.astype(BF)
    for c in near:
        c.wait()
    for k in range(4):
        lt2[256 * k:256 * k + 256, :] = ll2[:, 256 * k:256 * k + 256].astype(F32).T.astype(BF)
    for k in range(4):
        rows = slice(256 * k, 256 * k + 256)
        mid[rows, :] = dot(lt2[rows, :], rr2[...]).astype(BF)
    lax.fori_loop(1, 16, pass_on, 0)
    dkv[flat] = both(0)
    next(big)
    for c in parts:
        c.wait()
    next(io)

    for c in home:
        c.wait()
    lax.fori_loop(1, 16, wait(wide_copy), 0)
    lax.fori_loop(1, 16, wait(narrow_copy), 0)
    lax.fori_loop(0, 16, sent, 0)
    for h in range(16):
        lanes = slice(64 * h, 64 * h + 64)
        pair = dq[h]
        pay[:64, lanes] = pair[:, :64]
        pay[64:128, lanes] = pair[:, 64:]
        pair = dkv[h]
        pay[:128, 1024 + 64 * h:1088 + 64 * h] = pair[:, :64]
        pay[:128, 2048 + 64 * h:2112 + 64 * h] = pair[:, 64:]
    pay[128:144, :1024] = jnp.concatenate([gb[...], jnp.zeros((8, 1024), F32)], axis=0).astype(BF)
    pay[128:144, 1024:] = jnp.zeros((16, 2048), BF)
    to_core = wire(pay, rr, core)
    next(io)
    for c in loads:
        c.wait()
    for k in range(4):
        cols = slice(256 * k, 256 * k + 256)
        total = dr_ref[:, cols]
        for m in range(3):
            total += dot(pay[:128, 1024 * m:1024 * m + 1024], weights[k, m], NT)
        gt[:, cols] = total
    next(io)
    to_core.wait_recv()
    for z in range(2):
        for m in range(3):
            cols = slice(1024 * m, 1024 * m + 1024)
            total = dot(lt[256 * z:256 * z + 256, :128], pay[:128, cols])
            total += dot(lt[256 * z:256 * z + 256, 128:], rr[:128, cols])
            tail[z, 256 * m:256 * m + 256, :] = total.astype(BF)
    next(small)
    for z in range(2):
        v0[z] = (pay[128:144, mine[z]].astype(F32) + rr[128:144, mine[z]].astype(F32))[:8]
    vfar = wire(v0.at[1], vf, far)
    next(big)
    next(io)
    next(small)
    next(big)
    next(io)
    vfar.wait_recv()
    v1[...] = v0[0] + vf[...]
    vone = [wire(v1, vx.at[s], xp[s]) for s in range(3)]
    next(small)
    next(io)
    next(big)
    next(small)
    next(io)
    for c in vone:
        c.wait_recv()
    tx[...] = v1[...] + vx[0] + vx[1] + vx[2]
    vtwo = [wire(tx, vy.at[s], yp[s]) for s in range(3)]
    next(small)
    next(big)
    next(io)
    next(small)
    next(big)
    for c in vtwo:
        c.wait_recv()
    ty[...] = tx[...] + vy[0] + vy[1] + vy[2]
    vthree = wire(ty, vz, zp)
    next(small)
    next(big)
    next(small)
    next(big)
    next(io)
    next(small)
    next(small)
    next(big)
    vthree.wait()
    s_vec[...] = (ty[...] + vz[...]) * scale
    for c in vone + vtwo + [to_core, vfar]:
        c.wait_send()
    next(small)
    next(io)
    next(big)
    next(small)


def finish(dkvp, dqp, dr, gb, wall, gpay, zpay, zr, xs, tok, parts):
    n = SUM_COPIES + BEGUN_COPIES + PAIR_COPIES + 4 + 2 + 7
    return pl.pallas_call(
        finish_kernel,
        out_shape=[
            shp((128, 1024), F32), shp((1280, 1024), BF), shp((1024, 1024), BF), shp((768, 1024), BF), shp((8, 256), F32),
        ],
        in_specs=[VM, ANY, VM, VM] + [ANY] * 12,
        out_specs=[VM] * 5,
        scratch_shapes=pair_scratch(1280, True) + first_scratch() + pair_scratch(768, False) + [
            pltpu.VMEM((16, 128, 128), BF), pltpu.VMEM((16, 128, 128), BF), pltpu.VMEM((16, 128, 128), BF),
            pltpu.VMEM((16, 64, 128), BF), pltpu.VMEM((4, 3, 256, 1024), BF),
            pltpu.VMEM((512, 1024), BF), pltpu.VMEM((512, 1024), BF), pltpu.VMEM((1024, 512), BF),
            pltpu.VMEM((1024, 1024), BF), pltpu.VMEM((144, 3072), BF),
            pltpu.VMEM((256, 512), BF), pltpu.VMEM((144, 3072), BF), pltpu.VMEM((2, 768, 1024), BF),
            pltpu.VMEM((2, 8, 256), F32), pltpu.VMEM((8, 256), F32), pltpu.VMEM((8, 256), F32),
            pltpu.VMEM((3, 8, 256), F32), pltpu.VMEM((3, 8, 256), F32),
            pltpu.VMEM((8, 256), F32), pltpu.VMEM((8, 256), F32), pltpu.VMEM((8, 256), F32),
            DMA((16,)), DMA((16,)), DMA((16,)), DMA((16,)), DMA((16,)), DMA((16,)),
            DMA((n,)), DMA((n,)), DMA((16,)), DMA((1,)),
        ],
        compiler_params=pltpu.CompilerParams(collective_id=6, has_side_effects=True, vmem_limit_bytes=LIMIT),
        name="finish",
    )(dkvp, dqp, dr, gb, wall, gpay, zpay, zr, xs, tok, *parts)


def scale_kernel(o, i0, i1, i2, i3, u, q, k, v, out_q, out_k, out_v, out_o, out_i, out_u):
    scale = 1.0 / math.sqrt(16384)
    for src, dst in ((q, out_q), (k, out_k), (v, out_v), (o, out_o), (u, out_u)):
        dst[...] = src[...].astype(F32) * scale
    for n, src in enumerate((i0, i1, i2, i3)):
        out_i[:, 1024 * n:1024 * n + 1024] = src[...].astype(F32) * scale


def scaled(io, u, tail):
    def rows(first, n=32):
        return pl.BlockSpec((n, 1024), lambda j: (first // n + j, 0))

    return pl.pallas_call(
        scale_kernel,
        grid=(8,),
        out_shape=[shp((256, 1024), F32)] * 4 + [shp((256, 4096), F32), shp((1024, 1024), F32)],
        in_specs=[rows(0)] + [rows(256 + 256 * k) for k in range(4)] + [rows(0, 128)] + [rows(256 * k) for k in range(3)],
        out_specs=[rows(0)] * 4 + [pl.BlockSpec((32, 4096), lambda j: (j, 0)), rows(0, 128)],
        compiler_params=pltpu.CompilerParams(vmem_limit_bytes=LIMIT),
        name="scaled",
    )(*[io] * 5, u, *[tail] * 3)


FLIP_CORE = [(0, 1), (1, 0), (2, 3), (3, 2)]
FLIP_FAR = [(0, 2), (2, 0), (1, 3), (3, 1)]


def along_x(s):
    return [(c, c // 16 * 16 + (c // 4 + s) % 4 * 4 + c % 4) for c in range(32)]


def along_y(s):
    return [(c, c // 4 * 4 + (c + s) % 4) for c in range(32)]


def body(
    tokens, w_query, w_key, w_value, w_output, w_inner, w_outer, ln_gain, ln_bias, block_mask, block_pairs, cotangent,
):
    tok = tokens.reshape(128, 1024)
    cot = cotangent.reshape(128, 1024)
    lnp = jnp.concatenate([ln_gain, ln_bias, jnp.zeros((4, 256), F32)], axis=0)
    blk = block_pairs.reshape(-1)
    own = (w_query, w_key, w_value)
    outer = w_outer.reshape(8, 4, 32, 1024)
    wall, xs, lnf, *rest = front(tok, own, lnp, w_output, w_inner, outer)
    core_shard, (qa, qb, diag_a, diag_b, kvr, qr) = rest[:3], rest[3:]
    x1, x3 = (lax.ppermute(qa, "ctx", along_x(s)) for s in (1, 3))
    y1, y3 = (lax.ppermute(qb, "ctx", along_y(s)) for s in (1, 3))
    o, ot, lse = attend(blk, block_mask, kvr, qr)
    x1, x3, y1, y3, o = lax.optimization_barrier((x1, x3, y1, y3, o))
    y_out, dr1, zpay, gpay, gb, dor, own_a, plus_a, minus_a, own_b, plus_b, minus_b = heart(
        o, tok, cot, lnf, lnp, ((w_output, w_inner, outer), core_shard), (qa, x1, x3, qb, y1, y3, diag_a, diag_b)
    )
    zr = lax.ppermute(zpay, "wsh", FLIP_FAR)
    plus_a = lax.ppermute(plus_a, "ctx", along_x(1))
    minus_a = lax.ppermute(minus_a, "ctx", along_x(3))
    plus_b = lax.ppermute(plus_b, "ctx", along_y(1))
    minus_b = lax.ppermute(minus_b, "ctx", along_y(3))
    dkvp, dqp = attend_back(blk, block_mask, kvr, qr, dor, ot, lse)
    zr, plus_a, minus_a, plus_b, minus_b, dkvp = lax.optimization_barrier((zr, plus_a, minus_a, plus_b, minus_b, dkvp))
    grad_tok, io, u, tail, s_vec = finish(
        dkvp, dqp, dr1, gb, wall, gpay, zpay, zr, xs, tok, (own_a, plus_a, minus_a, own_b, plus_b, minus_b)
    )
    s_q, s_k, s_v, s_o, s_i, s_u = scaled(io, u, tail)
    out_shape = tokens.shape
    return (
        y_out.reshape(out_shape), grad_tok.reshape(out_shape), s_q, s_k, s_v, s_o, s_i, s_u, s_vec[0:2], s_vec[2:4],
    )


def solution(mesh):
    return jax.shard_map(
        body,
        mesh=mesh,
        in_specs=(
            P("wsh", "ctx", None, None),
            P("wsh", None), P("wsh", None), P("wsh", None), P("wsh", None), P("wsh", None), P("wsh", None),
            P(None, "wsh"), P(None, "wsh"),
            P("wsh", None, None),
            P(),
            P("wsh", "ctx", None, None),
        ),
        out_specs=(
            P("wsh", "ctx", None, None), P("wsh", "ctx", None, None),
            P("wsh", None), P("wsh", None), P("wsh", None), P("wsh", None), P("wsh", None), P("wsh", None),
            P(None, "wsh"), P(None, "wsh"),
        ),
        check_vma=False,
    )
```

```python
import math

import jax
import jax.numpy as jnp
from jax import lax
from jax.experimental import pallas as pl
from jax.experimental.pallas import tpu as pltpu
from jax.sharding import PartitionSpec as P

MESH = pl.DeviceIdType.MESH
BF = jnp.bfloat16
F32 = jnp.float32
ANY = pl.BlockSpec(memory_space=pl.ANY)
VM = pl.BlockSpec(memory_space=pltpu.VMEM)
SM = pl.BlockSpec(memory_space=pltpu.SMEM)
DMA = pltpu.SemaphoreType.DMA
LIMIT = 56 * 1024 * 1024
EPS = 1e-05
NEG = -1e30


def shp(shape, dtype):
    return jax.ShapeDtypeStruct(shape, dtype)


def dot(a, b, dims=((1,), (0,))):
    return lax.dot_general(a, b, (dims, ((), ())), preferred_element_type=F32)


NN = ((1,), (0,))
NT = ((1,), (1,))
TN = ((0,), (0,))


def place():
    c = lax.axis_index("ctx")
    w = lax.axis_index("wsh")
    return c // 16, (c // 4) % 4, c % 4, w // 2, w % 2


def device(zl, x, y, zh, co):
    return {"ctx": zl * 16 + x * 4 + y, "wsh": zh * 2 + co}


def greet(peers):
    bar = pltpu.get_barrier_semaphore()
    for p in peers:
        pl.semaphore_signal(bar, inc=1, device_id=p, device_id_type=MESH)
    pl.semaphore_wait(bar, len(peers))


class Wire:
    def __init__(self, send, recv):
        self.send, self.recv, self.n = send, recv, 0

    def __call__(self, src, dst, peer):
        k = self.n
        self.n += 1
        copy = pltpu.make_async_remote_copy(
            src_ref=src, dst_ref=dst, send_sem=self.send.at[k], recv_sem=self.recv.at[k],
            device_id=peer, device_id_type=MESH,
        )
        copy.start()
        return copy


def front_kernel(*refs):
    x_ref, wq, wk, wv, x_any, ln_ref, wo, wi, wu = refs[:9]
    wall, xs, lnf, co_ref, ci_ref, cu_ref, qa_ref, qb_ref, da_ref, db_ref, kvr, qr = refs[9:21]
    weights, acc, kvp, qp, ss, rs, sw, rw, sf, rf, sn, rn, ls = refs[21:]
    zl, x, y, zh, co = place()
    me = zh * 2 + co
    slots = [me, zh * 2 + 1 - co, (1 - zh) * 2 + co, (1 - zh) * 2 + 1 - co]
    here = lax.axis_index("ctx")
    flat = here % 16
    core = device(zl, x, y, zh, 1 - co)
    far = device(zl, x, y, 1 - zh, co)
    diag = device(zl, x, y, 1 - zh, 1 - co)
    zp = device(1 - zl, x, y, zh, co)
    xp = [device(zl, (x + s) % 4, y, zh, co) for s in (1, 2, 3)]
    yp = [device(zl, x, (y + s) % 4, zh, co) for s in (1, 2, 3)]
    bar = pltpu.get_barrier_semaphore()

    def greet_one(i, carry):
        pl.semaphore_signal(bar, inc=1, device_id={"ctx": zl * 16 + (flat + i) % 16}, device_id_type=MESH)
        return carry

    for p in (far, core, diag, zp):
        pl.semaphore_signal(bar, inc=1, device_id=p, device_id_type=MESH)
    lax.fori_loop(1, 16, greet_one, 0)
    ws = (wq, wk, wv)
    local = [pltpu.make_async_copy(ws[m], weights.at[me, m], ls.at[m]) for m in range(3)]
    for c in local:
        c.start()
    pl.semaphore_wait(bar, 19)
    wire = Wire(ss, rs)
    rows_a = pl.ds(pl.multiple_of(x * 32, 32), 32)
    rows_b = pl.ds(pl.multiple_of(128 + y * 32, 32), 32)
    first_a, first_b = [], []
    for m in range(3):
        first_a.append(wire(ws[m].at[rows_a], weights.at[me, m, rows_a], far))
        first_b.append(wire(ws[m].at[rows_b], weights.at[me, m, rows_b], far))
    near = [wire(ws[m], weights.at[me, m], core) for m in range(3)]
    quarters = []
    for ref, k, n in ((qa_ref, x, y), (qb_ref, 4 + y, x)):
        rows = pl.ds(pl.multiple_of(k * 32, 32), 32)
        cols = pl.ds(pl.multiple_of(n * 256, 256), 256)
        quarters.append(wire(wo.at[rows, cols], ref.at[0, :, cols], far))
        for b in range(4):
            at = pl.ds(pl.multiple_of(1024 * b + n * 256, 256), 256)
            quarters.append(wire(wi.at[rows, at], ref.at[1 + b, :, cols], far))
        quarters.append(wire(wu.at[k, :, :, cols], ref.at[5:9, :, cols], far))
    rest = []
    for p in (core, far, diag):
        rest.append(wire(ln_ref, lnf.at[me], p))
    for n, idx in enumerate((slots[1], slots[3])):
        rest.append(wire(x_any.at[:, pl.ds(pl.multiple_of(idx * 256, 256), 256)], xs.at[n], core))
    for src, dst in ((wo, co_ref), (wi, ci_ref), (wu, cu_ref)):
        rest.append(wire(src, dst, core))

    def add(k, fresh):
        cols = x_ref[:, pl.ds(pl.multiple_of(slots[k] * 256, 256), 256)]
        for m in range(3):
            part = dot(cols, weights[slots[k], m])
            acc[m] = part if fresh else acc[m] + part

    for c in first_a:
        c.wait_recv()
    second = []
    for m in range(3):
        part = weights.at[slots[2], m, rows_a]
        for p in xp:
            second.append(wire(part, part, p))
    for c in first_b:
        c.wait_recv()
    for m in range(3):
        part = weights.at[slots[2], m, rows_b]
        for p in yp:
            second.append(wire(part, part, p))
    for c in local:
        c.wait()
    add(0, True)
    for c in near:
        c.wait_recv()
    add(1, False)
    for c in quarters:
        c.wait_recv()
    subs = []
    for ref, n, peers in ((qa_ref, y, yp), (qb_ref, x, xp)):
        spot = ref.at[:, :, pl.ds(pl.multiple_of(n * 256, 256), 256)]
        for p in peers:
            subs.append(wire(spot, spot, p))
    for c in second:
        c.wait_recv()
    last = [wire(weights.at[slots[2], m], weights.at[slots[2], m], core) for m in range(3)]
    add(2, False)
    for c in last:
        c.wait_recv()
    add(3, False)
    keep = pltpu.make_async_copy(weights, wall, ls.at[0])
    keep.start()
    for j in range(8):
        lanes = slice(128 * j, 128 * j + 128)
        q = (acc[0, :, lanes].astype(BF).astype(F32) * 0.125).astype(BF)
        k = acc[1, :, lanes].astype(BF)
        v = acc[2, :, lanes].astype(BF)
        for u in range(2):
            part = slice(64 * u, 64 * u + 64)
            kvp[2 * j + u] = jnp.concatenate([k[:, part], v[:, part]], axis=1)
            qp[2 * j + u] = jnp.concatenate([q[:64, part], q[64:, part]], axis=1)

    def plane(i):
        return {"ctx": zl * 16 + (flat + i) % 16}

    def wide_copy(i):
        return pltpu.make_async_remote_copy(
            src_ref=kvp.at[(flat + i) % 16], dst_ref=kvr.at[here], send_sem=sw.at[i], recv_sem=rw.at[i],
            device_id=plane(i), device_id_type=MESH,
        )

    def narrow_copy(i):
        return pltpu.make_async_remote_copy(
            src_ref=qp.at[(flat + i) % 16], dst_ref=qr.at[flat], send_sem=sn.at[i], recv_sem=rn.at[i],
            device_id=plane(i), device_id_type=MESH,
        )

    def pass_copy(i):
        spot = kvr.at[zl * 16 + (flat + 16 - i) % 16]
        return pltpu.make_async_remote_copy(
            src_ref=spot, dst_ref=spot, send_sem=sf.at[i], recv_sem=rf.at[i], device_id=zp, device_id_type=MESH,
        )

    def start_wide(i, carry):
        wide_copy(i).start()
        return carry

    def start_narrow(i, carry):
        narrow_copy(i).start()
        return carry

    def pass_on(i, carry):
        wide_copy(i).wait_recv()
        pass_copy(i).start()
        return carry

    def wait_all(i, carry):
        wide_copy(i).wait_send()
        narrow_copy(i).wait()
        pass_copy(i).wait()
        return carry

    to_z = wire(kvp.at[flat], kvr.at[here], zp)
    lax.fori_loop(1, 16, start_wide, 0)
    lax.fori_loop(1, 16, start_narrow, 0)
    home = [
        pltpu.make_async_copy(kvp.at[flat], kvr.at[here], ls.at[1]),
        pltpu.make_async_copy(qp.at[flat], qr.at[flat], ls.at[2]),
    ]
    for c in home:
        c.start()
    lax.fori_loop(1, 16, pass_on, 0)
    for c in subs:
        c.wait_recv()
    for src, dst in ((qa_ref, da_ref), (qb_ref, db_ref)):
        rest.append(wire(src, dst, core))
    for c in home:
        c.wait()
    keep.wait()
    lax.fori_loop(1, 16, wait_all, 0)
    to_z.wait()
    for c in first_a + first_b + near + second + last + quarters + subs:
        c.wait_send()
    for c in rest:
        c.wait()


def front(tok, own, lnp, wo, wi, wu):
    n = 6 + 3 + 12 + 3 + 2 + 18 + 3 + 1 + 6 + 3 + 2
    piece = shp((9, 32, 1024), BF)
    return pl.pallas_call(
        front_kernel,
        out_shape=[shp((4, 3, 256, 1024), BF), shp((2, 128, 256), BF), shp((4, 8, 256), F32)]
        + [shp(wo.shape, BF), shp(wi.shape, BF), shp(wu.shape, BF)] + [piece] * 4
        + [shp((32, 128, 128), BF), shp((16, 64, 128), BF)],
        in_specs=[VM] + [ANY] * 8,
        out_specs=[ANY] * 12,
        scratch_shapes=[
            pltpu.VMEM((4, 3, 256, 1024), BF), pltpu.VMEM((3, 128, 1024), F32),
            pltpu.VMEM((16, 128, 128), BF), pltpu.VMEM((16, 64, 128), BF),
            DMA((n,)), DMA((n,)), DMA((16,)), DMA((16,)), DMA((16,)), DMA((16,)), DMA((16,)), DMA((16,)), DMA((3,)),
        ],
        compiler_params=pltpu.CompilerParams(collective_id=1, has_side_effects=True, vmem_limit_bytes=LIMIT),
        cost_estimate=pl.CostEstimate(flops=16 << 30, bytes_accessed=32 << 20, transcendentals=0),
        name="front",
    )(tok, *own, tok, lnp, wo, wi, wu)


def attention_setup(blk, mask, kvr, qr, kvs, kaug, kvt, bias, qs, inv, order, oblk):
    first = (lax.axis_index("ctx") // 16) * 32

    def note(s, carry):
        inv[blk[s]] = s
        return carry

    lax.fori_loop(0, 64, note, 0)

    def pick(b, count):
        local = inv[b] - first
        order[count] = local
        oblk[count] = b
        mine = jnp.logical_and(local >= 0, local < 32)
        return count + mine.astype(jnp.int32)

    lax.fori_loop(0, 64, pick, 0)
    for s in range(64):
        at = pl.ds(pl.multiple_of(blk[s] * 64, 64), 64)
        kvs[at, :] = kvr[s // 2, (s % 2) * 64:(s % 2) * 64 + 64, :]
    for j in range(16):
        pair = qr[j]
        qs[2 * j] = pair[:, :64]
        qs[2 * j + 1] = pair[:, 64:]
    rows = lax.broadcasted_iota(jnp.int32, (512, 64), 0) // 64
    lanes = lax.broadcasted_iota(jnp.int32, (512, 64), 1)
    for c in range(8):
        part = kvs[512 * c:512 * c + 512, :]
        hot = jnp.where(rows + 8 * c == lanes, 1.0, 0.0).astype(BF)
        kaug[512 * c:512 * c + 512, :] = jnp.concatenate([part[:, :64], hot], axis=1)
        kvt[c] = part.astype(F32).T.astype(BF)
    qi = lax.broadcasted_iota(jnp.int32, (64, 64), 0)
    ki = lax.broadcasted_iota(jnp.int32, (64, 64), 1)
    bias[...] = jnp.where(jnp.logical_and(mask[0] != 0, ki < qi), 0.0, NEG)


def triangle():
    key = lax.broadcasted_iota(jnp.int32, (64, 256), 0)
    query = lax.broadcasted_iota(jnp.int32, (64, 256), 1) % 64
    return key <= query


def attend_kernel(
    blk, mask, kvr, qr, o_ref, ot_ref, lse_ref, kvs, kaug, kvt, bias, qs, qa, os, inv, order, oblk, tops, totals, mixes
):
    attention_setup(blk, mask, kvr, qr, kvs, kaug, kvt, bias, qs, inv, order, oblk)

    def diagonal(g):
        score, vals = [], []
        for u in range(4):
            i = oblk[4 * g + u]
            q = qs[order[4 * g + u]]
            row = jnp.broadcast_to(bias[pl.ds(i, 1), :], (64, 64)).astype(BF)
            qa[g, 64 * u:64 * u + 64, :] = jnp.concatenate([q, row], axis=1)
            kv = kvs[pl.ds(pl.multiple_of(i * 64, 64), 64), :]
            score.append(dot(kv[:, :64], q, NT))
            vals.append(kv[:, 64:])
        s = jnp.where(triangle(), jnp.concatenate(score, axis=1), NEG)
        top = jnp.max(s, axis=0, keepdims=True)
        p = jnp.exp(s - top)
        total = jnp.sum(p, axis=0, keepdims=True)
        pb = p.astype(BF)
        mix = jnp.concatenate([dot(vals[u], pb[:, 64 * u:64 * u + 64], TN) for u in range(4)], axis=1)
        tops[g], totals[g], mixes[g] = top, total, mix

    def diagonals(k, carry):
        for j in range(4):
            diagonal(4 * k + j)
        return carry

    lax.fori_loop(0, 2, diagonals, 0)

    def tile(g, carry):
        top, total, mix = tops[g], totals[g], mixes[g]
        queries = qa[g]

        def chunk(c, state):
            top, total, mix = state
            keys = kaug[pl.ds(pl.multiple_of(c * 512, 512), 512), :]
            s = dot(keys, queries, NT)
            new = jnp.maximum(top, jnp.max(s, axis=0, keepdims=True))
            shrink = jnp.exp(top - new)
            p = jnp.exp(s - new)
            total = total * shrink + jnp.sum(p, axis=0, keepdims=True)
            mix = mix * shrink + dot(kvt[c, 64:, :], p.astype(BF))
            return new, total, mix

        chunks = (oblk[4 * g + 3] + 7) // 8
        def pair(c, state):
            top, total, mix = state
            parts = [dot(kaug[pl.ds(pl.multiple_of(c * 1024 + 512 * k, 512), 512), :], queries, NT) for k in range(2)]
            new = top
            for s in parts:
                new = jnp.maximum(new, jnp.max(s, axis=0, keepdims=True))
            shrink = jnp.exp(top - new)
            total, mix = total * shrink, mix * shrink
            for k, s in enumerate(parts):
                p = jnp.exp(s - new)
                total += jnp.sum(p, axis=0, keepdims=True)
                mix += dot(kvt[2 * c + k, 64:, :], p.astype(BF))
            return new, total, mix

        top, total, mix = lax.fori_loop(0, chunks // 2, pair, (top, total, mix))
        top, total, mix = lax.fori_loop(chunks // 2 * 2, chunks, chunk, (top, total, mix))
        out = mix / total
        ot_ref[g] = out
        lse_ref[g] = top + jnp.log(total)
        back = out.T.astype(BF)
        for u in range(4):
            os[order[4 * g + u]] = back[64 * u:64 * u + 64, :]
        return carry

    lax.fori_loop(0, 8, tile, 0)
    for j in range(16):
        o_ref[j] = jnp.concatenate([os[2 * j], os[2 * j + 1]], axis=1)


def attention_scratch():
    return [
        pltpu.VMEM((4096, 128), BF),
        pltpu.VMEM((4096, 128), BF),
        pltpu.VMEM((8, 128, 512), BF),
        pltpu.VMEM((64, 64), F32),
        pltpu.VMEM((32, 64, 64), BF),
        pltpu.VMEM((8, 256, 128), BF),
        pltpu.VMEM((32, 64, 64), BF),
        pltpu.SMEM((64,), jnp.int32),
        pltpu.SMEM((72,), jnp.int32),
        pltpu.SMEM((72,), jnp.int32),
    ]


def attend(blk, mask, kvr, qr):
    return pl.pallas_call(
        attend_kernel,
        out_shape=[shp((16, 64, 128), BF), shp((8, 64, 256), F32), shp((8, 1, 256), F32)],
        in_specs=[SM, VM, VM, VM],
        out_specs=[VM] * 3,
        scratch_shapes=attention_scratch()
        + [pltpu.VMEM((8, 1, 256), F32), pltpu.VMEM((8, 1, 256), F32), pltpu.VMEM((8, 64, 256), F32)],
        compiler_params=pltpu.CompilerParams(vmem_limit_bytes=LIMIT),
        cost_estimate=pl.CostEstimate(flops=10 << 30, bytes_accessed=32 << 20, transcendentals=4 << 20),
        name="attend",
    )(blk, mask, kvr, qr)


def attend_back_kernel(
    blk, mask, kvr, qr, dor, ot_ref, lse_ref, dkv_ref, dq_ref,
    kvs, kaug, kvt, bias, qs, qa, dqs, inv, order, oblk, dos, qz, dz, dkv, deltas, dqt,
):
    attention_setup(blk, mask, kvr, qr, kvs, kaug, kvt, bias, qs, inv, order, oblk)
    for j in range(16):
        pair = dor[j]
        dos[2 * j] = pair[:, :64]
        dos[2 * j + 1] = pair[:, 64:]
    dkv[...] = jnp.zeros_like(dkv)
    zero = jnp.zeros((64, 64), BF)

    def diagonal(g):
        score, dprob, places, keys_own, q_own, d_own = [], [], [], [], [], []
        for u in range(4):
            i = oblk[4 * g + u]
            q = qs[order[4 * g + u]]
            do = dos[order[4 * g + u]]
            rows = slice(64 * u, 64 * u + 64)
            row = jnp.broadcast_to(bias[pl.ds(i, 1), :], (64, 64)).astype(BF)
            qa[g, rows, :] = jnp.concatenate([q, row], axis=1)
            qz[g, rows, :] = jnp.concatenate([q, zero], axis=1)
            dz[g, rows, :] = jnp.concatenate([zero, do], axis=1)
            at = pl.ds(pl.multiple_of(i * 64, 64), 64)
            kv = kvs[at, :]
            score.append(dot(kv[:, :64], q, NT))
            dprob.append(dot(kv[:, 64:], do, NT))
            places.append(at)
            keys_own.append(kv[:, :64])
            q_own.append(q)
            d_own.append(do)
        lse = lse_ref[g]
        dot_t = dz[g][:, 64:].astype(F32).T
        delta = jnp.sum(ot_ref[g] * dot_t, axis=0, keepdims=True)
        s = jnp.where(triangle(), jnp.concatenate(score, axis=1), NEG)
        p = jnp.exp(s - lse)
        ds = (p * (jnp.concatenate(dprob, axis=1) - delta)).astype(BF)
        pb = p.astype(BF)
        dq = []
        for u in range(4):
            lanes = slice(64 * u, 64 * u + 64)
            grad = jnp.concatenate([dot(ds[:, lanes], q_own[u]), dot(pb[:, lanes], d_own[u])], axis=1)
            dkv[places[u], :] += grad
            dq.append(dot(keys_own[u], ds[:, lanes], TN))
        deltas[g] = delta
        dqt[g] = jnp.concatenate(dq, axis=1)

    def diagonals(k, carry):
        for j in range(4):
            diagonal(4 * k + j)
        return carry

    lax.fori_loop(0, 2, diagonals, 0)

    def tile(g, carry):
        lse, delta = lse_ref[g], deltas[g]
        queries, qpad, dpad = qa[g], qz[g], dz[g]

        def chunk(c, dq):
            at = pl.ds(pl.multiple_of(c * 512, 512), 512)
            p = jnp.exp(dot(kaug[at, :], queries, NT) - lse)
            dp = dot(kvs[at, :], dpad, NT)
            ds = (p * (dp - delta)).astype(BF)
            dkv[at, :] += dot(ds, qpad) + dot(p.astype(BF), dpad)
            return dq + dot(kvt[c, :64, :], ds)

        chunks = (oblk[4 * g + 3] + 7) // 8
        dq = lax.fori_loop(0, chunks // 2, lambda c, dq: chunk(2 * c + 1, chunk(2 * c, dq)), dqt[g])
        dq = lax.fori_loop(chunks // 2 * 2, chunks, chunk, dq)
        back = (dq * 0.125).T.astype(BF)
        for u in range(4):
            dqs[order[4 * g + u]] = back[64 * u:64 * u + 64, :]
        return carry

    lax.fori_loop(0, 8, tile, 0)
    for j in range(16):
        dq_ref[j] = jnp.concatenate([dqs[2 * j], dqs[2 * j + 1]], axis=1)
    for s in range(64):
        at = pl.ds(pl.multiple_of(blk[s] * 64, 64), 64)
        dkv_ref[s // 2, (s % 2) * 64:(s % 2) * 64 + 64, :] = dkv[at, :].astype(BF)


def attend_back(blk, mask, kvr, qr, dor, ot, lse):
    return pl.pallas_call(
        attend_back_kernel,
        out_shape=[shp((32, 128, 128), BF), shp((16, 64, 128), BF)],
        in_specs=[SM] + [VM] * 6,
        out_specs=[VM] * 2,
        scratch_shapes=attention_scratch()
        + [
            pltpu.VMEM((32, 64, 64), BF),
            pltpu.VMEM((8, 256, 128), BF),
            pltpu.VMEM((8, 256, 128), BF),
            pltpu.VMEM((4096, 128), F32),
            pltpu.VMEM((8, 1, 256), F32),
            pltpu.VMEM((8, 64, 256), F32),
        ],
        compiler_params=pltpu.CompilerParams(vmem_limit_bytes=LIMIT),
        cost_estimate=pl.CostEstimate(flops=1 << 30, bytes_accessed=4 << 20, transcendentals=0),
        name="attend_back",
    )(blk, mask, kvr, qr, dor, ot, lse)


def norm_parts(v):
    center = v - jnp.mean(v, axis=1, keepdims=True)
    r = lax.rsqrt(jnp.mean(center * center, axis=1, keepdims=True) + EPS)
    return center * r, r


def norm_back(e, gain, z, r):
    g = e * gain
    return r * (g - jnp.mean(g, axis=1, keepdims=True) - z * jnp.mean(g * z, axis=1, keepdims=True))


def heart_kernel(*refs):
    o_ref, x_ref, e_ref, ln_ref, ln_own = refs[:5]
    shards = (refs[5:8], refs[8:11])
    qa, x1, x3, qb, y1, y3, diag_a, diag_b = refs[11:19]
    y_ref, dr_ref, zpay, gpay, gb_ref, dor = refs[19:25]
    cuts = (refs[25:28], refs[28:31])
    (wo, wi, wu, us, gs, nl, ob, orx, dos, rr, ll, cl, lt, mid,
     sw, sp, ss, rs, send_o, recv_o, send_do, recv_do, ls, lo) = refs[31:]
    zl, x, y, zh, co = place()
    w = zh * 2 + co
    flat = lax.axis_index("ctx") % 16
    where = [w, zh * 2 + 1 - co, (1 - zh) * 2 + co, (1 - zh) * 2 + 1 - co]
    core = device(zl, x, y, zh, 1 - co)
    bar = pltpu.get_barrier_semaphore()

    def plane(i):
        return {"ctx": zl * 16 + (flat + i) % 16}

    def greet_one(i, carry):
        pl.semaphore_signal(bar, inc=1, device_id=plane(i), device_id_type=MESH)
        return carry

    pl.semaphore_signal(bar, inc=1, device_id=core, device_id_type=MESH)
    lax.fori_loop(1, 16, greet_one, 0)
    copies = [[], [], []]
    for r, (a, b, c) in enumerate(shards):
        rows = pl.ds(pl.multiple_of(where[r] * 256, 256), 256)
        copies[0].append(pltpu.make_async_copy(a, wo.at[rows], sw.at[r, 0]))
        for k in range(4):
            cols = slice(1024 * k, 1024 * k + 1024)
            copies[1].append(pltpu.make_async_copy(b.at[:, cols], wi.at[k, rows], sw.at[r, 1 + k]))
        groups = pl.ds(where[r] * 8, 8)
        copies[2].append(pltpu.make_async_copy(c, wu.at[groups], sw.at[r, 5]))

    def spots(t, h, q):
        rows = pl.ds(pl.multiple_of(t * 256 + h * 128 + q * 32, 32), 32)
        return wo.at[rows], wi.at[:, rows], wu.at[t * 8 + h * 4 + q]

    quarters = [(qa, 0, x), (x1, 0, (x + 3) % 4), (x3, 0, (x + 1) % 4)]
    quarters += [(qb, 1, y), (y1, 1, (y + 3) % 4), (y3, 1, (y + 1) % 4)]
    held = [(where[2],) + q for q in quarters] + [(where[3], diag_a, 0, x), (where[3], diag_b, 1, y)]
    for n, (t, ref, h, q) in enumerate(held):
        to = spots(t, h, q)
        for k, src in enumerate((ref.at[0], ref.at[1:5], ref.at[5:9])):
            copies[k].append(pltpu.make_async_copy(src, to[k], sp.at[n, k]))
    for group in copies:
        for c in group:
            c.start()
    pl.semaphore_wait(bar, 16)
    wire = Wire(ss, rs)

    def over(src, dst, send, recv):
        def copy(i):
            return pltpu.make_async_remote_copy(
                src_ref=src.at[(flat + i) % 16], dst_ref=dst.at[flat], send_sem=send.at[i], recv_sem=recv.at[i],
                device_id=plane(i), device_id_type=MESH,
            )

        def start_one(i, carry):
            copy(i).start()
            return carry

        def wait_one(i, carry):
            copy(i).wait()
            return carry

        return start_one, wait_one

    start_o, wait_o = over(o_ref, orx, send_o, recv_o)
    lax.fori_loop(1, 16, start_o, 0)
    home = pltpu.make_async_copy(o_ref.at[flat], orx.at[flat], ls.at[0])
    home.start()
    shared = [[], [], []]
    passed = [[], [], []]
    ends = (
        (device(zl, (x + 1) % 4, y, zh, co), device(zl, (x + 3) % 4, y, zh, co)),
        (device(zl, x, (y + 1) % 4, zh, co), device(zl, x, (y + 3) % 4, zh, co)),
    )
    for k in range(3):
        for h in range(2):
            (one, _, q1), (three, _, q3) = quarters[3 * h + 1], quarters[3 * h + 2]
            up_to, down_to = spots(where[2], h, q1)[k], spots(where[2], h, q3)[k]
            if k == 0:
                passed[k].append([wire(one.at[0], up_to, ends[h][0])])
            else:
                first = 4 * k - 3
                passed[k].append([
                    wire(one.at[first:first + 2], up_to.at[0:2], ends[h][0]),
                    wire(three.at[first + 2:first + 4], down_to.at[2:4], ends[h][1]),
                ])
    for k in range(3):
        for n in (1, 2, 4, 5):
            ref, h, q = quarters[n]
            src = (ref.at[0], ref.at[1:5], ref.at[5:9])[k]
            shared[k].append(wire(src, spots(where[2], h, q)[k], core))

    def loaded(k):
        for c in copies[k]:
            c.wait()
        for c in shared[k]:
            c.wait_recv()

    home.wait()
    lax.fori_loop(1, 16, wait_o, 0)

    def pass_on(k):
        for h, at in enumerate((x, y)):
            for c in passed[k][h]:
                c.wait_recv()
            spot = spots(where[2], h, (at + 2) % 4)[k]
            shared[k].append(wire(spot, spot, core))

    pass_on(0)
    ln = jnp.concatenate([jnp.where(w == k, ln_own[...], ln_ref[k]) for k in range(4)], axis=1)
    gain0, gain1, bias0, bias1 = (ln[k:k + 1, :] for k in range(4))
    for h in range(16):
        pair = orx[h]
        ob[:64, 64 * h:64 * h + 64] = pair[:, :64]
        ob[64:, 64 * h:64 * h + 64] = pair[:, 64:]
    loaded(0)
    z0, r0 = norm_parts(x_ref[...].astype(F32) + dot(ob[...], wo[...]))
    n1 = z0 * gain0 + bias0
    nl[...] = n1.astype(BF)
    pass_on(1)
    loaded(1)
    pass_on(2)

    half = math.sqrt(0.5)

    def up(c, carry):
        u = dot(nl[...], wi[c])
        us[c] = u
        gs[:, pl.ds(pl.multiple_of(c * 1024, 1024), 1024)] = (0.5 * u * (1.0 + lax.erf(u * half))).astype(BF)
        return carry

    lax.fori_loop(0, 4, up, 0)
    loaded(2)

    def down(c, total):
        cols = pl.ds(pl.multiple_of(c * 1024, 1024), 1024)
        return total + dot(gs[:, cols], wu[pl.ds(c * 8, 8)].reshape(1024, 1024))

    r2 = lax.fori_loop(0, 4, down, n1)
    z1, r1 = norm_parts(r2)
    y_ref[...] = z1 * gain1 + bias1
    e = e_ref[...].astype(F32)
    dr2 = norm_back(e, gain1, z1, r1)
    dm = dr2.astype(BF)
    gb_ref[1:2, :] = jnp.sum(e * z1, axis=0, keepdims=True)
    gb_ref[3:4, :] = jnp.sum(e, axis=0, keepdims=True)

    def back(c, total):
        u = us[c]
        dg = dot(dm, wu[pl.ds(c * 8, 8)].reshape(1024, 1024), NT)
        slope = 0.5 * (1.0 + lax.erf(u * half)) + u * (jnp.exp(-0.5 * u * u) * (1.0 / math.sqrt(2 * math.pi)))
        du = (dg * slope).astype(BF)
        rr[0:128, 1024 * c:1024 * c + 1024] = du
        return total + dot(du, wi[c], NT)

    few = [pl.ds(pl.multiple_of(where[r] * 256, 256), 256) for r in range(4)]
    many = [pl.ds(pl.multiple_of(where[r] * 1024, 1024), 1024) for r in range(4)]
    for ref, rows, at, r in ((ll, 128, 0, 0), (ll, 128, 512, 2), (cl, 128, 0, 1), (cl, 128, 512, 3)):
        ref[:rows, at:at + 256] = nl[:, few[r]]
        ref[:rows, at + 256:at + 512] = ob[:, few[r]]
    near = [wire(cl, ll.at[128:256, :], core)]
    dn1 = dr2
    for c in range(4):
        dn1 = back(c, dn1)
        cols = slice(1024 * c, 1024 * c + 1024)
        near.append(wire(rr.at[0:128, cols], rr.at[128:256, cols], core))
    gb_ref[0:1, :] = jnp.sum(dn1 * z0, axis=0, keepdims=True)
    gb_ref[2:3, :] = jnp.sum(dn1, axis=0, keepdims=True)
    gb_ref[4:8, :] = jnp.zeros((4, 1024), F32)
    dr1 = norm_back(dn1, gain0, z0, r0)
    dr_ref[...] = dr1
    da = dr1.astype(BF)
    rr[0:128, 4096:5120] = da
    near.append(wire(rr.at[0:128, 4096:5120], rr.at[128:256, 4096:5120], core))
    do = dot(da, wo[...], NT).astype(BF)
    for h in range(16):
        lanes = slice(64 * h, 64 * h + 64)
        dos[h] = jnp.concatenate([do[:64, lanes], do[64:, lanes]], axis=1)
    start_do, wait_do = over(dos, dor, send_do, recv_do)
    lax.fori_loop(1, 16, start_do, 0)
    home = pltpu.make_async_copy(dos.at[flat], dor.at[flat], ls.at[1])
    home.start()
    zpay[:, 1024:2048] = dm
    for r, (ref, at) in enumerate(((gpay, 0), (gpay, 1024), (zpay, 0), (zpay, 2048))):
        ref[:, at:at + 1024] = gs[:, many[r]]
    for c in near:
        c.wait_recv()
    for k in range(4):
        lt[256 * k:256 * k + 256, :] = ll[:, 256 * k:256 * k + 256].astype(F32).T.astype(BF)
    out = []
    for z in range(2):
        mid[z, 0:256, :] = dot(lt[512 * z + 256:512 * z + 512, :], rr[:, 4096:5120]).astype(BF)
        for k in range(4):
            rows = slice(256 + 256 * k, 512 + 256 * k)
            mid[z, rows, :] = dot(lt[512 * z:512 * z + 256, :], rr[:, 1024 * k:1024 * k + 1024]).astype(BF)
    for h, (at, (own, plus, minus)) in enumerate(zip((x, y), cuts)):

        def rows(s, first, size):
            return pl.ds(pl.multiple_of(h * 640 + (at + s) % 4 * 160 + first, 16), size)

        for src, dst in (
            (rows(0, 0, 160), own),
            (rows(1, 0, 160), plus.at[:, :160]), (rows(2, 0, 80), plus.at[:, 160:]),
            (rows(3, 0, 160), minus.at[:, :160]), (rows(2, 80, 80), minus.at[:, 160:]),
        ):
            out.append(pltpu.make_async_copy(mid.at[:, src], dst, lo.at[len(out)]))
    for c in out:
        c.start()
    home.wait()
    lax.fori_loop(1, 16, wait_do, 0)
    for c in near:
        c.wait_send()
    for group in shared + [c for k in range(3) for c in passed[k]]:
        for c in group:
            c.wait_send()
    for c in out:
        c.wait()


def heart(o, tok, cot, lnf, lnp, shards, parts):
    cut = [shp((2, 160, 1024), BF), shp((2, 240, 1024), BF), shp((2, 240, 1024), BF)]
    n = 12 + 10 + 6 + 6
    return pl.pallas_call(
        heart_kernel,
        out_shape=[
            shp((128, 1024), F32), shp((128, 1024), F32),
            shp((128, 3072), BF), shp((128, 2048), BF), shp((8, 1024), F32), shp((16, 64, 128), BF),
        ] + cut + cut,
        in_specs=[ANY] + [VM] * 4 + [ANY] * 14,
        out_specs=[VM] * 5 + [ANY] * 7,
        scratch_shapes=[
            pltpu.VMEM((1024, 1024), BF),
            pltpu.VMEM((4, 1024, 1024), BF),
            pltpu.VMEM((32, 4, 32, 1024), BF),
            pltpu.VMEM((4, 128, 1024), F32),
            pltpu.VMEM((128, 4096), BF),
            pltpu.VMEM((128, 1024), BF),
            pltpu.VMEM((128, 1024), BF),
            pltpu.VMEM((16, 64, 128), BF),
            pltpu.VMEM((16, 64, 128), BF),
            pltpu.VMEM((256, 5120), BF),
            pltpu.VMEM((256, 1024), BF),
            pltpu.VMEM((128, 1024), BF),
            pltpu.VMEM((1024, 256), BF),
            pltpu.VMEM((2, 1280, 1024), BF),
            DMA((2, 6)), DMA((8, 3)), DMA((n,)), DMA((n,)), DMA((16,)), DMA((16,)), DMA((16,)), DMA((16,)),
            DMA((2,)), DMA((10,)),
        ],
        compiler_params=pltpu.CompilerParams(collective_id=5, has_side_effects=True, vmem_limit_bytes=LIMIT),
        cost_estimate=pl.CostEstimate(flops=16 << 30, bytes_accessed=32 << 20, transcendentals=2 << 20),
        name="heart",
    )(o, tok, cot, lnf, lnp, *shards[0], *shards[1], *parts)


class Spread:
    def __init__(self, wire, plus, minus, at, piece, bufs):
        self.wire, self.plus, self.minus, self.at, self.piece = wire, plus, minus, at, piece
        self.rp, self.rm, self.m, self.f = bufs

    def part(self, s, u):
        return self.piece((self.at + s) % 4, u)

    def start(self):
        self.a = self.wire(self.part(2, 0), self.m.at[0], self.plus)
        self.b = self.wire(self.part(2, 1), self.m.at[1], self.minus)
        self.c = self.wire(self.part(1, 1), self.rp.at[1], self.plus)
        self.d = self.wire(self.part(3, 0), self.rm.at[0], self.minus)

    def relay(self):
        self.a.wait_recv()
        self.f[0] = (self.part(1, 0)[...].astype(F32) + self.m[0].astype(F32)).astype(BF)
        self.e = self.wire(self.f.at[0], self.rp.at[0], self.plus)
        self.b.wait_recv()
        self.f[1] = (self.part(3, 1)[...].astype(F32) + self.m[1].astype(F32)).astype(BF)
        self.g = self.wire(self.f.at[1], self.rm.at[1], self.minus)

    def total(self):
        for c in (self.c, self.d, self.e, self.g):
            c.wait_recv()
        return [
            self.part(0, u)[...].astype(F32) + self.rp[u].astype(F32) + self.rm[u].astype(F32) for u in range(2)
        ]

    def sent(self):
        for c in (self.a, self.b, self.c, self.d, self.e, self.g):
            c.wait_send()


class Gather:
    def __init__(self, wire, plus, minus, at, block):
        self.wire, self.plus, self.minus, self.at, self.block = wire, plus, minus, at, block

    def send(self, s, u, peer):
        spot = self.block((self.at + s) % 4, u)
        return self.wire(spot, spot, peer)

    def start(self):
        self.p0 = self.send(0, 0, self.plus)
        self.m1 = self.send(0, 1, self.minus)
        self.p1 = self.send(0, 1, self.plus)
        self.m0 = self.send(0, 0, self.minus)

    def relay(self):
        self.p0.wait_recv()
        self.rp = self.send(3, 0, self.plus)
        self.m1.wait_recv()
        self.rm = self.send(1, 1, self.minus)

    def done(self):
        for c in (self.p1, self.m0, self.rp, self.rm):
            c.wait()
        for c in (self.p0, self.m1):
            c.wait_send()


class DirectSpread:
    def __init__(self, wire, peers, at, piece, bufs):
        self.wire, self.peers, self.at, self.piece, self.bufs = wire, peers, at, piece, bufs

    def start(self):
        self.copies = []
        for s in range(3):
            for u in range(2):
                src = self.piece((self.at + s + 1) % 4, u)
                self.copies.append(self.wire(src, self.bufs[s].at[u], self.peers[s]))

    def relay(self):
        pass

    def total(self):
        for c in self.copies:
            c.wait_recv()
        out = []
        for u in range(2):
            total = self.piece(self.at, u)[...].astype(F32)
            for s in range(3):
                total += self.bufs[s][u].astype(F32)
            out.append(total)
        return out

    def sent(self):
        for c in self.copies:
            c.wait_send()


class DirectGather:
    def __init__(self, wire, peers, at, block):
        self.wire, self.peers, self.at, self.block = wire, peers, at, block

    def start(self):
        self.copies = []
        for u in range(2):
            spot = self.block(self.at, u)
            for p in self.peers:
                self.copies.append(self.wire(spot, spot, p))

    def relay(self):
        pass

    def done(self):
        for c in self.copies:
            c.wait()


class Sum:
    direct = False

    def cut(self, g, rows):
        return g.at[rows]

    def __init__(self, g, hc, refs, wire, where, xp, yp, zp):
        bufs1, s1, bufs2, s2, self.r3, full = refs[:4], refs[4], refs[5:9], refs[9], refs[10], refs[11]
        zl, x, y, zh, co = where
        self.wire, self.zp, self.zl = wire, zp, zl
        self.s1, self.s2, self.last, self.full = s1, s2, s2, full
        hh = hc // 2
        first, second = (xp, yp), (yp, xp)
        self.at1, self.at2 = (x, y), (y, x)
        self.peers = [(first[h][0], first[h][2]) for h in range(2)]

        def rows(h, k, u):
            return pl.ds(pl.multiple_of(h * 4 * hc + k * hc + u * hh, 16), hh)

        def cols(k, width):
            return pl.ds(pl.multiple_of(k * width, 128), width)

        self.rows, self.cols = rows, cols

        def one(h):
            return lambda k, u: self.cut(g, rows(h, k, u))

        def two(h):
            return lambda k, u: s1.at[h, u, :, cols(k, 256)]

        def five(h):
            return lambda k, u: full.at[rows(h, self.at1[h], u), cols(k, 256)]

        def six(h):
            return lambda k, u: full.at[rows(h, k, u)]

        def ends(peers):
            return wire, peers[0], peers[2]

        if g is not None:
            self.one = [Spread(*ends(first[h]), self.at1[h], one(h), [r.at[h] for r in bufs1]) for h in range(2)]
        if self.direct:
            self.two = [DirectSpread(wire, second[h], self.at2[h], two(h), [r.at[h] for r in bufs2]) for h in range(2)]
            self.five = [DirectGather(wire, second[h], self.at2[h], five(h)) for h in range(2)]
        else:
            self.two = [Spread(*ends(second[h]), self.at2[h], two(h), [r.at[h] for r in bufs2]) for h in range(2)]
            self.five = [Gather(*ends(second[h]), self.at2[h], five(h)) for h in range(2)]
        self.six = [Gather(*ends(first[h]), self.at1[h], six(h)) for h in range(2)]

    def begin(self):
        for t in self.one:
            t.start()

    def relay(self):
        for t in self.one:
            t.relay()

    def totals(self, h):
        return self.one[h].total()

    def across(self):
        pass

    def settle(self):
        for t in self.one:
            t.sent()

    def steps(self):
        self.begin()
        yield
        self.relay()
        yield
        for h in range(2):
            for u, total in enumerate(self.totals(h)):
                self.s1[h, u] = total.astype(BF)
            self.two[h].start()
        yield
        for t in self.two:
            t.relay()
        yield
        for h in range(2):
            for u, total in enumerate(self.two[h].total()):
                self.s2[h, u] = total.astype(BF)
        self.across()
        yield
        three = []
        for h in range(2):
            self.ready(h)
            three.append(self.wire(self.last.at[h, :, :, self.cols(1 - self.zl, 128)], self.r3.at[h], self.zp))
        yield
        four = []
        for h in range(2):
            three[h].wait_recv()
            for u in range(2):
                total = self.last[h, u, :, self.cols(self.zl, 128)].astype(F32) + self.r3[h, u].astype(F32)
                spot = self.full.at[self.rows(h, self.at1[h], u), self.cols(self.at2[h] * 2 + self.zl, 128)]
                spot[...] = total.astype(BF)
                four.append(self.wire(spot, spot, self.zp))
        yield
        for h in range(2):
            four[2 * h].wait()
            four[2 * h + 1].wait()
            self.five[h].start()
        yield
        for t in self.five:
            t.relay()
        yield
        for h in range(2):
            self.five[h].done()
            self.six[h].start()
        yield
        for t in self.six:
            t.relay()
        yield
        for t in self.two:
            t.sent()
        for c in three:
            c.wait_send()
        self.settle()
        for t in self.six:
            t.done()
        yield

    def ready(self, h):
        pass


class PairSum(Sum):
    direct = True

    def cut(self, g, rows):
        return g.at[:, rows]

    def __init__(self, g, hc, refs, wire, where, xp, yp, zp, far):
        self.rf, self.s3 = refs[:2]
        super().__init__(g, hc, refs[2:], wire, where, xp, yp, zp)
        self.far, self.hh, self.last = far, hc // 2, self.s3

    def totals(self, h):
        return [t.reshape(2 * self.hh, 1024) for t in self.one[h].total()]

    def across(self):
        self.crossed = [self.wire(self.s2.at[h, :, self.hh:], self.rf.at[h], self.far) for h in range(2)]

    def ready(self, h):
        self.crossed[h].wait_recv()
        for u in range(2):
            self.s3[h, u] = (self.s2[h, u, :self.hh].astype(F32) + self.rf[h, u].astype(F32)).astype(BF)

    def settle(self):
        for t in self.one:
            t.sent()
        for c in self.crossed:
            c.wait_send()


class BegunSum(PairSum):
    direct = False

    def __init__(self, hc, refs, wire, where, xp, yp, zp, far, own, plus, minus):
        self.own, self.fwd = refs[:2]
        super().__init__(None, hc, list(refs[2:4]) + [None] * 4 + list(refs[4:]), wire, where, xp, yp, zp, far)
        self.plus, self.minus = plus, minus

    def begin(self):
        hc = 2 * self.hh
        self.passed = []
        for h in range(2):
            plus, minus = self.peers[h]
            self.passed.append((
                self.wire(self.plus[h].at[:, hc:], self.fwd.at[h, 0], plus),
                self.wire(self.minus[h].at[:, hc:], self.fwd.at[h, 1], minus),
            ))

    def relay(self):
        pass

    def totals(self, h):
        hh = self.hh
        for c in self.passed[h]:
            c.wait_recv()
        out = []
        for u in range(2):
            rows = slice(u * hh, u * hh + hh)
            total = self.own[h, 0, :, rows].astype(F32) + self.own[h, 1, :, rows].astype(F32)
            total += self.own[h, 2, :, rows].astype(F32) + self.fwd[h, u].astype(F32)
            out.append(total.reshape(2 * hh, 1024))
        return out

    def settle(self):
        for c in self.crossed:
            c.wait_send()
        for pair in self.passed:
            for c in pair:
                c.wait_send()


class FirstSum:
    def __init__(self, g, refs, wire, where, xp, yp, zp):
        bufs1, s1, bufs2, rz, half, full = refs[:4], refs[4], refs[5:9], refs[9], refs[10], refs[11]
        zl, x, y, zh, co = where
        self.g, self.wire, self.zp, self.zl = g, wire, zp, zl
        self.s1, self.rz, self.half, self.full = s1, rz, half, full
        first, second = (xp, yp), (yp, xp)
        self.at1, self.at2 = (x, y), (y, x)

        def cols(k):
            return pl.ds(pl.multiple_of(k * 256, 128), 256)

        def one(h):
            return lambda k, u: half.at[pl.ds(pl.multiple_of(h * 256 + k * 64 + u * 32, 32), 32)]

        def two(h):
            return lambda k, u: s1.at[h, u, :, cols(k)]

        def rows(h, k, z):
            return pl.ds(pl.multiple_of(z * 512 + h * 256 + k * 64, 64), 64)

        def five(h):
            return lambda k, z: full.at[rows(h, self.at1[h], z), cols(k)]

        def six(h):
            return lambda k, z: full.at[rows(h, k, z)]

        self.spot = lambda h: full.at[rows(h, self.at1[h], zl), cols(self.at2[h])]
        self.one = [Spread(wire, first[h][0], first[h][2], self.at1[h], one(h), [r.at[h] for r in bufs1]) for h in range(2)]
        self.two = [DirectSpread(wire, second[h], self.at2[h], two(h), [r.at[h] for r in bufs2]) for h in range(2)]
        self.five = [Gather(wire, second[h][0], second[h][2], self.at2[h], five(h)) for h in range(2)]
        self.six = [Gather(wire, first[h][0], first[h][2], self.at1[h], six(h)) for h in range(2)]

    def steps(self):
        zs = []
        for h in range(2):
            src = self.g.at[pl.ds(pl.multiple_of((1 - self.zl) * 512 + h * 256, 256), 256)]
            zs.append(self.wire(src, self.rz.at[h], self.zp))
        yield
        for h in range(2):
            zs[h].wait_recv()
            mine = self.g[pl.ds(pl.multiple_of(self.zl * 512 + h * 256, 256), 256), :]
            self.half[256 * h:256 * h + 256, :] = (mine.astype(F32) + self.rz[h].astype(F32)).astype(BF)
            self.one[h].start()
        yield
        for t in self.one:
            t.relay()
        yield
        for h in range(2):
            for u, total in enumerate(self.one[h].total()):
                self.s1[h, u] = total.astype(BF)
            self.two[h].start()
        yield
        four = []
        for h in range(2):
            spot = self.spot(h)
            spot[...] = jnp.concatenate(self.two[h].total(), axis=0).astype(BF)
            four.append(self.wire(spot, spot, self.zp))
        yield
        for h in range(2):
            four[h].wait()
            self.five[h].start()
        yield
        for t in self.five:
            t.relay()
        yield
        for h in range(2):
            self.five[h].done()
            self.six[h].start()
        yield
        for t in self.six:
            t.relay()
        yield
        for t in self.one + self.two:
            t.sent()
        for c in zs:
            c.wait_send()
        for t in self.six:
            t.done()
        yield


SUM_COPIES = 2 + 12 + 12 + 2 + 12 + 12


BEGUN_COPIES = 4 + 12 + 2 + 2 + 4 + 12 + 12
PAIR_COPIES = 12 + 12 + 2 + 2 + 4 + 12 + 12


def first_scratch():
    return (
        [pltpu.VMEM((2, 2, 32, 1024), BF)] * 5
        + [pltpu.VMEM((2, 2, 32, 256), BF)] * 4
        + [pltpu.VMEM((2, 256, 1024), BF), pltpu.VMEM((512, 1024), BF)]
    )


def pair_scratch(rows, begun):
    hh = rows // 16
    begin = [pltpu.VMEM((2, 3, 2, 2 * hh, 1024), BF), pltpu.VMEM((2, 2, 2, hh, 1024), BF)]
    first = [pltpu.VMEM((2, 2, 2, hh, 1024), BF)] * 4
    return (
        (begin if begun else [])
        + [pltpu.VMEM((2, 2, hh, 256), BF)] * 2
        + ([] if begun else first)
        + [pltpu.VMEM((2, 2, 2 * hh, 1024), BF)]
        + [pltpu.VMEM((2, 2, 2 * hh, 256), BF)] * 4
        + [pltpu.VMEM((2, 2, 2 * hh, 256), BF), pltpu.VMEM((2, 2, hh, 128), BF)]
    )


def finish_kernel(*refs):
    dkvp, dqp, dr_ref, gb, wall, gpay, zpay, zr, xs, x_ref = refs[:10]
    got = ((refs[10], refs[13]), (refs[11], refs[14]), (refs[12], refs[15]))

    gt, io_full, u_full, tail_full, s_vec = refs[16:21]
    io_refs = list(refs[21:32]) + [io_full]
    u_refs, tail_refs = list(refs[32:43]) + [u_full], list(refs[43:56]) + [tail_full]
    (dkv, zb, sb, dq, weights, ll2, rr2, lt2, mid, pay, ll, rr, tail, v0, vf, v1, vx, vy, vz, tx, ty,
     sz, rz, sw, rw, sn, rn, ss, rs, ls, lw) = refs[56:]
    scale = 1.0 / math.sqrt(16384)
    where = place()
    zl, x, y, zh, co = where
    w = zh * 2 + co
    me = lax.axis_index("ctx")
    flat = me % 16
    core = device(zl, x, y, zh, 1 - co)
    far = device(zl, x, y, 1 - zh, co)
    xp = [device(zl, (x + s) % 4, y, zh, co) for s in (1, 2, 3)]
    yp = [device(zl, x, (y + s) % 4, zh, co) for s in (1, 2, 3)]
    zp = device(1 - zl, x, y, zh, co)
    bar = pltpu.get_barrier_semaphore()

    def greet_one(i, carry):
        pl.semaphore_signal(bar, inc=1, device_id={"ctx": zl * 16 + (flat + i) % 16}, device_id_type=MESH)
        return carry

    for p in (core, far, zp):
        pl.semaphore_signal(bar, inc=1, device_id=p, device_id_type=MESH)
    lax.fori_loop(1, 16, greet_one, 0)

    mine = [pl.ds(pl.multiple_of(k * 256, 256), 256) for k in (w, (1 - zh) * 2 + co)]
    parts = []
    for h in range(2):
        for n in range(3):
            parts.append(pltpu.make_async_copy(got[n][h].at[:, :160], io_refs[0].at[h, n], ls.at[10 + 3 * h + n]))
    local = [
        pltpu.make_async_copy(gpay.at[:, :1024], ll2.at[0:128, :], ls.at[0]),
        pltpu.make_async_copy(zpay.at[:, 1024:2048], rr2.at[0:128, :], ls.at[1]),
        pltpu.make_async_copy(zr.at[:, :1024], ll2.at[256:384, :], ls.at[2]),
        pltpu.make_async_copy(zr.at[:, 1024:2048], rr2.at[256:384, :], ls.at[3]),
    ]
    for k in range(2):
        cols = slice(256 * k, 256 * k + 256)
        local.append(pltpu.make_async_copy(x_ref.at[:, mine[k]], ll.at[0:128, cols], ls.at[4 + k]))
        local.append(pltpu.make_async_copy(xs.at[k], ll.at[128:256, cols], ls.at[6 + k]))
    for c in local + parts:
        c.start()
    loads = [pltpu.make_async_copy(wall, weights, lw.at[0])]
    loads[0].start()
    pl.semaphore_wait(bar, 18)

    def narrow_copy(i):
        p = (flat + i) % 16
        return pltpu.make_async_remote_copy(
            src_ref=dqp.at[p], dst_ref=dq.at[flat], send_sem=sn.at[i], recv_sem=rn.at[i],
            device_id={"ctx": zl * 16 + p}, device_id_type=MESH,
        )

    def z_copy(i):
        return pltpu.make_async_remote_copy(
            src_ref=dkvp.at[(1 - zl) * 16 + (flat + i) % 16], dst_ref=zb.at[i], send_sem=sz.at[i], recv_sem=rz.at[i],
            device_id=zp, device_id_type=MESH,
        )

    def wide_copy(i):
        p = (flat + i) % 16
        return pltpu.make_async_remote_copy(
            src_ref=sb.at[i], dst_ref=dkv.at[flat], send_sem=sw.at[i], recv_sem=rw.at[i],
            device_id={"ctx": zl * 16 + p}, device_id_type=MESH,
        )

    def start(make):
        def one(i, carry):
            make(i).start()
            return carry
        return one

    def wait(make):
        def one(i, carry):
            make(i).wait()
            return carry
        return one

    def both(i):
        z_copy(i).wait_recv()
        return (dkvp[zl * 16 + (flat + i) % 16].astype(F32) + zb[i].astype(F32)).astype(BF)

    def pass_on(i, carry):
        sb[i] = both(i)
        wide_copy(i).start()
        return carry

    def sent(i, carry):
        z_copy(i).wait_send()
        return carry

    lax.fori_loop(1, 16, start(z_copy), 0)
    z_copy(0).start()
    lax.fori_loop(1, 16, start(narrow_copy), 0)
    home = [pltpu.make_async_copy(dqp.at[flat], dq.at[flat], ls.at[9])]
    for c in home:
        c.start()
    wire = Wire(ss, rs)
    near = [
        wire(gpay.at[:, 1024:], ll2.at[128:256, :], core),
        wire(zpay.at[:, 1024:2048], rr2.at[128:256, :], core),
        wire(zr.at[:, 2048:], ll2.at[384:512, :], core),
        wire(zr.at[:, 1024:2048], rr2.at[384:512, :], core),
    ]
    io = BegunSum(160, io_refs, wire, where, xp, yp, zp, far, *got).steps()
    big = FirstSum(mid, u_refs, wire, where, xp, yp, zp).steps()
    small = PairSum(tail, 96, tail_refs, wire, where, xp, yp, zp, far).steps()
    next(io)
    next(io)
    for c in local:
        c.wait()
    lt = ll[...].astype(F32).T.astype(BF)
    for c in near:
        c.wait()
    for k in range(4):
        lt2[256 * k:256 * k + 256, :] = ll2[:, 256 * k:256 * k + 256].astype(F32).T.astype(BF)
    for k in range(4):
        rows = slice(256 * k, 256 * k + 256)
        mid[rows, :] = dot(lt2[rows, :], rr2[...]).astype(BF)
    lax.fori_loop(1, 16, pass_on, 0)
    dkv[flat] = both(0)
    next(big)
    for c in parts:
        c.wait()
    next(io)

    for c in home:
        c.wait()
    lax.fori_loop(1, 16, wait(wide_copy), 0)
    lax.fori_loop(1, 16, wait(narrow_copy), 0)
    lax.fori_loop(0, 16, sent, 0)
    for h in range(16):
        lanes = slice(64 * h, 64 * h + 64)
        pair = dq[h]
        pay[:64, lanes] = pair[:, :64]
        pay[64:128, lanes] = pair[:, 64:]
        pair = dkv[h]
        pay[:128, 1024 + 64 * h:1088 + 64 * h] = pair[:, :64]
        pay[:128, 2048 + 64 * h:2112 + 64 * h] = pair[:, 64:]
    pay[128:144, :1024] = jnp.concatenate([gb[...], jnp.zeros((8, 1024), F32)], axis=0).astype(BF)
    pay[128:144, 1024:] = jnp.zeros((16, 2048), BF)
    to_core = wire(pay, rr, core)
    next(io)
    for c in loads:
        c.wait()
    for k in range(4):
        cols = slice(256 * k, 256 * k + 256)
        total = dr_ref[:, cols]
        for m in range(3):
            total += dot(pay[:128, 1024 * m:1024 * m + 1024], weights[k, m], NT)
        gt[:, cols] = total
    to_core.wait_recv()
    for z in range(2):
        for m in range(3):
            cols = slice(1024 * m, 1024 * m + 1024)
            total = dot(lt[256 * z:256 * z + 256, :128], pay[:128, cols])
            total += dot(lt[256 * z:256 * z + 256, 128:], rr[:128, cols])
            tail[z, 256 * m:256 * m + 256, :] = total.astype(BF)
    next(small)
    next(io)
    for z in range(2):
        v0[z] = (pay[128:144, mine[z]].astype(F32) + rr[128:144, mine[z]].astype(F32))[:8]
    vfar = wire(v0.at[1], vf, far)
    next(big)
    next(io)
    next(small)
    next(big)
    next(io)
    vfar.wait_recv()
    v1[...] = v0[0] + vf[...]
    vone = [wire(v1, vx.at[s], xp[s]) for s in range(3)]
    next(small)
    next(io)
    next(big)
    next(small)
    next(io)
    for c in vone:
        c.wait_recv()
    tx[...] = v1[...] + vx[0] + vx[1] + vx[2]
    vtwo = [wire(tx, vy.at[s], yp[s]) for s in range(3)]
    next(small)
    next(big)
    next(io)
    next(small)
    next(big)
    for c in vtwo:
        c.wait_recv()
    ty[...] = tx[...] + vy[0] + vy[1] + vy[2]
    vthree = wire(ty, vz, zp)
    next(small)
    next(big)
    next(small)
    next(big)
    next(io)
    next(small)
    next(small)
    next(big)
    vthree.wait()
    s_vec[...] = (ty[...] + vz[...]) * scale
    for c in vone + vtwo + [to_core, vfar]:
        c.wait_send()
    next(small)
    next(io)
    next(big)
    next(small)


def finish(dkvp, dqp, dr, gb, wall, gpay, zpay, zr, xs, tok, parts):
    n = SUM_COPIES + BEGUN_COPIES + PAIR_COPIES + 4 + 2 + 7
    return pl.pallas_call(
        finish_kernel,
        out_shape=[
            shp((128, 1024), F32), shp((1280, 1024), BF), shp((1024, 1024), BF), shp((768, 1024), BF), shp((8, 256), F32),
        ],
        in_specs=[VM, ANY, VM, VM] + [ANY] * 12,
        out_specs=[VM] * 5,
        scratch_shapes=pair_scratch(1280, True) + first_scratch() + pair_scratch(768, False) + [
            pltpu.VMEM((16, 128, 128), BF), pltpu.VMEM((16, 128, 128), BF), pltpu.VMEM((16, 128, 128), BF),
            pltpu.VMEM((16, 64, 128), BF), pltpu.VMEM((4, 3, 256, 1024), BF),
            pltpu.VMEM((512, 1024), BF), pltpu.VMEM((512, 1024), BF), pltpu.VMEM((1024, 512), BF),
            pltpu.VMEM((1024, 1024), BF), pltpu.VMEM((144, 3072), BF),
            pltpu.VMEM((256, 512), BF), pltpu.VMEM((144, 3072), BF), pltpu.VMEM((2, 768, 1024), BF),
            pltpu.VMEM((2, 8, 256), F32), pltpu.VMEM((8, 256), F32), pltpu.VMEM((8, 256), F32),
            pltpu.VMEM((3, 8, 256), F32), pltpu.VMEM((3, 8, 256), F32),
            pltpu.VMEM((8, 256), F32), pltpu.VMEM((8, 256), F32), pltpu.VMEM((8, 256), F32),
            DMA((16,)), DMA((16,)), DMA((16,)), DMA((16,)), DMA((16,)), DMA((16,)),
            DMA((n,)), DMA((n,)), DMA((16,)), DMA((1,)),
        ],
        compiler_params=pltpu.CompilerParams(collective_id=6, has_side_effects=True, vmem_limit_bytes=LIMIT),
        name="finish",
    )(dkvp, dqp, dr, gb, wall, gpay, zpay, zr, xs, tok, *parts)


def scale_kernel(o, i0, i1, i2, i3, u, q, k, v, out_q, out_k, out_v, out_o, out_i, out_u):
    scale = 1.0 / math.sqrt(16384)
    for src, dst in ((q, out_q), (k, out_k), (v, out_v), (o, out_o), (u, out_u)):
        dst[...] = src[...].astype(F32) * scale
    for n, src in enumerate((i0, i1, i2, i3)):
        out_i[:, 1024 * n:1024 * n + 1024] = src[...].astype(F32) * scale


def scaled(io, u, tail):
    def rows(first, n=32):
        return pl.BlockSpec((n, 1024), lambda j: (first // n + j, 0))

    return pl.pallas_call(
        scale_kernel,
        grid=(8,),
        out_shape=[shp((256, 1024), F32)] * 4 + [shp((256, 4096), F32), shp((1024, 1024), F32)],
        in_specs=[rows(0)] + [rows(256 + 256 * k) for k in range(4)] + [rows(0, 128)] + [rows(256 * k) for k in range(3)],
        out_specs=[rows(0)] * 4 + [pl.BlockSpec((32, 4096), lambda j: (j, 0)), rows(0, 128)],
        compiler_params=pltpu.CompilerParams(vmem_limit_bytes=LIMIT),
        name="scaled",
    )(*[io] * 5, u, *[tail] * 3)


FLIP_CORE = [(0, 1), (1, 0), (2, 3), (3, 2)]
FLIP_FAR = [(0, 2), (2, 0), (1, 3), (3, 1)]


def along_x(s):
    return [(c, c // 16 * 16 + (c // 4 + s) % 4 * 4 + c % 4) for c in range(32)]


def along_y(s):
    return [(c, c // 4 * 4 + (c + s) % 4) for c in range(32)]


def body(
    tokens, w_query, w_key, w_value, w_output, w_inner, w_outer, ln_gain, ln_bias, block_mask, block_pairs, cotangent,
):
    tok = tokens.reshape(128, 1024)
    cot = cotangent.reshape(128, 1024)
    lnp = jnp.concatenate([ln_gain, ln_bias, jnp.zeros((4, 256), F32)], axis=0)
    blk = block_pairs.reshape(-1)
    own = (w_query, w_key, w_value)
    outer = w_outer.reshape(8, 4, 32, 1024)
    wall, xs, lnf, *rest = front(tok, own, lnp, w_output, w_inner, outer)
    core_shard, (qa, qb, diag_a, diag_b, kvr, qr) = rest[:3], rest[3:]
    x1, x3 = (lax.ppermute(qa, "ctx", along_x(s)) for s in (1, 3))
    y1, y3 = (lax.ppermute(qb, "ctx", along_y(s)) for s in (1, 3))
    o, ot, lse = attend(blk, block_mask, kvr, qr)
    x1, x3, y1, y3, o = lax.optimization_barrier((x1, x3, y1, y3, o))
    y_out, dr1, zpay, gpay, gb, dor, own_a, plus_a, minus_a, own_b, plus_b, minus_b = heart(
        o, tok, cot, lnf, lnp, ((w_output, w_inner, outer), core_shard), (qa, x1, x3, qb, y1, y3, diag_a, diag_b)
    )
    zr = lax.ppermute(zpay, "wsh", FLIP_FAR)
    plus_a = lax.ppermute(plus_a, "ctx", along_x(1))
    minus_a = lax.ppermute(minus_a, "ctx", along_x(3))
    plus_b = lax.ppermute(plus_b, "ctx", along_y(1))
    minus_b = lax.ppermute(minus_b, "ctx", along_y(3))
    dkvp, dqp = attend_back(blk, block_mask, kvr, qr, dor, ot, lse)
    zr, plus_a, minus_a, plus_b, minus_b, dkvp = lax.optimization_barrier((zr, plus_a, minus_a, plus_b, minus_b, dkvp))
    grad_tok, io, u, tail, s_vec = finish(
        dkvp, dqp, dr1, gb, wall, gpay, zpay, zr, xs, tok, (own_a, plus_a, minus_a, own_b, plus_b, minus_b)
    )
    s_q, s_k, s_v, s_o, s_i, s_u = scaled(io, u, tail)
    out_shape = tokens.shape
    return (
        y_out.reshape(out_shape), grad_tok.reshape(out_shape), s_q, s_k, s_v, s_o, s_i, s_u, s_vec[0:2], s_vec[2:4],
    )


def solution(mesh):
    return jax.shard_map(
        body,
        mesh=mesh,
        in_specs=(
            P("wsh", "ctx", None, None),
            P("wsh", None), P("wsh", None), P("wsh", None), P("wsh", None), P("wsh", None), P("wsh", None),
            P(None, "wsh"), P(None, "wsh"),
            P("wsh", None, None),
            P(),
            P("wsh", "ctx", None, None),
        ),
        out_specs=(
            P("wsh", "ctx", None, None), P("wsh", "ctx", None, None),
            P("wsh", None), P("wsh", None), P("wsh", None), P("wsh", None), P("wsh", None), P("wsh", None),
            P(None, "wsh"), P(None, "wsh"),
        ),
        check_vma=False,
    )
```
